128 devices in a mesh: dp: 32 (over x, z, core), hid: 4 (over y).
Axes of the slice: x: 4, y: 4, z: 4, core: 2. Of those that a mesh axis runs over, the one named last changes fastest.
Arguments:
- tokens: bfloat16 [16384, 1024], P(('dp', 'hid')), may hold values from -6 to 6
- w_query: bfloat16 [1024, 1024], replicated, may hold values from -0.1875 to 0.1875
- w_key: bfloat16 [1024, 512], replicated, may hold values from -0.1875 to 0.1875
- w_value: bfloat16 [1024, 512], replicated, may hold values from -0.1875 to 0.1875
- w_output: bfloat16 [1024, 1024], replicated, may hold values from -1 to 1
- gain_attn: float32 [1024], replicated, may hold values from 0.5 to 1.5
- gain_moe: float32 [1024], replicated, may hold values from 0.5 to 1.5
- router: bfloat16 [1024, 32], replicated, may hold values from -0.09375 to 0.09375
- w_gate: bfloat16 [32, 1024, 512], P('dp', None, 'hid'), may hold values from -0.1875 to 0.1875
- w_up: bfloat16 [32, 1024, 512], P('dp', None, 'hid'), may hold values from -0.1875 to 0.1875
- w_down: bfloat16 [32, 512, 1024], P('dp', 'hid'), may hold values from -0.75 to 0.75
- cotangent: bfloat16 [16384, 1024], P(('dp', 'hid')), may hold values from -6 to 6
- routes: int32 [16384, 8], P(('dp', 'hid')), may hold values from 0 to 31, all different within a row; in each aligned block of 128 rows (0 to 127, 128 to 255, ...) at most 48 rows name the same one
- lengths: int32 [32], P('dp'), may hold values from 385 to 512, as said below
Outputs:
- layer_out: bfloat16 [16384, 1024], P(('dp', 'hid'))
- grad_input: float32 [16384, 1024], P(('dp', 'hid'))
- grad_w_query: float32 [1024, 1024], replicated
- grad_w_key: float32 [1024, 512], replicated
- grad_w_value: float32 [1024, 512], replicated
- grad_w_output: float32 [1024, 1024], replicated
- grad_gain_attn: float32 [1024], replicated
- grad_gain_moe: float32 [1024], replicated
- grad_router: float32 [1024, 32], replicated
- grad_gate: float32 [32, 1024, 512], P('dp', None, 'hid')
- grad_up: float32 [32, 1024, 512], P('dp', None, 'hid')
- grad_down: float32 [32, 512, 1024], P('dp', 'hid')
- counts: int32 [32], replicated
The draws below stay inside these ranges and needn't reach their ends.
Inputs may be any that keep to these rules, and one draw needn't show every extreme that they name: `routes`: each row names 8 different experts. Among the 128 rows of one device no expert is named more than 48 times, and in every draw some expert is named exactly 48 times by the rows of some device. `lengths`: every length exceeds 3 * 128; in every draw some sequence has exactly 512 tokens.
All inputs are finite; a program needn't handle non-finite values.
Results may differ from the reference program's by a relative error of at most 0.018.
Values may be sent and summed in bfloat16 or wider, within the bound.
A program may use at most 256 MiB of HBM per device.

```python
import math
import jax
import jax.numpy as jnp
import numpy as np
from jax import lax

D = 1024
HEADS = 16
KV_HEADS = 8
HEAD_DIM = 64
EXPERTS = 32
TOP = 8
FF = 512
TOK_DEV = 128
CAP = 48
SEQ_LEN = 512
NSEQ = 32
TOKENS = 16384
DEVICES = 128


def draw_lengths(key, part):
    key = jax.random.fold_in(key, 11)
    length_key, which_key = jax.random.split(key)
    lowest = 3 * SEQ_LEN // 4 + 1
    drawn = jax.random.randint(length_key, (NSEQ,), lowest, SEQ_LEN + 1, dtype=jnp.int32)
    chosen = jax.random.randint(which_key, (), 0, NSEQ, dtype=jnp.int32)
    return jnp.where(jnp.arange(NSEQ, dtype=jnp.int32) == chosen, SEQ_LEN, drawn).astype(jnp.int32)


def block_levels(rng, extent, shards, smallest, top_value):
    level = 1.0
    for position, parts in shards:
        heights = jax.random.uniform(jax.random.fold_in(jax.random.fold_in(rng, 6), position), (parts,), jnp.float32, smallest / len(shards), top_value / len(shards))
        level = level * jnp.repeat(jnp.exp(heights), extent[position] // parts).reshape((-1,) + (1,) * (len(extent) - 1 - position))
    return level


def deal_out(key, own, number, rows, amount, top, limit, lean):
    ranking = jax.random.permutation(key, amount)
    crowded, ordinary = shares(amount, rows * top, limit, lean, True), shares(amount, rows * top, limit, lean, False)
    places = jnp.arange(amount)

    def named(sizes, offset_by):
        used = int((sizes > 0).sum())
        fixed = max(1, used // 4)
        moved = fixed + (places - fixed + offset_by * (used - fixed)) % max(1, amount - fixed)
        return jnp.zeros((amount,), jnp.int32).at[ranking[jnp.where(places < fixed, places, moved)]].set(jnp.asarray(sizes, jnp.int32))

    sizes = jnp.where(number % 4 == 0, named(crowded, number // 4), named(ordinary, number - number // 4 - 1))
    mixed = jax.random.permutation(jax.random.fold_in(own, 3), amount)
    giver, sink = mixed[0:amount // 2 * 2:2], mixed[1:amount // 2 * 2:2]
    margin = jnp.minimum(sizes[giver] - 1, limit - sizes[sink]) // 2
    margin = jnp.where((giver == ranking[0]) | (sink == ranking[0]) | (sizes[sink] == 0), 0, jnp.maximum(margin, 0))
    moved = jax.random.randint(jax.random.fold_in(own, 4), (amount // 2,), 0, 1 << 20) % (margin + 1)
    sizes = sizes.at[giver].add(-moved).at[sink].add(moved)
    members = jnp.searchsorted(jnp.cumsum(sizes), jnp.arange(rows * top), side="right").astype(jnp.int32)
    grid = members.reshape(top, rows).T
    grid = grid[jax.random.permutation(jax.random.fold_in(own, 1), rows)]
    offset_by = jax.random.randint(jax.random.fold_in(own, 2), (rows, 1), 0, top)
    return jnp.take_along_axis(grid, (jnp.arange(top)[None, :] + offset_by) % top, axis=1)


def shares(number_of, total, most, slope, full):
    loads = [(1 << 20) // math.isqrt(grade ** slope) + 1 for grade in range(1, number_of + 1)]
    largest = most if full else min(most, max(-(-total // number_of), total * loads[0] // sum(loads)))
    least = 1 if total - largest >= number_of - 1 else 0
    holding, surplus = [largest] + [least] * (number_of - 1), total - largest - least * (number_of - 1)
    while surplus > 0:
        candidates = [i for i in range(1, number_of) if holding[i] < largest] or [i for i in range(1, number_of) if holding[i] < most]
        pool, remaining = sum([loads[i] for i in candidates]), surplus
        for i in candidates:
            more = min(most - holding[i], max(1, remaining * loads[i] // pool), surplus)
            holding[i] = holding[i] + more
            surplus = surplus - more
    return np.array(holding)


def noise(stream_key, shape, scale, most, pieces=(), kind=jnp.bfloat16):
    gain = block_levels(stream_key, shape, pieces, -0.22, 0.18) if pieces else 1.0
    values = jax.random.normal(stream_key, shape, jnp.float32) * scale * gain
    return jnp.minimum(jnp.maximum(values, -most), most).astype(kind)


def setup_inputs(seed: int = 0) -> dict:
    seeds = jax.random.split(jax.random.key(seed), 15)
    tokens = noise(seeds[0], (TOKENS, D), 1.0, 6.0, ((0, 128),))
    w_query = noise(seeds[1], (D, HEADS * HEAD_DIM), D ** -0.5, 0.1875)
    w_key = noise(seeds[2], (D, KV_HEADS * HEAD_DIM), D ** -0.5, 0.1875)
    w_value = noise(seeds[3], (D, KV_HEADS * HEAD_DIM), D ** -0.5, 0.1875)
    w_output = noise(seeds[4], (HEADS * HEAD_DIM, D), 32 ** -0.5, 1.0)
    gain_attn = jnp.clip(1.0 + 0.1 * jax.random.normal(seeds[5], (D,), jnp.float32), 0.5, 1.5)
    gain_moe = jnp.clip(1.0 + 0.1 * jax.random.normal(seeds[6], (D,), jnp.float32), 0.5, 1.5)
    router = noise(seeds[7], (D, EXPERTS), 0.015625, 0.09375)
    w_gate = noise(seeds[8], (EXPERTS, D, FF), D ** -0.5, 0.1875, ((0, 32), (2, 4)))
    w_up = noise(seeds[9], (EXPERTS, D, FF), D ** -0.5, 0.1875, ((0, 32), (2, 4)))
    w_down = noise(seeds[10], (EXPERTS, FF, D), 64 ** -0.5, 0.75, ((0, 32), (1, 4)))
    cotangent = noise(seeds[11], (TOKENS, D), 1.0, 6.0, ((0, 128),))
    routes_keys = jax.random.split(jax.random.fold_in(seeds[12], 1), TOKENS // TOK_DEV)
    routes_turns = jax.random.permutation(jax.random.fold_in(seeds[12], 3), TOKENS // TOK_DEV)
    routes = jax.vmap(lambda own, number: deal_out(jax.random.fold_in(seeds[12], 2), own, number, TOK_DEV, EXPERTS, TOP, CAP, 1))(routes_keys, routes_turns).reshape((TOKENS, TOP))
    lengths = draw_lengths(jax.random.fold_in(seeds[14], 71), 0)
    return dict(tokens=tokens, w_query=w_query, w_key=w_key, w_value=w_value, w_output=w_output, gain_attn=gain_attn, gain_moe=gain_moe, router=router, w_gate=w_gate, w_up=w_up, w_down=w_down, cotangent=cotangent, routes=routes, lengths=lengths)


@jax.custom_vjp
def low(v):
    return lax.optimization_barrier(v.astype(jnp.bfloat16)).astype(jnp.float32)

@jax.custom_vjp
def low_back(v):
    return v

def low_keep(v):
    return (low(v), None)

def low_pass(kept, grad):
    return (grad,)

def back_keep(v):
    return (v, None)

def back_low(kept, grad):
    return (low(grad),)
low.defvjp(low_keep, low_pass)
low_back.defvjp(back_keep, back_low)

def high_dot(left, right):
    return jnp.dot(left, right, precision=lax.Precision.HIGHEST)

def rms_scale(values, gain_vector):
    return values * lax.rsqrt(lax.optimization_barrier(jnp.mean(values * values, axis=-1, keepdims=True)) + 1e-06) * gain_vector

def rope_tables(row_count):
    half_dim = HEAD_DIM // 2
    inverse = 10000.0 ** (-jnp.arange(half_dim, dtype=jnp.float32) / half_dim)
    phases = jnp.arange(row_count, dtype=jnp.float32)[:, None] * inverse[None, :]
    return (jnp.sin(phases)[:, None, :], jnp.cos(phases)[:, None, :])

def rotate(values, sine_table, cosine_table):
    half_dim = values.shape[-1] // 2
    front_half = values[..., :half_dim]
    back_half = values[..., half_dim:]
    return jnp.concatenate([front_half * cosine_table - back_half * sine_table, back_half * cosine_table + front_half * sine_table], axis=-1)

def attend_one(packed):
    queries, keys, values, length = packed
    grouped = queries.reshape(SEQ_LEN, KV_HEADS, HEADS // KV_HEADS, HEAD_DIM)
    raw_scores = jnp.einsum('tkgd,skd->kgts', grouped, keys, precision=lax.Precision.HIGHEST) * HEAD_DIM ** (-0.5)
    raw_scores = low_back(raw_scores)
    positions = jnp.arange(SEQ_LEN, dtype=jnp.int32)
    allowed = (positions[None, :] <= positions[:, None]) & (positions[None, :] < length)
    masked = jnp.where(allowed, raw_scores, -1e+30)
    softmaxed = low(jax.nn.softmax(masked, axis=-1))
    mixed_rows = jnp.einsum('kgts,skd->tkgd', softmaxed, values, precision=lax.Precision.HIGHEST)
    return mixed_rows.reshape(SEQ_LEN, HEADS * HEAD_DIM)

def reference(tokens, w_query, w_key, w_value, w_output, gain_attn, gain_moe, router, w_gate, w_up, w_down, cotangent, routes, lengths):
    blocks = routes.reshape(DEVICES, TOK_DEV * TOP)
    onehot = (blocks[:, :, None] == jnp.arange(EXPERTS, dtype=jnp.int32)).astype(jnp.int32)
    slot_rank = lax.optimization_barrier(jnp.sum((jnp.cumsum(onehot, axis=1) - 1) * onehot, axis=2))
    slot_index = blocks * (DEVICES * CAP) + jnp.arange(DEVICES, dtype=jnp.int32)[:, None] * CAP + slot_rank
    assign = jnp.full((EXPERTS * DEVICES * CAP,), TOKENS * TOP, jnp.int32)
    assign = assign.at[slot_index.reshape(-1)].set(jnp.arange(TOKENS * TOP, dtype=jnp.int32))
    assign = assign.reshape(EXPERTS, DEVICES * CAP)
    sine_table, cosine_table = rope_tables(SEQ_LEN)

    def forward(inputs, wq, wk, wv, wo, gain_one, gain_two, router_f, gate_f, up_f, down_f):
        normed_low = low(rms_scale(inputs, gain_one))
        query_raw = low_back(high_dot(normed_low, wq)).reshape(NSEQ, SEQ_LEN, HEADS, HEAD_DIM)
        key_raw = low_back(high_dot(normed_low, wk)).reshape(NSEQ, SEQ_LEN, KV_HEADS, HEAD_DIM)
        value_low = low(low_back(high_dot(normed_low, wv))).reshape(NSEQ, SEQ_LEN, KV_HEADS, HEAD_DIM)
        query_low = low(rotate(query_raw, sine_table, cosine_table))
        key_low = low(rotate(key_raw, sine_table, cosine_table))
        mixed_rows = lax.map(jax.checkpoint(attend_one), (query_low, key_low, value_low, lengths))
        mixed_low = low(low_back(mixed_rows.reshape(TOKENS, HEADS * HEAD_DIM)))
        hidden = inputs + low_back(high_dot(mixed_low, wo))
        normed_two = low(rms_scale(hidden, gain_two))
        logits = low_back(high_dot(normed_two, router_f))
        picked = jnp.take_along_axis(logits, routes, axis=1)
        gate_weights = jax.nn.softmax(picked, axis=-1)
        gate_pad = jnp.concatenate([gate_weights.reshape(-1), jnp.zeros((1,), jnp.float32)])
        rows_pad = jnp.concatenate([normed_two, jnp.zeros((1, D), jnp.float32)], axis=0)

        def expert_term(assign_row, gate_mat, up_mat, down_mat):
            owner_token = assign_row // TOP
            rows = low_back(rows_pad[owner_token])
            gate_part = low_back(high_dot(rows, gate_mat))
            up_part = low_back(high_dot(rows, up_mat))
            act_low = low(jax.nn.silu(gate_part) * up_part)
            out_rows = low(low_back(high_dot(act_low, down_mat)))
            weighted = gate_pad[assign_row][:, None] * out_rows
            return jnp.zeros((TOKENS + 1, D), jnp.float32).at[owner_token].add(weighted)[:TOKENS]

        def expert_step(running, stacked):
            return (running + jax.checkpoint(expert_term)(*stacked), None)
        moe_sum, _ = lax.scan(expert_step, jnp.zeros((TOKENS, D), jnp.float32), (assign, gate_f, up_f, down_f))
        return hidden + moe_sum
    primals = (tokens.astype(jnp.float32), w_query.astype(jnp.float32), w_key.astype(jnp.float32), w_value.astype(jnp.float32), w_output.astype(jnp.float32), gain_attn.astype(jnp.float32), gain_moe.astype(jnp.float32), router.astype(jnp.float32), w_gate.astype(jnp.float32), w_up.astype(jnp.float32), w_down.astype(jnp.float32))
    result, pullback = jax.vjp(forward, *primals)
    token_ids = jnp.arange(TOKENS, dtype=jnp.int32)
    live_rows = (token_ids % SEQ_LEN < lengths[token_ids // SEQ_LEN]).astype(jnp.float32)
    grads = pullback(cotangent.astype(jnp.float32) * live_rows[:, None])
    counts = lax.optimization_barrier(jnp.sum((routes.reshape(-1)[:, None] == jnp.arange(EXPERTS, dtype=jnp.int32)).astype(jnp.int32), axis=0))
    return (result.astype(jnp.bfloat16), grads[0], grads[1], grads[2], grads[3], grads[4], grads[5], grads[6], grads[7], grads[8], grads[9], grads[10], counts)
```

```python
import jax
import jax.numpy as jnp
from jax import lax
from jax.experimental import pallas as pl
from jax.experimental.pallas import tpu as pltpu
from jax.sharding import PartitionSpec as P

D = 1024
HEADS = 16
KV_HEADS = 8
HEAD_DIM = 64
EXPERTS = 32
TOP = 8
FF = 512
TOK = 128

MESH = pl.DeviceIdType.MESH
BF = jnp.bfloat16
F32 = jnp.float32
SLOTS = 48
VMEM_BYTES = 60 * 2**20


def wrap(value):
    return lax.rem(value + 4, 4)


def place():
    dp = lax.axis_index("dp")
    y = lax.axis_index("hid")
    core = lax.rem(dp, 2)
    x = lax.div(dp, 8)
    z = lax.rem(lax.div(dp, 2), 4)
    p = jnp.where(core == 0, x, z)
    q = jnp.where(core == 0, z, x)
    return p, q, y, core


def device(p, q, y, core):
    p, q = wrap(p), wrap(q)
    return (jnp.where(core == 0, p * 8 + q * 2, q * 8 + p * 2) + core, wrap(y))


def chip_of(p, q, core):
    p, q = wrap(p), wrap(q)
    return jnp.where(core == 0, p * 4 + q, q * 4 + p)


def greet(devices):
    barrier = pltpu.get_barrier_semaphore()
    for other in devices:
        pl.semaphore_signal(barrier, inc=1, device_id=other, device_id_type=MESH)
    pl.semaphore_wait(barrier, len(devices))


class Sends:
    def __init__(self, send_sem, recv_sem):
        self.send_sem, self.recv_sem, self.made = send_sem, recv_sem, []

    def start(self, source, target, recv, to):
        copy = pltpu.make_async_remote_copy(
            src_ref=source,
            dst_ref=target,
            send_sem=self.send_sem.at[len(self.made)],
            recv_sem=self.recv_sem.at[recv],
            device_id=to,
            device_id_type=MESH,
        )
        copy.start()
        self.made.append(copy)

    def arrived(self, ref, recv):
        pltpu.make_async_copy(ref, ref, self.recv_sem.at[recv]).wait()

    def drain(self):
        for copy in self.made:
            copy.wait_send()
        self.made = []


def slab(buffer, p, q):
    return buffer.at[wrap(p) * 4 + wrap(q)]


def moe_kernel(
    x_ref, gt_ref, u_hbm, wg_hbm, wu_hbm, wd_hbm,
    grad_out, o_hbm, gg_out, dwg_hbm, dwu_hbm, dwd_hbm,
    xs, us, wg, wu, wd, gin, rank, ggo, picks, rows, rows_up, slot_grads, acts, gparts, uparts,
    outs, pairs, o_buf, p_buf, rb, rc, rd, re, dwg, dwu, dwd,
    send_sem, recv_sem, g_send, g_recv, gg_send, gg_recv, local_sem,
):
    p, q, y, core = place()
    me = device(p, q, y, core)
    right, left = device(p + 1, q, y, core), device(p - 1, q, y, core)
    up, down = device(p, q + 1, y, core), device(p, q - 1, y, core)
    others = [device(p + a, q + b, y, core) for a in range(4) for b in range(4) if a or b]
    loads = [
        pltpu.make_async_copy(src, dst, local_sem.at[i])
        for i, (src, dst) in enumerate(((u_hbm, us), (wg_hbm, wg), (wu_hbm, wu), (wd_hbm, wd)))
    ]
    for load in loads:
        load.start()
    greet(others)
    net = Sends(send_sem, recv_sem)
    my_chip = chip_of(p, q, core)

    own = slab(xs, p, q)
    net.start(x_ref, own, 0, right)
    net.start(x_ref, own, 1, left)
    net.start(x_ref, own, 4, up)
    net.start(x_ref, own, 8, down)

    def gate_copy(i):
        a, b = lax.div(i, 4), lax.rem(i, 4)
        return pltpu.make_async_remote_copy(
            src_ref=gt_ref.at[chip_of(p + a, q + b, core)],
            dst_ref=gin.at[p * 4 + q],
            send_sem=g_send.at[i],
            recv_sem=g_recv.at[wrap(-a) * 4 + wrap(-b)],
            device_id=device(p + a, q + b, y, core),
            device_id_type=MESH,
        )

    def start_gate(i, _):
        gate_copy(i).start()
        return 0

    lax.fori_loop(1, 16, start_gate, 0)
    gin[p * 4 + q] = gt_ref[my_chip]
    own[...] = x_ref[...]

    s = slab(xs, p - 1, q)
    net.arrived(s, 0)
    net.start(s.at[0:64], s.at[0:64], 2, right)
    net.start(s, s, 5, up)
    s = slab(xs, p + 1, q)
    net.arrived(s, 1)
    net.start(s.at[64:128], s.at[64:128], 3, left)
    net.start(s, s, 10, down)
    s = slab(xs, p, q - 1)
    net.arrived(s, 4)
    net.start(s, s, 12, up)
    s = slab(xs, p + 2, q)
    net.arrived(s.at[0:64], 2)
    net.arrived(s.at[64:128], 3)
    net.start(s, s, 11, down)
    s = slab(xs, p - 1, q - 1)
    net.arrived(s, 5)
    net.start(s, s, 13, up)
    s = slab(xs, p + 1, q)
    net.start(s, s, 6, up)
    s = slab(xs, p + 2, q)
    net.start(s, s, 7, up)
    s = slab(xs, p - 1, q)
    net.start(s, s, 9, down)

    def take_gate(i, _):
        pltpu.make_async_copy(gin.at[0], gin.at[0], g_recv.at[i]).wait()
        return 0

    lax.fori_loop(1, 16, take_gate, 0)
    ids = lax.broadcasted_iota(jnp.int32, (TOK, TOK), 0)
    cols = lax.broadcasted_iota(jnp.int32, (TOK, TOK), 1)
    before = jnp.where(ids < cols, 1.0, 0.0).astype(BF)
    routed = jnp.where(gin[...].reshape(TOK, TOK) > 0, 1.0, 0.0).astype(BF)
    rank[...] = jnp.dot(routed, before, preferred_element_type=F32).reshape(16, 8, TOK)
    for load in loads:
        load.wait()
    ggo[...] = jnp.zeros_like(ggo)
    slot_ids = lax.broadcasted_iota(jnp.int32, (SLOTS, TOK), 0).astype(F32)

    def source_of(g, j):
        b = jnp.where(g == 0, 0, jnp.where(g == 1, 2, jnp.where(g == 2, 3, 1)))
        a = jnp.where(j == 0, 0, jnp.where(j == 1, 3, jnp.where(j == 2, 1, 2)))
        return wrap(p + a) * 4 + wrap(q + b)

    def pick_source(g, j):
        src = source_of(g, j)
        token_rows, up_rows = xs[src], us[src]
        base = pl.multiple_of(g * 4 * SLOTS + j * SLOTS, 16)
        for e in range(2):
            gate_row = gin[src, e : e + 1, :]
            hit = (rank[src, e : e + 1, :] == slot_ids) & (gate_row > 0)
            pick = jnp.where(hit, 1.0, 0.0)
            pick_low = pick.astype(BF)
            picks[src, e * SLOTS : (e + 1) * SLOTS, :] = pick_low
            gate_col = jnp.sum(pick * gate_row, axis=1, keepdims=True)
            rows[e, pl.ds(base, SLOTS), :] = jnp.dot(
                pick_low, token_rows, preferred_element_type=F32
            ).astype(BF)
            picked = jnp.dot(pick_low, up_rows, preferred_element_type=F32)
            rows_up[e, pl.ds(pl.multiple_of(j * SLOTS, 16), SLOTS), :] = picked.astype(BF)
            slot_grads[e, pl.ds(base, SLOTS), :] = (picked * gate_col).astype(BF)

    def run_expert(g, e):
        base = pl.multiple_of(g * 4 * SLOTS, 16)
        span = pl.ds(base, 4 * SLOTS)
        taken = rows[e, span, :]
        gate = jnp.dot(taken, wg[e], preferred_element_type=F32)
        upv = jnp.dot(taken, wu[e], preferred_element_type=F32)
        sig = 1.0 / (1.0 + jnp.exp(-gate))
        silu = gate * sig
        act = (silu * upv).astype(BF)
        acts[e, span, :] = act
        out = jnp.dot(act, wd[e], preferred_element_type=F32).astype(BF)
        outs[e] = out
        gg_col = jnp.sum(out.astype(F32) * rows_up[e].astype(F32), axis=1, keepdims=True)
        for j in range(4):
            src = source_of(g, j)
            pick = picks[src, pl.ds(pl.multiple_of(e * SLOTS, 16), SLOTS), :].astype(F32)
            part = gg_col[j * SLOTS : (j + 1) * SLOTS]
            ggo[src, pl.ds(e, 1), :] = jnp.sum(pick * part, axis=0, keepdims=True)
        grad_act = lax.dot_general(
            slot_grads[e, span, :], wd[e], (((1,), (1,)), ((), ())), preferred_element_type=F32
        )
        ggp = (grad_act * upv * sig * (1.0 + gate * (1.0 - sig))).astype(BF)
        gup = (grad_act * silu).astype(BF)
        gparts[e, span, :] = ggp
        uparts[e, span, :] = gup
        pair = lax.dot_general(ggp, wg[e], (((1,), (1,)), ((), ())), preferred_element_type=F32)
        pair += lax.dot_general(gup, wu[e], (((1,), (1,)), ((), ())), preferred_element_type=F32)
        pairs[e] = pair.astype(BF)

    def spread(g, j):
        src = source_of(g, j)
        pick = picks[src]
        span = pl.ds(pl.multiple_of(j * SLOTS, 16), SLOTS)
        gates = jnp.concatenate(
            [
                pick[e * SLOTS : (e + 1) * SLOTS].astype(F32) * gin[src, e : e + 1, :]
                for e in range(2)
            ],
            axis=0,
        ).astype(BF)
        both = jnp.concatenate([outs[0, span, :], outs[1, span, :]], axis=0)
        o_buf[src] = lax.dot_general(
            gates, both, (((0,), (0,)), ((), ())), preferred_element_type=F32
        ).astype(BF)
        both = jnp.concatenate([pairs[0, span, :], pairs[1, span, :]], axis=0)
        p_buf[src] = lax.dot_general(
            pick, both, (((0,), (0,)), ((), ())), preferred_element_type=F32
        ).astype(BF)

    def chunk(g):
        lax.fori_loop(0, 4, lambda j, c: (pick_source(g, j), c)[1], 0)
        lax.fori_loop(0, 2, lambda e, c: (run_expert(g, e), c)[1], 0)
        lax.fori_loop(0, 4, lambda j, c: (spread(g, j), c)[1], 0)

    OFF = (0, -1, 1, 2)
    R = 16

    def make(source, target, recv, to, index):
        return pltpu.make_async_remote_copy(
            src_ref=source,
            dst_ref=target,
            send_sem=send_sem.at[index],
            recv_sem=recv_sem.at[recv],
            device_id=to,
            device_id_type=MESH,
        )

    first = len(net.made)
    far = [
        lambda: make(slab(xs, p + 1, q + 1), slab(xs, p + 1, q + 1), 14, down, first),
        lambda: make(slab(xs, p + 2, q + 1), slab(xs, p + 2, q + 1), 15, down, first + 1),
    ]
    bounce = [
        (lambda j=j: make(slab(p_buf, p + OFF[j], q + 2), rb.at[j], R + j, up if j < 2 else down, first + 2 + j))
        for j in range(4)
    ]
    to_down = [
        (lambda j=j: make(slab(p_buf, p + OFF[j], q - 1), rc.at[4 + j], R + 8 + j, down, first + 6 + j))
        for j in range(4)
    ]
    to_up = [
        (lambda j=j: make(slab(p_buf, p + OFF[j], q + 1), rc.at[j], R + 4 + j, up, first + 10 + j))
        for j in range(4)
    ]

    def add_bounce(j):
        net.arrived(rb.at[j], R + j)
        target = slab(p_buf, p + OFF[j], q + 1 if j < 2 else q - 1)
        target[...] = (target[...].astype(F32) + rb[j].astype(F32)).astype(BF)

    def step(g, carry):
        @pl.when(g == 1)
        def _():
            net.arrived(slab(xs, p + 1, q + 1), 10)
            far[0]().start()
            net.arrived(slab(xs, p + 2, q + 1), 11)
            far[1]().start()
            net.arrived(slab(xs, p, q + 2), 12)
            net.arrived(slab(xs, p - 1, q + 2), 13)
            net.arrived(slab(xs, p + 1, q + 2), 14)
            net.arrived(slab(xs, p + 2, q + 2), 15)

        @pl.when(g == 2)
        def _():
            net.arrived(slab(xs, p + 1, q - 1), 6)
            net.arrived(slab(xs, p + 2, q - 1), 7)

        @pl.when(g == 3)
        def _():
            net.arrived(slab(xs, p, q + 1), 8)
            net.arrived(slab(xs, p - 1, q + 1), 9)

        chunk(g)

        @pl.when(g == 1)
        def _():
            for j in range(4):
                bounce[j]().start()

        @pl.when(g == 2)
        def _():
            to_down[0]().start()
            to_down[1]().start()
            for j in (3, 2):
                add_bounce(j)
                to_down[j]().start()

        @pl.when(g == 3)
        def _():
            to_up[3]().start()
            to_up[2]().start()
            for j in (1, 0):
                add_bounce(j)
                to_up[j]().start()

        return carry

    lax.fori_loop(0, 4, step, 0)

    def gg_copy(i):
        a, b = lax.div(i, 4), lax.rem(i, 4)
        return pltpu.make_async_remote_copy(
            src_ref=ggo.at[wrap(p + a) * 4 + wrap(q + b)],
            dst_ref=gg_out.at[my_chip],
            send_sem=gg_send.at[i],
            recv_sem=gg_recv.at[wrap(-a) * 4 + wrap(-b)],
            device_id=device(p + a, q + b, y, core),
            device_id_type=MESH,
        )

    def start_gg(i, _):
        gg_copy(i).start()
        return 0

    lax.fori_loop(1, 16, start_gg, 0)
    gg_out[my_chip] = ggo[p * 4 + q]
    o_store = pltpu.make_async_copy(o_buf, o_hbm, local_sem.at[4])
    o_store.start()

    def weight_tile(e, t):
        cols = pl.ds(pl.multiple_of(t * 256, 256), 256)
        dims = (((0,), (0,)), ((), ()))
        lhs = rows[e, :, cols]
        dwg[e, cols, :] = lax.dot_general(lhs, gparts[e], dims, preferred_element_type=F32).astype(BF)
        dwu[e, cols, :] = lax.dot_general(lhs, uparts[e], dims, preferred_element_type=F32).astype(BF)
        dwd[e, :, cols] = lax.dot_general(
            acts[e], slot_grads[e, :, cols], dims, preferred_element_type=F32
        ).astype(BF)

    def weight_grads(e):
        lax.fori_loop(0, 4, lambda t, c: (weight_tile(e, t), c)[1], 0)

    weight_grads(0)

    def gather_sum(j):
        net.arrived(rc.at[j], R + 4 + j)
        net.arrived(rc.at[4 + j], R + 8 + j)
        target = slab(p_buf, p + OFF[j], q)
        target[...] = (
            target[...].astype(F32) + rc[j].astype(F32) + rc[4 + j].astype(F32)
        ).astype(BF)

    last = first + 14
    lo, hi = pl.ds(0, 64), pl.ds(64, 64)
    far_slab, next_slab, prev_slab = slab(p_buf, p + 2, q), slab(p_buf, p + 1, q), slab(p_buf, p - 1, q)
    tail = [
        make(far_slab.at[lo], rd.at[lo], R + 12, right, last),
        make(far_slab.at[hi], rd.at[hi], R + 13, left, last + 1),
        make(next_slab.at[hi], re.at[0, hi], R + 14, right, last + 2),
        make(prev_slab.at[lo], re.at[1, lo], R + 15, left, last + 3),
        make(next_slab.at[lo], re.at[0, lo], R + 16, right, last + 4),
        make(prev_slab.at[hi], re.at[1, hi], R + 17, left, last + 5),
    ]
    gather_sum(3)
    tail[0].start()
    tail[1].start()
    gather_sum(2)
    tail[2].start()
    gather_sum(1)
    tail[3].start()
    net.arrived(rd.at[lo], R + 12)
    next_slab[lo] = (next_slab[lo].astype(F32) + rd[lo].astype(F32)).astype(BF)
    tail[4].start()
    net.arrived(rd.at[hi], R + 13)
    prev_slab[hi] = (prev_slab[hi].astype(F32) + rd[hi].astype(F32)).astype(BF)
    tail[5].start()
    gather_sum(0)
    weight_grads(1)
    stores = [
        pltpu.make_async_copy(src, dst, local_sem.at[i])
        for i, (src, dst) in enumerate(((dwg, dwg_hbm), (dwu, dwu_hbm), (dwd, dwd_hbm)))
    ]
    for store in stores:
        store.start()
    net.arrived(re.at[0, hi], R + 14)
    net.arrived(re.at[1, lo], R + 15)
    net.arrived(re.at[0, lo], R + 16)
    net.arrived(re.at[1, hi], R + 17)
    grad_out[...] = slab(p_buf, p, q)[...].astype(F32) + re[0].astype(F32) + re[1].astype(F32)

    def take_gg(i, _):
        pltpu.make_async_copy(ggo.at[0], ggo.at[0], gg_recv.at[i]).wait()
        return 0

    lax.fori_loop(1, 16, take_gg, 0)
    net.drain()
    for copy in far + bounce + to_down + to_up:
        copy().wait_send()
    for copy in tail:
        copy.wait_send()

    def drain_small(i, _):
        gate_copy(i).wait_send()
        gg_copy(i).wait_send()
        return 0

    lax.fori_loop(1, 16, drain_small, 0)
    o_store.wait()
    for store in stores:
        store.wait()


def moe(x, gt, u, wg, wu, wd):
    any_space = pl.BlockSpec(memory_space=pl.ANY)
    vmem = pl.BlockSpec(memory_space=pltpu.VMEM)
    shape = jax.ShapeDtypeStruct
    slots = 16 * SLOTS
    dma = pltpu.SemaphoreType.DMA
    return pl.pallas_call(
        moe_kernel,
        out_shape=(
            shape((TOK, D), F32),
            shape((16, TOK, D), BF),
            shape((16, 8, TOK), F32),
            shape((2, D, FF), BF),
            shape((2, D, FF), BF),
            shape((2, FF, D), BF),
        ),
        in_specs=[vmem, vmem, any_space, any_space, any_space, any_space],
        out_specs=(vmem, any_space, vmem, any_space, any_space, any_space),
        scratch_shapes=[
            pltpu.VMEM((16, TOK, D), BF),
            pltpu.VMEM((16, TOK, D), BF),
            pltpu.VMEM((2, D, FF), BF),
            pltpu.VMEM((2, D, FF), BF),
            pltpu.VMEM((2, FF, D), BF),
            pltpu.VMEM((16, 8, TOK), F32),
            pltpu.VMEM((16, 8, TOK), F32),
            pltpu.VMEM((16, 8, TOK), F32),
            pltpu.VMEM((16, 2 * SLOTS, TOK), BF),
            pltpu.VMEM((2, slots, D), BF),
            pltpu.VMEM((2, 4 * SLOTS, D), BF),
            pltpu.VMEM((2, slots, D), BF),
            pltpu.VMEM((2, slots, FF), BF),
            pltpu.VMEM((2, slots, FF), BF),
            pltpu.VMEM((2, slots, FF), BF),
            pltpu.VMEM((2, 4 * SLOTS, D), BF),
            pltpu.VMEM((2, 4 * SLOTS, D), BF),
            pltpu.VMEM((16, TOK, D), BF),
            pltpu.VMEM((16, TOK, D), BF),
            pltpu.VMEM((4, TOK, D), BF),
            pltpu.VMEM((8, TOK, D), BF),
            pltpu.VMEM((TOK, D), BF),
            pltpu.VMEM((2, TOK, D), BF),
            pltpu.VMEM((2, D, FF), BF),
            pltpu.VMEM((2, D, FF), BF),
            pltpu.VMEM((2, FF, D), BF),
            dma((40,)),
            dma((34,)),
            dma((16,)),
            dma((16,)),
            dma((16,)),
            dma((16,)),
            dma((5,)),
        ],
        compiler_params=pltpu.CompilerParams(
            collective_id=1, has_side_effects=True, vmem_limit_bytes=VMEM_BYTES
        ),
        name="experts",
    )(x, gt, u, wg, wu, wd)


def rms_forward(values, gain_vector):
    inverse_root = lax.rsqrt(jnp.mean(values * values, axis=-1, keepdims=True) + 1e-06)
    return (values * inverse_root * gain_vector, inverse_root)


def rms_backward(values, inverse_root, gain_vector, upstream):
    scaled = upstream * gain_vector
    grad_gain = jnp.sum(upstream * values * inverse_root, axis=0)
    grad_values = inverse_root * scaled - values * inverse_root**3 * jnp.mean(
        scaled * values, axis=-1, keepdims=True
    )
    return (grad_values, grad_gain)


def rope_tables(first_pos, row_count, head_width):
    half_dim = head_width // 2
    inverse = 10000.0 ** (-jnp.arange(half_dim, dtype=jnp.float32) / half_dim)
    phases = (first_pos + jnp.arange(row_count, dtype=jnp.float32))[:, None] * inverse[None, :]
    return (jnp.sin(phases)[:, None, :], jnp.cos(phases)[:, None, :])


def rotate(values, sine_table, cosine_table):
    half_dim = values.shape[-1] // 2
    front_half = values[..., :half_dim]
    back_half = values[..., half_dim:]
    return jnp.concatenate(
        [
            front_half * cosine_table - back_half * sine_table,
            back_half * cosine_table + front_half * sine_table,
        ],
        axis=-1,
    )


def unrotate(grad_values, sine_table, cosine_table):
    half_dim = grad_values.shape[-1] // 2
    front_half = grad_values[..., :half_dim]
    back_half = grad_values[..., half_dim:]
    return jnp.concatenate(
        [
            front_half * cosine_table + back_half * sine_table,
            back_half * cosine_table - front_half * sine_table,
        ],
        axis=-1,
    )


def shards(
    tokens,
    w_query,
    w_key,
    w_value,
    w_output,
    gain_attn,
    gain_moe,
    router,
    w_gate,
    w_up,
    w_down,
    cotangent,
    routes,
    lengths,
):
    tok_count = tokens.shape[0]
    hid_pos = lax.axis_index("hid")
    first_pos = (hid_pos * tok_count).astype(jnp.float32)
    group_size = HEADS // KV_HEADS
    score_scale = HEAD_DIM ** (-0.5)
    inputs = tokens.astype(jnp.float32)
    normed, root_attn = rms_forward(inputs, gain_attn)
    normed_low = normed.astype(jnp.bfloat16)
    sine_table, cosine_table = rope_tables(first_pos, tok_count, HEAD_DIM)
    query_raw = jnp.dot(normed_low, w_query, preferred_element_type=jnp.float32).reshape(
        tok_count, HEADS, HEAD_DIM
    )
    key_raw = jnp.dot(normed_low, w_key, preferred_element_type=jnp.float32).reshape(
        tok_count, KV_HEADS, HEAD_DIM
    )
    value_low = (
        jnp.dot(normed_low, w_value, preferred_element_type=jnp.float32)
        .astype(jnp.bfloat16)
        .reshape(tok_count, KV_HEADS, HEAD_DIM)
    )
    query_low = rotate(query_raw, sine_table, cosine_table).astype(jnp.bfloat16)
    key_low = rotate(key_raw, sine_table, cosine_table).astype(jnp.bfloat16)
    keys_all, values_all = (
        lax.all_gather(key_low, "hid", axis=0, tiled=True),
        lax.all_gather(value_low, "hid", axis=0, tiled=True),
    )
    seq_count = keys_all.shape[0]
    grouped = query_low.reshape(tok_count, KV_HEADS, group_size, HEAD_DIM)
    query_pos = hid_pos * tok_count + jnp.arange(tok_count, dtype=jnp.int32)
    key_pos = jnp.arange(seq_count, dtype=jnp.int32)
    allowed = (key_pos[None, :] <= query_pos[:, None]) & (key_pos[None, :] < lengths[0])

    def masked_scores():
        raw_scores = (
            jnp.einsum("tkgd,skd->kgts", grouped, keys_all, preferred_element_type=jnp.float32)
            * score_scale
        )
        return jnp.where(allowed, raw_scores, -1e30)

    masked = masked_scores()
    top_score = jnp.max(masked, axis=-1, keepdims=True)
    log_total = top_score + jnp.log(jnp.sum(jnp.exp(masked - top_score), axis=-1, keepdims=True))
    softmaxed_low = jnp.exp(masked - log_total).astype(jnp.bfloat16)
    mixed_low = jnp.einsum(
        "kgts,skd->tkgd", softmaxed_low, values_all, preferred_element_type=jnp.float32
    )
    mixed_low = mixed_low.reshape(tok_count, HEADS * HEAD_DIM).astype(jnp.bfloat16)
    hidden = inputs + jnp.dot(mixed_low, w_output, preferred_element_type=jnp.float32)
    normed_two, root_moe = rms_forward(hidden, gain_moe)
    normed_two_low = normed_two.astype(jnp.bfloat16)
    logits = jnp.dot(normed_two_low, router, preferred_element_type=jnp.float32)
    route_onehot = (routes[:, :, None] == jnp.arange(EXPERTS, dtype=jnp.int32)).astype(jnp.float32)
    picked = jnp.sum(logits[:, None, :] * route_onehot, axis=-1)
    gate_weights = jax.nn.softmax(picked, axis=-1)
    core_groups = [[2 * i for i in range(16)], [2 * i + 1 for i in range(16)]]
    pair_groups = [[2 * i, 2 * i + 1] for i in range(16)]
    dense_gates = jnp.sum(gate_weights[:, :, None] * route_onehot, axis=1)
    gate_tiles = jnp.pad(dense_gates.T.reshape(16, 2, TOK), ((0, 0), (0, 6), (0, 0)))
    live_rows = (query_pos < lengths[0]).astype(jnp.float32)
    upstream_low = jnp.where(live_rows[:, None] > 0, cotangent, jnp.zeros_like(cotangent))
    upstream = upstream_low.astype(jnp.float32)
    core = lax.rem(lax.axis_index("dp"), 2)

    def by_place(rows):
        rows = rows.reshape(4, 4, TOK, D)
        return jnp.where(core == 0, rows, rows.transpose(1, 0, 2, 3)).reshape(16, TOK, D)

    upstream_all = by_place(lax.all_gather(upstream_low, "dp", axis_index_groups=core_groups))
    weights = jnp.stack([w_gate[0], w_up[0], w_down[0].T])
    weights = lax.all_gather(weights, "hid")
    weights = lax.all_gather(weights, "dp", axis_index_groups=pair_groups)
    full = weights.transpose(0, 2, 3, 1, 4).reshape(2, 3, D, FF)
    grad_rows, out_parts, grad_gates_t, part_gate, part_up, part_down = moe(
        normed_two_low,
        gate_tiles,
        upstream_all,
        full[:, 0],
        full[:, 1],
        full[:, 2].transpose(0, 2, 1),
    )
    moe_out = lax.psum_scatter(by_place(out_parts), "dp", axis_index_groups=core_groups)
    layer_out = (hidden + moe_out.astype(jnp.float32)).astype(jnp.bfloat16)
    parts = jnp.stack([part_gate, part_up, part_down.transpose(0, 2, 1)], axis=1)
    parts = parts.reshape(2, 3, D, 4, TOK).transpose(0, 3, 1, 2, 4)
    parts = lax.psum_scatter(parts, "dp", axis_index_groups=pair_groups)
    parts = lax.psum_scatter(parts, "hid").astype(jnp.float32)
    grad_gate, grad_up, grad_down = parts[0][None], parts[1][None], parts[2].T[None]
    grad_gates = jnp.einsum("et,tke->tk", grad_gates_t[:, :2].reshape(EXPERTS, TOK), route_onehot, precision=lax.Precision.HIGHEST)
    grad_picked = gate_weights * (
        grad_gates - jnp.sum(gate_weights * grad_gates, axis=-1, keepdims=True)
    )
    grad_logits = jnp.sum(grad_picked[:, :, None] * route_onehot, axis=1).astype(jnp.bfloat16)
    grad_router = jnp.einsum(
        "td,te->de", normed_two_low, grad_logits, preferred_element_type=jnp.float32
    )
    grad_normed_two = grad_rows + jnp.einsum(
        "te,de->td", grad_logits, router, preferred_element_type=jnp.float32
    )
    grad_hidden_part, grad_gain_moe = rms_backward(hidden, root_moe, gain_moe, grad_normed_two)
    grad_hidden = upstream + grad_hidden_part
    grad_hidden_low = grad_hidden.astype(jnp.bfloat16)
    grad_w_output = jnp.einsum(
        "tf,td->fd", mixed_low, grad_hidden_low, preferred_element_type=jnp.float32
    )
    grad_mixed = jnp.einsum(
        "td,fd->tf", grad_hidden_low, w_output, preferred_element_type=jnp.float32
    )
    grad_mixed = grad_mixed.astype(jnp.bfloat16).reshape(tok_count, KV_HEADS, group_size, HEAD_DIM)
    softmaxed = jnp.exp(masked_scores() - log_total)
    grad_probs = jnp.einsum(
        "tkgd,skd->kgts", grad_mixed, values_all, preferred_element_type=jnp.float32
    )
    grad_scores = (
        softmaxed * (grad_probs - jnp.sum(softmaxed * grad_probs, axis=-1, keepdims=True))
    ).astype(jnp.bfloat16)
    grad_query = (
        jnp.einsum("kgts,skd->tkgd", grad_scores, keys_all, preferred_element_type=jnp.float32)
        * score_scale
    )
    grad_key_part = (
        jnp.einsum("kgts,tkgd->skd", grad_scores, grouped, preferred_element_type=jnp.float32)
        * score_scale
    )
    grad_value_part = jnp.einsum(
        "kgts,tkgd->skd", softmaxed_low, grad_mixed, preferred_element_type=jnp.float32
    )
    grad_key, grad_value = (
        lax.psum_scatter(
            grad_key_part.astype(jnp.bfloat16), "hid", scatter_dimension=0, tiled=True
        ).astype(jnp.float32),
        lax.psum_scatter(
            grad_value_part.astype(jnp.bfloat16), "hid", scatter_dimension=0, tiled=True
        ).astype(jnp.float32),
    )
    grad_query_low = unrotate(
        grad_query.reshape(tok_count, HEADS, HEAD_DIM), sine_table, cosine_table
    )
    grad_query_low = grad_query_low.astype(jnp.bfloat16).reshape(tok_count, HEADS * HEAD_DIM)
    grad_key_low = (
        unrotate(grad_key, sine_table, cosine_table)
        .astype(jnp.bfloat16)
        .reshape(tok_count, KV_HEADS * HEAD_DIM)
    )
    grad_value_low = grad_value.astype(jnp.bfloat16).reshape(tok_count, KV_HEADS * HEAD_DIM)
    grad_w_query = jnp.einsum(
        "td,tf->df", normed_low, grad_query_low, preferred_element_type=jnp.float32
    )
    grad_w_key = jnp.einsum(
        "td,tf->df", normed_low, grad_key_low, preferred_element_type=jnp.float32
    )
    grad_w_value = jnp.einsum(
        "td,tf->df", normed_low, grad_value_low, preferred_element_type=jnp.float32
    )
    grad_normed = (
        jnp.einsum("tf,df->td", grad_query_low, w_query, preferred_element_type=jnp.float32)
        + jnp.einsum("tf,df->td", grad_key_low, w_key, preferred_element_type=jnp.float32)
        + jnp.einsum("tf,df->td", grad_value_low, w_value, preferred_element_type=jnp.float32)
    )
    grad_input_part, grad_gain_attn = rms_backward(inputs, root_attn, gain_attn, grad_normed)
    grad_input = grad_hidden + grad_input_part
    counts_local = jnp.sum(route_onehot, axis=(0, 1))
    summed = lax.psum(
        (
            grad_w_query,
            grad_w_key,
            grad_w_value,
            grad_w_output,
            grad_gain_attn,
            grad_gain_moe,
            grad_router,
            counts_local,
        ),
        ("dp", "hid"),
    )
    counts = summed[7].astype(jnp.int32)
    return (
        layer_out,
        grad_input,
        summed[0],
        summed[1],
        summed[2],
        summed[3],
        summed[4],
        summed[5],
        summed[6],
        grad_gate,
        grad_up,
        grad_down,
        counts,
    )


def solution(mesh):
    in_specs = (
        P(("dp", "hid"), None),
        P(),
        P(),
        P(),
        P(),
        P(),
        P(),
        P(),
        P("dp", None, "hid"),
        P("dp", None, "hid"),
        P("dp", "hid", None),
        P(("dp", "hid"), None),
        P(("dp", "hid"), None),
        P("dp"),
    )
    out_specs = (
        P(("dp", "hid"), None),
        P(("dp", "hid"), None),
        P(),
        P(),
        P(),
        P(),
        P(),
        P(),
        P(),
        P("dp", None, "hid"),
        P("dp", None, "hid"),
        P("dp", "hid", None),
        P(),
    )
    return jax.shard_map(shards, mesh=mesh, in_specs=in_specs, out_specs=out_specs, check_vma=False)
```

```python
import jax
import jax.numpy as jnp
import numpy as np
from jax import lax
from jax.experimental import pallas as pl
from jax.experimental.pallas import tpu as pltpu
from jax.sharding import PartitionSpec as P

D = 1024
HEADS = 16
KV_HEADS = 8
HEAD_DIM = 64
EXPERTS = 32
TOP = 8
FF = 512
TOK = 128

MESH = pl.DeviceIdType.MESH
BF = jnp.bfloat16
F32 = jnp.float32
SLOTS = 48
VMEM_BYTES = 60 * 2**20


def wrap(value):
    return lax.rem(value + 4, 4)


def place():
    dp = lax.axis_index("dp")
    y = lax.axis_index("hid")
    core = lax.rem(dp, 2)
    x = lax.div(dp, 8)
    z = lax.rem(lax.div(dp, 2), 4)
    p = jnp.where(core == 0, x, z)
    q = jnp.where(core == 0, z, x)
    return p, q, y, core


def device(p, q, y, core):
    p, q = wrap(p), wrap(q)
    return (jnp.where(core == 0, p * 8 + q * 2, q * 8 + p * 2) + core, wrap(y))


def chip_of(p, q, core):
    p, q = wrap(p), wrap(q)
    return jnp.where(core == 0, p * 4 + q, q * 4 + p)


def greet(devices):
    barrier = pltpu.get_barrier_semaphore()
    for other in devices:
        pl.semaphore_signal(barrier, inc=1, device_id=other, device_id_type=MESH)
    pl.semaphore_wait(barrier, len(devices))


class Sends:
    def __init__(self, send_sem, recv_sem):
        self.send_sem, self.recv_sem, self.made = send_sem, recv_sem, []

    def start(self, source, target, recv, to):
        copy = pltpu.make_async_remote_copy(
            src_ref=source,
            dst_ref=target,
            send_sem=self.send_sem.at[len(self.made)],
            recv_sem=self.recv_sem.at[recv],
            device_id=to,
            device_id_type=MESH,
        )
        copy.start()
        self.made.append(copy)

    def arrived(self, ref, recv):
        pltpu.make_async_copy(ref, ref, self.recv_sem.at[recv]).wait()

    def drain(self):
        for copy in self.made:
            copy.wait_send()
        self.made = []


def slab(buffer, p, q):
    return buffer.at[wrap(p) * 4 + wrap(q)]


def moe_kernel(
    x_ref, gt_ref, u_hbm, wg_hbm, wu_hbm, wd_hbm,
    grad_out, o_hbm, gg_out, dwg_hbm, dwu_hbm, dwd_hbm,
    xs, us, wg, wu, wd, gin, rank, ggo, picks, rows, rows_up, slot_grads, acts, gparts, uparts,
    outs, pairs, o_buf, p_buf, rb, rc, rd, re, dwg, dwu, dwd,
    send_sem, recv_sem, g_send, g_recv, gg_send, gg_recv, local_sem,
):
    p, q, y, core = place()
    me = device(p, q, y, core)
    right, left = device(p + 1, q, y, core), device(p - 1, q, y, core)
    up, down = device(p, q + 1, y, core), device(p, q - 1, y, core)
    others = [device(p + a, q + b, y, core) for a in range(4) for b in range(4) if a or b]
    loads = [
        pltpu.make_async_copy(src, dst, local_sem.at[i])
        for i, (src, dst) in enumerate(((u_hbm, us), (wg_hbm, wg), (wu_hbm, wu), (wd_hbm, wd)))
    ]
    for load in loads:
        load.start()
    greet(others)
    net = Sends(send_sem, recv_sem)
    my_chip = chip_of(p, q, core)

    own = slab(xs, p, q)
    net.start(x_ref, own, 0, right)
    net.start(x_ref, own, 1, left)
    net.start(x_ref, own, 4, up)
    net.start(x_ref, own, 8, down)

    def gate_copy(i):
        a, b = lax.div(i, 4), lax.rem(i, 4)
        return pltpu.make_async_remote_copy(
            src_ref=gt_ref.at[chip_of(p + a, q + b, core)],
            dst_ref=gin.at[p * 4 + q],
            send_sem=g_send.at[i],
            recv_sem=g_recv.at[wrap(-a) * 4 + wrap(-b)],
            device_id=device(p + a, q + b, y, core),
            device_id_type=MESH,
        )

    def start_gate(i, _):
        gate_copy(i).start()
        return 0

    lax.fori_loop(1, 16, start_gate, 0)
    gin[p * 4 + q] = gt_ref[my_chip]
    own[...] = x_ref[...]

    s = slab(xs, p - 1, q)
    net.arrived(s, 0)
    net.start(s.at[0:64], s.at[0:64], 2, right)
    net.start(s, s, 5, up)
    s = slab(xs, p + 1, q)
    net.arrived(s, 1)
    net.start(s.at[64:128], s.at[64:128], 3, left)
    net.start(s, s, 10, down)
    s = slab(xs, p, q - 1)
    net.arrived(s, 4)
    net.start(s, s, 12, up)
    s = slab(xs, p + 2, q)
    net.arrived(s.at[0:64], 2)
    net.arrived(s.at[64:128], 3)
    net.start(s, s, 11, down)
    s = slab(xs, p - 1, q - 1)
    net.arrived(s, 5)
    net.start(s, s, 13, up)
    s = slab(xs, p + 1, q)
    net.start(s, s, 6, up)
    s = slab(xs, p + 2, q)
    net.start(s, s, 7, up)
    s = slab(xs, p - 1, q)
    net.start(s, s, 9, down)

    def take_gate(i, _):
        pltpu.make_async_copy(gin.at[0], gin.at[0], g_recv.at[i]).wait()
        return 0

    lax.fori_loop(1, 16, take_gate, 0)
    ids = lax.broadcasted_iota(jnp.int32, (TOK, TOK), 0)
    cols = lax.broadcasted_iota(jnp.int32, (TOK, TOK), 1)
    before = jnp.where(ids < cols, 1.0, 0.0).astype(BF)
    routed = jnp.where(gin[...].reshape(TOK, TOK) > 0, 1.0, 0.0).astype(BF)
    rank[...] = jnp.dot(routed, before, preferred_element_type=F32).reshape(16, 8, TOK)
    for load in loads:
        load.wait()
    ggo[...] = jnp.zeros_like(ggo)
    slot_ids = lax.broadcasted_iota(jnp.int32, (SLOTS, TOK), 0).astype(F32)

    def source_of(g, j):
        b = jnp.where(g == 0, 0, jnp.where(g == 1, 2, jnp.where(g == 2, 3, 1)))
        a = jnp.where(j == 0, 0, jnp.where(j == 1, 3, jnp.where(j == 2, 1, 2)))
        return wrap(p + a) * 4 + wrap(q + b)

    def pick_source(g, j):
        src = source_of(g, j)
        token_rows, up_rows = xs[src], us[src]
        base = pl.multiple_of(g * 4 * SLOTS + j * SLOTS, 16)
        for e in range(2):
            gate_row = gin[src, e : e + 1, :]
            hit = (rank[src, e : e + 1, :] == slot_ids) & (gate_row > 0)
            pick = jnp.where(hit, 1.0, 0.0)
            pick_low = pick.astype(BF)
            picks[src, e * SLOTS : (e + 1) * SLOTS, :] = pick_low
            gate_col = jnp.sum(pick * gate_row, axis=1, keepdims=True)
            rows[e, pl.ds(base, SLOTS), :] = jnp.dot(
                pick_low, token_rows, preferred_element_type=F32
            ).astype(BF)
            picked = jnp.dot(pick_low, up_rows, preferred_element_type=F32)
            rows_up[e, pl.ds(pl.multiple_of(j * SLOTS, 16), SLOTS), :] = picked.astype(BF)
            slot_grads[e, pl.ds(base, SLOTS), :] = (picked * gate_col).astype(BF)

    def run_expert(g, e):
        base = pl.multiple_of(g * 4 * SLOTS, 16)
        span = pl.ds(base, 4 * SLOTS)
        taken = rows[e, span, :]
        gate = jnp.dot(taken, wg[e], preferred_element_type=F32)
        upv = jnp.dot(taken, wu[e], preferred_element_type=F32)
        sig = 1.0 / (1.0 + jnp.exp(-gate))
        silu = gate * sig
        act = (silu * upv).astype(BF)
        acts[e, span, :] = act
        out = jnp.dot(act, wd[e], preferred_element_type=F32).astype(BF)
        outs[e] = out
        gg_col = jnp.sum(out.astype(F32) * rows_up[e].astype(F32), axis=1, keepdims=True)
        for j in range(4):
            src = source_of(g, j)
            pick = picks[src, pl.ds(pl.multiple_of(e * SLOTS, 16), SLOTS), :].astype(F32)
            part = gg_col[j * SLOTS : (j + 1) * SLOTS]
            ggo[src, pl.ds(e, 1), :] = jnp.sum(pick * part, axis=0, keepdims=True)
        grad_act = lax.dot_general(
            slot_grads[e, span, :], wd[e], (((1,), (1,)), ((), ())), preferred_element_type=F32
        )
        ggp = (grad_act * upv * sig * (1.0 + gate * (1.0 - sig))).astype(BF)
        gup = (grad_act * silu).astype(BF)
        gparts[e, span, :] = ggp
        uparts[e, span, :] = gup
        pair = lax.dot_general(ggp, wg[e], (((1,), (1,)), ((), ())), preferred_element_type=F32)
        pair += lax.dot_general(gup, wu[e], (((1,), (1,)), ((), ())), preferred_element_type=F32)
        pairs[e] = pair.astype(BF)

    def spread(g, j):
        src = source_of(g, j)
        pick = picks[src]
        span = pl.ds(pl.multiple_of(j * SLOTS, 16), SLOTS)
        gates = jnp.concatenate(
            [
                pick[e * SLOTS : (e + 1) * SLOTS].astype(F32) * gin[src, e : e + 1, :]
                for e in range(2)
            ],
            axis=0,
        ).astype(BF)
        both = jnp.concatenate([outs[0, span, :], outs[1, span, :]], axis=0)
        o_buf[src] = lax.dot_general(
            gates, both, (((0,), (0,)), ((), ())), preferred_element_type=F32
        ).astype(BF)
        both = jnp.concatenate([pairs[0, span, :], pairs[1, span, :]], axis=0)
        p_buf[src] = lax.dot_general(
            pick, both, (((0,), (0,)), ((), ())), preferred_element_type=F32
        ).astype(BF)

    def chunk(g):
        lax.fori_loop(0, 4, lambda j, c: (pick_source(g, j), c)[1], 0)
        lax.fori_loop(0, 2, lambda e, c: (run_expert(g, e), c)[1], 0)
        lax.fori_loop(0, 4, lambda j, c: (spread(g, j), c)[1], 0)

    OFF = (0, -1, 1, 2)
    R = 16

    def make(source, target, recv, to, index):
        return pltpu.make_async_remote_copy(
            src_ref=source,
            dst_ref=target,
            send_sem=send_sem.at[index],
            recv_sem=recv_sem.at[recv],
            device_id=to,
            device_id_type=MESH,
        )

    first = len(net.made)
    far = [
        lambda: make(slab(xs, p + 1, q + 1), slab(xs, p + 1, q + 1), 14, down, first),
        lambda: make(slab(xs, p + 2, q + 1), slab(xs, p + 2, q + 1), 15, down, first + 1),
    ]
    bounce = [
        (lambda j=j: make(slab(p_buf, p + OFF[j], q + 2), rb.at[j], R + j, up if j < 2 else down, first + 2 + j))
        for j in range(4)
    ]
    to_down = [
        (lambda j=j: make(slab(p_buf, p + OFF[j], q - 1), rc.at[4 + j], R + 8 + j, down, first + 6 + j))
        for j in range(4)
    ]
    to_up = [
        (lambda j=j: make(slab(p_buf, p + OFF[j], q + 1), rc.at[j], R + 4 + j, up, first + 10 + j))
        for j in range(4)
    ]

    def add_bounce(j):
        net.arrived(rb.at[j], R + j)
        target = slab(p_buf, p + OFF[j], q + 1 if j < 2 else q - 1)
        target[...] = (target[...].astype(F32) + rb[j].astype(F32)).astype(BF)

    def step(g, carry):
        @pl.when(g == 1)
        def _():
            net.arrived(slab(xs, p + 1, q + 1), 10)
            far[0]().start()
            net.arrived(slab(xs, p + 2, q + 1), 11)
            far[1]().start()
            net.arrived(slab(xs, p, q + 2), 12)
            net.arrived(slab(xs, p - 1, q + 2), 13)
            net.arrived(slab(xs, p + 1, q + 2), 14)
            net.arrived(slab(xs, p + 2, q + 2), 15)

        @pl.when(g == 2)
        def _():
            net.arrived(slab(xs, p + 1, q - 1), 6)
            net.arrived(slab(xs, p + 2, q - 1), 7)

        @pl.when(g == 3)
        def _():
            net.arrived(slab(xs, p, q + 1), 8)
            net.arrived(slab(xs, p - 1, q + 1), 9)

        chunk(g)

        @pl.when(g == 1)
        def _():
            for j in range(4):
                bounce[j]().start()

        @pl.when(g == 2)
        def _():
            to_down[0]().start()
            to_down[1]().start()
            for j in (3, 2):
                add_bounce(j)
                to_down[j]().start()

        @pl.when(g == 3)
        def _():
            to_up[3]().start()
            to_up[2]().start()
            for j in (1, 0):
                add_bounce(j)
                to_up[j]().start()

        return carry

    lax.fori_loop(0, 4, step, 0)

    def gg_copy(i):
        a, b = lax.div(i, 4), lax.rem(i, 4)
        return pltpu.make_async_remote_copy(
            src_ref=ggo.at[wrap(p + a) * 4 + wrap(q + b)],
            dst_ref=gg_out.at[my_chip],
            send_sem=gg_send.at[i],
            recv_sem=gg_recv.at[wrap(-a) * 4 + wrap(-b)],
            device_id=device(p + a, q + b, y, core),
            device_id_type=MESH,
        )

    def start_gg(i, _):
        gg_copy(i).start()
        return 0

    lax.fori_loop(1, 16, start_gg, 0)
    gg_out[my_chip] = ggo[p * 4 + q]
    o_store = pltpu.make_async_copy(o_buf, o_hbm, local_sem.at[4])
    o_store.start()

    def weight_tile(e, t):
        cols = pl.ds(pl.multiple_of(t * 256, 256), 256)
        dims = (((0,), (0,)), ((), ()))
        lhs = rows[e, :, cols]
        dwg[e, cols, :] = lax.dot_general(lhs, gparts[e], dims, preferred_element_type=F32).astype(BF)
        dwu[e, cols, :] = lax.dot_general(lhs, uparts[e], dims, preferred_element_type=F32).astype(BF)
        dwd[e, :, cols] = lax.dot_general(
            acts[e], slot_grads[e, :, cols], dims, preferred_element_type=F32
        ).astype(BF)

    def weight_grads(e):
        lax.fori_loop(0, 4, lambda t, c: (weight_tile(e, t), c)[1], 0)

    weight_grads(0)

    def gather_sum(j):
        net.arrived(rc.at[j], R + 4 + j)
        net.arrived(rc.at[4 + j], R + 8 + j)
        target = slab(p_buf, p + OFF[j], q)
        target[...] = (
            target[...].astype(F32) + rc[j].astype(F32) + rc[4 + j].astype(F32)
        ).astype(BF)

    last = first + 14
    lo, hi = pl.ds(0, 64), pl.ds(64, 64)
    far_slab, next_slab, prev_slab = slab(p_buf, p + 2, q), slab(p_buf, p + 1, q), slab(p_buf, p - 1, q)
    tail = [
        make(far_slab.at[lo], rd.at[lo], R + 12, right, last),
        make(far_slab.at[hi], rd.at[hi], R + 13, left, last + 1),
        make(next_slab.at[hi], re.at[0, hi], R + 14, right, last + 2),
        make(prev_slab.at[lo], re.at[1, lo], R + 15, left, last + 3),
        make(next_slab.at[lo], re.at[0, lo], R + 16, right, last + 4),
        make(prev_slab.at[hi], re.at[1, hi], R + 17, left, last + 5),
    ]
    gather_sum(3)
    tail[0].start()
    tail[1].start()
    gather_sum(2)
    tail[2].start()
    gather_sum(1)
    tail[3].start()
    net.arrived(rd.at[lo], R + 12)
    next_slab[lo] = (next_slab[lo].astype(F32) + rd[lo].astype(F32)).astype(BF)
    tail[4].start()
    net.arrived(rd.at[hi], R + 13)
    prev_slab[hi] = (prev_slab[hi].astype(F32) + rd[hi].astype(F32)).astype(BF)
    tail[5].start()
    gather_sum(0)
    weight_grads(1)
    stores = [
        pltpu.make_async_copy(src, dst, local_sem.at[i])
        for i, (src, dst) in enumerate(((dwg, dwg_hbm), (dwu, dwu_hbm), (dwd, dwd_hbm)))
    ]
    for store in stores:
        store.start()
    net.arrived(re.at[0, hi], R + 14)
    net.arrived(re.at[1, lo], R + 15)
    net.arrived(re.at[0, lo], R + 16)
    net.arrived(re.at[1, hi], R + 17)
    grad_out[...] = slab(p_buf, p, q)[...].astype(F32) + re[0].astype(F32) + re[1].astype(F32)

    def take_gg(i, _):
        pltpu.make_async_copy(ggo.at[0], ggo.at[0], gg_recv.at[i]).wait()
        return 0

    lax.fori_loop(1, 16, take_gg, 0)
    net.drain()
    for copy in far + bounce + to_down + to_up:
        copy().wait_send()
    for copy in tail:
        copy.wait_send()

    def drain_small(i, _):
        gate_copy(i).wait_send()
        gg_copy(i).wait_send()
        return 0

    lax.fori_loop(1, 16, drain_small, 0)
    o_store.wait()
    for store in stores:
        store.wait()


def moe(x, gt, u, wg, wu, wd):
    any_space = pl.BlockSpec(memory_space=pl.ANY)
    vmem = pl.BlockSpec(memory_space=pltpu.VMEM)
    shape = jax.ShapeDtypeStruct
    slots = 16 * SLOTS
    dma = pltpu.SemaphoreType.DMA
    return pl.pallas_call(
        moe_kernel,
        out_shape=(
            shape((TOK, D), F32),
            shape((16, TOK, D), BF),
            shape((16, 8, TOK), F32),
            shape((2, D, FF), BF),
            shape((2, D, FF), BF),
            shape((2, FF, D), BF),
        ),
        in_specs=[vmem, vmem, any_space, any_space, any_space, any_space],
        out_specs=(vmem, any_space, vmem, any_space, any_space, any_space),
        scratch_shapes=[
            pltpu.VMEM((16, TOK, D), BF),
            pltpu.VMEM((16, TOK, D), BF),
            pltpu.VMEM((2, D, FF), BF),
            pltpu.VMEM((2, D, FF), BF),
            pltpu.VMEM((2, FF, D), BF),
            pltpu.VMEM((16, 8, TOK), F32),
            pltpu.VMEM((16, 8, TOK), F32),
            pltpu.VMEM((16, 8, TOK), F32),
            pltpu.VMEM((16, 2 * SLOTS, TOK), BF),
            pltpu.VMEM((2, slots, D), BF),
            pltpu.VMEM((2, 4 * SLOTS, D), BF),
            pltpu.VMEM((2, slots, D), BF),
            pltpu.VMEM((2, slots, FF), BF),
            pltpu.VMEM((2, slots, FF), BF),
            pltpu.VMEM((2, slots, FF), BF),
            pltpu.VMEM((2, 4 * SLOTS, D), BF),
            pltpu.VMEM((2, 4 * SLOTS, D), BF),
            pltpu.VMEM((16, TOK, D), BF),
            pltpu.VMEM((16, TOK, D), BF),
            pltpu.VMEM((4, TOK, D), BF),
            pltpu.VMEM((8, TOK, D), BF),
            pltpu.VMEM((TOK, D), BF),
            pltpu.VMEM((2, TOK, D), BF),
            pltpu.VMEM((2, D, FF), BF),
            pltpu.VMEM((2, D, FF), BF),
            pltpu.VMEM((2, FF, D), BF),
            dma((40,)),
            dma((34,)),
            dma((16,)),
            dma((16,)),
            dma((16,)),
            dma((16,)),
            dma((5,)),
        ],
        compiler_params=pltpu.CompilerParams(
            collective_id=1, has_side_effects=True, vmem_limit_bytes=VMEM_BYTES
        ),
        name="experts",
    )(x, gt, u, wg, wu, wd)


HALF = HEAD_DIM // 2
SCALE = HEAD_DIM**-0.5


def turn_tables():
    inverse = 10000.0 ** (-np.arange(HALF, dtype=np.float32) / HALF)
    phases = np.arange(4 * TOK, dtype=np.float32)[:, None] * inverse[None, :]
    cosine = np.tile(np.cos(phases), (1, 4)).astype(np.float32)
    sine = np.sin(phases)
    sine = np.tile(np.concatenate([-sine, sine], axis=1), (1, 2)).astype(np.float32)
    return cosine, sine


def lanes(rows, width=128):
    return lax.broadcasted_iota(jnp.int32, (rows, width), 1)


def turn(chunk, cosine, sine):
    front = lax.rem(lanes(chunk.shape[0]), HEAD_DIM) < HALF
    swapped = jnp.where(front, pltpu.roll(chunk, 128 - HALF, 1), pltpu.roll(chunk, HALF, 1))
    return chunk * cosine + swapped * sine


def stack_heads(chunk, half):
    low = lanes(chunk.shape[0]) < HEAD_DIM
    rolled = pltpu.roll(chunk, HEAD_DIM, 1)
    if half == 0:
        pair = (jnp.where(low, chunk, 0.0), jnp.where(low, rolled, 0.0))
    else:
        pair = (jnp.where(low, 0.0, rolled), jnp.where(low, 0.0, chunk))
    return jnp.concatenate(pair, axis=0).astype(BF)


def unstack_heads(pair, half):
    first, second = pair[:TOK], pair[TOK:]
    low = lanes(TOK) < HEAD_DIM
    if half == 0:
        return jnp.where(low, first, pltpu.roll(second, HEAD_DIM, 1))
    return jnp.where(low, pltpu.roll(first, HEAD_DIM, 1), second)


def root(values):
    return lax.rsqrt(jnp.mean(values * values, axis=1, keepdims=True) + 1e-06)


def widen():
    row = lax.broadcasted_iota(jnp.int32, (EXPERTS, TOK), 0)
    lane = lax.broadcasted_iota(jnp.int32, (EXPERTS, TOK), 1)
    return jnp.where(lane == lax.div(row, 2) * 8 + lax.rem(row, 2), 1.0, 0.0).astype(BF)


def routed_mask(routes):
    lane = lanes(TOK)
    expert = jnp.where(lax.rem(lane, 8) < 2, lax.div(lane, 8) * 2 + lax.rem(lane, 8), -1)
    hit = jnp.zeros((TOK, TOK), F32)
    for k in range(TOP):
        hit = hit + jnp.where(routes[:, k : k + 1] == expert, 1.0, 0.0)
    return hit > 0


class PlaneGather:
    def __init__(self, net, spot, slabs, base):
        self.net, self.spot, self.slabs, self.base = net, spot, slabs, base
        p, q, y, core = spot
        self.right, self.left = device(p + 1, q, y, core), device(p - 1, q, y, core)
        self.up, self.down = device(p, q + 1, y, core), device(p, q - 1, y, core)

    def slab(self, a, b):
        return slab(self.slabs, self.spot[0] + a, self.spot[1] + b)

    def send(self, ref, recv, to):
        self.net.start(ref, ref, self.base + recv, to)

    def arrived(self, ref, recv):
        self.net.arrived(ref, self.base + recv)

    def begin(self, own):
        for recv, to in ((0, self.right), (1, self.left), (4, self.up), (8, self.down)):
            self.net.start(own, self.slab(0, 0), self.base + recv, to)

    def second(self):
        s = self.slab(-1, 0)
        self.arrived(s, 0)
        self.send(s.at[0:64], 2, self.right)
        self.send(s, 5, self.up)
        s = self.slab(1, 0)
        self.arrived(s, 1)
        self.send(s.at[64:128], 3, self.left)
        self.send(s, 10, self.down)

    def third(self):
        s = self.slab(0, -1)
        self.arrived(s, 4)
        self.send(s, 12, self.up)
        s = self.slab(2, 0)
        self.arrived(s.at[0:64], 2)
        self.arrived(s.at[64:128], 3)
        self.send(s, 11, self.down)
        s = self.slab(-1, -1)
        self.arrived(s, 5)
        self.send(s, 13, self.up)
        self.send(self.slab(1, 0), 6, self.up)
        self.send(self.slab(2, 0), 7, self.up)
        self.send(self.slab(-1, 0), 9, self.down)

    def fourth(self):
        for a, recv, far in ((1, 10, 14), (2, 11, 15)):
            s = self.slab(a, 1)
            self.arrived(s, recv)
            self.send(s, far, self.down)

    def finish(self):
        for a, b, recv in (
            (1, -1, 6), (2, -1, 7), (0, 1, 8), (-1, 1, 9),
            (0, 2, 12), (-1, 2, 13), (1, 2, 14), (2, 2, 15),
        ):
            self.arrived(self.slab(a, b), recv)


def front_kernel(
    tok_ref, wq_hbm, wk_hbm, wv_hbm, wo_hbm, ga_ref, gm_ref, router_ref, cot_ref, routes_ref,
    len_ref, cos_ref, sin_ref, wgs_hbm, wus_hbm, wds_hbm,
    hidden_ref, x_ref, gt_ref, gates_ref, mixed_ref, query_ref, kv_ref, probs_hbm,
    u_all, wg_all, wu_all, wd_all,
    wq, wk, wv, wo, u_own, kv, probs, bias,
    send_sem, recv_sem, local_sem,
):
    p, q, y, core = place()
    spot = (p, q, y, core)
    sibling = device(p, q, y, 1 - core)
    sibling = (sibling[0] * 0 + chip_of(p, q, core) * 2 + 1 - core, y)
    ahead, behind = device(p, q, y + 1, core), device(p, q, y - 1, core)
    net = Sends(send_sem, recv_sem)
    loads = {
        name: pltpu.make_async_copy(src, dst, local_sem.at[i])
        for i, (name, src, dst) in enumerate(
            (("k", wk_hbm, wk), ("v", wv_hbm, wv), ("q", wq_hbm, wq), ("o", wo_hbm, wo))
        )
    }
    for load in loads.values():
        load.start()
    gather = PlaneGather(net, spot, u_all, 0)
    first = pl.multiple_of(y * TOK, TOK)
    row = lax.broadcasted_iota(jnp.int32, (TOK, 1), 0) + y * TOK
    length = len_ref[0]
    u_own[...] = jnp.where(row < length, cot_ref[...].astype(F32), 0.0).astype(BF)
    greet([gather.right, gather.left, gather.up, gather.down, ahead, behind, sibling])
    gather.begin(u_own)
    keep_own = pltpu.make_async_copy(u_own, gather.slab(0, 0), local_sem.at[4])
    keep_own.start()

    tokens = tok_ref[...].astype(F32)
    normed = (tokens * root(tokens) * ga_ref[...]).astype(BF)
    cosine, sine = cos_ref[pl.ds(first, TOK), :], sin_ref[pl.ds(first, TOK), :]
    loads["k"].wait()
    keys = jnp.dot(normed, wk[...], preferred_element_type=F32)
    for c in range(4):
        span = slice(c * 128, (c + 1) * 128)
        kv[y, :, span] = turn(keys[:, span], cosine, sine).astype(BF)
    loads["v"].wait()
    kv[y, :, 512:1024] = jnp.dot(normed, wv[...], preferred_element_type=F32).astype(BF)
    own = kv.at[y]
    net.start(own, own, 16, ahead)
    net.start(own, own, 17, behind)

    def weight(a, e, yy, rows=None):
        block = pl.ds(pl.multiple_of(wrap(yy) * TOK, TOK), TOK)
        if a == 2:
            return wd_all.at[e, block, :]
        full = (wg_all, wu_all)[a]
        return full.at[e, :, block] if rows is None else full.at[e, rows, block]

    shards = (wgs_hbm.at[0], wus_hbm.at[0], wds_hbm.at[0])
    top, bottom = pl.ds(0, 512), pl.ds(512, 512)
    keep = []
    for a in range(3):
        net.start(shards[a], weight(a, core, y), 20 + a, ahead)
        net.start(shards[a], weight(a, core, y), 23 + a, behind)
        net.start(shards[a], weight(a, core, y), 30 + a, sibling)
        keep.append(pltpu.make_async_copy(shards[a], weight(a, core, y), local_sem.at[5 + a]))
        keep[-1].start()

    loads["q"].wait()
    queries = jnp.dot(normed, wq[...], preferred_element_type=F32)
    for c in range(8):
        span = slice(c * 128, (c + 1) * 128)
        query_ref[:, span] = turn(queries[:, span], cosine, sine).astype(BF)
    key_pos = lanes(TOK, 512)
    bias[...] = jnp.where((key_pos <= row) & (key_pos < length), 0.0, -1e30)
    gather.second()
    s = kv.at[wrap(y - 1)]
    net.arrived(s, 16)
    net.start(s.at[0:64], s.at[0:64], 18, ahead)
    s = kv.at[wrap(y + 1)]
    net.arrived(s, 17)
    net.start(s.at[64:128], s.at[64:128], 19, behind)
    gather.third()
    s = kv.at[wrap(y + 2)]
    net.arrived(s.at[0:64], 18)
    net.arrived(s.at[64:128], 19)

    def attend(c, carry):
        span = pl.ds(pl.multiple_of(c * 128, 128), 128)
        keys = kv[:, :, span].reshape(512, 128)
        values = kv[:, :, pl.ds(pl.multiple_of(512 + c * 128, 128), 128)].reshape(512, 128)
        for half in range(2):
            m = c * 2 + half
            mine = pl.ds(pl.multiple_of(m * 128, 128), 128)
            pair = stack_heads(query_ref[:, mine].astype(F32), half)
            scores = lax.dot_general(
                pair, keys, (((1,), (1,)), ((), ())), preferred_element_type=F32
            )
            scores = scores * SCALE + jnp.concatenate([bias[...], bias[...]], axis=0)
            scores = jnp.exp(scores - jnp.max(scores, axis=1, keepdims=True))
            low = (scores * (1.0 / jnp.sum(scores, axis=1, keepdims=True))).astype(BF)
            probs[m] = low
            out = jnp.dot(low, values, preferred_element_type=F32)
            mixed_ref[:, mine] = unstack_heads(out, half).astype(BF)
        return carry

    lax.fori_loop(0, 2, attend, 0)
    gather.fourth()
    for a in range(3):
        net.arrived(weight(a, core, y - 1), 20 + a)
    net.start(weight(0, core, y - 1), weight(0, core, y - 1), 26, ahead)
    net.start(weight(1, core, y - 1, top), weight(1, core, y - 1, top), 27, ahead)
    for a in range(3):
        net.arrived(weight(a, core, y + 1), 23 + a)
    net.start(weight(1, core, y + 1, bottom), weight(1, core, y + 1, bottom), 28, behind)
    net.start(weight(2, core, y + 1), weight(2, core, y + 1), 29, behind)
    for a in range(3):
        net.start(weight(a, core, y - 1), weight(a, core, y - 1), 33 + a, sibling)
        net.start(weight(a, core, y + 1), weight(a, core, y + 1), 36 + a, sibling)
    lax.fori_loop(2, 4, attend, 0)
    keep_probs = pltpu.make_async_copy(probs, probs_hbm, local_sem.at[8])
    keep_probs.start()
    loads["o"].wait()
    hidden = tokens + jnp.dot(mixed_ref[...], wo[...], preferred_element_type=F32)
    hidden_ref[...] = hidden
    x = (hidden * root(hidden) * gm_ref[...]).astype(BF)
    x_ref[...] = x
    wide = jnp.dot(router_ref[...], widen(), preferred_element_type=F32).astype(BF)
    logits = jnp.dot(x, wide, preferred_element_type=F32)
    routed = routed_mask(routes_ref[...])
    logits = jnp.where(routed, logits, -1e30)
    weights = jnp.where(routed, jnp.exp(logits - jnp.max(logits, axis=1, keepdims=True)), 0.0)
    weights = weights * (1.0 / jnp.sum(weights, axis=1, keepdims=True))
    gates_ref[...] = weights
    gt_ref[...] = weights.T.reshape(16, 8, TOK)
    kv_ref[...] = kv[...]

    net.arrived(weight(0, core, y + 2), 26)
    net.arrived(weight(1, core, y + 2, top), 27)
    net.arrived(weight(1, core, y + 2, bottom), 28)
    net.arrived(weight(2, core, y + 2), 29)
    for a in range(3):
        net.start(weight(a, core, y + 2), weight(a, core, y + 2), 39 + a, sibling)
    gather.finish()
    for i, step in enumerate((0, -1, 1, 2)):
        for a in range(3):
            net.arrived(weight(a, 1 - core, y + step), 30 + 3 * i + a)
    net.drain()
    keep_own.wait()
    keep_probs.wait()
    for copy in keep:
        copy.wait()


def front(tokens, wq, wk, wv, wo, ga, gm, router, cotangent, routes, lengths, wg, wu, wd):
    cosine, sine = turn_tables()
    any_space = pl.BlockSpec(memory_space=pl.ANY)
    vmem = pl.BlockSpec(memory_space=pltpu.VMEM)
    smem = pl.BlockSpec(memory_space=pltpu.SMEM)
    shape = jax.ShapeDtypeStruct
    dma = pltpu.SemaphoreType.DMA
    return pl.pallas_call(
        front_kernel,
        out_shape=(
            shape((TOK, D), F32),
            shape((TOK, D), BF),
            shape((16, 8, TOK), F32),
            shape((TOK, TOK), F32),
            shape((TOK, D), BF),
            shape((TOK, D), BF),
            shape((4, TOK, D), BF),
            shape((8, 2 * TOK, 512), BF),
            shape((16, TOK, D), BF),
            shape((2, D, FF), BF),
            shape((2, D, FF), BF),
            shape((2, FF, D), BF),
        ),
        in_specs=[vmem] + [any_space] * 4 + [vmem] * 5 + [smem] + [vmem] * 2 + [any_space] * 3,
        out_specs=(vmem,) * 7 + (any_space,) * 5,
        scratch_shapes=[
            pltpu.VMEM((D, D), BF),
            pltpu.VMEM((D, 512), BF),
            pltpu.VMEM((D, 512), BF),
            pltpu.VMEM((D, D), BF),
            pltpu.VMEM((TOK, D), BF),
            pltpu.VMEM((4, TOK, D), BF),
            pltpu.VMEM((8, 2 * TOK, 512), BF),
            pltpu.VMEM((TOK, 512), F32),
            dma((52,)),
            dma((42,)),
            dma((9,)),
        ],
        compiler_params=pltpu.CompilerParams(
            collective_id=3, has_side_effects=True, vmem_limit_bytes=VMEM_BYTES
        ),
        name="front",
    )(
        tokens, wq, wk, wv, wo, ga.reshape(1, D), gm.reshape(1, D), router, cotangent, routes,
        lengths, jnp.asarray(cosine), jnp.asarray(sine), wg, wu, wd,
    )


def total_kernel(
    a_hbm, b_hbm, c_hbm, s_hbm, a_out, b_out, c_out, s_out,
    mine, other, mine_s, other_s, from_low, from_high, from_low_s, from_high_s, bounced, bounced_s,
    spread, spread_s, done, done_s,
    sib_send, sib_recv, ring_send, ring_recv, plane_send, plane_recv, back_send, back_recv,
    round_send, round_recv, last_send, last_recv, local_sem,
):
    dp, y = lax.axis_index("dp"), lax.axis_index("hid")
    core = lax.rem(dp, 2)
    here = (lax.div(dp, 8), y, lax.rem(lax.div(dp, 2), 4))

    def at(spot, on=None):
        spot = [wrap(v) for v in spot]
        return (spot[0] * 8 + spot[2] * 2 + (core if on is None else on), spot[1])

    def along(k, step):
        return at([here[i] + (step if i == k else 0) for i in range(3)])

    sibling = at(here, 1 - core)
    ring = [(along(k, 1), along(k, -1)) for k in range(3)]
    planes = [(1, 2), (0, 2), (0, 1)]
    greeted = [sibling]
    for dx in range(4):
        for dy in range(4):
            for dz in range(4):
                if (dx or dy or dz) and not (dx and dy and dz):
                    greeted.append(at([here[0] + dx, here[1] + dy, here[2] + dz]))
    ins, results = (a_hbm, b_hbm, c_hbm, s_hbm), (a_out, b_out, c_out, s_out)
    axes = (0, 1, 2, 0)
    halves = [mine.at[k] for k in range(3)] + [mine_s]
    theirs = [other.at[k] for k in range(3)] + [other_s]
    lows = [from_low.at[k] for k in range(3)] + [from_low_s]
    highs = [from_high.at[k] for k in range(3)] + [from_high_s]
    hops = [bounced.at[k] for k in range(3)] + [bounced_s]
    pieces = [spread.at[k] for k in range(3)] + [spread_s]
    slabs = [done.at[k] for k in range(3)] + [done_s]
    parts = range(4)
    own_rows = pl.ds(pl.multiple_of(core * 512, 512), 512)
    their_rows = pl.ds(pl.multiple_of((1 - core) * 512, 512), 512)

    def remote(source, target, send, recv, to):
        return pltpu.make_async_remote_copy(
            src_ref=source, dst_ref=target, send_sem=send, recv_sem=recv,
            device_id=to, device_id_type=MESH,
        )

    def arrived(ref, sem):
        pltpu.make_async_copy(ref, ref, sem).wait()

    loads = [
        pltpu.make_async_copy(ins[k].at[own_rows], halves[k], local_sem.at[k]) for k in parts
    ]
    for load in loads:
        load.start()
    greet(greeted)
    sent = []

    def go(*copy):
        copy = remote(*copy)
        copy.start()
        sent.append(copy)

    for k in parts:
        go(ins[k].at[their_rows], theirs[k], sib_send.at[k], sib_recv.at[k], sibling)

    def rows_of(k, step):
        start = pl.multiple_of(wrap(here[axes[k]] + step) * 128, 128)
        return halves[k].at[pl.ds(start, 128)]

    lo, hi = pl.ds(0, 64), pl.ds(64, 64)

    def add(target, *terms):
        total = target[...].astype(F32)
        for term in terms:
            total += term[...].astype(F32)
        target[...] = total.astype(target.dtype)

    def merge_rows(k, step):
        start = pl.multiple_of(wrap(here[axes[k]] + step) * 128, 128)
        span = pl.ds(start, 128)
        add(halves[k].at[span], theirs[k].at[span])

    for k in parts:
        loads[k].wait()
        arrived(theirs[k], sib_recv.at[k])
        plus, minus = ring[axes[k]]
        merge_rows(k, 2)
        far = rows_of(k, 2)
        go(far.at[lo], hops[k].at[lo], ring_send.at[k, 0], ring_recv.at[k, 0], plus)
        go(far.at[hi], hops[k].at[hi], ring_send.at[k, 1], ring_recv.at[k, 1], minus)
        merge_rows(k, 1)
        go(rows_of(k, 1).at[hi], lows[k].at[hi], ring_send.at[k, 2], ring_recv.at[k, 2], plus)
        merge_rows(k, -1)
        go(rows_of(k, -1).at[lo], highs[k].at[lo], ring_send.at[k, 3], ring_recv.at[k, 3], minus)
        merge_rows(k, 0)
    for k in parts:
        plus, minus = ring[axes[k]]
        arrived(hops[k].at[lo], ring_recv.at[k, 0])
        near = rows_of(k, 1).at[lo]
        add(near, hops[k].at[lo])
        go(near, lows[k].at[lo], ring_send.at[k, 4], ring_recv.at[k, 4], plus)
        arrived(hops[k].at[hi], ring_recv.at[k, 1])
        near = rows_of(k, -1).at[hi]
        add(near, hops[k].at[hi])
        go(near, highs[k].at[hi], ring_send.at[k, 5], ring_recv.at[k, 5], minus)

    def piece(k, ref, u, v):
        if k == 3:
            return ref.at[pl.ds(pl.multiple_of((u * 4 + v) * 8, 8), 8)]
        return ref.at[
            pl.ds(pl.multiple_of(u * 32, 32), 32), pl.ds(pl.multiple_of(v * 256, 256), 256)
        ]

    def member(k, i):
        u, v = planes[axes[k]]
        spot = list(here)
        spot[u] = wrap(here[u] + lax.div(i, 4))
        spot[v] = wrap(here[v] + lax.rem(i, 4))
        return spot[u], spot[v], at(spot)

    def mirror(i):
        return wrap(-lax.div(i, 4)) * 4 + wrap(-lax.rem(i, 4))

    def piece_copy(k, i):
        u, v, to = member(k, i)
        return remote(
            piece(k, rows_of(k, 0), u, v),
            pieces[k].at[mirror(i)],
            plane_send.at[k, i],
            plane_recv.at[k, mirror(i)],
            to,
        )

    def back_copy(k, i):
        u, v = planes[axes[k]]
        spot = piece(k, slabs[k], here[u], here[v])
        return remote(spot, spot, back_send.at[k, i], back_recv.at[k, mirror(i)], member(k, i)[2])

    def each(make, act):
        def one(i, carry):
            act(make(i))
            return carry

        lax.fori_loop(1, 16, one, 0)

    for k in parts:
        for i in (2, 4):
            arrived(lows[k].at[hi if i == 2 else lo], ring_recv.at[k, i])
        for i in (3, 5):
            arrived(highs[k].at[lo if i == 3 else hi], ring_recv.at[k, i])
        add(rows_of(k, 0), lows[k], highs[k])
        each(lambda i: piece_copy(k, i), lambda copy: copy.start())
    for k in parts:
        u, v = planes[axes[k]]
        pieces[k][0] = piece(k, rows_of(k, 0), here[u], here[v])[...]
        each(
            lambda i: pltpu.make_async_copy(pieces[k].at[0], pieces[k].at[0], plane_recv.at[k, i]),
            lambda copy: copy.wait(),
        )
        total = jnp.sum(pieces[k][...].astype(F32), axis=0)
        piece(k, slabs[k], here[u], here[v])[...] = total.astype(slabs[k].dtype)
        each(lambda i: back_copy(k, i), lambda copy: copy.start())

    def final(k, step, span=None):
        start = pl.multiple_of(core * 512 + wrap(here[axes[k]] + step) * 128, 128)
        if span is not None:
            start, size = start + span, 64
        else:
            size = 128
        return results[k].at[pl.ds(pl.multiple_of(start, 64), size)]

    stores = []
    for k in parts:
        plus, minus = ring[axes[k]]
        each(
            lambda i: pltpu.make_async_copy(pieces[k].at[0], pieces[k].at[0], back_recv.at[k, i]),
            lambda copy: copy.wait(),
        )
        go(slabs[k], final(k, 0), round_send.at[k, 0], round_recv.at[k, 0], plus)
        go(slabs[k], final(k, 0), round_send.at[k, 1], round_recv.at[k, 1], minus)
        go(slabs[k], final(k, 0), last_send.at[k, 0], last_recv.at[k, 0], sibling)
        store = pltpu.make_async_copy(slabs[k], final(k, 0), local_sem.at[k])
        store.start()
        stores.append(store)
    for k in parts:
        plus, minus = ring[axes[k]]
        arrived(final(k, -1), round_recv.at[k, 0])
        spot = final(k, -1, 0)
        go(spot, spot, round_send.at[k, 2], round_recv.at[k, 2], plus)
        go(final(k, -1), final(k, -1), last_send.at[k, 1], last_recv.at[k, 1], sibling)
        arrived(final(k, 1), round_recv.at[k, 1])
        spot = final(k, 1, 64)
        go(spot, spot, round_send.at[k, 3], round_recv.at[k, 3], minus)
        go(final(k, 1), final(k, 1), last_send.at[k, 2], last_recv.at[k, 2], sibling)
    for k in parts:
        arrived(final(k, 2, 0), round_recv.at[k, 2])
        arrived(final(k, 2, 64), round_recv.at[k, 3])
        go(final(k, 2), final(k, 2), last_send.at[k, 3], last_recv.at[k, 3], sibling)
    for k in parts:
        for i in range(4):
            arrived(final(k, 0), last_recv.at[k, i])
    for copy in sent:
        copy.wait_send()
    for k in parts:
        each(lambda i: piece_copy(k, i), lambda copy: copy.wait_send())
        each(lambda i: back_copy(k, i), lambda copy: copy.wait_send())
    for store in stores:
        store.wait()


def total(a, b, c, s):
    any_space = pl.BlockSpec(memory_space=pl.ANY)
    shape = jax.ShapeDtypeStruct
    dma = pltpu.SemaphoreType.DMA
    vmem = pltpu.VMEM
    return pl.pallas_call(
        total_kernel,
        out_shape=(shape((D, D), BF),) * 3 + (shape((D, TOK), F32),),
        in_specs=[any_space] * 4,
        out_specs=(any_space,) * 4,
        scratch_shapes=[
            vmem((3, 512, D), BF),
            vmem((3, 512, D), BF),
            vmem((512, TOK), F32),
            vmem((512, TOK), F32),
            vmem((3, 128, D), BF),
            vmem((3, 128, D), BF),
            vmem((128, TOK), F32),
            vmem((128, TOK), F32),
            vmem((3, 128, D), BF),
            vmem((128, TOK), F32),
            vmem((3, 16, 32, 256), BF),
            vmem((16, 8, TOK), F32),
            vmem((3, 128, D), BF),
            vmem((128, TOK), F32),
            dma((4,)),
            dma((4,)),
            dma((4, 6)),
            dma((4, 6)),
            dma((4, 16)),
            dma((4, 16)),
            dma((4, 16)),
            dma((4, 16)),
            dma((4, 4)),
            dma((4, 4)),
            dma((4, 4)),
            dma((4, 4)),
            dma((4,)),
        ],
        compiler_params=pltpu.CompilerParams(
            collective_id=2, has_side_effects=True, vmem_limit_bytes=VMEM_BYTES
        ),
        name="total",
    )(a, b, c, s)


def rms_forward(values, gain_vector):
    inverse_root = lax.rsqrt(jnp.mean(values * values, axis=-1, keepdims=True) + 1e-06)
    return (values * inverse_root * gain_vector, inverse_root)


def rms_backward(values, inverse_root, gain_vector, upstream):
    scaled = upstream * gain_vector
    grad_gain = jnp.sum(upstream * values * inverse_root, axis=0)
    grad_values = inverse_root * scaled - values * inverse_root**3 * jnp.mean(
        scaled * values, axis=-1, keepdims=True
    )
    return (grad_values, grad_gain)


def rope_tables(first_pos, row_count, head_width):
    half_dim = head_width // 2
    inverse = 10000.0 ** (-jnp.arange(half_dim, dtype=jnp.float32) / half_dim)
    phases = (first_pos + jnp.arange(row_count, dtype=jnp.float32))[:, None] * inverse[None, :]
    return (jnp.sin(phases)[:, None, :], jnp.cos(phases)[:, None, :])


def rotate(values, sine_table, cosine_table):
    half_dim = values.shape[-1] // 2
    front_half = values[..., :half_dim]
    back_half = values[..., half_dim:]
    return jnp.concatenate(
        [
            front_half * cosine_table - back_half * sine_table,
            back_half * cosine_table + front_half * sine_table,
        ],
        axis=-1,
    )


def unrotate(grad_values, sine_table, cosine_table):
    half_dim = grad_values.shape[-1] // 2
    front_half = grad_values[..., :half_dim]
    back_half = grad_values[..., half_dim:]
    return jnp.concatenate(
        [
            front_half * cosine_table + back_half * sine_table,
            back_half * cosine_table - front_half * sine_table,
        ],
        axis=-1,
    )


def shards(
    tokens,
    w_query,
    w_key,
    w_value,
    w_output,
    gain_attn,
    gain_moe,
    router,
    w_gate,
    w_up,
    w_down,
    cotangent,
    routes,
    lengths,
):
    tok_count = tokens.shape[0]
    hid_pos = lax.axis_index("hid")
    first_pos = (hid_pos * tok_count).astype(jnp.float32)
    group_size = HEADS // KV_HEADS
    score_scale = HEAD_DIM ** (-0.5)
    inputs = tokens.astype(jnp.float32)
    normed, root_attn = rms_forward(inputs, gain_attn)
    normed_low = normed.astype(jnp.bfloat16)
    sine_table, cosine_table = rope_tables(first_pos, tok_count, HEAD_DIM)
    (
        hidden, normed_two_low, gate_tiles, gates, mixed_low, query_low, kv, probs,
        upstream_all, full_gate, full_up, full_down,
    ) = front(
        tokens, w_query, w_key, w_value, w_output, gain_attn, gain_moe, router, cotangent, routes,
        lengths, w_gate, w_up, w_down,
    )
    root_moe = lax.rsqrt(jnp.mean(hidden * hidden, axis=-1, keepdims=True) + 1e-06)
    route_onehot = (routes[:, :, None] == jnp.arange(EXPERTS, dtype=jnp.int32)).astype(jnp.float32)
    kv = kv.reshape(512, D)
    keys_all = kv[:, :512].reshape(512, KV_HEADS, HEAD_DIM)
    values_all = kv[:, 512:].reshape(512, KV_HEADS, HEAD_DIM)
    grouped = query_low.reshape(tok_count, KV_HEADS, group_size, HEAD_DIM)
    query_pos = hid_pos * tok_count + jnp.arange(tok_count, dtype=jnp.int32)
    score_scale = HEAD_DIM ** (-0.5)
    softmaxed_low = probs.reshape(KV_HEADS, group_size, tok_count, 512)
    softmaxed = softmaxed_low.astype(jnp.float32)
    gate_weights = jnp.sum(gates.reshape(tok_count, 16, 8)[:, :, :2].reshape(tok_count, 1, EXPERTS) * route_onehot, axis=-1)
    core_groups = [[2 * i for i in range(16)], [2 * i + 1 for i in range(16)]]
    pair_groups = [[2 * i, 2 * i + 1] for i in range(16)]
    live_rows = (query_pos < lengths[0]).astype(jnp.float32)
    upstream_low = jnp.where(live_rows[:, None] > 0, cotangent, jnp.zeros_like(cotangent))
    upstream = upstream_low.astype(jnp.float32)
    core = lax.rem(lax.axis_index("dp"), 2)

    def by_place(rows):
        rows = rows.reshape(4, 4, TOK, D)
        return jnp.where(core == 0, rows, rows.transpose(1, 0, 2, 3)).reshape(16, TOK, D)

    grad_rows, out_parts, grad_gates_t, part_gate, part_up, part_down = moe(
        normed_two_low,
        gate_tiles,
        upstream_all,
        full_gate,
        full_up,
        full_down,
    )
    moe_out = lax.psum_scatter(by_place(out_parts), "dp", axis_index_groups=core_groups)
    layer_out = (hidden + moe_out.astype(jnp.float32)).astype(jnp.bfloat16)
    parts = jnp.stack([part_gate, part_up, part_down.transpose(0, 2, 1)], axis=1)
    parts = parts.reshape(2, 3, D, 4, TOK).transpose(0, 3, 1, 2, 4)
    parts = lax.psum_scatter(parts, "dp", axis_index_groups=pair_groups)
    parts = lax.psum_scatter(parts, "hid").astype(jnp.float32)
    grad_gate, grad_up, grad_down = parts[0][None], parts[1][None], parts[2].T[None]
    grad_gates = jnp.einsum("et,tke->tk", grad_gates_t[:, :2].reshape(EXPERTS, TOK), route_onehot, precision=lax.Precision.HIGHEST)
    grad_picked = gate_weights * (
        grad_gates - jnp.sum(gate_weights * grad_gates, axis=-1, keepdims=True)
    )
    grad_logits = jnp.sum(grad_picked[:, :, None] * route_onehot, axis=1).astype(jnp.bfloat16)
    grad_router = jnp.einsum(
        "td,te->de", normed_two_low, grad_logits, preferred_element_type=jnp.float32
    )
    grad_normed_two = grad_rows + jnp.einsum(
        "te,de->td", grad_logits, router, preferred_element_type=jnp.float32
    )
    grad_hidden_part, grad_gain_moe = rms_backward(hidden, root_moe, gain_moe, grad_normed_two)
    grad_hidden = upstream + grad_hidden_part
    grad_hidden_low = grad_hidden.astype(jnp.bfloat16)
    grad_w_output = jnp.einsum(
        "tf,td->fd", mixed_low, grad_hidden_low, preferred_element_type=jnp.float32
    )
    grad_mixed = jnp.einsum(
        "td,fd->tf", grad_hidden_low, w_output, preferred_element_type=jnp.float32
    )
    grad_mixed = grad_mixed.astype(jnp.bfloat16).reshape(tok_count, KV_HEADS, group_size, HEAD_DIM)
    grad_probs = jnp.einsum(
        "tkgd,skd->kgts", grad_mixed, values_all, preferred_element_type=jnp.float32
    )
    grad_scores = (
        softmaxed * (grad_probs - jnp.sum(softmaxed * grad_probs, axis=-1, keepdims=True))
    ).astype(jnp.bfloat16)
    grad_query = (
        jnp.einsum("kgts,skd->tkgd", grad_scores, keys_all, preferred_element_type=jnp.float32)
        * score_scale
    )
    grad_key_part = (
        jnp.einsum("kgts,tkgd->skd", grad_scores, grouped, preferred_element_type=jnp.float32)
        * score_scale
    )
    grad_value_part = jnp.einsum(
        "kgts,tkgd->skd", softmaxed_low, grad_mixed, preferred_element_type=jnp.float32
    )
    grad_key, grad_value = (
        lax.psum_scatter(
            grad_key_part.astype(jnp.bfloat16), "hid", scatter_dimension=0, tiled=True
        ).astype(jnp.float32),
        lax.psum_scatter(
            grad_value_part.astype(jnp.bfloat16), "hid", scatter_dimension=0, tiled=True
        ).astype(jnp.float32),
    )
    grad_query_low = unrotate(
        grad_query.reshape(tok_count, HEADS, HEAD_DIM), sine_table, cosine_table
    )
    grad_query_low = grad_query_low.astype(jnp.bfloat16).reshape(tok_count, HEADS * HEAD_DIM)
    grad_key_low = (
        unrotate(grad_key, sine_table, cosine_table)
        .astype(jnp.bfloat16)
        .reshape(tok_count, KV_HEADS * HEAD_DIM)
    )
    grad_value_low = grad_value.astype(jnp.bfloat16).reshape(tok_count, KV_HEADS * HEAD_DIM)
    grad_w_query = jnp.einsum(
        "td,tf->df", normed_low, grad_query_low, preferred_element_type=jnp.float32
    )
    grad_w_key = jnp.einsum(
        "td,tf->df", normed_low, grad_key_low, preferred_element_type=jnp.float32
    )
    grad_w_value = jnp.einsum(
        "td,tf->df", normed_low, grad_value_low, preferred_element_type=jnp.float32
    )
    grad_normed = (
        jnp.einsum("tf,df->td", grad_query_low, w_query, preferred_element_type=jnp.float32)
        + jnp.einsum("tf,df->td", grad_key_low, w_key, preferred_element_type=jnp.float32)
        + jnp.einsum("tf,df->td", grad_value_low, w_value, preferred_element_type=jnp.float32)
    )
    grad_input_part, grad_gain_attn = rms_backward(inputs, root_attn, gain_attn, grad_normed)
    grad_input = grad_hidden + grad_input_part
    counts_local = jnp.sum(route_onehot, axis=(0, 1))
    narrow = jnp.concatenate(
        [
            grad_router,
            grad_gain_attn[:, None],
            grad_gain_moe[:, None],
            jnp.pad(counts_local, (0, D - EXPERTS))[:, None],
            jnp.zeros((D, TOK - EXPERTS - 3), jnp.float32),
        ],
        axis=1,
    )
    sum_q, sum_o, sum_kv, narrow = total(
        grad_w_query.astype(BF),
        grad_w_output.astype(BF),
        jnp.concatenate([grad_w_key, grad_w_value], axis=1).astype(BF),
        narrow,
    )
    sum_kv = sum_kv.astype(jnp.float32)
    return (
        layer_out,
        grad_input,
        sum_q.astype(jnp.float32),
        sum_kv[:, :512],
        sum_kv[:, 512:],
        sum_o.astype(jnp.float32),
        narrow[:, EXPERTS],
        narrow[:, EXPERTS + 1],
        narrow[:, :EXPERTS],
        grad_gate,
        grad_up,
        grad_down,
        narrow[:EXPERTS, EXPERTS + 2].astype(jnp.int32),
    )


def solution(mesh):
    in_specs = (
        P(("dp", "hid"), None),
        P(),
        P(),
        P(),
        P(),
        P(),
        P(),
        P(),
        P("dp", None, "hid"),
        P("dp", None, "hid"),
        P("dp", "hid", None),
        P(("dp", "hid"), None),
        P(("dp", "hid"), None),
        P("dp"),
    )
    out_specs = (
        P(("dp", "hid"), None),
        P(("dp", "hid"), None),
        P(),
        P(),
        P(),
        P(),
        P(),
        P(),
        P(),
        P("dp", None, "hid"),
        P("dp", None, "hid"),
        P("dp", "hid", None),
        P(),
    )
    return jax.shard_map(shards, mesh=mesh, in_specs=in_specs, out_specs=out_specs, check_vma=False)
```

```python
import jax
import jax.numpy as jnp
import numpy as np
from jax import lax
from jax.experimental import pallas as pl
from jax.experimental.pallas import tpu as pltpu
from jax.sharding import PartitionSpec as P

D = 1024
HEADS = 16
KV_HEADS = 8
HEAD_DIM = 64
EXPERTS = 32
TOP = 8
FF = 512
TOK = 128

MESH = pl.DeviceIdType.MESH
BF = jnp.bfloat16
F32 = jnp.float32
SLOTS = 48
VMEM_BYTES = 60 * 2**20


def wrap(value):
    return lax.rem(value + 4, 4)


def place():
    dp = lax.axis_index("dp")
    y = lax.axis_index("hid")
    core = lax.rem(dp, 2)
    x = lax.div(dp, 8)
    z = lax.rem(lax.div(dp, 2), 4)
    p = jnp.where(core == 0, x, z)
    q = jnp.where(core == 0, z, x)
    return p, q, y, core


def device(p, q, y, core):
    p, q = wrap(p), wrap(q)
    return (jnp.where(core == 0, p * 8 + q * 2, q * 8 + p * 2) + core, wrap(y))


def chip_of(p, q, core):
    p, q = wrap(p), wrap(q)
    return jnp.where(core == 0, p * 4 + q, q * 4 + p)


def greet(devices):
    barrier = pltpu.get_barrier_semaphore()
    for other in devices:
        pl.semaphore_signal(barrier, inc=1, device_id=other, device_id_type=MESH)
    pl.semaphore_wait(barrier, len(devices))


class Sends:
    def __init__(self, send_sem, recv_sem):
        self.send_sem, self.recv_sem, self.made = send_sem, recv_sem, []

    def start(self, source, target, recv, to):
        copy = pltpu.make_async_remote_copy(
            src_ref=source,
            dst_ref=target,
            send_sem=self.send_sem.at[len(self.made)],
            recv_sem=self.recv_sem.at[recv],
            device_id=to,
            device_id_type=MESH,
        )
        copy.start()
        self.made.append(copy)

    def arrived(self, ref, recv):
        pltpu.make_async_copy(ref, ref, self.recv_sem.at[recv]).wait()

    def drain(self):
        for copy in self.made:
            copy.wait_send()
        self.made = []


def slab(buffer, p, q):
    return buffer.at[wrap(p) * 4 + wrap(q)]


def moe_kernel(
    x_ref, gt_ref, u_hbm, wg_hbm, wu_hbm, wd_hbm,
    grad_out, o_hbm, gg_out, dwg_hbm, dwu_hbm, dwd_hbm,
    xs, us, wg, wu, wd, gin, rank, ggo, picks, rows, rows_up, slot_grads, acts, gparts, uparts,
    outs, pairs, o_buf, p_buf, rb, rc, rd, re, dwg, dwu, dwd,
    send_sem, recv_sem, g_send, g_recv, gg_send, gg_recv, local_sem,
):
    p, q, y, core = place()
    me = device(p, q, y, core)
    right, left = device(p + 1, q, y, core), device(p - 1, q, y, core)
    up, down = device(p, q + 1, y, core), device(p, q - 1, y, core)
    others = [device(p + a, q + b, y, core) for a in range(4) for b in range(4) if a or b]
    loads = [
        pltpu.make_async_copy(src, dst, local_sem.at[i])
        for i, (src, dst) in enumerate(((u_hbm, us), (wg_hbm, wg), (wu_hbm, wu), (wd_hbm, wd)))
    ]
    for load in loads:
        load.start()
    greet(others)
    net = Sends(send_sem, recv_sem)
    my_chip = chip_of(p, q, core)

    own = slab(xs, p, q)
    net.start(x_ref, own, 0, right)
    net.start(x_ref, own, 1, left)
    net.start(x_ref, own, 4, up)
    net.start(x_ref, own, 8, down)

    def gate_copy(i):
        a, b = lax.div(i, 4), lax.rem(i, 4)
        return pltpu.make_async_remote_copy(
            src_ref=gt_ref.at[chip_of(p + a, q + b, core)],
            dst_ref=gin.at[p * 4 + q],
            send_sem=g_send.at[i],
            recv_sem=g_recv.at[wrap(-a) * 4 + wrap(-b)],
            device_id=device(p + a, q + b, y, core),
            device_id_type=MESH,
        )

    def start_gate(i, _):
        gate_copy(i).start()
        return 0

    lax.fori_loop(1, 16, start_gate, 0)
    gin[p * 4 + q] = gt_ref[my_chip]
    own[...] = x_ref[...]

    s = slab(xs, p - 1, q)
    net.arrived(s, 0)
    net.start(s.at[0:64], s.at[0:64], 2, right)
    net.start(s, s, 5, up)
    s = slab(xs, p + 1, q)
    net.arrived(s, 1)
    net.start(s.at[64:128], s.at[64:128], 3, left)
    net.start(s, s, 10, down)
    s = slab(xs, p, q - 1)
    net.arrived(s, 4)
    net.start(s, s, 12, up)
    s = slab(xs, p + 2, q)
    net.arrived(s.at[0:64], 2)
    net.arrived(s.at[64:128], 3)
    net.start(s, s, 11, down)
    s = slab(xs, p - 1, q - 1)
    net.arrived(s, 5)
    net.start(s, s, 13, up)
    s = slab(xs, p + 1, q)
    net.start(s, s, 6, up)
    s = slab(xs, p + 2, q)
    net.start(s, s, 7, up)
    s = slab(xs, p - 1, q)
    net.start(s, s, 9, down)

    def take_gate(i, _):
        pltpu.make_async_copy(gin.at[0], gin.at[0], g_recv.at[i]).wait()
        return 0

    lax.fori_loop(1, 16, take_gate, 0)
    ids = lax.broadcasted_iota(jnp.int32, (TOK, TOK), 0)
    cols = lax.broadcasted_iota(jnp.int32, (TOK, TOK), 1)
    before = jnp.where(ids < cols, 1.0, 0.0).astype(BF)
    routed = jnp.where(gin[...].reshape(TOK, TOK) > 0, 1.0, 0.0).astype(BF)
    rank[...] = jnp.dot(routed, before, preferred_element_type=F32).reshape(16, 8, TOK)
    for load in loads:
        load.wait()
    ggo[...] = jnp.zeros_like(ggo)
    slot_ids = lax.broadcasted_iota(jnp.int32, (SLOTS, TOK), 0).astype(F32)

    def source_of(g, j):
        b = jnp.where(g == 0, 0, jnp.where(g == 1, 2, jnp.where(g == 2, 3, 1)))
        a = jnp.where(j == 0, 0, jnp.where(j == 1, 3, jnp.where(j == 2, 1, 2)))
        return wrap(p + a) * 4 + wrap(q + b)

    def pick_source(g, j):
        src = source_of(g, j)
        token_rows, up_rows = xs[src], us[src]
        base = pl.multiple_of(g * 4 * SLOTS + j * SLOTS, 16)
        for e in range(2):
            gate_row = gin[src, e : e + 1, :]
            hit = (rank[src, e : e + 1, :] == slot_ids) & (gate_row > 0)
            pick = jnp.where(hit, 1.0, 0.0)
            pick_low = pick.astype(BF)
            picks[src, e * SLOTS : (e + 1) * SLOTS, :] = pick_low
            gate_col = jnp.sum(pick * gate_row, axis=1, keepdims=True)
            rows[e, pl.ds(base, SLOTS), :] = jnp.dot(
                pick_low, token_rows, preferred_element_type=F32
            ).astype(BF)
            picked = jnp.dot(pick_low, up_rows, preferred_element_type=F32)
            rows_up[e, pl.ds(pl.multiple_of(j * SLOTS, 16), SLOTS), :] = picked.astype(BF)
            slot_grads[e, pl.ds(base, SLOTS), :] = (picked * gate_col).astype(BF)

    def run_expert(g, e):
        base = pl.multiple_of(g * 4 * SLOTS, 16)
        span = pl.ds(base, 4 * SLOTS)
        taken = rows[e, span, :]
        gate = jnp.dot(taken, wg[e], preferred_element_type=F32)
        upv = jnp.dot(taken, wu[e], preferred_element_type=F32)
        sig = 1.0 / (1.0 + jnp.exp(-gate))
        silu = gate * sig
        act = (silu * upv).astype(BF)
        acts[e, span, :] = act
        out = jnp.dot(act, wd[e], preferred_element_type=F32).astype(BF)
        outs[e] = out
        gg_col = jnp.sum(out.astype(F32) * rows_up[e].astype(F32), axis=1, keepdims=True)
        for j in range(4):
            src = source_of(g, j)
            pick = picks[src, pl.ds(pl.multiple_of(e * SLOTS, 16), SLOTS), :].astype(F32)
            part = gg_col[j * SLOTS : (j + 1) * SLOTS]
            ggo[src, pl.ds(e, 1), :] = jnp.sum(pick * part, axis=0, keepdims=True)
        grad_act = lax.dot_general(
            slot_grads[e, span, :], wd[e], (((1,), (1,)), ((), ())), preferred_element_type=F32
        )
        ggp = (grad_act * upv * sig * (1.0 + gate * (1.0 - sig))).astype(BF)
        gup = (grad_act * silu).astype(BF)
        gparts[e, span, :] = ggp
        uparts[e, span, :] = gup
        pair = lax.dot_general(ggp, wg[e], (((1,), (1,)), ((), ())), preferred_element_type=F32)
        pair += lax.dot_general(gup, wu[e], (((1,), (1,)), ((), ())), preferred_element_type=F32)
        pairs[e] = pair.astype(BF)

    def spread(g, j):
        src = source_of(g, j)
        pick = picks[src]
        span = pl.ds(pl.multiple_of(j * SLOTS, 16), SLOTS)
        gates = jnp.concatenate(
            [
                pick[e * SLOTS : (e + 1) * SLOTS].astype(F32) * gin[src, e : e + 1, :]
                for e in range(2)
            ],
            axis=0,
        ).astype(BF)
        both = jnp.concatenate([outs[0, span, :], outs[1, span, :]], axis=0)
        o_buf[src] = lax.dot_general(
            gates, both, (((0,), (0,)), ((), ())), preferred_element_type=F32
        ).astype(BF)
        both = jnp.concatenate([pairs[0, span, :], pairs[1, span, :]], axis=0)
        p_buf[src] = lax.dot_general(
            pick, both, (((0,), (0,)), ((), ())), preferred_element_type=F32
        ).astype(BF)

    def chunk(g):
        lax.fori_loop(0, 4, lambda j, c: (pick_source(g, j), c)[1], 0)
        lax.fori_loop(0, 2, lambda e, c: (run_expert(g, e), c)[1], 0)
        lax.fori_loop(0, 4, lambda j, c: (spread(g, j), c)[1], 0)

    OFF = (0, -1, 1, 2)
    R = 16

    def make(source, target, recv, to, index):
        return pltpu.make_async_remote_copy(
            src_ref=source,
            dst_ref=target,
            send_sem=send_sem.at[index],
            recv_sem=recv_sem.at[recv],
            device_id=to,
            device_id_type=MESH,
        )

    first = len(net.made)
    far = [
        lambda: make(slab(xs, p + 1, q + 1), slab(xs, p + 1, q + 1), 14, down, first),
        lambda: make(slab(xs, p + 2, q + 1), slab(xs, p + 2, q + 1), 15, down, first + 1),
    ]
    bounce = [
        (lambda j=j: make(slab(p_buf, p + OFF[j], q + 2), rb.at[j], R + j, up if j < 2 else down, first + 2 + j))
        for j in range(4)
    ]
    to_down = [
        (lambda j=j: make(slab(p_buf, p + OFF[j], q - 1), rc.at[4 + j], R + 8 + j, down, first + 6 + j))
        for j in range(4)
    ]
    to_up = [
        (lambda j=j: make(slab(p_buf, p + OFF[j], q + 1), rc.at[j], R + 4 + j, up, first + 10 + j))
        for j in range(4)
    ]

    def add_bounce(j):
        net.arrived(rb.at[j], R + j)
        target = slab(p_buf, p + OFF[j], q + 1 if j < 2 else q - 1)
        target[...] = (target[...].astype(F32) + rb[j].astype(F32)).astype(BF)

    def step(g, carry):
        @pl.when(g == 1)
        def _():
            net.arrived(slab(xs, p + 1, q + 1), 10)
            far[0]().start()
            net.arrived(slab(xs, p + 2, q + 1), 11)
            far[1]().start()
            net.arrived(slab(xs, p, q + 2), 12)
            net.arrived(slab(xs, p - 1, q + 2), 13)
            net.arrived(slab(xs, p + 1, q + 2), 14)
            net.arrived(slab(xs, p + 2, q + 2), 15)

        @pl.when(g == 2)
        def _():
            net.arrived(slab(xs, p + 1, q - 1), 6)
            net.arrived(slab(xs, p + 2, q - 1), 7)

        @pl.when(g == 3)
        def _():
            net.arrived(slab(xs, p, q + 1), 8)
            net.arrived(slab(xs, p - 1, q + 1), 9)

        chunk(g)

        @pl.when(g == 1)
        def _():
            for j in range(4):
                bounce[j]().start()

        @pl.when(g == 2)
        def _():
            to_down[0]().start()
            to_down[1]().start()
            for j in (3, 2):
                add_bounce(j)
                to_down[j]().start()

        @pl.when(g == 3)
        def _():
            to_up[3]().start()
            to_up[2]().start()
            for j in (1, 0):
                add_bounce(j)
                to_up[j]().start()

        return carry

    lax.fori_loop(0, 4, step, 0)

    def gg_copy(i):
        a, b = lax.div(i, 4), lax.rem(i, 4)
        return pltpu.make_async_remote_copy(
            src_ref=ggo.at[wrap(p + a) * 4 + wrap(q + b)],
            dst_ref=gg_out.at[my_chip],
            send_sem=gg_send.at[i],
            recv_sem=gg_recv.at[wrap(-a) * 4 + wrap(-b)],
            device_id=device(p + a, q + b, y, core),
            device_id_type=MESH,
        )

    def start_gg(i, _):
        gg_copy(i).start()
        return 0

    lax.fori_loop(1, 16, start_gg, 0)
    gg_out[my_chip] = ggo[p * 4 + q]
    o_store = pltpu.make_async_copy(o_buf, o_hbm, local_sem.at[4])
    o_store.start()

    def weight_tile(e, t):
        cols = pl.ds(pl.multiple_of(t * 256, 256), 256)
        dims = (((0,), (0,)), ((), ()))
        lhs = rows[e, :, cols]
        dwg[e, cols, :] = lax.dot_general(lhs, gparts[e], dims, preferred_element_type=F32).astype(BF)
        dwu[e, cols, :] = lax.dot_general(lhs, uparts[e], dims, preferred_element_type=F32).astype(BF)
        dwd[e, :, cols] = lax.dot_general(
            acts[e], slot_grads[e, :, cols], dims, preferred_element_type=F32
        ).astype(BF)

    def weight_grads(e):
        lax.fori_loop(0, 4, lambda t, c: (weight_tile(e, t), c)[1], 0)

    weight_grads(0)

    def gather_sum(j):
        net.arrived(rc.at[j], R + 4 + j)
        net.arrived(rc.at[4 + j], R + 8 + j)
        target = slab(p_buf, p + OFF[j], q)
        target[...] = (
            target[...].astype(F32) + rc[j].astype(F32) + rc[4 + j].astype(F32)
        ).astype(BF)

    last = first + 14
    lo, hi = pl.ds(0, 64), pl.ds(64, 64)
    far_slab, next_slab, prev_slab = slab(p_buf, p + 2, q), slab(p_buf, p + 1, q), slab(p_buf, p - 1, q)
    tail = [
        make(far_slab.at[lo], rd.at[lo], R + 12, right, last),
        make(far_slab.at[hi], rd.at[hi], R + 13, left, last + 1),
        make(next_slab.at[hi], re.at[0, hi], R + 14, right, last + 2),
        make(prev_slab.at[lo], re.at[1, lo], R + 15, left, last + 3),
        make(next_slab.at[lo], re.at[0, lo], R + 16, right, last + 4),
        make(prev_slab.at[hi], re.at[1, hi], R + 17, left, last + 5),
    ]
    gather_sum(3)
    tail[0].start()
    tail[1].start()
    gather_sum(2)
    tail[2].start()
    gather_sum(1)
    tail[3].start()
    net.arrived(rd.at[lo], R + 12)
    next_slab[lo] = (next_slab[lo].astype(F32) + rd[lo].astype(F32)).astype(BF)
    tail[4].start()
    net.arrived(rd.at[hi], R + 13)
    prev_slab[hi] = (prev_slab[hi].astype(F32) + rd[hi].astype(F32)).astype(BF)
    tail[5].start()
    gather_sum(0)
    weight_grads(1)
    stores = [
        pltpu.make_async_copy(src, dst, local_sem.at[i])
        for i, (src, dst) in enumerate(((dwg, dwg_hbm), (dwu, dwu_hbm), (dwd, dwd_hbm)))
    ]
    for store in stores:
        store.start()
    net.arrived(re.at[0, hi], R + 14)
    net.arrived(re.at[1, lo], R + 15)
    net.arrived(re.at[0, lo], R + 16)
    net.arrived(re.at[1, hi], R + 17)
    grad_out[...] = slab(p_buf, p, q)[...].astype(F32) + re[0].astype(F32) + re[1].astype(F32)

    def take_gg(i, _):
        pltpu.make_async_copy(ggo.at[0], ggo.at[0], gg_recv.at[i]).wait()
        return 0

    lax.fori_loop(1, 16, take_gg, 0)
    net.drain()
    for copy in far + bounce + to_down + to_up:
        copy().wait_send()
    for copy in tail:
        copy.wait_send()

    def drain_small(i, _):
        gate_copy(i).wait_send()
        gg_copy(i).wait_send()
        return 0

    lax.fori_loop(1, 16, drain_small, 0)
    o_store.wait()
    for store in stores:
        store.wait()


def moe(x, gt, u, wg, wu, wd):
    any_space = pl.BlockSpec(memory_space=pl.ANY)
    vmem = pl.BlockSpec(memory_space=pltpu.VMEM)
    shape = jax.ShapeDtypeStruct
    slots = 16 * SLOTS
    dma = pltpu.SemaphoreType.DMA
    return pl.pallas_call(
        moe_kernel,
        out_shape=(
            shape((TOK, D), F32),
            shape((16, TOK, D), BF),
            shape((16, 8, TOK), F32),
            shape((2, D, FF), BF),
            shape((2, D, FF), BF),
            shape((2, FF, D), BF),
        ),
        in_specs=[vmem, vmem, any_space, any_space, any_space, any_space],
        out_specs=(vmem, any_space, vmem, any_space, any_space, any_space),
        scratch_shapes=[
            pltpu.VMEM((16, TOK, D), BF),
            pltpu.VMEM((16, TOK, D), BF),
            pltpu.VMEM((2, D, FF), BF),
            pltpu.VMEM((2, D, FF), BF),
            pltpu.VMEM((2, FF, D), BF),
            pltpu.VMEM((16, 8, TOK), F32),
            pltpu.VMEM((16, 8, TOK), F32),
            pltpu.VMEM((16, 8, TOK), F32),
            pltpu.VMEM((16, 2 * SLOTS, TOK), BF),
            pltpu.VMEM((2, slots, D), BF),
            pltpu.VMEM((2, 4 * SLOTS, D), BF),
            pltpu.VMEM((2, slots, D), BF),
            pltpu.VMEM((2, slots, FF), BF),
            pltpu.VMEM((2, slots, FF), BF),
            pltpu.VMEM((2, slots, FF), BF),
            pltpu.VMEM((2, 4 * SLOTS, D), BF),
            pltpu.VMEM((2, 4 * SLOTS, D), BF),
            pltpu.VMEM((16, TOK, D), BF),
            pltpu.VMEM((16, TOK, D), BF),
            pltpu.VMEM((4, TOK, D), BF),
            pltpu.VMEM((8, TOK, D), BF),
            pltpu.VMEM((TOK, D), BF),
            pltpu.VMEM((2, TOK, D), BF),
            pltpu.VMEM((2, D, FF), BF),
            pltpu.VMEM((2, D, FF), BF),
            pltpu.VMEM((2, FF, D), BF),
            dma((40,)),
            dma((34,)),
            dma((16,)),
            dma((16,)),
            dma((16,)),
            dma((16,)),
            dma((5,)),
        ],
        compiler_params=pltpu.CompilerParams(
            collective_id=1, has_side_effects=True, vmem_limit_bytes=VMEM_BYTES
        ),
        name="experts",
    )(x, gt, u, wg, wu, wd)


HALF = HEAD_DIM // 2
SCALE = HEAD_DIM**-0.5


def turn_tables():
    inverse = 10000.0 ** (-np.arange(HALF, dtype=np.float32) / HALF)
    phases = np.arange(4 * TOK, dtype=np.float32)[:, None] * inverse[None, :]
    cosine = np.tile(np.cos(phases), (1, 4)).astype(np.float32)
    sine = np.sin(phases)
    sine = np.tile(np.concatenate([-sine, sine], axis=1), (1, 2)).astype(np.float32)
    return cosine, sine


def lanes(rows, width=128):
    return lax.broadcasted_iota(jnp.int32, (rows, width), 1)


def turn(chunk, cosine, sine):
    front = lax.rem(lanes(chunk.shape[0]), HEAD_DIM) < HALF
    swapped = jnp.where(front, pltpu.roll(chunk, 128 - HALF, 1), pltpu.roll(chunk, HALF, 1))
    return chunk * cosine + swapped * sine


def stack_heads(chunk, half):
    low = lanes(chunk.shape[0]) < HEAD_DIM
    rolled = pltpu.roll(chunk, HEAD_DIM, 1)
    if half == 0:
        pair = (jnp.where(low, chunk, 0.0), jnp.where(low, rolled, 0.0))
    else:
        pair = (jnp.where(low, 0.0, rolled), jnp.where(low, 0.0, chunk))
    return jnp.concatenate(pair, axis=0).astype(BF)


def unstack_heads(pair, half):
    first, second = pair[:TOK], pair[TOK:]
    low = lanes(TOK) < HEAD_DIM
    if half == 0:
        return jnp.where(low, first, pltpu.roll(second, HEAD_DIM, 1))
    return jnp.where(low, pltpu.roll(first, HEAD_DIM, 1), second)


def root(values):
    return lax.rsqrt(jnp.mean(values * values, axis=1, keepdims=True) + 1e-06)


def widen():
    row = lax.broadcasted_iota(jnp.int32, (EXPERTS, TOK), 0)
    lane = lax.broadcasted_iota(jnp.int32, (EXPERTS, TOK), 1)
    return jnp.where(lane == lax.div(row, 2) * 8 + lax.rem(row, 2), 1.0, 0.0).astype(BF)


def routed_mask(routes):
    lane = lanes(TOK)
    expert = jnp.where(lax.rem(lane, 8) < 2, lax.div(lane, 8) * 2 + lax.rem(lane, 8), -1)
    hit = jnp.zeros((TOK, TOK), F32)
    for k in range(TOP):
        hit = hit + jnp.where(routes[:, k : k + 1] == expert, 1.0, 0.0)
    return hit > 0


class PlaneGather:
    def __init__(self, net, spot, slabs, base):
        self.net, self.spot, self.slabs, self.base = net, spot, slabs, base
        p, q, y, core = spot
        self.right, self.left = device(p + 1, q, y, core), device(p - 1, q, y, core)
        self.up, self.down = device(p, q + 1, y, core), device(p, q - 1, y, core)

    def slab(self, a, b):
        return slab(self.slabs, self.spot[0] + a, self.spot[1] + b)

    def send(self, ref, recv, to):
        self.net.start(ref, ref, self.base + recv, to)

    def arrived(self, ref, recv):
        self.net.arrived(ref, self.base + recv)

    def begin(self, own):
        for recv, to in ((0, self.right), (1, self.left), (4, self.up), (8, self.down)):
            self.net.start(own, self.slab(0, 0), self.base + recv, to)

    def second(self):
        s = self.slab(-1, 0)
        self.arrived(s, 0)
        self.send(s.at[0:64], 2, self.right)
        self.send(s, 5, self.up)
        s = self.slab(1, 0)
        self.arrived(s, 1)
        self.send(s.at[64:128], 3, self.left)
        self.send(s, 10, self.down)

    def third(self):
        s = self.slab(0, -1)
        self.arrived(s, 4)
        self.send(s, 12, self.up)
        s = self.slab(2, 0)
        self.arrived(s.at[0:64], 2)
        self.arrived(s.at[64:128], 3)
        self.send(s, 11, self.down)
        s = self.slab(-1, -1)
        self.arrived(s, 5)
        self.send(s, 13, self.up)
        self.send(self.slab(1, 0), 6, self.up)
        self.send(self.slab(2, 0), 7, self.up)
        self.send(self.slab(-1, 0), 9, self.down)

    def fourth(self):
        for a, recv, far in ((1, 10, 14), (2, 11, 15)):
            s = self.slab(a, 1)
            self.arrived(s, recv)
            self.send(s, far, self.down)

    def finish(self):
        for a, b, recv in (
            (1, -1, 6), (2, -1, 7), (0, 1, 8), (-1, 1, 9),
            (0, 2, 12), (-1, 2, 13), (1, 2, 14), (2, 2, 15),
        ):
            self.arrived(self.slab(a, b), recv)


def front_kernel(
    tok_ref, wq_hbm, wk_hbm, wv_hbm, wo_hbm, ga_ref, gm_ref, router_ref, cot_ref, routes_ref,
    len_ref, cos_ref, sin_ref, wgs_hbm, wus_hbm, wds_hbm,
    hidden_ref, x_ref, gt_ref, gates_ref, mixed_ref, query_ref, kv_ref, probs_hbm,
    u_all, wg_all, wu_all, wd_all,
    wq, wk, wv, wo, u_own, kv, probs, bias,
    send_sem, recv_sem, local_sem,
):
    p, q, y, core = place()
    spot = (p, q, y, core)
    sibling = device(p, q, y, 1 - core)
    sibling = (sibling[0] * 0 + chip_of(p, q, core) * 2 + 1 - core, y)
    ahead, behind = device(p, q, y + 1, core), device(p, q, y - 1, core)
    net = Sends(send_sem, recv_sem)
    loads = {
        name: pltpu.make_async_copy(src, dst, local_sem.at[i])
        for i, (name, src, dst) in enumerate(
            (("k", wk_hbm, wk), ("v", wv_hbm, wv), ("q", wq_hbm, wq), ("o", wo_hbm, wo))
        )
    }
    for load in loads.values():
        load.start()
    gather = PlaneGather(net, spot, u_all, 0)
    first = pl.multiple_of(y * TOK, TOK)
    row = lax.broadcasted_iota(jnp.int32, (TOK, 1), 0) + y * TOK
    length = len_ref[0]
    u_own[...] = jnp.where(row < length, cot_ref[...].astype(F32), 0.0).astype(BF)
    greet([gather.right, gather.left, gather.up, gather.down, ahead, behind, sibling])
    gather.begin(u_own)
    keep_own = pltpu.make_async_copy(u_own, gather.slab(0, 0), local_sem.at[4])
    keep_own.start()

    tokens = tok_ref[...].astype(F32)
    normed = (tokens * root(tokens) * ga_ref[...]).astype(BF)
    cosine, sine = cos_ref[pl.ds(first, TOK), :], sin_ref[pl.ds(first, TOK), :]
    loads["k"].wait()
    keys = jnp.dot(normed, wk[...], preferred_element_type=F32)
    for c in range(4):
        span = slice(c * 128, (c + 1) * 128)
        kv[y, :, span] = turn(keys[:, span], cosine, sine).astype(BF)
    loads["v"].wait()
    kv[y, :, 512:1024] = jnp.dot(normed, wv[...], preferred_element_type=F32).astype(BF)
    own = kv.at[y]
    net.start(own, own, 16, ahead)
    net.start(own, own, 17, behind)

    def weight(a, e, yy, rows=None):
        block = pl.ds(pl.multiple_of(wrap(yy) * TOK, TOK), TOK)
        if a == 2:
            return wd_all.at[e, block, :]
        full = (wg_all, wu_all)[a]
        return full.at[e, :, block] if rows is None else full.at[e, rows, block]

    shards = (wgs_hbm.at[0], wus_hbm.at[0], wds_hbm.at[0])
    top, bottom = pl.ds(0, 512), pl.ds(512, 512)
    keep = []
    for a in range(3):
        net.start(shards[a], weight(a, core, y), 20 + a, ahead)
        net.start(shards[a], weight(a, core, y), 23 + a, behind)
        net.start(shards[a], weight(a, core, y), 30 + a, sibling)
        keep.append(pltpu.make_async_copy(shards[a], weight(a, core, y), local_sem.at[5 + a]))
        keep[-1].start()

    loads["q"].wait()
    queries = jnp.dot(normed, wq[...], preferred_element_type=F32)
    for c in range(8):
        span = slice(c * 128, (c + 1) * 128)
        query_ref[:, span] = turn(queries[:, span], cosine, sine).astype(BF)
    key_pos = lanes(TOK, 512)
    bias[...] = jnp.where((key_pos <= row) & (key_pos < length), 0.0, -1e30)
    gather.second()
    s = kv.at[wrap(y - 1)]
    net.arrived(s, 16)
    net.start(s.at[0:64], s.at[0:64], 18, ahead)
    s = kv.at[wrap(y + 1)]
    net.arrived(s, 17)
    net.start(s.at[64:128], s.at[64:128], 19, behind)
    gather.third()
    s = kv.at[wrap(y + 2)]
    net.arrived(s.at[0:64], 18)
    net.arrived(s.at[64:128], 19)

    def attend(c, carry):
        span = pl.ds(pl.multiple_of(c * 128, 128), 128)
        keys = kv[:, :, span].reshape(512, 128)
        values = kv[:, :, pl.ds(pl.multiple_of(512 + c * 128, 128), 128)].reshape(512, 128)
        for half in range(2):
            m = c * 2 + half
            mine = pl.ds(pl.multiple_of(m * 128, 128), 128)
            pair = stack_heads(query_ref[:, mine].astype(F32), half)
            scores = lax.dot_general(
                pair, keys, (((1,), (1,)), ((), ())), preferred_element_type=F32
            )
            scores = scores * SCALE + jnp.concatenate([bias[...], bias[...]], axis=0)
            scores = jnp.exp(scores - jnp.max(scores, axis=1, keepdims=True))
            low = (scores * (1.0 / jnp.sum(scores, axis=1, keepdims=True))).astype(BF)
            probs[m] = low
            out = jnp.dot(low, values, preferred_element_type=F32)
            mixed_ref[:, mine] = unstack_heads(out, half).astype(BF)
        return carry

    lax.fori_loop(0, 2, attend, 0)
    gather.fourth()
    for a in range(3):
        net.arrived(weight(a, core, y - 1), 20 + a)
    net.start(weight(0, core, y - 1), weight(0, core, y - 1), 26, ahead)
    net.start(weight(1, core, y - 1, top), weight(1, core, y - 1, top), 27, ahead)
    for a in range(3):
        net.arrived(weight(a, core, y + 1), 23 + a)
    net.start(weight(1, core, y + 1, bottom), weight(1, core, y + 1, bottom), 28, behind)
    net.start(weight(2, core, y + 1), weight(2, core, y + 1), 29, behind)
    for a in range(3):
        net.start(weight(a, core, y - 1), weight(a, core, y - 1), 33 + a, sibling)
        net.start(weight(a, core, y + 1), weight(a, core, y + 1), 36 + a, sibling)
    lax.fori_loop(2, 4, attend, 0)
    keep_probs = pltpu.make_async_copy(probs, probs_hbm, local_sem.at[8])
    keep_probs.start()
    loads["o"].wait()
    hidden = tokens + jnp.dot(mixed_ref[...], wo[...], preferred_element_type=F32)
    hidden_ref[...] = hidden
    x = (hidden * root(hidden) * gm_ref[...]).astype(BF)
    x_ref[...] = x
    wide = jnp.dot(router_ref[...], widen(), preferred_element_type=F32).astype(BF)
    logits = jnp.dot(x, wide, preferred_element_type=F32)
    routed = routed_mask(routes_ref[...])
    logits = jnp.where(routed, logits, -1e30)
    weights = jnp.where(routed, jnp.exp(logits - jnp.max(logits, axis=1, keepdims=True)), 0.0)
    weights = weights * (1.0 / jnp.sum(weights, axis=1, keepdims=True))
    gates_ref[...] = weights
    gt_ref[...] = weights.T.reshape(16, 8, TOK)
    kv_ref[...] = kv[...]

    net.arrived(weight(0, core, y + 2), 26)
    net.arrived(weight(1, core, y + 2, top), 27)
    net.arrived(weight(1, core, y + 2, bottom), 28)
    net.arrived(weight(2, core, y + 2), 29)
    for a in range(3):
        net.start(weight(a, core, y + 2), weight(a, core, y + 2), 39 + a, sibling)
    gather.finish()
    for i, step in enumerate((0, -1, 1, 2)):
        for a in range(3):
            net.arrived(weight(a, 1 - core, y + step), 30 + 3 * i + a)
    net.drain()
    keep_own.wait()
    keep_probs.wait()
    for copy in keep:
        copy.wait()


def front(tokens, wq, wk, wv, wo, ga, gm, router, cotangent, routes, lengths, wg, wu, wd):
    cosine, sine = turn_tables()
    any_space = pl.BlockSpec(memory_space=pl.ANY)
    vmem = pl.BlockSpec(memory_space=pltpu.VMEM)
    smem = pl.BlockSpec(memory_space=pltpu.SMEM)
    shape = jax.ShapeDtypeStruct
    dma = pltpu.SemaphoreType.DMA
    return pl.pallas_call(
        front_kernel,
        out_shape=(
            shape((TOK, D), F32),
            shape((TOK, D), BF),
            shape((16, 8, TOK), F32),
            shape((TOK, TOK), F32),
            shape((TOK, D), BF),
            shape((TOK, D), BF),
            shape((4, TOK, D), BF),
            shape((8, 2 * TOK, 512), BF),
            shape((16, TOK, D), BF),
            shape((2, D, FF), BF),
            shape((2, D, FF), BF),
            shape((2, FF, D), BF),
        ),
        in_specs=[vmem] + [any_space] * 4 + [vmem] * 5 + [smem] + [vmem] * 2 + [any_space] * 3,
        out_specs=(vmem,) * 7 + (any_space,) * 5,
        scratch_shapes=[
            pltpu.VMEM((D, D), BF),
            pltpu.VMEM((D, 512), BF),
            pltpu.VMEM((D, 512), BF),
            pltpu.VMEM((D, D), BF),
            pltpu.VMEM((TOK, D), BF),
            pltpu.VMEM((4, TOK, D), BF),
            pltpu.VMEM((8, 2 * TOK, 512), BF),
            pltpu.VMEM((TOK, 512), F32),
            dma((52,)),
            dma((42,)),
            dma((9,)),
        ],
        compiler_params=pltpu.CompilerParams(
            collective_id=3, has_side_effects=True, vmem_limit_bytes=VMEM_BYTES
        ),
        name="front",
    )(
        tokens, wq, wk, wv, wo, ga.reshape(1, D), gm.reshape(1, D), router, cotangent, routes,
        lengths, jnp.asarray(cosine), jnp.asarray(sine), wg, wu, wd,
    )


def accumulate(target, *terms):
    total = target[...].astype(F32)
    for term in terms:
        total += term[...].astype(F32)
    target[...] = total.astype(target.dtype)


class PlaneReduce:
    OFF = (0, -1, 1, 2)

    def __init__(self, net, spot, slabs, rb, rc, rd, re, base):
        self.net, self.spot, self.slabs, self.base = net, spot, slabs, base
        self.rb, self.rc, self.rd, self.re = rb, rc, rd, re
        p, q, y, core = spot
        self.right, self.left = device(p + 1, q, y, core), device(p - 1, q, y, core)
        self.up, self.down = device(p, q + 1, y, core), device(p, q - 1, y, core)

    def slab(self, a, b):
        return slab(self.slabs, self.spot[0] + a, self.spot[1] + b)

    def send(self, source, target, recv, to):
        self.net.start(source, target, self.base + recv, to)

    def arrived(self, ref, recv):
        self.net.arrived(ref, self.base + recv)

    def bounce(self):
        for j in range(4):
            to = self.up if j < 2 else self.down
            self.send(self.slab(self.OFF[j], 2), self.rb.at[j], j, to)

    def to_up(self, j):
        self.send(self.slab(self.OFF[j], 1), self.rc.at[j], 4 + j, self.up)

    def to_down(self, j):
        self.send(self.slab(self.OFF[j], -1), self.rc.at[4 + j], 8 + j, self.down)

    def begin(self):
        self.bounce()
        for j in (3, 2):
            self.to_up(j)
        for j in (0, 1):
            self.to_down(j)

    def middle(self):
        for j in (3, 1, 2, 0):
            self.arrived(self.rb.at[j], j)
            accumulate(self.slab(self.OFF[j], 1 if j < 2 else -1), self.rb.at[j])
            (self.to_up if j < 2 else self.to_down)(j)

    def column(self, j):
        self.arrived(self.rc.at[j], 4 + j)
        self.arrived(self.rc.at[4 + j], 8 + j)
        accumulate(self.slab(self.OFF[j], 0), self.rc.at[j], self.rc.at[4 + j])

    def third(self):
        lo, hi = pl.ds(0, 64), pl.ds(64, 64)
        rd, re = self.rd, self.re
        self.column(3)
        self.send(self.slab(2, 0).at[lo], rd.at[lo], 12, self.right)
        self.send(self.slab(2, 0).at[hi], rd.at[hi], 13, self.left)
        self.column(2)
        self.send(self.slab(1, 0).at[hi], re.at[0, hi], 14, self.right)
        self.column(1)
        self.send(self.slab(-1, 0).at[lo], re.at[1, lo], 15, self.left)

    def fourth(self):
        lo, hi = pl.ds(0, 64), pl.ds(64, 64)
        rd, re = self.rd, self.re
        self.arrived(rd.at[lo], 12)
        accumulate(self.slab(1, 0).at[lo], rd.at[lo])
        self.send(self.slab(1, 0).at[lo], re.at[0, lo], 16, self.right)
        self.arrived(rd.at[hi], 13)
        accumulate(self.slab(-1, 0).at[hi], rd.at[hi])
        self.send(self.slab(-1, 0).at[hi], re.at[1, hi], 17, self.left)
        self.column(0)

    def finish(self):
        lo, hi = pl.ds(0, 64), pl.ds(64, 64)
        re = self.re
        self.arrived(re.at[0, hi], 14)
        self.arrived(re.at[1, lo], 15)
        self.arrived(re.at[0, lo], 16)
        self.arrived(re.at[1, hi], 17)
        return self.slab(0, 0)[...].astype(F32) + re[0].astype(F32) + re[1].astype(F32)


class RingReduce:
    def __init__(self, net, base, ahead, behind, portion, hops, lows, highs):
        self.net, self.base, self.ahead, self.behind = net, base, ahead, behind
        self.portion, self.hops, self.lows, self.highs = portion, hops, lows, highs
        self.n = len(hops[0])

    def send(self, sources, targets, group, to):
        for i, (source, target) in enumerate(zip(sources, targets)):
            self.net.start(source, target, self.base + group * self.n + i, to)

    def arrived(self, refs, group):
        for i, ref in enumerate(refs):
            self.net.arrived(ref, self.base + group * self.n + i)

    def begin(self):
        self.send(self.portion(2, 0), self.hops[0], 0, self.ahead)
        self.send(self.portion(2, 1), self.hops[1], 1, self.behind)

    def direct(self):
        self.send(self.portion(1, 1), self.lows[1], 2, self.ahead)
        self.send(self.portion(-1, 0), self.highs[0], 3, self.behind)

    def middle(self):
        for which, step, targets, to in (
            (0, 1, self.lows[0], self.ahead),
            (1, -1, self.highs[1], self.behind),
        ):
            self.arrived(self.hops[which], which)
            refs = self.portion(step, which)
            for ref, hop in zip(refs, self.hops[which]):
                accumulate(ref, hop)
            self.send(refs, targets, 4 + which, to)

    def finish(self):
        self.arrived(self.lows[1], 2)
        self.arrived(self.highs[0], 3)
        self.arrived(self.lows[0], 4)
        self.arrived(self.highs[1], 5)


def back_kernel(
    rows_ref, gg_ref, x_ref, gates_ref, hidden_ref, gm_ref, ga_ref, router_ref, cot_ref, tok_ref,
    mixed_ref, query_ref, kv_ref, cos_ref, sin_ref, routes_ref, len_ref,
    probs_hbm, wo_hbm, wq_hbm, wk_hbm, wv_hbm, o_hbm, pg_hbm, pu_hbm, pd_hbm,
    layer_ref, input_ref, dq_out, do_out, dkv_out, narrow_ref, gate_out, up_out, down_out,
    probs, wo, wq, wk, wv, o_buf, rb, rc, rd, re,
    pg, pu, pd, sg, su, sd, hop_g, hop_ua, hop_ub, hop_d, low_g, low_u, low_d, high_g, high_u, high_d,
    grad_mixed, grad_query, grad_kv, kv_hops, kv_low, kv_high,
    send_sem, recv_sem, local_sem,
):
    p, q, y, core = place()
    spot = (p, q, y, core)
    sibling = (chip_of(p, q, core) * 2 + 1 - core, y)
    ahead, behind = device(p, q, y + 1, core), device(p, q, y - 1, core)
    net = Sends(send_sem, recv_sem)
    pairs = (
        (o_hbm, o_buf), (wo_hbm, wo), (probs_hbm, probs), (wq_hbm, wq), (wk_hbm, wk), (wv_hbm, wv),
        (pg_hbm.at[core], pg), (pu_hbm.at[core], pu), (pd_hbm.at[core], pd),
    )
    loads = [pltpu.make_async_copy(s, d, local_sem.at[i]) for i, (s, d) in enumerate(pairs)]
    for load in loads:
        load.start()
    plane = PlaneReduce(net, spot, o_buf, rb, rc, rd, re, 0)
    greet([plane.right, plane.left, plane.up, plane.down, ahead, behind, sibling])
    loads[0].wait()
    plane.begin()
    for i, (source, target) in enumerate(((pg_hbm, sg), (pu_hbm, su), (pd_hbm, sd))):
        net.start(source.at[1 - core], target, 18 + i, sibling)

    first = pl.multiple_of(y * TOK, TOK)
    row = lax.broadcasted_iota(jnp.int32, (TOK, 1), 0) + y * TOK
    upstream = jnp.where(row < len_ref[0], cot_ref[...].astype(F32), 0.0)
    gates = gates_ref[...]
    grad_gates = gg_ref[...].reshape(TOK, TOK).T
    grad_logits = gates * (grad_gates - jnp.sum(gates * grad_gates, axis=1, keepdims=True))
    grad_logits = grad_logits.astype(BF)
    wide = jnp.dot(router_ref[...], widen(), preferred_element_type=F32).astype(BF)
    by_row = (((0,), (0,)), ((), ()))
    by_col = (((1,), (1,)), ((), ()))
    grad_normed = rows_ref[...] + lax.dot_general(
        grad_logits, wide, by_col, preferred_element_type=F32
    )
    hidden = hidden_ref[...]
    scale = root(hidden)
    grad_gain_moe = jnp.sum(grad_normed * hidden * scale, axis=0, keepdims=True)
    scaled = grad_normed * gm_ref[...]
    pull = jnp.mean(scaled * hidden, axis=1, keepdims=True)
    grad_hidden = upstream + scale * scaled - hidden * (scale * scale * scale) * pull
    input_ref[...] = grad_hidden
    low = grad_hidden.astype(BF)
    loads[1].wait()
    grad_mixed[...] = lax.dot_general(low, wo[...], by_col, preferred_element_type=F32).astype(BF)
    narrow_ref[...] = lax.dot_general(grad_logits, x_ref[...], by_row, preferred_element_type=F32)
    counts = jnp.sum(jnp.where(routed_mask(routes_ref[...]), 1.0, 0.0), axis=0, keepdims=True)
    narrow_ref[3:4, :] = grad_gain_moe
    narrow_ref[4:5, :] = jnp.zeros((1, D), F32)
    narrow_ref[4:5, 0:TOK] = counts
    plane.middle()

    def block(ref, step, rows=None):
        span = pl.ds(pl.multiple_of(wrap(y + step) * TOK, TOK), TOK)
        return ref.at[:, span] if rows is None else ref.at[rows, span]

    def down_block(ref, step):
        return ref.at[pl.ds(pl.multiple_of(wrap(y + step) * TOK, TOK), TOK)]

    top, bottom = pl.ds(0, 512), pl.ds(512, 512)

    def weight_portion(step, which):
        if which == 0:
            return [block(pg, step), block(pu, step, top)]
        return [block(pu, step, bottom), down_block(pd, step)]

    def weight_merge(step):
        accumulate(block(pg, step), block(sg, step))
        accumulate(block(pu, step), block(su, step))
        accumulate(down_block(pd, step), down_block(sd, step))

    weights = RingReduce(
        net, 24, ahead, behind, weight_portion,
        ([hop_g, hop_ua], [hop_ub, hop_d]),
        ([low_g, low_u.at[top]], [low_u.at[bottom], low_d]),
        ([high_g, high_u.at[top]], [high_u.at[bottom], high_d]),
    )
    for load in loads[6:]:
        load.wait()
    for i, ref in enumerate((sg, su, sd)):
        net.arrived(ref, 18 + i)
    weight_merge(2)
    weights.begin()

    cosine, sine = cos_ref[pl.ds(first, TOK), :], sin_ref[pl.ds(first, TOK), :]
    loads[2].wait()

    def attend(c, carry):
        span = pl.ds(pl.multiple_of(c * 128, 128), 128)
        value_span = pl.ds(pl.multiple_of(512 + c * 128, 128), 128)
        keys = kv_ref[:, :, span].reshape(512, 128)
        values = kv_ref[:, :, value_span].reshape(512, 128)
        grad_keys = jnp.zeros((512, 128), F32)
        grad_values = jnp.zeros((512, 128), F32)
        for half in range(2):
            m = c * 2 + half
            mine = pl.ds(pl.multiple_of(m * 128, 128), 128)
            pair = stack_heads(query_ref[:, mine].astype(F32), half)
            grad_pair = stack_heads(grad_mixed[:, mine].astype(F32), half)
            grad_probs = lax.dot_general(grad_pair, values, by_col, preferred_element_type=F32)
            prob = probs[m]
            wide_prob = prob.astype(F32)
            middle = jnp.sum(wide_prob * grad_probs, axis=1, keepdims=True)
            grad_scores = (wide_prob * (grad_probs - middle)).astype(BF)
            back = jnp.dot(grad_scores, keys, preferred_element_type=F32) * SCALE
            grad_query[:, mine] = turn(unstack_heads(back, half), cosine, -sine).astype(BF)
            grad_keys += lax.dot_general(grad_scores, pair, by_row, preferred_element_type=F32)
            grad_values += lax.dot_general(prob, grad_pair, by_row, preferred_element_type=F32)
        grad_kv[:, :, span] = (grad_keys * SCALE).astype(BF).reshape(4, TOK, 128)
        grad_kv[:, :, value_span] = grad_values.astype(BF).reshape(4, TOK, 128)
        return carry

    lax.fori_loop(0, 4, attend, 0)
    lo, hi = pl.ds(0, 64), pl.ds(64, 64)
    sums = RingReduce(
        net, 36, ahead, behind,
        lambda step, which: [grad_kv.at[wrap(y + step), hi if which else lo]],
        ([kv_hops.at[0]], [kv_hops.at[1]]),
        ([kv_low.at[lo]], [kv_low.at[hi]]),
        ([kv_high.at[lo]], [kv_high.at[hi]]),
    )
    sums.begin()
    sums.direct()
    plane.third()
    do_out[...] = lax.dot_general(
        mixed_ref[...], low, by_row, preferred_element_type=F32
    ).astype(BF)
    sums.middle()
    plane.fourth()
    tokens = tok_ref[...].astype(F32)
    scale = root(tokens)
    normed = (tokens * scale * ga_ref[...]).astype(BF)
    dq_out[...] = lax.dot_general(
        normed, grad_query[...], by_row, preferred_element_type=F32
    ).astype(BF)
    for load in loads[3:6]:
        load.wait()
    grad_normed = lax.dot_general(grad_query[...], wq[...], by_col, preferred_element_type=F32)
    weight_merge(1)
    weight_merge(-1)
    weights.direct()
    weights.middle()
    weight_merge(0)
    sums.finish()
    both = grad_kv[y].astype(F32) + kv_low[...].astype(F32) + kv_high[...].astype(F32)
    grad_key = jnp.concatenate(
        [turn(both[:, c * 128 : (c + 1) * 128], cosine, -sine) for c in range(4)], axis=1
    ).astype(BF)
    grad_value = both[:, 512:].astype(BF)
    dkv_out[:, 0:512] = lax.dot_general(
        normed, grad_key, by_row, preferred_element_type=F32
    ).astype(BF)
    dkv_out[:, 512:1024] = lax.dot_general(
        normed, grad_value, by_row, preferred_element_type=F32
    ).astype(BF)
    grad_normed += lax.dot_general(grad_key, wk[...], by_col, preferred_element_type=F32)
    grad_normed += lax.dot_general(grad_value, wv[...], by_col, preferred_element_type=F32)
    narrow_ref[2:3, :] = jnp.sum(grad_normed * tokens * scale, axis=0, keepdims=True)
    scaled = grad_normed * ga_ref[...]
    pull = jnp.mean(scaled * tokens, axis=1, keepdims=True)
    input_ref[...] += scale * scaled - tokens * (scale * scale * scale) * pull
    layer_ref[...] = (hidden_ref[...] + plane.finish()).astype(BF)
    weights.finish()
    gate_out[...] = (
        block(pg, 0)[...].astype(F32) + low_g[...].astype(F32) + high_g[...].astype(F32)
    )
    up_out[...] = block(pu, 0)[...].astype(F32) + low_u[...].astype(F32) + high_u[...].astype(F32)
    down_out[...] = (
        down_block(pd, 0)[...].astype(F32) + low_d[...].astype(F32) + high_d[...].astype(F32)
    )
    net.drain()


def back(operands, arrays):
    any_space = pl.BlockSpec(memory_space=pl.ANY)
    vmem = pl.BlockSpec(memory_space=pltpu.VMEM)
    smem = pl.BlockSpec(memory_space=pltpu.SMEM)
    shape = jax.ShapeDtypeStruct
    dma = pltpu.SemaphoreType.DMA
    low = lambda *size: pltpu.VMEM(size, BF)
    return pl.pallas_call(
        back_kernel,
        out_shape=(
            shape((TOK, D), BF),
            shape((TOK, D), F32),
            shape((D, D), BF),
            shape((D, D), BF),
            shape((D, D), BF),
            shape((TOK, D), F32),
            shape((D, TOK), F32),
            shape((D, TOK), F32),
            shape((TOK, D), F32),
        ),
        in_specs=[vmem] * 16 + [smem] + [any_space] * 9,
        out_specs=(vmem,) * 9,
        scratch_shapes=[
            low(8, 2 * TOK, 512),
            low(D, D),
            low(D, D),
            low(D, 512),
            low(D, 512),
            low(16, TOK, D),
            low(4, TOK, D),
            low(8, TOK, D),
            low(TOK, D),
            low(2, TOK, D),
            low(D, FF),
            low(D, FF),
            low(FF, D),
            low(D, FF),
            low(D, FF),
            low(FF, D),
            low(D, TOK),
            low(512, TOK),
            low(512, TOK),
            low(TOK, D),
            low(D, TOK),
            low(D, TOK),
            low(TOK, D),
            low(D, TOK),
            low(D, TOK),
            low(TOK, D),
            low(TOK, D),
            low(TOK, D),
            low(4, TOK, D),
            low(2, 64, D),
            low(TOK, D),
            low(TOK, D),
            dma((48,)),
            dma((42,)),
            dma((9,)),
        ],
        compiler_params=pltpu.CompilerParams(
            collective_id=4, has_side_effects=True, vmem_limit_bytes=VMEM_BYTES
        ),
        name="back",
    )(*operands, *arrays)


def total_kernel(
    a_hbm, b_hbm, c_hbm, s_hbm, a_out, b_out, c_out, s_out,
    mine, other, mine_s, other_s, from_low, from_high, from_low_s, from_high_s, bounced, bounced_s,
    spread, spread_s, done, done_s,
    sib_send, sib_recv, ring_send, ring_recv, plane_send, plane_recv, back_send, back_recv,
    round_send, round_recv, last_send, last_recv, local_sem,
):
    dp, y = lax.axis_index("dp"), lax.axis_index("hid")
    core = lax.rem(dp, 2)
    here = (lax.div(dp, 8), y, lax.rem(lax.div(dp, 2), 4))

    def at(spot, on=None):
        spot = [wrap(v) for v in spot]
        return (spot[0] * 8 + spot[2] * 2 + (core if on is None else on), spot[1])

    def along(k, step):
        return at([here[i] + (step if i == k else 0) for i in range(3)])

    sibling = at(here, 1 - core)
    ring = [(along(k, 1), along(k, -1)) for k in range(3)]
    planes = [(1, 2), (0, 2), (0, 1)]
    greeted = [sibling]
    for dx in range(4):
        for dy in range(4):
            for dz in range(4):
                if (dx or dy or dz) and not (dx and dy and dz):
                    greeted.append(at([here[0] + dx, here[1] + dy, here[2] + dz]))
    ins, results = (a_hbm, b_hbm, c_hbm, s_hbm), (a_out, b_out, c_out, s_out)
    axes = (0, 1, 2, 0)
    halves = [mine.at[k] for k in range(3)] + [mine_s]
    theirs = [other.at[k] for k in range(3)] + [other_s]
    lows = [from_low.at[k] for k in range(3)] + [from_low_s]
    highs = [from_high.at[k] for k in range(3)] + [from_high_s]
    hops = [bounced.at[k] for k in range(3)] + [bounced_s]
    pieces = [spread.at[k] for k in range(3)] + [spread_s]
    slabs = [done.at[k] for k in range(3)] + [done_s]
    parts = range(4)
    sizes = (128, 128, 128, 16)

    def half_of(k, which):
        return ins[k].at[pl.ds(pl.multiple_of(which * sizes[k] * 4, sizes[k] * 4), sizes[k] * 4)]


    def remote(source, target, send, recv, to):
        return pltpu.make_async_remote_copy(
            src_ref=source, dst_ref=target, send_sem=send, recv_sem=recv,
            device_id=to, device_id_type=MESH,
        )

    def arrived(ref, sem):
        pltpu.make_async_copy(ref, ref, sem).wait()

    loads = [
        pltpu.make_async_copy(half_of(k, core), halves[k], local_sem.at[k]) for k in parts
    ]
    for load in loads:
        load.start()
    greet(greeted)
    sent = []

    def go(*copy):
        copy = remote(*copy)
        copy.start()
        sent.append(copy)

    for k in parts:
        go(half_of(k, 1 - core), theirs[k], sib_send.at[k], sib_recv.at[k], sibling)

    def rows_of(k, step):
        start = pl.multiple_of(wrap(here[axes[k]] + step) * sizes[k], sizes[k])
        return halves[k].at[pl.ds(start, sizes[k])]

    los = [pl.ds(0, size // 2) for size in sizes]
    his = [pl.ds(size // 2, size // 2) for size in sizes]

    def add(target, *terms):
        total = target[...].astype(F32)
        for term in terms:
            total += term[...].astype(F32)
        target[...] = total.astype(target.dtype)

    def merge_rows(k, step):
        start = pl.multiple_of(wrap(here[axes[k]] + step) * sizes[k], sizes[k])
        span = pl.ds(start, sizes[k])
        add(halves[k].at[span], theirs[k].at[span])

    for k in parts:
        lo, hi = los[k], his[k]
        loads[k].wait()
        arrived(theirs[k], sib_recv.at[k])
        plus, minus = ring[axes[k]]
        merge_rows(k, 2)
        far = rows_of(k, 2)
        go(far.at[lo], hops[k].at[lo], ring_send.at[k, 0], ring_recv.at[k, 0], plus)
        go(far.at[hi], hops[k].at[hi], ring_send.at[k, 1], ring_recv.at[k, 1], minus)
        merge_rows(k, 1)
        go(rows_of(k, 1).at[hi], lows[k].at[hi], ring_send.at[k, 2], ring_recv.at[k, 2], plus)
        merge_rows(k, -1)
        go(rows_of(k, -1).at[lo], highs[k].at[lo], ring_send.at[k, 3], ring_recv.at[k, 3], minus)
        merge_rows(k, 0)
    for k in parts:
        lo, hi = los[k], his[k]
        plus, minus = ring[axes[k]]
        arrived(hops[k].at[lo], ring_recv.at[k, 0])
        near = rows_of(k, 1).at[lo]
        add(near, hops[k].at[lo])
        go(near, lows[k].at[lo], ring_send.at[k, 4], ring_recv.at[k, 4], plus)
        arrived(hops[k].at[hi], ring_recv.at[k, 1])
        near = rows_of(k, -1).at[hi]
        add(near, hops[k].at[hi])
        go(near, highs[k].at[hi], ring_send.at[k, 5], ring_recv.at[k, 5], minus)

    def piece(k, ref, u, v):
        if k == 3:
            row, lane = lax.div(u, 2) * 8, (lax.rem(u, 2) * 4 + v) * 128
            return ref.at[pl.ds(pl.multiple_of(row, 8), 8), pl.ds(pl.multiple_of(lane, 128), 128)]
        return ref.at[
            pl.ds(pl.multiple_of(u * 32, 32), 32), pl.ds(pl.multiple_of(v * 256, 256), 256)
        ]

    def member(k, i):
        u, v = planes[axes[k]]
        spot = list(here)
        spot[u] = wrap(here[u] + lax.div(i, 4))
        spot[v] = wrap(here[v] + lax.rem(i, 4))
        return spot[u], spot[v], at(spot)

    def mirror(i):
        return wrap(-lax.div(i, 4)) * 4 + wrap(-lax.rem(i, 4))

    def piece_copy(k, i):
        u, v, to = member(k, i)
        return remote(
            piece(k, rows_of(k, 0), u, v),
            pieces[k].at[mirror(i)],
            plane_send.at[k, i],
            plane_recv.at[k, mirror(i)],
            to,
        )

    def back_copy(k, i):
        u, v = planes[axes[k]]
        spot = piece(k, slabs[k], here[u], here[v])
        return remote(spot, spot, back_send.at[k, i], back_recv.at[k, mirror(i)], member(k, i)[2])

    def each(make, act):
        def one(i, carry):
            act(make(i))
            return carry

        lax.fori_loop(1, 16, one, 0)

    for k in parts:
        lo, hi = los[k], his[k]
        for i in (2, 4):
            arrived(lows[k].at[hi if i == 2 else lo], ring_recv.at[k, i])
        for i in (3, 5):
            arrived(highs[k].at[lo if i == 3 else hi], ring_recv.at[k, i])
        add(rows_of(k, 0), lows[k], highs[k])
        each(lambda i: piece_copy(k, i), lambda copy: copy.start())
    for k in parts:
        u, v = planes[axes[k]]
        pieces[k][0] = piece(k, rows_of(k, 0), here[u], here[v])[...]
        each(
            lambda i: pltpu.make_async_copy(pieces[k].at[0], pieces[k].at[0], plane_recv.at[k, i]),
            lambda copy: copy.wait(),
        )
        total = jnp.sum(pieces[k][...].astype(F32), axis=0)
        piece(k, slabs[k], here[u], here[v])[...] = total.astype(slabs[k].dtype)
        each(lambda i: back_copy(k, i), lambda copy: copy.start())

    def final(k, step, span=None):
        size = sizes[k]
        start = core * size * 4 + wrap(here[axes[k]] + step) * size
        if span is not None:
            size = size // 2
            start += span * size
        return results[k].at[pl.ds(pl.multiple_of(start, size), size)]

    stores = []
    for k in parts:
        plus, minus = ring[axes[k]]
        each(
            lambda i: pltpu.make_async_copy(pieces[k].at[0], pieces[k].at[0], back_recv.at[k, i]),
            lambda copy: copy.wait(),
        )
        go(slabs[k], final(k, 0), round_send.at[k, 0], round_recv.at[k, 0], plus)
        go(slabs[k], final(k, 0), round_send.at[k, 1], round_recv.at[k, 1], minus)
        go(slabs[k], final(k, 0), last_send.at[k, 0], last_recv.at[k, 0], sibling)
        store = pltpu.make_async_copy(slabs[k], final(k, 0), local_sem.at[k])
        store.start()
        stores.append(store)
    for k in parts:
        plus, minus = ring[axes[k]]
        arrived(final(k, -1), round_recv.at[k, 0])
        spot = final(k, -1, 0)
        go(spot, spot, round_send.at[k, 2], round_recv.at[k, 2], plus)
        go(final(k, -1), final(k, -1), last_send.at[k, 1], last_recv.at[k, 1], sibling)
        arrived(final(k, 1), round_recv.at[k, 1])
        spot = final(k, 1, 1)
        go(spot, spot, round_send.at[k, 3], round_recv.at[k, 3], minus)
        go(final(k, 1), final(k, 1), last_send.at[k, 2], last_recv.at[k, 2], sibling)
    for k in parts:
        arrived(final(k, 2, 0), round_recv.at[k, 2])
        arrived(final(k, 2, 1), round_recv.at[k, 3])
        go(final(k, 2), final(k, 2), last_send.at[k, 3], last_recv.at[k, 3], sibling)
    for k in parts:
        for i in range(4):
            arrived(final(k, 0), last_recv.at[k, i])
    for copy in sent:
        copy.wait_send()
    for k in parts:
        each(lambda i: piece_copy(k, i), lambda copy: copy.wait_send())
        each(lambda i: back_copy(k, i), lambda copy: copy.wait_send())
    for store in stores:
        store.wait()


def total(a, b, c, s):
    any_space = pl.BlockSpec(memory_space=pl.ANY)
    shape = jax.ShapeDtypeStruct
    dma = pltpu.SemaphoreType.DMA
    vmem = pltpu.VMEM
    return pl.pallas_call(
        total_kernel,
        out_shape=(shape((D, D), BF),) * 3 + (shape((TOK, D), F32),),
        in_specs=[any_space] * 4,
        out_specs=(any_space,) * 4,
        scratch_shapes=[
            vmem((3, 512, D), BF),
            vmem((3, 512, D), BF),
            vmem((64, D), F32),
            vmem((64, D), F32),
            vmem((3, 128, D), BF),
            vmem((3, 128, D), BF),
            vmem((16, D), F32),
            vmem((16, D), F32),
            vmem((3, 128, D), BF),
            vmem((16, D), F32),
            vmem((3, 16, 32, 256), BF),
            vmem((16, 8, TOK), F32),
            vmem((3, 128, D), BF),
            vmem((16, D), F32),
            dma((4,)),
            dma((4,)),
            dma((4, 6)),
            dma((4, 6)),
            dma((4, 16)),
            dma((4, 16)),
            dma((4, 16)),
            dma((4, 16)),
            dma((4, 4)),
            dma((4, 4)),
            dma((4, 4)),
            dma((4, 4)),
            dma((4,)),
        ],
        compiler_params=pltpu.CompilerParams(
            collective_id=2, has_side_effects=True, vmem_limit_bytes=VMEM_BYTES
        ),
        name="total",
    )(a, b, c, s)


def shards(
    tokens,
    w_query,
    w_key,
    w_value,
    w_output,
    gain_attn,
    gain_moe,
    router,
    w_gate,
    w_up,
    w_down,
    cotangent,
    routes,
    lengths,
):
    (
        hidden, x, gate_tiles, gates, mixed, query, kv, probs, upstream_all, full_gate, full_up,
        full_down,
    ) = front(
        tokens, w_query, w_key, w_value, w_output, gain_attn, gain_moe, router, cotangent, routes,
        lengths, w_gate, w_up, w_down,
    )
    grad_rows, out_parts, grad_gates, part_gate, part_up, part_down = moe(
        x, gate_tiles, upstream_all, full_gate, full_up, full_down
    )
    cosine, sine = turn_tables()
    layer_out, grad_input, sum_q, sum_o, sum_kv, narrow, grad_gate, grad_up, grad_down = back(
        (
            grad_rows, grad_gates, x, gates, hidden, gain_moe.reshape(1, D),
            gain_attn.reshape(1, D), router, cotangent, tokens, mixed, query, kv,
            jnp.asarray(cosine), jnp.asarray(sine), routes, lengths,
        ),
        (
            probs, w_output, w_query, w_key, w_value, out_parts, part_gate, part_up, part_down,
        ),
    )
    sum_q, sum_o, sum_kv, narrow = total(sum_q, sum_o, sum_kv, narrow)
    sum_kv = sum_kv.astype(F32)
    return (
        layer_out,
        grad_input,
        sum_q.astype(F32),
        sum_kv[:, :512],
        sum_kv[:, 512:],
        sum_o.astype(F32),
        narrow[2],
        narrow[3],
        narrow.reshape(16, 8, D)[:, :2].reshape(EXPERTS, D).T,
        grad_gate[None],
        grad_up[None],
        grad_down[None],
        narrow[4, :TOK].reshape(16, 8)[:, :2].reshape(EXPERTS).astype(jnp.int32),
    )


def solution(mesh):
    in_specs = (
        P(("dp", "hid"), None),
        P(),
        P(),
        P(),
        P(),
        P(),
        P(),
        P(),
        P("dp", None, "hid"),
        P("dp", None, "hid"),
        P("dp", "hid", None),
        P(("dp", "hid"), None),
        P(("dp", "hid"), None),
        P("dp"),
    )
    out_specs = (
        P(("dp", "hid"), None),
        P(("dp", "hid"), None),
        P(),
        P(),
        P(),
        P(),
        P(),
        P(),
        P(),
        P("dp", None, "hid"),
        P("dp", None, "hid"),
        P("dp", "hid", None),
        P(),
    )
    return jax.shard_map(shards, mesh=mesh, in_specs=in_specs, out_specs=out_specs, check_vma=False)
```

```python
import jax
import jax.numpy as jnp
import numpy as np
from jax import lax
from jax.experimental import pallas as pl
from jax.experimental.pallas import tpu as pltpu
from jax.sharding import PartitionSpec as P

D = 1024
HEADS = 16
KV_HEADS = 8
HEAD_DIM = 64
EXPERTS = 32
TOP = 8
FF = 512
TOK = 128

MESH = pl.DeviceIdType.MESH
BF = jnp.bfloat16
F32 = jnp.float32
SLOTS = 48
VMEM_BYTES = 60 * 2**20


def wrap(value):
    return lax.rem(value + 4, 4)


def place():
    dp = lax.axis_index("dp")
    y = lax.axis_index("hid")
    core = lax.rem(dp, 2)
    x = lax.div(dp, 8)
    z = lax.rem(lax.div(dp, 2), 4)
    p = jnp.where(core == 0, x, z)
    q = jnp.where(core == 0, z, x)
    return p, q, y, core


def device(p, q, y, core):
    p, q = wrap(p), wrap(q)
    return (jnp.where(core == 0, p * 8 + q * 2, q * 8 + p * 2) + core, wrap(y))


def chip_of(p, q, core):
    p, q = wrap(p), wrap(q)
    return jnp.where(core == 0, p * 4 + q, q * 4 + p)


def greet(devices):
    barrier = pltpu.get_barrier_semaphore()
    for other in devices:
        pl.semaphore_signal(barrier, inc=1, device_id=other, device_id_type=MESH)
    pl.semaphore_wait(barrier, len(devices))


class Sends:
    def __init__(self, send_sem, recv_sem):
        self.send_sem, self.recv_sem, self.made = send_sem, recv_sem, []

    def start(self, source, target, recv, to):
        copy = pltpu.make_async_remote_copy(
            src_ref=source,
            dst_ref=target,
            send_sem=self.send_sem.at[len(self.made)],
            recv_sem=self.recv_sem.at[recv],
            device_id=to,
            device_id_type=MESH,
        )
        copy.start()
        self.made.append(copy)

    def arrived(self, ref, recv):
        pltpu.make_async_copy(ref, ref, self.recv_sem.at[recv]).wait()

    def drain(self):
        for copy in self.made:
            copy.wait_send()
        self.made = []


def slab(buffer, p, q):
    return buffer.at[wrap(p) * 4 + wrap(q)]


HALF = HEAD_DIM // 2
SCALE = HEAD_DIM**-0.5


def turn_tables():
    inverse = 10000.0 ** (-np.arange(HALF, dtype=np.float32) / HALF)
    phases = np.arange(4 * TOK, dtype=np.float32)[:, None] * inverse[None, :]
    cosine = np.tile(np.cos(phases), (1, 4)).astype(np.float32)
    sine = np.sin(phases)
    sine = np.tile(np.concatenate([-sine, sine], axis=1), (1, 2)).astype(np.float32)
    return cosine, sine


def lanes(rows, width=128):
    return lax.broadcasted_iota(jnp.int32, (rows, width), 1)


def turn(chunk, cosine, sine):
    front = lax.rem(lanes(chunk.shape[0]), HEAD_DIM) < HALF
    swapped = jnp.where(front, pltpu.roll(chunk, 128 - HALF, 1), pltpu.roll(chunk, HALF, 1))
    return chunk * cosine + swapped * sine


def stack_heads(chunk, half):
    low = lanes(chunk.shape[0]) < HEAD_DIM
    rolled = pltpu.roll(chunk, HEAD_DIM, 1)
    if half == 0:
        pair = (jnp.where(low, chunk, 0.0), jnp.where(low, rolled, 0.0))
    else:
        pair = (jnp.where(low, 0.0, rolled), jnp.where(low, 0.0, chunk))
    return jnp.concatenate(pair, axis=0).astype(BF)


def unstack_heads(pair, half):
    first, second = pair[:TOK], pair[TOK:]
    low = lanes(TOK) < HEAD_DIM
    if half == 0:
        return jnp.where(low, first, pltpu.roll(second, HEAD_DIM, 1))
    return jnp.where(low, pltpu.roll(first, HEAD_DIM, 1), second)


def root(values):
    return lax.rsqrt(jnp.mean(values * values, axis=1, keepdims=True) + 1e-06)


def widen():
    row = lax.broadcasted_iota(jnp.int32, (EXPERTS, TOK), 0)
    lane = lax.broadcasted_iota(jnp.int32, (EXPERTS, TOK), 1)
    return jnp.where(lane == lax.div(row, 2) * 8 + lax.rem(row, 2), 1.0, 0.0).astype(BF)


def routed_mask(routes):
    lane = lanes(TOK)
    expert = jnp.where(lax.rem(lane, 8) < 2, lax.div(lane, 8) * 2 + lax.rem(lane, 8), -1)
    hit = jnp.zeros((TOK, TOK), F32)
    for k in range(TOP):
        hit = hit + jnp.where(routes[:, k : k + 1] == expert, 1.0, 0.0)
    return hit > 0


class PlaneGather:
    def __init__(self, net, spot, slabs, base):
        self.net, self.spot, self.slabs, self.base = net, spot, slabs, base
        p, q, y, core = spot
        self.right, self.left = device(p + 1, q, y, core), device(p - 1, q, y, core)
        self.up, self.down = device(p, q + 1, y, core), device(p, q - 1, y, core)

    def slab(self, a, b):
        return slab(self.slabs, self.spot[0] + a, self.spot[1] + b)

    def send(self, ref, recv, to):
        self.net.start(ref, ref, self.base + recv, to)

    def arrived(self, ref, recv):
        self.net.arrived(ref, self.base + recv)

    def begin(self, own):
        for recv, to in ((0, self.right), (1, self.left), (4, self.up), (8, self.down)):
            self.net.start(own, self.slab(0, 0), self.base + recv, to)

    def second(self):
        s = self.slab(-1, 0)
        self.arrived(s, 0)
        self.send(s.at[0:64], 2, self.right)
        self.send(s, 5, self.up)
        s = self.slab(1, 0)
        self.arrived(s, 1)
        self.send(s.at[64:128], 3, self.left)
        self.send(s, 10, self.down)

    def third(self):
        s = self.slab(0, -1)
        self.arrived(s, 4)
        self.send(s, 12, self.up)
        s = self.slab(2, 0)
        self.arrived(s.at[0:64], 2)
        self.arrived(s.at[64:128], 3)
        self.send(s, 11, self.down)
        s = self.slab(-1, -1)
        self.arrived(s, 5)
        self.send(s, 13, self.up)
        self.send(self.slab(1, 0), 6, self.up)
        self.send(self.slab(2, 0), 7, self.up)
        self.send(self.slab(-1, 0), 9, self.down)

    def fourth(self, which):
        a, recv, far = ((1, 10, 14), (2, 11, 15))[which]
        s = self.slab(a, 1)
        self.arrived(s, recv)
        self.send(s, far, self.down)

    def finish(self):
        for a, b, recv in (
            (1, -1, 6), (2, -1, 7), (0, 1, 8), (-1, 1, 9),
            (0, 2, 12), (-1, 2, 13), (1, 2, 14), (2, 2, 15),
        ):
            self.arrived(self.slab(a, b), recv)


def main_kernel(
    tok_ref, wq_hbm, wk_hbm, wv_hbm, wo_hbm, ga_ref, gm_ref, router_ref, cot_ref, routes_ref,
    len_ref, cos_ref, sin_ref, wgs_hbm, wus_hbm, wds_hbm,
    hidden_ref, x_ref, gates_ref, mixed_ref, query_ref, kv_ref, grad_out, gg_out,
    probs_hbm, o_hbm, dwg_hbm, dwu_hbm, dwd_hbm,
    wqo, wk, wv, u_own, kv, probs, bias, gt,
    xs, us, wg, wu, wd, gin, rank, ggo, picks, rows, slot_grads, acts, gparts, uparts,
    outs, pairs, o_buf, p_buf, rb, rc, rd, re, dwg, dwu,
    send_sem, recv_sem, g_send, g_recv, gg_send, gg_recv, local_sem,
):
    p, q, y, core = place()
    spot = (p, q, y, core)
    sibling = (chip_of(p, q, core) * 2 + 1 - core, y)
    ahead, behind = device(p, q, y + 1, core), device(p, q, y - 1, core)
    up, down = device(p, q + 1, y, core), device(p, q - 1, y, core)
    right, left = device(p + 1, q, y, core), device(p - 1, q, y, core)
    others = [device(p + a, q + b, y, core) for a in range(4) for b in range(4) if a or b]
    my_chip = chip_of(p, q, core)
    net = Sends(send_sem, recv_sem)
    wq, wo = wqo.at[0], wqo.at[1]
    loads = {
        name: pltpu.make_async_copy(src, dst, local_sem.at[i])
        for i, (name, src, dst) in enumerate(
            (("k", wk_hbm, wk), ("v", wv_hbm, wv), ("q", wq_hbm, wq), ("o", wo_hbm, wo))
        )
    }
    for load in loads.values():
        load.start()
    gather = PlaneGather(net, spot, us, 0)
    tokens_in = PlaneGather(net, spot, xs, 42)
    first = pl.multiple_of(y * TOK, TOK)
    row = lax.broadcasted_iota(jnp.int32, (TOK, 1), 0) + y * TOK
    length = len_ref[0]
    u_own[...] = jnp.where(row < length, cot_ref[...].astype(F32), 0.0).astype(BF)
    greet(others + [ahead, behind, sibling])
    gather.begin(u_own)
    keep_own = pltpu.make_async_copy(u_own, gather.slab(0, 0), local_sem.at[4])
    keep_own.start()

    def weight(a, e, yy, rows=None):
        block = pl.ds(pl.multiple_of(wrap(yy) * TOK, TOK), TOK)
        if a == 2:
            return wd.at[e, block, :]
        full = (wg, wu)[a]
        return full.at[e, :, block] if rows is None else full.at[e, rows, block]

    shards = (wgs_hbm.at[0], wus_hbm.at[0], wds_hbm.at[0])
    top, bottom = pl.ds(0, 512), pl.ds(512, 512)
    keep = []

    def send_weight(a):
        net.start(shards[a], weight(a, core, y), 20 + a, ahead)
        net.start(shards[a], weight(a, core, y), 23 + a, behind)
        net.start(shards[a], weight(a, core, y), 30 + a, sibling)
        keep.append(pltpu.make_async_copy(shards[a], weight(a, core, y), local_sem.at[5 + a]))
        keep[-1].start()

    def pass_weight(a):
        before, after = weight(a, core, y - 1), weight(a, core, y + 1)
        net.arrived(before, 20 + a)
        if a == 0:
            net.start(before, before, 26, ahead)
        if a == 1:
            spot = weight(1, core, y - 1, top)
            net.start(spot, spot, 27, ahead)
        net.start(before, before, 33 + a, sibling)
        net.arrived(after, 23 + a)
        if a == 1:
            spot = weight(1, core, y + 1, bottom)
            net.start(spot, spot, 28, behind)
        if a == 2:
            net.start(after, after, 29, behind)
        net.start(after, after, 36 + a, sibling)

    send_weight(0)
    tokens = tok_ref[...].astype(F32)
    normed = (tokens * root(tokens) * ga_ref[...]).astype(BF)
    cosine, sine = cos_ref[pl.ds(first, TOK), :], sin_ref[pl.ds(first, TOK), :]
    loads["k"].wait()
    keys = jnp.dot(normed, wk[...], preferred_element_type=F32)
    for c in range(4):
        span = slice(c * 128, (c + 1) * 128)
        kv[y, :, span] = turn(keys[:, span], cosine, sine).astype(BF)
    loads["v"].wait()
    kv[y, :, 512:1024] = jnp.dot(normed, wv[...], preferred_element_type=F32).astype(BF)
    own = kv.at[y]
    net.start(own, own, 16, ahead)
    net.start(own, own, 17, behind)

    loads["q"].wait()
    queries = jnp.dot(normed, wq[...], preferred_element_type=F32)
    for c in range(8):
        span = slice(c * 128, (c + 1) * 128)
        query_ref[:, span] = turn(queries[:, span], cosine, sine).astype(BF)
    key_pos = lanes(TOK, 512)
    bias[...] = jnp.where((key_pos <= row) & (key_pos < length), 0.0, -1e30)
    gather.second()
    s = kv.at[wrap(y - 1)]
    net.arrived(s, 16)
    net.start(s.at[0:64], s.at[0:64], 18, ahead)
    s = kv.at[wrap(y + 1)]
    net.arrived(s, 17)
    net.start(s.at[64:128], s.at[64:128], 19, behind)
    gather.third()
    s = kv.at[wrap(y + 2)]
    net.arrived(s.at[0:64], 18)
    net.arrived(s.at[64:128], 19)
    send_weight(1)
    send_weight(2)
    pass_weight(0)
    gather.fourth(0)

    def attend(c, carry):
        span = pl.ds(pl.multiple_of(c * 128, 128), 128)
        keys = kv[:, :, span].reshape(512, 128)
        values = kv[:, :, pl.ds(pl.multiple_of(512 + c * 128, 128), 128)].reshape(512, 128)
        for half in range(2):
            m = c * 2 + half
            mine = pl.ds(pl.multiple_of(m * 128, 128), 128)
            pair = stack_heads(query_ref[:, mine].astype(F32), half)
            scores = lax.dot_general(
                pair, keys, (((1,), (1,)), ((), ())), preferred_element_type=F32
            )
            scores = scores * SCALE + jnp.concatenate([bias[...], bias[...]], axis=0)
            scores = jnp.exp(scores - jnp.max(scores, axis=1, keepdims=True))
            low = (scores * (1.0 / jnp.sum(scores, axis=1, keepdims=True))).astype(BF)
            probs[m] = low
            out = jnp.dot(low, values, preferred_element_type=F32)
            mixed_ref[:, mine] = unstack_heads(out, half).astype(BF)
        return carry

    lax.fori_loop(0, 4, attend, 0)
    gather.fourth(1)
    keep_probs = pltpu.make_async_copy(probs, probs_hbm, local_sem.at[8])
    keep_probs.start()
    loads["o"].wait()
    hidden = tokens + jnp.dot(mixed_ref[...], wo[...], preferred_element_type=F32)
    hidden_ref[...] = hidden
    x = (hidden * root(hidden) * gm_ref[...]).astype(BF)
    x_ref[...] = x
    tokens_in.begin(x_ref)
    tokens_in.slab(0, 0)[...] = x
    wide = jnp.dot(router_ref[...], widen(), preferred_element_type=F32).astype(BF)
    logits = jnp.dot(x, wide, preferred_element_type=F32)
    routed = routed_mask(routes_ref[...])
    logits = jnp.where(routed, logits, -1e30)
    weights = jnp.where(routed, jnp.exp(logits - jnp.max(logits, axis=1, keepdims=True)), 0.0)
    weights = weights * (1.0 / jnp.sum(weights, axis=1, keepdims=True))
    gates_ref[...] = weights
    gt[...] = weights.T.reshape(16, 8, TOK)

    def gate_copy(i):
        a, b = lax.div(i, 4), lax.rem(i, 4)
        return pltpu.make_async_remote_copy(
            src_ref=gt.at[chip_of(p + a, q + b, core)],
            dst_ref=gin.at[p * 4 + q],
            send_sem=g_send.at[i],
            recv_sem=g_recv.at[wrap(-a) * 4 + wrap(-b)],
            device_id=device(p + a, q + b, y, core),
            device_id_type=MESH,
        )

    def start_gate(i, _):
        gate_copy(i).start()
        return 0

    lax.fori_loop(1, 16, start_gate, 0)
    gin[p * 4 + q] = gt[my_chip]

    kv_ref[...] = kv[...]
    tokens_in.second()
    pass_weight(1)
    tokens_in.third()
    pass_weight(2)

    def take_gate(i, _):
        pltpu.make_async_copy(gin.at[0], gin.at[0], g_recv.at[i]).wait()
        return 0

    lax.fori_loop(1, 16, take_gate, 0)
    ids = lax.broadcasted_iota(jnp.int32, (TOK, TOK), 0)
    cols = lax.broadcasted_iota(jnp.int32, (TOK, TOK), 1)
    before = jnp.where(ids < cols, 1.0, 0.0).astype(BF)
    routed = jnp.where(gin[...].reshape(TOK, TOK) > 0, 1.0, 0.0).astype(BF)
    rank[...] = jnp.dot(routed, before, preferred_element_type=F32).reshape(16, 8, TOK)
    gather.finish()
    ggo[...] = jnp.zeros_like(ggo)
    slot_ids = lax.broadcasted_iota(jnp.int32, (SLOTS, TOK), 0).astype(F32)

    def source_of(g, j):
        side = jnp.where((j < 2) == (g == 1), 3, 1)
        b = jnp.where(g == 0, 0, jnp.where(g == 2, 2, side))
        a = jnp.where(j == 0, 0, jnp.where(j == 1, 3, jnp.where(j == 2, 1, 2)))
        return wrap(p + a) * 4 + wrap(q + b)

    def pick_source(g, j):
        src = source_of(g, j)
        token_rows, up_rows = xs[src], us[src]
        base = pl.multiple_of(g * 4 * SLOTS + j * SLOTS, 16)
        for e in range(2):
            gate_row = gin[src, e : e + 1, :]
            hit = (rank[src, e : e + 1, :] == slot_ids) & (gate_row > 0)
            pick = jnp.where(hit, 1.0, 0.0)
            pick_low = pick.astype(BF)
            picks[src, e * SLOTS : (e + 1) * SLOTS, :] = pick_low
            gate_col = jnp.sum(pick * gate_row, axis=1, keepdims=True)
            rows[e, pl.ds(base, SLOTS), :] = jnp.dot(
                pick_low, token_rows, preferred_element_type=F32
            ).astype(BF)
            picked = jnp.dot(pick_low, up_rows, preferred_element_type=F32)
            wqo[e, pl.ds(base, SLOTS), :] = picked.astype(BF)
            slot_grads[e, pl.ds(base, SLOTS), :] = (picked * gate_col).astype(BF)

    def run_expert(g, e):
        base = pl.multiple_of(g * 4 * SLOTS, 16)
        span = pl.ds(base, 4 * SLOTS)
        taken = rows[e, span, :]
        gate = jnp.dot(taken, wg[e], preferred_element_type=F32)
        upv = jnp.dot(taken, wu[e], preferred_element_type=F32)
        sig = 1.0 / (1.0 + jnp.exp(-gate))
        silu = gate * sig
        act = (silu * upv).astype(BF)
        acts[e, span, :] = act
        grad_act = lax.dot_general(
            slot_grads[e, span, :], wd[e], (((1,), (1,)), ((), ())), preferred_element_type=F32
        )
        ggp = (grad_act * upv * sig * (1.0 + gate * (1.0 - sig))).astype(BF)
        gup = (grad_act * silu).astype(BF)
        gparts[e, span, :] = ggp
        uparts[e, span, :] = gup
        pair = lax.dot_general(ggp, wg[e], (((1,), (1,)), ((), ())), preferred_element_type=F32)
        pair += lax.dot_general(gup, wu[e], (((1,), (1,)), ((), ())), preferred_element_type=F32)
        pairs[e] = pair.astype(BF)

    def spread(g, j):
        src = source_of(g, j)
        span = pl.ds(pl.multiple_of(j * SLOTS, 16), SLOTS)
        both = jnp.concatenate([pairs[0, span, :], pairs[1, span, :]], axis=0)
        p_buf[src] = lax.dot_general(
            picks[src], both, (((0,), (0,)), ((), ())), preferred_element_type=F32
        ).astype(BF)

    def run_output(g, e):
        span = pl.ds(pl.multiple_of(g * 4 * SLOTS, 16), 4 * SLOTS)
        out = jnp.dot(acts[e, span, :], wd[e], preferred_element_type=F32).astype(BF)
        outs[e] = out
        gg_col = jnp.sum(out.astype(F32) * wqo[e, span, :].astype(F32), axis=1, keepdims=True)
        for j in range(4):
            src = source_of(g, j)
            pick = picks[src, pl.ds(pl.multiple_of(e * SLOTS, 16), SLOTS), :].astype(F32)
            part = gg_col[j * SLOTS : (j + 1) * SLOTS]
            ggo[src, pl.ds(e, 1), :] = jnp.sum(pick * part, axis=0, keepdims=True)

    def spread_output(g, j):
        src = source_of(g, j)
        pick = picks[src]
        span = pl.ds(pl.multiple_of(j * SLOTS, 16), SLOTS)
        gates = jnp.concatenate(
            [
                pick[e * SLOTS : (e + 1) * SLOTS].astype(F32) * gin[src, e : e + 1, :]
                for e in range(2)
            ],
            axis=0,
        ).astype(BF)
        both = jnp.concatenate([outs[0, span, :], outs[1, span, :]], axis=0)
        o_buf[src] = lax.dot_general(
            gates, both, (((0,), (0,)), ((), ())), preferred_element_type=F32
        ).astype(BF)

    def output(g, carry):
        lax.fori_loop(0, 2, lambda e, c: (run_output(g, e), c)[1], 0)
        lax.fori_loop(0, 4, lambda j, c: (spread_output(g, j), c)[1], 0)
        return carry

    def pick(g):
        lax.fori_loop(0, 4, lambda j, c: (pick_source(g, j), c)[1], 0)

    OFF = (0, -1, 1, 2)
    R = 58

    def make(source, target, recv, to, index):
        return pltpu.make_async_remote_copy(
            src_ref=source,
            dst_ref=target,
            send_sem=send_sem.at[index],
            recv_sem=recv_sem.at[recv],
            device_id=to,
            device_id_type=MESH,
        )

    first = 80
    bounce = [
        (lambda j=j: make(slab(p_buf, p + OFF[j], q + 2), rb.at[j], R + j, up if j < 2 else down, first + j))
        for j in range(4)
    ]
    to_down = [
        (lambda j=j: make(slab(p_buf, p + OFF[j], q - 1), rc.at[4 + j], R + 8 + j, down, first + 4 + j))
        for j in range(4)
    ]
    to_up = [
        (lambda j=j: make(slab(p_buf, p + OFF[j], q + 1), rc.at[j], R + 4 + j, up, first + 8 + j))
        for j in range(4)
    ]

    def add_bounce(j):
        net.arrived(rb.at[j], R + j)
        target = slab(p_buf, p + OFF[j], q + 1 if j < 2 else q - 1)
        target[...] = (target[...].astype(F32) + rb[j].astype(F32)).astype(BF)

    def step(g, carry):
        @pl.when(g == 2)
        def _():
            for j in range(4):
                tokens_in.arrived(slab(xs, p + OFF[j], q + 2), 12 + j)

        @pl.when(g == 3)
        def _():
            tokens_in.arrived(slab(xs, p + 1, q - 1), 6)
            tokens_in.arrived(slab(xs, p + 2, q - 1), 7)
            tokens_in.arrived(slab(xs, p, q + 1), 8)
            tokens_in.arrived(slab(xs, p - 1, q + 1), 9)
            for j in range(2):
                to_down[j]().start()
                to_up[3 - j]().start()

        @pl.when(g >= 2)
        def _():
            pick(g)

        lax.fori_loop(0, 2, lambda e, c: (run_expert(g, e), c)[1], 0)
        lax.fori_loop(0, 4, lambda j, c: (spread(g, j), c)[1], 0)

        @pl.when(g == 2)
        def _():
            for j in range(4):
                bounce[j]().start()

        @pl.when(g == 3)
        def _():
            for j in (3, 1, 2, 0):
                add_bounce(j)
                (to_up if j < 2 else to_down)[j]().start()

        return carry

    keep_own.wait()
    pick(0)
    tokens_in.fourth(0)
    tokens_in.fourth(1)
    pick(1)
    net.arrived(weight(0, core, y + 2), 26)
    net.arrived(weight(1, core, y + 2, top), 27)
    net.arrived(weight(1, core, y + 2, bottom), 28)
    net.arrived(weight(2, core, y + 2), 29)
    for a in range(3):
        net.start(weight(a, core, y + 2), weight(a, core, y + 2), 39 + a, sibling)
    for i, ahead_by in enumerate((0, -1, 1, 2)):
        for a in range(3):
            net.arrived(weight(a, 1 - core, y + ahead_by), 30 + 3 * i + a)
    for copy in keep:
        copy.wait()
    lax.fori_loop(0, 4, step, 0)
    lax.fori_loop(0, 2, output, 0)

    def weight_tile(e, t):
        cols = pl.ds(pl.multiple_of(t * 256, 256), 256)
        dims = (((0,), (0,)), ((), ()))
        lhs = rows[e, :, cols]
        dwg[e, cols, :] = lax.dot_general(lhs, gparts[e], dims, preferred_element_type=F32).astype(BF)
        dwu[e, cols, :] = lax.dot_general(lhs, uparts[e], dims, preferred_element_type=F32).astype(BF)
        us[4 * e : 4 * e + 4, :, cols] = (
            lax.dot_general(acts[e], slot_grads[e, :, cols], dims, preferred_element_type=F32)
            .astype(BF)
            .reshape(4, TOK, 256)
        )

    def weight_grads(e):
        lax.fori_loop(0, 4, lambda t, c: (weight_tile(e, t), c)[1], 0)

    net.drain()
    weight_grads(0)

    def gather_sum(j):
        net.arrived(rc.at[j], R + 4 + j)
        net.arrived(rc.at[4 + j], R + 8 + j)
        target = slab(p_buf, p + OFF[j], q)
        target[...] = (
            target[...].astype(F32) + rc[j].astype(F32) + rc[4 + j].astype(F32)
        ).astype(BF)

    last = first + 12
    lo, hi = pl.ds(0, 64), pl.ds(64, 64)
    far_slab, next_slab, prev_slab = slab(p_buf, p + 2, q), slab(p_buf, p + 1, q), slab(p_buf, p - 1, q)
    tail = [
        make(far_slab.at[lo], rd.at[lo], R + 12, right, last),
        make(far_slab.at[hi], rd.at[hi], R + 13, left, last + 1),
        make(next_slab.at[hi], re.at[0, hi], R + 14, right, last + 2),
        make(prev_slab.at[lo], re.at[1, lo], R + 15, left, last + 3),
        make(next_slab.at[lo], re.at[0, lo], R + 16, right, last + 4),
        make(prev_slab.at[hi], re.at[1, hi], R + 17, left, last + 5),
    ]
    gather_sum(3)
    tail[0].start()
    tail[1].start()
    gather_sum(2)
    tail[2].start()
    gather_sum(1)
    tail[3].start()
    lax.fori_loop(2, 4, output, 0)

    def gg_copy(i):
        a, b = lax.div(i, 4), lax.rem(i, 4)
        return pltpu.make_async_remote_copy(
            src_ref=ggo.at[wrap(p + a) * 4 + wrap(q + b)],
            dst_ref=gg_out.at[my_chip],
            send_sem=gg_send.at[i],
            recv_sem=gg_recv.at[wrap(-a) * 4 + wrap(-b)],
            device_id=device(p + a, q + b, y, core),
            device_id_type=MESH,
        )

    def start_gg(i, _):
        gg_copy(i).start()
        return 0

    lax.fori_loop(1, 16, start_gg, 0)
    gg_out[my_chip] = ggo[p * 4 + q]
    o_store = pltpu.make_async_copy(o_buf, o_hbm, local_sem.at[9])
    o_store.start()
    net.arrived(rd.at[lo], R + 12)
    next_slab[lo] = (next_slab[lo].astype(F32) + rd[lo].astype(F32)).astype(BF)
    tail[4].start()
    net.arrived(rd.at[hi], R + 13)
    prev_slab[hi] = (prev_slab[hi].astype(F32) + rd[hi].astype(F32)).astype(BF)
    tail[5].start()
    gather_sum(0)
    weight_grads(1)
    stores = [
        pltpu.make_async_copy(src, dst, local_sem.at[10 + i])
        for i, (src, dst) in enumerate(((dwg, dwg_hbm), (dwu, dwu_hbm), (us.at[0:8], dwd_hbm)))
    ]
    for store in stores:
        store.start()
    net.arrived(re.at[0, hi], R + 14)
    net.arrived(re.at[1, lo], R + 15)
    net.arrived(re.at[0, lo], R + 16)
    net.arrived(re.at[1, hi], R + 17)
    grad_out[...] = slab(p_buf, p, q)[...].astype(F32) + re[0].astype(F32) + re[1].astype(F32)

    def take_gg(i, _):
        pltpu.make_async_copy(ggo.at[0], ggo.at[0], gg_recv.at[i]).wait()
        return 0

    lax.fori_loop(1, 16, take_gg, 0)
    for copy in bounce + to_down + to_up:
        copy().wait_send()
    for copy in tail:
        copy.wait_send()

    def drain_small(i, _):
        gate_copy(i).wait_send()
        gg_copy(i).wait_send()
        return 0

    lax.fori_loop(1, 16, drain_small, 0)
    o_store.wait()
    for store in stores:
        store.wait()
    keep_probs.wait()


def main(tokens, wq, wk, wv, wo, ga, gm, router, cotangent, routes, lengths, wg, wu, wd):
    cosine, sine = turn_tables()
    any_space = pl.BlockSpec(memory_space=pl.ANY)
    vmem = pl.BlockSpec(memory_space=pltpu.VMEM)
    smem = pl.BlockSpec(memory_space=pltpu.SMEM)
    shape = jax.ShapeDtypeStruct
    dma = pltpu.SemaphoreType.DMA
    slots = 16 * SLOTS
    low = lambda *size: pltpu.VMEM(size, BF)
    return pl.pallas_call(
        main_kernel,
        out_shape=(
            shape((TOK, D), F32),
            shape((TOK, D), BF),
            shape((TOK, TOK), F32),
            shape((TOK, D), BF),
            shape((TOK, D), BF),
            shape((4, TOK, D), BF),
            shape((TOK, D), F32),
            shape((16, 8, TOK), F32),
            shape((8, 2 * TOK, 512), BF),
            shape((16, TOK, D), BF),
            shape((2, D, FF), BF),
            shape((2, D, FF), BF),
            shape((8, TOK, D), BF),
        ),
        in_specs=[vmem] + [any_space] * 4 + [vmem] * 5 + [smem] + [vmem] * 2 + [any_space] * 3,
        out_specs=(vmem,) * 8 + (any_space,) * 5,
        scratch_shapes=[
            low(2, D, D),
            low(D, 512),
            low(D, 512),
            low(TOK, D),
            low(4, TOK, D),
            low(8, 2 * TOK, 512),
            pltpu.VMEM((TOK, 512), F32),
            pltpu.VMEM((16, 8, TOK), F32),
            low(16, TOK, D),
            low(16, TOK, D),
            low(2, D, FF),
            low(2, D, FF),
            low(2, FF, D),
            pltpu.VMEM((16, 8, TOK), F32),
            pltpu.VMEM((16, 8, TOK), F32),
            pltpu.VMEM((16, 8, TOK), F32),
            low(16, 2 * SLOTS, TOK),
            low(2, slots, D),
            low(2, slots, D),
            low(2, slots, FF),
            low(2, slots, FF),
            low(2, slots, FF),
            low(2, 4 * SLOTS, D),
            low(2, 4 * SLOTS, D),
            low(16, TOK, D),
            low(16, TOK, D),
            low(4, TOK, D),
            low(8, TOK, D),
            low(TOK, D),
            low(2, TOK, D),
            low(2, D, FF),
            low(2, D, FF),
            dma((100,)),
            dma((76,)),
            dma((16,)),
            dma((16,)),
            dma((16,)),
            dma((16,)),
            dma((13,)),
        ],
        compiler_params=pltpu.CompilerParams(
            collective_id=1, has_side_effects=True, vmem_limit_bytes=VMEM_BYTES
        ),
        name="main",
    )(
        tokens, wq, wk, wv, wo, ga.reshape(1, D), gm.reshape(1, D), router, cotangent, routes,
        lengths, jnp.asarray(cosine), jnp.asarray(sine), wg, wu, wd,
    )


def accumulate(target, *terms):
    total = target[...].astype(F32)
    for term in terms:
        total += term[...].astype(F32)
    target[...] = total.astype(target.dtype)


class PlaneReduce:
    OFF = (0, -1, 1, 2)

    def __init__(self, net, spot, slabs, rb, rc, rd, re, base):
        self.net, self.spot, self.slabs, self.base = net, spot, slabs, base
        self.rb, self.rc, self.rd, self.re = rb, rc, rd, re
        p, q, y, core = spot
        self.right, self.left = device(p + 1, q, y, core), device(p - 1, q, y, core)
        self.up, self.down = device(p, q + 1, y, core), device(p, q - 1, y, core)

    def slab(self, a, b):
        return slab(self.slabs, self.spot[0] + a, self.spot[1] + b)

    def send(self, source, target, recv, to):
        self.net.start(source, target, self.base + recv, to)

    def arrived(self, ref, recv):
        self.net.arrived(ref, self.base + recv)

    def bounce(self):
        for j in range(4):
            to = self.up if j < 2 else self.down
            self.send(self.slab(self.OFF[j], 2), self.rb.at[j], j, to)

    def to_up(self, j):
        self.send(self.slab(self.OFF[j], 1), self.rc.at[j], 4 + j, self.up)

    def to_down(self, j):
        self.send(self.slab(self.OFF[j], -1), self.rc.at[4 + j], 8 + j, self.down)

    def begin(self):
        self.bounce()
        for j in (3, 2):
            self.to_up(j)
        for j in (0, 1):
            self.to_down(j)

    def middle(self):
        for j in (3, 1, 2, 0):
            self.arrived(self.rb.at[j], j)
            accumulate(self.slab(self.OFF[j], 1 if j < 2 else -1), self.rb.at[j])
            (self.to_up if j < 2 else self.to_down)(j)

    def column(self, j):
        self.arrived(self.rc.at[j], 4 + j)
        self.arrived(self.rc.at[4 + j], 8 + j)
        accumulate(self.slab(self.OFF[j], 0), self.rc.at[j], self.rc.at[4 + j])

    def third(self):
        lo, hi = pl.ds(0, 64), pl.ds(64, 64)
        rd, re = self.rd, self.re
        self.column(3)
        self.send(self.slab(2, 0).at[lo], rd.at[lo], 12, self.right)
        self.send(self.slab(2, 0).at[hi], rd.at[hi], 13, self.left)
        self.column(2)
        self.send(self.slab(1, 0).at[hi], re.at[0, hi], 14, self.right)
        self.column(1)
        self.send(self.slab(-1, 0).at[lo], re.at[1, lo], 15, self.left)

    def fourth(self):
        lo, hi = pl.ds(0, 64), pl.ds(64, 64)
        rd, re = self.rd, self.re
        self.arrived(rd.at[lo], 12)
        accumulate(self.slab(1, 0).at[lo], rd.at[lo])
        self.send(self.slab(1, 0).at[lo], re.at[0, lo], 16, self.right)
        self.arrived(rd.at[hi], 13)
        accumulate(self.slab(-1, 0).at[hi], rd.at[hi])
        self.send(self.slab(-1, 0).at[hi], re.at[1, hi], 17, self.left)
        self.column(0)

    def finish(self):
        lo, hi = pl.ds(0, 64), pl.ds(64, 64)
        re = self.re
        self.arrived(re.at[0, hi], 14)
        self.arrived(re.at[1, lo], 15)
        self.arrived(re.at[0, lo], 16)
        self.arrived(re.at[1, hi], 17)
        return self.slab(0, 0)[...].astype(F32) + re[0].astype(F32) + re[1].astype(F32)


class RingReduce:
    def __init__(self, net, base, ahead, behind, portion, hops, lows, highs):
        self.net, self.base, self.ahead, self.behind = net, base, ahead, behind
        self.portion, self.hops, self.lows, self.highs = portion, hops, lows, highs
        self.n = len(hops[0])

    def send(self, sources, targets, group, to):
        for i, (source, target) in enumerate(zip(sources, targets)):
            self.net.start(source, target, self.base + group * self.n + i, to)

    def arrived(self, refs, group):
        for i, ref in enumerate(refs):
            self.net.arrived(ref, self.base + group * self.n + i)

    def begin(self):
        self.send(self.portion(2, 0), self.hops[0], 0, self.ahead)
        self.send(self.portion(2, 1), self.hops[1], 1, self.behind)

    def direct(self):
        self.send(self.portion(1, 1), self.lows[1], 2, self.ahead)
        self.send(self.portion(-1, 0), self.highs[0], 3, self.behind)

    def middle(self):
        for which, step, targets, to in (
            (0, 1, self.lows[0], self.ahead),
            (1, -1, self.highs[1], self.behind),
        ):
            self.arrived(self.hops[which], which)
            refs = self.portion(step, which)
            for ref, hop in zip(refs, self.hops[which]):
                accumulate(ref, hop)
            self.send(refs, targets, 4 + which, to)

    def finish(self):
        self.arrived(self.lows[1], 2)
        self.arrived(self.highs[0], 3)
        self.arrived(self.lows[0], 4)
        self.arrived(self.highs[1], 5)


def back_kernel(
    rows_ref, gg_ref, x_ref, gates_ref, hidden_ref, gm_ref, ga_ref, router_ref, cot_ref, tok_ref,
    mixed_ref, query_ref, kv_ref, cos_ref, sin_ref, routes_ref, len_ref,
    probs_hbm, wo_hbm, wq_hbm, wk_hbm, wv_hbm, o_hbm, pg_hbm, pu_hbm, pd_hbm,
    layer_ref, input_ref, dq_out, do_out, dkv_out, narrow_ref, gate_out, up_out, down_out,
    probs, wo, wq, wk, wv, o_buf, rb, rc, rd, re,
    pg, pu, pd, sg, su, sd, hop_g, hop_ua, hop_ub, hop_d, low_g, low_u, low_d, high_g, high_u, high_d,
    grad_mixed, grad_query, grad_kv, kv_hops, kv_low, kv_high,
    send_sem, recv_sem, local_sem,
):
    p, q, y, core = place()
    spot = (p, q, y, core)
    sibling = (chip_of(p, q, core) * 2 + 1 - core, y)
    ahead, behind = device(p, q, y + 1, core), device(p, q, y - 1, core)
    net = Sends(send_sem, recv_sem)
    pairs = (
        (o_hbm, o_buf), (wo_hbm, wo), (probs_hbm, probs), (wq_hbm, wq), (wk_hbm, wk), (wv_hbm, wv),
        (pg_hbm.at[core], pg), (pu_hbm.at[core], pu), (pd_hbm.at[core], pd),
    )
    loads = [pltpu.make_async_copy(s, d, local_sem.at[i]) for i, (s, d) in enumerate(pairs)]
    for load in loads:
        load.start()
    plane = PlaneReduce(net, spot, o_buf, rb, rc, rd, re, 0)
    greet([plane.right, plane.left, plane.up, plane.down, ahead, behind, sibling])
    loads[0].wait()
    plane.begin()
    for i, (source, target) in enumerate(((pg_hbm, sg), (pu_hbm, su), (pd_hbm, sd))):
        net.start(source.at[1 - core], target, 18 + i, sibling)

    first = pl.multiple_of(y * TOK, TOK)
    row = lax.broadcasted_iota(jnp.int32, (TOK, 1), 0) + y * TOK
    upstream = jnp.where(row < len_ref[0], cot_ref[...].astype(F32), 0.0)
    gates = gates_ref[...]
    grad_gates = gg_ref[...].reshape(TOK, TOK).T
    grad_logits = gates * (grad_gates - jnp.sum(gates * grad_gates, axis=1, keepdims=True))
    grad_logits = grad_logits.astype(BF)
    wide = jnp.dot(router_ref[...], widen(), preferred_element_type=F32).astype(BF)
    by_row = (((0,), (0,)), ((), ()))
    by_col = (((1,), (1,)), ((), ()))
    grad_normed = rows_ref[...] + lax.dot_general(
        grad_logits, wide, by_col, preferred_element_type=F32
    )
    hidden = hidden_ref[...]
    scale = root(hidden)
    grad_gain_moe = jnp.sum(grad_normed * hidden * scale, axis=0, keepdims=True)
    scaled = grad_normed * gm_ref[...]
    pull = jnp.mean(scaled * hidden, axis=1, keepdims=True)
    grad_hidden = upstream + scale * scaled - hidden * (scale * scale * scale) * pull
    input_ref[...] = grad_hidden
    low = grad_hidden.astype(BF)
    loads[1].wait()
    grad_mixed[...] = lax.dot_general(low, wo[...], by_col, preferred_element_type=F32).astype(BF)
    narrow_ref[...] = lax.dot_general(grad_logits, x_ref[...], by_row, preferred_element_type=F32)
    counts = jnp.sum(jnp.where(routed_mask(routes_ref[...]), 1.0, 0.0), axis=0, keepdims=True)
    narrow_ref[3:4, :] = grad_gain_moe
    narrow_ref[4:5, :] = jnp.zeros((1, D), F32)
    narrow_ref[4:5, 0:TOK] = counts
    plane.middle()

    def block(ref, step, rows=None):
        span = pl.ds(pl.multiple_of(wrap(y + step) * TOK, TOK), TOK)
        return ref.at[:, span] if rows is None else ref.at[rows, span]

    def down_block(ref, step):
        return ref.at[pl.ds(pl.multiple_of(wrap(y + step) * TOK, TOK), TOK)]

    top, bottom = pl.ds(0, 512), pl.ds(512, 512)

    def weight_portion(step, which):
        if which == 0:
            return [block(pg, step), block(pu, step, top)]
        return [block(pu, step, bottom), down_block(pd, step)]

    def weight_merge(step):
        accumulate(block(pg, step), block(sg, step))
        accumulate(block(pu, step), block(su, step))
        accumulate(down_block(pd, step), down_block(sd, step))

    weights = RingReduce(
        net, 24, ahead, behind, weight_portion,
        ([hop_g, hop_ua], [hop_ub, hop_d]),
        ([low_g, low_u.at[top]], [low_u.at[bottom], low_d]),
        ([high_g, high_u.at[top]], [high_u.at[bottom], high_d]),
    )
    for load in loads[6:]:
        load.wait()
    for i, ref in enumerate((sg, su, sd)):
        net.arrived(ref, 18 + i)
    weight_merge(2)
    weights.begin()

    cosine, sine = cos_ref[pl.ds(first, TOK), :], sin_ref[pl.ds(first, TOK), :]
    loads[2].wait()

    def attend(c, carry):
        span = pl.ds(pl.multiple_of(c * 128, 128), 128)
        value_span = pl.ds(pl.multiple_of(512 + c * 128, 128), 128)
        keys = kv_ref[:, :, span].reshape(512, 128)
        values = kv_ref[:, :, value_span].reshape(512, 128)
        grad_keys = jnp.zeros((512, 128), F32)
        grad_values = jnp.zeros((512, 128), F32)
        for half in range(2):
            m = c * 2 + half
            mine = pl.ds(pl.multiple_of(m * 128, 128), 128)
            pair = stack_heads(query_ref[:, mine].astype(F32), half)
            grad_pair = stack_heads(grad_mixed[:, mine].astype(F32), half)
            grad_probs = lax.dot_general(grad_pair, values, by_col, preferred_element_type=F32)
            prob = probs[m]
            wide_prob = prob.astype(F32)
            middle = jnp.sum(wide_prob * grad_probs, axis=1, keepdims=True)
            grad_scores = (wide_prob * (grad_probs - middle)).astype(BF)
            back = jnp.dot(grad_scores, keys, preferred_element_type=F32) * SCALE
            grad_query[:, mine] = turn(unstack_heads(back, half), cosine, -sine).astype(BF)
            grad_keys += lax.dot_general(grad_scores, pair, by_row, preferred_element_type=F32)
            grad_values += lax.dot_general(prob, grad_pair, by_row, preferred_element_type=F32)
        grad_kv[:, :, span] = (grad_keys * SCALE).astype(BF).reshape(4, TOK, 128)
        grad_kv[:, :, value_span] = grad_values.astype(BF).reshape(4, TOK, 128)
        return carry

    lax.fori_loop(0, 4, attend, 0)
    lo, hi = pl.ds(0, 64), pl.ds(64, 64)
    sums = RingReduce(
        net, 36, ahead, behind,
        lambda step, which: [grad_kv.at[wrap(y + step), hi if which else lo]],
        ([kv_hops.at[0]], [kv_hops.at[1]]),
        ([kv_low.at[lo]], [kv_low.at[hi]]),
        ([kv_high.at[lo]], [kv_high.at[hi]]),
    )
    sums.begin()
    sums.direct()
    plane.third()
    do_out[...] = lax.dot_general(
        mixed_ref[...], low, by_row, preferred_element_type=F32
    ).astype(BF)
    sums.middle()
    plane.fourth()
    tokens = tok_ref[...].astype(F32)
    scale = root(tokens)
    normed = (tokens * scale * ga_ref[...]).astype(BF)
    dq_out[...] = lax.dot_general(
        normed, grad_query[...], by_row, preferred_element_type=F32
    ).astype(BF)
    for load in loads[3:6]:
        load.wait()
    grad_normed = lax.dot_general(grad_query[...], wq[...], by_col, preferred_element_type=F32)
    weight_merge(1)
    weight_merge(-1)
    weights.direct()
    weights.middle()
    weight_merge(0)
    sums.finish()
    both = grad_kv[y].astype(F32) + kv_low[...].astype(F32) + kv_high[...].astype(F32)
    grad_key = jnp.concatenate(
        [turn(both[:, c * 128 : (c + 1) * 128], cosine, -sine) for c in range(4)], axis=1
    ).astype(BF)
    grad_value = both[:, 512:].astype(BF)
    dkv_out[:, 0:512] = lax.dot_general(
        normed, grad_key, by_row, preferred_element_type=F32
    ).astype(BF)
    dkv_out[:, 512:1024] = lax.dot_general(
        normed, grad_value, by_row, preferred_element_type=F32
    ).astype(BF)
    grad_normed += lax.dot_general(grad_key, wk[...], by_col, preferred_element_type=F32)
    grad_normed += lax.dot_general(grad_value, wv[...], by_col, preferred_element_type=F32)
    narrow_ref[2:3, :] = jnp.sum(grad_normed * tokens * scale, axis=0, keepdims=True)
    scaled = grad_normed * ga_ref[...]
    pull = jnp.mean(scaled * tokens, axis=1, keepdims=True)
    input_ref[...] += scale * scaled - tokens * (scale * scale * scale) * pull
    layer_ref[...] = (hidden_ref[...] + plane.finish()).astype(BF)
    weights.finish()
    gate_out[...] = (
        block(pg, 0)[...].astype(F32) + low_g[...].astype(F32) + high_g[...].astype(F32)
    )
    up_out[...] = block(pu, 0)[...].astype(F32) + low_u[...].astype(F32) + high_u[...].astype(F32)
    down_out[...] = (
        down_block(pd, 0)[...].astype(F32) + low_d[...].astype(F32) + high_d[...].astype(F32)
    )
    net.drain()


def back(operands, arrays):
    any_space = pl.BlockSpec(memory_space=pl.ANY)
    vmem = pl.BlockSpec(memory_space=pltpu.VMEM)
    smem = pl.BlockSpec(memory_space=pltpu.SMEM)
    shape = jax.ShapeDtypeStruct
    dma = pltpu.SemaphoreType.DMA
    low = lambda *size: pltpu.VMEM(size, BF)
    return pl.pallas_call(
        back_kernel,
        out_shape=(
            shape((TOK, D), BF),
            shape((TOK, D), F32),
            shape((D, D), BF),
            shape((D, D), BF),
            shape((D, D), BF),
            shape((TOK, D), F32),
            shape((D, TOK), F32),
            shape((D, TOK), F32),
            shape((TOK, D), F32),
        ),
        in_specs=[vmem] * 16 + [smem] + [any_space] * 9,
        out_specs=(vmem,) * 9,
        scratch_shapes=[
            low(8, 2 * TOK, 512),
            low(D, D),
            low(D, D),
            low(D, 512),
            low(D, 512),
            low(16, TOK, D),
            low(4, TOK, D),
            low(8, TOK, D),
            low(TOK, D),
            low(2, TOK, D),
            low(D, FF),
            low(D, FF),
            low(FF, D),
            low(D, FF),
            low(D, FF),
            low(FF, D),
            low(D, TOK),
            low(512, TOK),
            low(512, TOK),
            low(TOK, D),
            low(D, TOK),
            low(D, TOK),
            low(TOK, D),
            low(D, TOK),
            low(D, TOK),
            low(TOK, D),
            low(TOK, D),
            low(TOK, D),
            low(4, TOK, D),
            low(2, 64, D),
            low(TOK, D),
            low(TOK, D),
            dma((48,)),
            dma((42,)),
            dma((9,)),
        ],
        compiler_params=pltpu.CompilerParams(
            collective_id=4, has_side_effects=True, vmem_limit_bytes=VMEM_BYTES
        ),
        name="back",
    )(*operands, *arrays)


def total_kernel(
    a_hbm, b_hbm, c_hbm, s_hbm, a_out, b_out, c_out, s_out,
    mine, other, mine_s, other_s, from_low, from_high, from_low_s, from_high_s, bounced, bounced_s,
    spread, spread_s, done, done_s,
    sib_send, sib_recv, ring_send, ring_recv, plane_send, plane_recv, back_send, back_recv,
    round_send, round_recv, last_send, last_recv, local_sem,
):
    dp, y = lax.axis_index("dp"), lax.axis_index("hid")
    core = lax.rem(dp, 2)
    here = (lax.div(dp, 8), y, lax.rem(lax.div(dp, 2), 4))

    def at(spot, on=None):
        spot = [wrap(v) for v in spot]
        return (spot[0] * 8 + spot[2] * 2 + (core if on is None else on), spot[1])

    def along(k, step):
        return at([here[i] + (step if i == k else 0) for i in range(3)])

    sibling = at(here, 1 - core)
    ring = [(along(k, 1), along(k, -1)) for k in range(3)]
    planes = [(1, 2), (0, 2), (0, 1)]
    greeted = [sibling]
    for dx in range(4):
        for dy in range(4):
            for dz in range(4):
                if (dx or dy or dz) and not (dx and dy and dz):
                    greeted.append(at([here[0] + dx, here[1] + dy, here[2] + dz]))
    ins, results = (a_hbm, b_hbm, c_hbm, s_hbm), (a_out, b_out, c_out, s_out)
    axes = (0, 1, 2, 0)
    halves = [mine.at[k] for k in range(3)] + [mine_s]
    theirs = [other.at[k] for k in range(3)] + [other_s]
    lows = [from_low.at[k] for k in range(3)] + [from_low_s]
    highs = [from_high.at[k] for k in range(3)] + [from_high_s]
    hops = [bounced.at[k] for k in range(3)] + [bounced_s]
    pieces = [spread.at[k] for k in range(3)] + [spread_s]
    slabs = [done.at[k] for k in range(3)] + [done_s]
    parts = range(4)
    sizes = (128, 128, 128, 16)

    def half_of(k, which):
        return ins[k].at[pl.ds(pl.multiple_of(which * sizes[k] * 4, sizes[k] * 4), sizes[k] * 4)]


    def remote(source, target, send, recv, to):
        return pltpu.make_async_remote_copy(
            src_ref=source, dst_ref=target, send_sem=send, recv_sem=recv,
            device_id=to, device_id_type=MESH,
        )

    def arrived(ref, sem):
        pltpu.make_async_copy(ref, ref, sem).wait()

    loads = [
        pltpu.make_async_copy(half_of(k, core), halves[k], local_sem.at[k]) for k in parts
    ]
    for load in loads:
        load.start()
    greet(greeted)
    sent = []

    def go(*copy):
        copy = remote(*copy)
        copy.start()
        sent.append(copy)

    for k in parts:
        go(half_of(k, 1 - core), theirs[k], sib_send.at[k], sib_recv.at[k], sibling)

    def rows_of(k, step):
        start = pl.multiple_of(wrap(here[axes[k]] + step) * sizes[k], sizes[k])
        return halves[k].at[pl.ds(start, sizes[k])]

    los = [pl.ds(0, size // 2) for size in sizes]
    his = [pl.ds(size // 2, size // 2) for size in sizes]

    def add(target, *terms):
        total = target[...].astype(F32)
        for term in terms:
            total += term[...].astype(F32)
        target[...] = total.astype(target.dtype)

    def merge_rows(k, step):
        start = pl.multiple_of(wrap(here[axes[k]] + step) * sizes[k], sizes[k])
        span = pl.ds(start, sizes[k])
        add(halves[k].at[span], theirs[k].at[span])

    for k in parts:
        lo, hi = los[k], his[k]
        loads[k].wait()
        arrived(theirs[k], sib_recv.at[k])
        plus, minus = ring[axes[k]]
        merge_rows(k, 2)
        far = rows_of(k, 2)
        go(far.at[lo], hops[k].at[lo], ring_send.at[k, 0], ring_recv.at[k, 0], plus)
        go(far.at[hi], hops[k].at[hi], ring_send.at[k, 1], ring_recv.at[k, 1], minus)
        merge_rows(k, 1)
        go(rows_of(k, 1).at[hi], lows[k].at[hi], ring_send.at[k, 2], ring_recv.at[k, 2], plus)
        merge_rows(k, -1)
        go(rows_of(k, -1).at[lo], highs[k].at[lo], ring_send.at[k, 3], ring_recv.at[k, 3], minus)
        merge_rows(k, 0)
    for k in parts:
        lo, hi = los[k], his[k]
        plus, minus = ring[axes[k]]
        arrived(hops[k].at[lo], ring_recv.at[k, 0])
        near = rows_of(k, 1).at[lo]
        add(near, hops[k].at[lo])
        go(near, lows[k].at[lo], ring_send.at[k, 4], ring_recv.at[k, 4], plus)
        arrived(hops[k].at[hi], ring_recv.at[k, 1])
        near = rows_of(k, -1).at[hi]
        add(near, hops[k].at[hi])
        go(near, highs[k].at[hi], ring_send.at[k, 5], ring_recv.at[k, 5], minus)

    def piece(k, ref, u, v):
        if k == 3:
            row, lane = lax.div(u, 2) * 8, (lax.rem(u, 2) * 4 + v) * 128
            return ref.at[pl.ds(pl.multiple_of(row, 8), 8), pl.ds(pl.multiple_of(lane, 128), 128)]
        return ref.at[
            pl.ds(pl.multiple_of(u * 32, 32), 32), pl.ds(pl.multiple_of(v * 256, 256), 256)
        ]

    def member(k, i):
        u, v = planes[axes[k]]
        spot = list(here)
        spot[u] = wrap(here[u] + lax.div(i, 4))
        spot[v] = wrap(here[v] + lax.rem(i, 4))
        return spot[u], spot[v], at(spot)

    def mirror(i):
        return wrap(-lax.div(i, 4)) * 4 + wrap(-lax.rem(i, 4))

    def piece_copy(k, i):
        u, v, to = member(k, i)
        return remote(
            piece(k, rows_of(k, 0), u, v),
            pieces[k].at[mirror(i)],
            plane_send.at[k, i],
            plane_recv.at[k, mirror(i)],
            to,
        )

    def back_copy(k, i):
        u, v = planes[axes[k]]
        spot = piece(k, slabs[k], here[u], here[v])
        return remote(spot, spot, back_send.at[k, i], back_recv.at[k, mirror(i)], member(k, i)[2])

    def each(make, act):
        def one(i, carry):
            act(make(i))
            return carry

        lax.fori_loop(1, 16, one, 0)

    for k in parts:
        lo, hi = los[k], his[k]
        for i in (2, 4):
            arrived(lows[k].at[hi if i == 2 else lo], ring_recv.at[k, i])
        for i in (3, 5):
            arrived(highs[k].at[lo if i == 3 else hi], ring_recv.at[k, i])
        add(rows_of(k, 0), lows[k], highs[k])
        each(lambda i: piece_copy(k, i), lambda copy: copy.start())
    for k in parts:
        u, v = planes[axes[k]]
        pieces[k][0] = piece(k, rows_of(k, 0), here[u], here[v])[...]
        each(
            lambda i: pltpu.make_async_copy(pieces[k].at[0], pieces[k].at[0], plane_recv.at[k, i]),
            lambda copy: copy.wait(),
        )
        total = jnp.sum(pieces[k][...].astype(F32), axis=0)
        piece(k, slabs[k], here[u], here[v])[...] = total.astype(slabs[k].dtype)
        each(lambda i: back_copy(k, i), lambda copy: copy.start())

    def final(k, step, span=None):
        size = sizes[k]
        start = core * size * 4 + wrap(here[axes[k]] + step) * size
        if span is not None:
            size = size // 2
            start += span * size
        return results[k].at[pl.ds(pl.multiple_of(start, size), size)]

    stores = []
    for k in parts:
        plus, minus = ring[axes[k]]
        each(
            lambda i: pltpu.make_async_copy(pieces[k].at[0], pieces[k].at[0], back_recv.at[k, i]),
            lambda copy: copy.wait(),
        )
        go(slabs[k], final(k, 0), round_send.at[k, 0], round_recv.at[k, 0], plus)
        go(slabs[k], final(k, 0), round_send.at[k, 1], round_recv.at[k, 1], minus)
        go(slabs[k], final(k, 0), last_send.at[k, 0], last_recv.at[k, 0], sibling)
        store = pltpu.make_async_copy(slabs[k], final(k, 0), local_sem.at[k])
        store.start()
        stores.append(store)
    for k in parts:
        plus, minus = ring[axes[k]]
        arrived(final(k, -1), round_recv.at[k, 0])
        spot = final(k, -1, 0)
        go(spot, spot, round_send.at[k, 2], round_recv.at[k, 2], plus)
        go(final(k, -1), final(k, -1), last_send.at[k, 1], last_recv.at[k, 1], sibling)
        arrived(final(k, 1), round_recv.at[k, 1])
        spot = final(k, 1, 1)
        go(spot, spot, round_send.at[k, 3], round_recv.at[k, 3], minus)
        go(final(k, 1), final(k, 1), last_send.at[k, 2], last_recv.at[k, 2], sibling)
    for k in parts:
        arrived(final(k, 2, 0), round_recv.at[k, 2])
        arrived(final(k, 2, 1), round_recv.at[k, 3])
        go(final(k, 2), final(k, 2), last_send.at[k, 3], last_recv.at[k, 3], sibling)
    for k in parts:
        for i in range(4):
            arrived(final(k, 0), last_recv.at[k, i])
    for copy in sent:
        copy.wait_send()
    for k in parts:
        each(lambda i: piece_copy(k, i), lambda copy: copy.wait_send())
        each(lambda i: back_copy(k, i), lambda copy: copy.wait_send())
    for store in stores:
        store.wait()


def total(a, b, c, s):
    any_space = pl.BlockSpec(memory_space=pl.ANY)
    shape = jax.ShapeDtypeStruct
    dma = pltpu.SemaphoreType.DMA
    vmem = pltpu.VMEM
    return pl.pallas_call(
        total_kernel,
        out_shape=(shape((D, D), BF),) * 3 + (shape((TOK, D), F32),),
        in_specs=[any_space] * 4,
        out_specs=(any_space,) * 4,
        scratch_shapes=[
            vmem((3, 512, D), BF),
            vmem((3, 512, D), BF),
            vmem((64, D), F32),
            vmem((64, D), F32),
            vmem((3, 128, D), BF),
            vmem((3, 128, D), BF),
            vmem((16, D), F32),
            vmem((16, D), F32),
            vmem((3, 128, D), BF),
            vmem((16, D), F32),
            vmem((3, 16, 32, 256), BF),
            vmem((16, 8, TOK), F32),
            vmem((3, 128, D), BF),
            vmem((16, D), F32),
            dma((4,)),
            dma((4,)),
            dma((4, 6)),
            dma((4, 6)),
            dma((4, 16)),
            dma((4, 16)),
            dma((4, 16)),
            dma((4, 16)),
            dma((4, 4)),
            dma((4, 4)),
            dma((4, 4)),
            dma((4, 4)),
            dma((4,)),
        ],
        compiler_params=pltpu.CompilerParams(
            collective_id=2, has_side_effects=True, vmem_limit_bytes=VMEM_BYTES
        ),
        name="total",
    )(a, b, c, s)


def shards(
    tokens,
    w_query,
    w_key,
    w_value,
    w_output,
    gain_attn,
    gain_moe,
    router,
    w_gate,
    w_up,
    w_down,
    cotangent,
    routes,
    lengths,
):
    (
        hidden, x, gates, mixed, query, kv, grad_rows, grad_gates, probs, out_parts, part_gate,
        part_up, part_down,
    ) = main(
        tokens, w_query, w_key, w_value, w_output, gain_attn, gain_moe, router, cotangent, routes,
        lengths, w_gate, w_up, w_down,
    )
    cosine, sine = turn_tables()
    layer_out, grad_input, sum_q, sum_o, sum_kv, narrow, grad_gate, grad_up, grad_down = back(
        (
            grad_rows, grad_gates, x, gates, hidden, gain_moe.reshape(1, D),
            gain_attn.reshape(1, D), router, cotangent, tokens, mixed, query, kv,
            jnp.asarray(cosine), jnp.asarray(sine), routes, lengths,
        ),
        (
            probs, w_output, w_query, w_key, w_value, out_parts, part_gate, part_up,
            part_down.reshape(2, FF, D),
        ),
    )
    sum_q, sum_o, sum_kv, narrow = total(sum_q, sum_o, sum_kv, narrow)
    sum_kv = sum_kv.astype(F32)
    return (
        layer_out,
        grad_input,
        sum_q.astype(F32),
        sum_kv[:, :512],
        sum_kv[:, 512:],
        sum_o.astype(F32),
        narrow[2],
        narrow[3],
        narrow.reshape(16, 8, D)[:, :2].reshape(EXPERTS, D).T,
        grad_gate[None],
        grad_up[None],
        grad_down[None],
        narrow[4, :TOK].reshape(16, 8)[:, :2].reshape(EXPERTS).astype(jnp.int32),
    )


def solution(mesh):
    in_specs = (
        P(("dp", "hid"), None),
        P(),
        P(),
        P(),
        P(),
        P(),
        P(),
        P(),
        P("dp", None, "hid"),
        P("dp", None, "hid"),
        P("dp", "hid", None),
        P(("dp", "hid"), None),
        P(("dp", "hid"), None),
        P("dp"),
    )
    out_specs = (
        P(("dp", "hid"), None),
        P(("dp", "hid"), None),
        P(),
        P(),
        P(),
        P(),
        P(),
        P(),
        P(),
        P("dp", None, "hid"),
        P("dp", None, "hid"),
        P("dp", "hid", None),
        P(),
    )
    return jax.shard_map(shards, mesh=mesh, in_specs=in_specs, out_specs=out_specs, check_vma=False)
```

```python
import jax
import jax.numpy as jnp
import numpy as np
from jax import lax
from jax.experimental import pallas as pl
from jax.experimental.pallas import tpu as pltpu
from jax.sharding import PartitionSpec as P

D = 1024
HEADS = 16
KV_HEADS = 8
HEAD_DIM = 64
EXPERTS = 32
TOP = 8
FF = 512
TOK = 128

MESH = pl.DeviceIdType.MESH
BF = jnp.bfloat16
F32 = jnp.float32
SLOTS = 48
VMEM_BYTES = 60 * 2**20


def wrap(value):
    return lax.rem(value + 4, 4)


def place():
    dp = lax.axis_index("dp")
    y = lax.axis_index("hid")
    core = lax.rem(dp, 2)
    x = lax.div(dp, 8)
    z = lax.rem(lax.div(dp, 2), 4)
    p = jnp.where(core == 0, x, z)
    q = jnp.where(core == 0, z, x)
    return p, q, y, core


def device(p, q, y, core):
    p, q = wrap(p), wrap(q)
    return (jnp.where(core == 0, p * 8 + q * 2, q * 8 + p * 2) + core, wrap(y))


def chip_of(p, q, core):
    p, q = wrap(p), wrap(q)
    return jnp.where(core == 0, p * 4 + q, q * 4 + p)


def greet(devices):
    barrier = pltpu.get_barrier_semaphore()
    for other in devices:
        pl.semaphore_signal(barrier, inc=1, device_id=other, device_id_type=MESH)
    pl.semaphore_wait(barrier, len(devices))


class Sends:
    def __init__(self, send_sem, recv_sem):
        self.send_sem, self.recv_sem, self.made = send_sem, recv_sem, []

    def start(self, source, target, recv, to):
        self.put(source, target, self.recv_sem.at[recv], to)

    def put(self, source, target, sem, to):
        copy = pltpu.make_async_remote_copy(
            src_ref=source,
            dst_ref=target,
            send_sem=self.send_sem.at[len(self.made)],
            recv_sem=sem,
            device_id=to,
            device_id_type=MESH,
        )
        copy.start()
        self.made.append(copy)

    def arrived(self, ref, recv):
        pltpu.make_async_copy(ref, ref, self.recv_sem.at[recv]).wait()

    def drain(self):
        for copy in self.made:
            copy.wait_send()
        self.made = []


def slab(buffer, p, q):
    return buffer.at[wrap(p) * 4 + wrap(q)]


HALF = HEAD_DIM // 2
SCALE = HEAD_DIM**-0.5


def turn_tables():
    inverse = 10000.0 ** (-np.arange(HALF, dtype=np.float32) / HALF)
    phases = np.arange(4 * TOK, dtype=np.float32)[:, None] * inverse[None, :]
    cosine = np.tile(np.cos(phases), (1, 4)).astype(np.float32)
    sine = np.sin(phases)
    sine = np.tile(np.concatenate([-sine, sine], axis=1), (1, 2)).astype(np.float32)
    return cosine, sine


def lanes(rows, width=128):
    return lax.broadcasted_iota(jnp.int32, (rows, width), 1)


def turn(chunk, cosine, sine):
    front = lax.rem(lanes(chunk.shape[0]), HEAD_DIM) < HALF
    swapped = jnp.where(front, pltpu.roll(chunk, 128 - HALF, 1), pltpu.roll(chunk, HALF, 1))
    return chunk * cosine + swapped * sine


def stack_heads(chunk, half):
    low = lanes(chunk.shape[0]) < HEAD_DIM
    rolled = pltpu.roll(chunk, HEAD_DIM, 1)
    if half == 0:
        pair = (jnp.where(low, chunk, 0.0), jnp.where(low, rolled, 0.0))
    else:
        pair = (jnp.where(low, 0.0, rolled), jnp.where(low, 0.0, chunk))
    return jnp.concatenate(pair, axis=0).astype(BF)


def unstack_heads(pair, half):
    first, second = pair[:TOK], pair[TOK:]
    low = lanes(TOK) < HEAD_DIM
    if half == 0:
        return jnp.where(low, first, pltpu.roll(second, HEAD_DIM, 1))
    return jnp.where(low, pltpu.roll(first, HEAD_DIM, 1), second)


def root(values):
    return lax.rsqrt(jnp.mean(values * values, axis=1, keepdims=True) + 1e-06)


def widen():
    row = lax.broadcasted_iota(jnp.int32, (EXPERTS, TOK), 0)
    lane = lax.broadcasted_iota(jnp.int32, (EXPERTS, TOK), 1)
    return jnp.where(lane == lax.div(row, 2) * 8 + lax.rem(row, 2), 1.0, 0.0).astype(BF)


def routed_mask(routes, expert):
    hit = jnp.zeros((TOK, TOK), F32)
    for k in range(TOP):
        hit = hit + jnp.where(routes[k : k + 1, :] == expert, 1.0, 0.0)
    return hit


def wide_experts():
    row = lax.broadcasted_iota(jnp.int32, (TOK, 1), 0)
    return jnp.where(lax.rem(row, 8) < 2, lax.div(row, 8) * 2 + lax.rem(row, 8), -1)


class PlaneGather:
    def __init__(self, net, spot, slabs, base):
        self.net, self.spot, self.slabs, self.base = net, spot, slabs, base
        p, q, y, core = spot
        self.right, self.left = device(p + 1, q, y, core), device(p - 1, q, y, core)
        self.up, self.down = device(p, q + 1, y, core), device(p, q - 1, y, core)

    def slab(self, a, b):
        return slab(self.slabs, self.spot[0] + a, self.spot[1] + b)

    def send(self, ref, recv, to):
        self.net.start(ref, ref, self.base + recv, to)

    def arrived(self, ref, recv):
        self.net.arrived(ref, self.base + recv)

    def begin(self, own):
        for recv, to in ((0, self.right), (1, self.left), (4, self.up), (8, self.down)):
            self.net.start(own, self.slab(0, 0), self.base + recv, to)

    def second(self):
        s = self.slab(-1, 0)
        self.arrived(s, 0)
        self.send(s.at[0:64], 2, self.right)
        self.send(s, 5, self.up)
        s = self.slab(1, 0)
        self.arrived(s, 1)
        self.send(s.at[64:128], 3, self.left)
        self.send(s, 10, self.down)

    def third(self):
        s = self.slab(0, -1)
        self.arrived(s, 4)
        self.send(s, 12, self.up)
        s = self.slab(2, 0)
        self.arrived(s.at[0:64], 2)
        self.arrived(s.at[64:128], 3)
        self.send(s, 11, self.down)
        s = self.slab(-1, -1)
        self.arrived(s, 5)
        self.send(s, 13, self.up)
        self.send(self.slab(1, 0), 6, self.up)
        self.send(self.slab(2, 0), 7, self.up)
        self.send(self.slab(-1, 0), 9, self.down)

    def fourth(self, which):
        a, recv, far = ((1, 10, 14), (2, 11, 15))[which]
        s = self.slab(a, 1)
        self.arrived(s, recv)
        self.send(s, far, self.down)

    def finish(self):
        for a, b, recv in (
            (1, -1, 6), (2, -1, 7), (0, 1, 8), (-1, 1, 9),
            (0, 2, 12), (-1, 2, 13), (1, 2, 14), (2, 2, 15),
        ):
            self.arrived(self.slab(a, b), recv)


def main_kernel(
    tok_ref, wq_hbm, wk_hbm, wv_hbm, wo_hbm, ga_ref, gm_ref, router_ref, cot_ref, routes_ref,
    len_ref, cos_ref, sin_ref, wgs_hbm, wus_hbm, wds_hbm,
    hidden_ref, x_ref, gates_ref, mixed_ref, query_ref, kv_ref, grad_out, gg_out,
    probs_hbm, o_hbm, dwg_hbm, dwu_hbm, dwd_hbm,
    wqo, wk, wv, u_own, kv, probs, bias, gt,
    xs, us, wg, wu, wd, gin, rank, ggo, picks, rows, slot_grads, acts, gparts, uparts,
    outs, pairs, o_buf, p_buf, rb, rc, rd, re, dwg, dwu,
    send_sem, recv_sem, g_send, g_recv, gg_send, gg_recv, local_sem,
):
    p, q, y, core = place()
    spot = (p, q, y, core)
    sibling = (chip_of(p, q, core) * 2 + 1 - core, y)
    ahead, behind = device(p, q, y + 1, core), device(p, q, y - 1, core)
    up, down = device(p, q + 1, y, core), device(p, q - 1, y, core)
    right, left = device(p + 1, q, y, core), device(p - 1, q, y, core)
    others = [device(p + a, q + b, y, core) for a in range(4) for b in range(4) if a or b]
    my_chip = chip_of(p, q, core)
    net = Sends(send_sem, recv_sem)
    wq, wo = wqo.at[0], wqo.at[1]
    loads = {
        name: pltpu.make_async_copy(src, dst, local_sem.at[i])
        for i, (name, src, dst) in enumerate(
            (("k", wk_hbm, wk), ("v", wv_hbm, wv), ("q", wq_hbm, wq), ("o", wo_hbm, wo))
        )
    }
    for load in loads.values():
        load.start()
    gather = PlaneGather(net, spot, us, 0)
    tokens_in = PlaneGather(net, spot, xs, 42)
    first = pl.multiple_of(y * TOK, TOK)
    row = lax.broadcasted_iota(jnp.int32, (TOK, 1), 0) + y * TOK
    length = len_ref[0]
    u_own[...] = jnp.where(row < length, cot_ref[...].astype(F32), 0.0).astype(BF)
    greet(others + [ahead, behind, sibling])
    gather.begin(u_own)
    keep_own = pltpu.make_async_copy(u_own, gather.slab(0, 0), local_sem.at[4])
    keep_own.start()

    def weight(a, e, yy, rows=None):
        block = pl.ds(pl.multiple_of(wrap(yy) * TOK, TOK), TOK)
        if a == 2:
            return wd.at[e, block, :]
        full = (wg, wu)[a]
        return full.at[e, :, block] if rows is None else full.at[e, rows, block]

    shards = (wgs_hbm.at[0], wus_hbm.at[0], wds_hbm.at[0])
    top, bottom = pl.ds(0, 512), pl.ds(512, 512)
    keep = []

    def send_weight(a):
        net.start(shards[a], weight(a, core, y), 20 + a, ahead)
        net.start(shards[a], weight(a, core, y), 23 + a, behind)
        net.start(shards[a], weight(a, core, y), 30 + a, sibling)
        keep.append(pltpu.make_async_copy(shards[a], weight(a, core, y), local_sem.at[5 + a]))
        keep[-1].start()

    def pass_weight(a):
        before, after = weight(a, core, y - 1), weight(a, core, y + 1)
        net.arrived(before, 20 + a)
        if a == 0:
            net.start(before, before, 26, ahead)
        if a == 1:
            spot = weight(1, core, y - 1, top)
            net.start(spot, spot, 27, ahead)
        net.start(before, before, 33 + a, sibling)
        net.arrived(after, 23 + a)
        if a == 1:
            spot = weight(1, core, y + 1, bottom)
            net.start(spot, spot, 28, behind)
        if a == 2:
            net.start(after, after, 29, behind)
        net.start(after, after, 36 + a, sibling)

    send_weight(0)
    tokens = tok_ref[...].astype(F32)
    normed = (tokens * root(tokens) * ga_ref[...]).astype(BF)
    cosine, sine = cos_ref[pl.ds(first, TOK), :], sin_ref[pl.ds(first, TOK), :]
    loads["k"].wait()
    keys = jnp.dot(normed, wk[...], preferred_element_type=F32)
    for c in range(4):
        span = slice(c * 128, (c + 1) * 128)
        kv[y, :, span] = turn(keys[:, span], cosine, sine).astype(BF)
    loads["v"].wait()
    kv[y, :, 512:1024] = jnp.dot(normed, wv[...], preferred_element_type=F32).astype(BF)
    own = kv.at[y]
    net.start(own, own, 16, ahead)
    net.start(own, own, 17, behind)

    loads["q"].wait()
    queries = jnp.dot(normed, wq[...], preferred_element_type=F32)
    for c in range(8):
        span = slice(c * 128, (c + 1) * 128)
        query_ref[:, span] = turn(queries[:, span], cosine, sine).astype(BF)
    key_pos = lanes(TOK, 512)
    bias[...] = jnp.where((key_pos <= row) & (key_pos < length), 0.0, -1e30)
    gather.second()
    s = kv.at[wrap(y - 1)]
    net.arrived(s, 16)
    net.start(s.at[0:64], s.at[0:64], 18, ahead)
    s = kv.at[wrap(y + 1)]
    net.arrived(s, 17)
    net.start(s.at[64:128], s.at[64:128], 19, behind)
    gather.third()
    s = kv.at[wrap(y + 2)]
    net.arrived(s.at[0:64], 18)
    net.arrived(s.at[64:128], 19)
    send_weight(1)
    send_weight(2)
    pass_weight(0)
    gather.fourth(0)

    def attend(c, carry):
        span = pl.ds(pl.multiple_of(c * 128, 128), 128)
        keys = kv[:, :, span].reshape(512, 128)
        values = kv[:, :, pl.ds(pl.multiple_of(512 + c * 128, 128), 128)].reshape(512, 128)
        for half in range(2):
            m = c * 2 + half
            mine = pl.ds(pl.multiple_of(m * 128, 128), 128)
            pair = stack_heads(query_ref[:, mine].astype(F32), half)
            scores = lax.dot_general(
                pair, keys, (((1,), (1,)), ((), ())), preferred_element_type=F32
            )
            scores = scores * SCALE + jnp.concatenate([bias[...], bias[...]], axis=0)
            scores = jnp.exp(scores - jnp.max(scores, axis=1, keepdims=True))
            low = (scores * (1.0 / jnp.sum(scores, axis=1, keepdims=True))).astype(BF)
            probs[m] = low
            out = jnp.dot(low, values, preferred_element_type=F32)
            mixed_ref[:, mine] = unstack_heads(out, half).astype(BF)
        return carry

    lax.fori_loop(0, 4, attend, 0)
    gather.fourth(1)
    keep_probs = pltpu.make_async_copy(probs, probs_hbm, local_sem.at[8])
    keep_probs.start()
    loads["o"].wait()
    hidden = tokens + jnp.dot(mixed_ref[...], wo[...], preferred_element_type=F32)
    hidden_ref[...] = hidden
    x = (hidden * root(hidden) * gm_ref[...]).astype(BF)
    x_ref[...] = x
    tokens_in.begin(x_ref)
    tokens_in.slab(0, 0)[...] = x
    wide = lax.dot_general(
        widen(), router_ref[...], (((0,), (0,)), ((), ())), preferred_element_type=F32
    ).astype(BF)
    logits = lax.dot_general(x, wide, (((1,), (1,)), ((), ())), preferred_element_type=F32)
    routed = routed_mask(routes_ref[...], wide_experts()).T > 0
    logits = jnp.where(routed, logits, -1e30)
    weights = jnp.where(routed, jnp.exp(logits - jnp.max(logits, axis=1, keepdims=True)), 0.0)
    weights = weights * (1.0 / jnp.sum(weights, axis=1, keepdims=True))
    gates_ref[...] = weights
    gt[...] = weights.T.reshape(16, 8, TOK)

    def gate_copy(i):
        a, b = lax.div(i, 4), lax.rem(i, 4)
        return pltpu.make_async_remote_copy(
            src_ref=gt.at[chip_of(p + a, q + b, core)],
            dst_ref=gin.at[p * 4 + q],
            send_sem=g_send.at[i],
            recv_sem=g_recv.at[wrap(-a) * 4 + wrap(-b)],
            device_id=device(p + a, q + b, y, core),
            device_id_type=MESH,
        )

    def start_gate(i, _):
        gate_copy(i).start()
        return 0

    lax.fori_loop(1, 16, start_gate, 0)
    gin[p * 4 + q] = gt[my_chip]

    kv_ref[...] = kv[...]
    tokens_in.second()
    pass_weight(1)
    tokens_in.third()
    pass_weight(2)

    def take_gate(i, _):
        pltpu.make_async_copy(gin.at[0], gin.at[0], g_recv.at[i]).wait()
        return 0

    lax.fori_loop(1, 16, take_gate, 0)
    ids = lax.broadcasted_iota(jnp.int32, (TOK, TOK), 0)
    cols = lax.broadcasted_iota(jnp.int32, (TOK, TOK), 1)
    before = jnp.where(ids < cols, 1.0, 0.0).astype(BF)
    routed = jnp.where(gin[...].reshape(TOK, TOK) > 0, 1.0, 0.0).astype(BF)
    rank[...] = jnp.dot(routed, before, preferred_element_type=F32).reshape(16, 8, TOK)
    gather.finish()
    ggo[...] = jnp.zeros_like(ggo)
    slot_ids = lax.broadcasted_iota(jnp.int32, (SLOTS, TOK), 0).astype(F32)

    def source_of(g, j):
        side = jnp.where((j < 2) == (g == 1), 3, 1)
        b = jnp.where(g == 0, 0, jnp.where(g == 2, 2, side))
        a = jnp.where(j == 0, 0, jnp.where(j == 1, 3, jnp.where(j == 2, 1, 2)))
        return wrap(p + a) * 4 + wrap(q + b)

    def pick_source(g, j):
        src = source_of(g, j)
        token_rows, up_rows = xs[src], us[src]
        base = pl.multiple_of(g * 4 * SLOTS + j * SLOTS, 16)
        for e in range(2):
            gate_row = gin[src, e : e + 1, :]
            hit = (rank[src, e : e + 1, :] == slot_ids) & (gate_row > 0)
            pick = jnp.where(hit, 1.0, 0.0)
            pick_low = pick.astype(BF)
            picks[src, e * SLOTS : (e + 1) * SLOTS, :] = pick_low
            gate_col = jnp.sum(pick * gate_row, axis=1, keepdims=True)
            rows[e, pl.ds(base, SLOTS), :] = jnp.dot(
                pick_low, token_rows, preferred_element_type=F32
            ).astype(BF)
            picked = jnp.dot(pick_low, up_rows, preferred_element_type=F32)
            wqo[e, pl.ds(base, SLOTS), :] = picked.astype(BF)
            slot_grads[e, pl.ds(base, SLOTS), :] = (picked * gate_col).astype(BF)

    def run_expert(g, e):
        base = pl.multiple_of(g * 4 * SLOTS, 16)
        span = pl.ds(base, 4 * SLOTS)
        taken = rows[e, span, :]
        gate = jnp.dot(taken, wg[e], preferred_element_type=F32)
        upv = jnp.dot(taken, wu[e], preferred_element_type=F32)
        sig = 1.0 / (1.0 + jnp.exp(-gate))
        silu = gate * sig
        act = (silu * upv).astype(BF)
        acts[e, span, :] = act
        grad_act = lax.dot_general(
            slot_grads[e, span, :], wd[e], (((1,), (1,)), ((), ())), preferred_element_type=F32
        )
        ggp = (grad_act * upv * sig * (1.0 + gate * (1.0 - sig))).astype(BF)
        gup = (grad_act * silu).astype(BF)
        gparts[e, span, :] = ggp
        uparts[e, span, :] = gup
        pair = lax.dot_general(ggp, wg[e], (((1,), (1,)), ((), ())), preferred_element_type=F32)
        pair += lax.dot_general(gup, wu[e], (((1,), (1,)), ((), ())), preferred_element_type=F32)
        pairs[e] = pair.astype(BF)

    def spread(g, j):
        src = source_of(g, j)
        span = pl.ds(pl.multiple_of(j * SLOTS, 16), SLOTS)
        both = jnp.concatenate([pairs[0, span, :], pairs[1, span, :]], axis=0)
        p_buf[src] = lax.dot_general(
            picks[src], both, (((0,), (0,)), ((), ())), preferred_element_type=F32
        ).astype(BF)

    def run_output(g, e):
        span = pl.ds(pl.multiple_of(g * 4 * SLOTS, 16), 4 * SLOTS)
        out = jnp.dot(acts[e, span, :], wd[e], preferred_element_type=F32).astype(BF)
        outs[e] = out
        gg_col = jnp.sum(out.astype(F32) * wqo[e, span, :].astype(F32), axis=1, keepdims=True)
        for j in range(4):
            src = source_of(g, j)
            pick = picks[src, pl.ds(pl.multiple_of(e * SLOTS, 16), SLOTS), :].astype(F32)
            part = gg_col[j * SLOTS : (j + 1) * SLOTS]
            ggo[src, pl.ds(e, 1), :] = jnp.sum(pick * part, axis=0, keepdims=True)

    def spread_output(g, j):
        src = source_of(g, j)
        pick = picks[src]
        span = pl.ds(pl.multiple_of(j * SLOTS, 16), SLOTS)
        gates = jnp.concatenate(
            [
                pick[e * SLOTS : (e + 1) * SLOTS].astype(F32) * gin[src, e : e + 1, :]
                for e in range(2)
            ],
            axis=0,
        ).astype(BF)
        both = jnp.concatenate([outs[0, span, :], outs[1, span, :]], axis=0)
        o_buf[src] = lax.dot_general(
            gates, both, (((0,), (0,)), ((), ())), preferred_element_type=F32
        ).astype(BF)

    def output(g, carry):
        lax.fori_loop(0, 2, lambda e, c: (run_output(g, e), c)[1], 0)
        lax.fori_loop(0, 4, lambda j, c: (spread_output(g, j), c)[1], 0)
        return carry

    def pick(g):
        lax.fori_loop(0, 4, lambda j, c: (pick_source(g, j), c)[1], 0)

    OFF = (0, -1, 1, 2)
    R = 58

    def make(source, target, recv, to, index):
        return pltpu.make_async_remote_copy(
            src_ref=source,
            dst_ref=target,
            send_sem=send_sem.at[index],
            recv_sem=recv_sem.at[recv],
            device_id=to,
            device_id_type=MESH,
        )

    first = 80
    bounce = [
        (lambda j=j: make(slab(p_buf, p + OFF[j], q + 2), rb.at[j], R + j, up if j < 2 else down, first + j))
        for j in range(4)
    ]
    to_down = [
        (lambda j=j: make(slab(p_buf, p + OFF[j], q - 1), rc.at[4 + j], R + 8 + j, down, first + 4 + j))
        for j in range(4)
    ]
    to_up = [
        (lambda j=j: make(slab(p_buf, p + OFF[j], q + 1), rc.at[j], R + 4 + j, up, first + 8 + j))
        for j in range(4)
    ]

    def add_bounce(j):
        net.arrived(rb.at[j], R + j)
        target = slab(p_buf, p + OFF[j], q + 1 if j < 2 else q - 1)
        target[...] = (target[...].astype(F32) + rb[j].astype(F32)).astype(BF)

    def step(g, carry):
        @pl.when(g == 2)
        def _():
            for j in range(4):
                tokens_in.arrived(slab(xs, p + OFF[j], q + 2), 12 + j)

        @pl.when(g == 3)
        def _():
            tokens_in.arrived(slab(xs, p + 1, q - 1), 6)
            tokens_in.arrived(slab(xs, p + 2, q - 1), 7)
            tokens_in.arrived(slab(xs, p, q + 1), 8)
            tokens_in.arrived(slab(xs, p - 1, q + 1), 9)
            for j in range(2):
                to_down[j]().start()
                to_up[3 - j]().start()

        @pl.when(g >= 2)
        def _():
            pick(g)

        lax.fori_loop(0, 2, lambda e, c: (run_expert(g, e), c)[1], 0)
        lax.fori_loop(0, 4, lambda j, c: (spread(g, j), c)[1], 0)

        @pl.when(g == 2)
        def _():
            for j in range(4):
                bounce[j]().start()

        @pl.when(g == 3)
        def _():
            for j in (3, 1, 2, 0):
                add_bounce(j)
                (to_up if j < 2 else to_down)[j]().start()

        return carry

    keep_own.wait()
    pick(0)
    tokens_in.fourth(0)
    tokens_in.fourth(1)
    pick(1)
    net.arrived(weight(0, core, y + 2), 26)
    net.arrived(weight(1, core, y + 2, top), 27)
    net.arrived(weight(1, core, y + 2, bottom), 28)
    net.arrived(weight(2, core, y + 2), 29)
    for a in range(3):
        net.start(weight(a, core, y + 2), weight(a, core, y + 2), 39 + a, sibling)
    for i, ahead_by in enumerate((0, -1, 1, 2)):
        for a in range(3):
            net.arrived(weight(a, 1 - core, y + ahead_by), 30 + 3 * i + a)
    for copy in keep:
        copy.wait()
    lax.fori_loop(0, 4, step, 0)
    lax.fori_loop(0, 2, output, 0)

    def weight_tile(e, t):
        cols = pl.ds(pl.multiple_of(t * 256, 256), 256)
        dims = (((0,), (0,)), ((), ()))
        lhs = rows[e, :, cols]
        dwg[e, cols, :] = lax.dot_general(lhs, gparts[e], dims, preferred_element_type=F32).astype(BF)
        dwu[e, cols, :] = lax.dot_general(lhs, uparts[e], dims, preferred_element_type=F32).astype(BF)
        us[4 * e : 4 * e + 4, :, cols] = (
            lax.dot_general(acts[e], slot_grads[e, :, cols], dims, preferred_element_type=F32)
            .astype(BF)
            .reshape(4, TOK, 256)
        )

    def weight_grads(e):
        lax.fori_loop(0, 4, lambda t, c: (weight_tile(e, t), c)[1], 0)

    net.drain()
    weight_grads(0)

    def gather_sum(j):
        net.arrived(rc.at[j], R + 4 + j)
        net.arrived(rc.at[4 + j], R + 8 + j)
        target = slab(p_buf, p + OFF[j], q)
        target[...] = (
            target[...].astype(F32) + rc[j].astype(F32) + rc[4 + j].astype(F32)
        ).astype(BF)

    last = first + 12
    lo, hi = pl.ds(0, 64), pl.ds(64, 64)
    far_slab, next_slab, prev_slab = slab(p_buf, p + 2, q), slab(p_buf, p + 1, q), slab(p_buf, p - 1, q)
    tail = [
        make(far_slab.at[lo], rd.at[lo], R + 12, right, last),
        make(far_slab.at[hi], rd.at[hi], R + 13, left, last + 1),
        make(next_slab.at[hi], re.at[0, hi], R + 14, right, last + 2),
        make(prev_slab.at[lo], re.at[1, lo], R + 15, left, last + 3),
        make(next_slab.at[lo], re.at[0, lo], R + 16, right, last + 4),
        make(prev_slab.at[hi], re.at[1, hi], R + 17, left, last + 5),
    ]
    gather_sum(3)
    tail[0].start()
    tail[1].start()
    gather_sum(2)
    tail[2].start()
    gather_sum(1)
    tail[3].start()
    lax.fori_loop(2, 4, output, 0)

    def gg_copy(i):
        a, b = lax.div(i, 4), lax.rem(i, 4)
        return pltpu.make_async_remote_copy(
            src_ref=ggo.at[wrap(p + a) * 4 + wrap(q + b)],
            dst_ref=gg_out.at[my_chip],
            send_sem=gg_send.at[i],
            recv_sem=gg_recv.at[wrap(-a) * 4 + wrap(-b)],
            device_id=device(p + a, q + b, y, core),
            device_id_type=MESH,
        )

    def start_gg(i, _):
        gg_copy(i).start()
        return 0

    lax.fori_loop(1, 16, start_gg, 0)
    gg_out[my_chip] = ggo[p * 4 + q]
    o_store = pltpu.make_async_copy(o_buf, o_hbm, local_sem.at[9])
    o_store.start()
    net.arrived(rd.at[lo], R + 12)
    next_slab[lo] = (next_slab[lo].astype(F32) + rd[lo].astype(F32)).astype(BF)
    tail[4].start()
    net.arrived(rd.at[hi], R + 13)
    prev_slab[hi] = (prev_slab[hi].astype(F32) + rd[hi].astype(F32)).astype(BF)
    tail[5].start()
    gather_sum(0)
    weight_grads(1)
    stores = [
        pltpu.make_async_copy(src, dst, local_sem.at[10 + i])
        for i, (src, dst) in enumerate(((dwg, dwg_hbm), (dwu, dwu_hbm), (us.at[0:8], dwd_hbm)))
    ]
    for store in stores:
        store.start()
    net.arrived(re.at[0, hi], R + 14)
    net.arrived(re.at[1, lo], R + 15)
    net.arrived(re.at[0, lo], R + 16)
    net.arrived(re.at[1, hi], R + 17)
    grad_out[...] = slab(p_buf, p, q)[...].astype(F32) + re[0].astype(F32) + re[1].astype(F32)

    def take_gg(i, _):
        pltpu.make_async_copy(ggo.at[0], ggo.at[0], gg_recv.at[i]).wait()
        return 0

    lax.fori_loop(1, 16, take_gg, 0)
    for copy in bounce + to_down + to_up:
        copy().wait_send()
    for copy in tail:
        copy.wait_send()

    def drain_small(i, _):
        gate_copy(i).wait_send()
        gg_copy(i).wait_send()
        return 0

    lax.fori_loop(1, 16, drain_small, 0)
    o_store.wait()
    for store in stores:
        store.wait()
    keep_probs.wait()


def main(tokens, wq, wk, wv, wo, ga, gm, router, cotangent, routes, lengths, wg, wu, wd):
    cosine, sine = turn_tables()
    any_space = pl.BlockSpec(memory_space=pl.ANY)
    vmem = pl.BlockSpec(memory_space=pltpu.VMEM)
    smem = pl.BlockSpec(memory_space=pltpu.SMEM)
    shape = jax.ShapeDtypeStruct
    dma = pltpu.SemaphoreType.DMA
    slots = 16 * SLOTS
    low = lambda *size: pltpu.VMEM(size, BF)
    return pl.pallas_call(
        main_kernel,
        out_shape=(
            shape((TOK, D), F32),
            shape((TOK, D), BF),
            shape((TOK, TOK), F32),
            shape((TOK, D), BF),
            shape((TOK, D), BF),
            shape((4, TOK, D), BF),
            shape((TOK, D), F32),
            shape((16, 8, TOK), F32),
            shape((8, 2 * TOK, 512), BF),
            shape((16, TOK, D), BF),
            shape((2, D, FF), BF),
            shape((2, D, FF), BF),
            shape((8, TOK, D), BF),
        ),
        in_specs=[vmem] + [any_space] * 4 + [vmem] * 5 + [smem] + [vmem] * 2 + [any_space] * 3,
        out_specs=(vmem,) * 8 + (any_space,) * 5,
        scratch_shapes=[
            low(2, D, D),
            low(D, 512),
            low(D, 512),
            low(TOK, D),
            low(4, TOK, D),
            low(8, 2 * TOK, 512),
            pltpu.VMEM((TOK, 512), F32),
            pltpu.VMEM((16, 8, TOK), F32),
            low(16, TOK, D),
            low(16, TOK, D),
            low(2, D, FF),
            low(2, D, FF),
            low(2, FF, D),
            pltpu.VMEM((16, 8, TOK), F32),
            pltpu.VMEM((16, 8, TOK), F32),
            pltpu.VMEM((16, 8, TOK), F32),
            low(16, 2 * SLOTS, TOK),
            low(2, slots, D),
            low(2, slots, D),
            low(2, slots, FF),
            low(2, slots, FF),
            low(2, slots, FF),
            low(2, 4 * SLOTS, D),
            low(2, 4 * SLOTS, D),
            low(16, TOK, D),
            low(16, TOK, D),
            low(4, TOK, D),
            low(8, TOK, D),
            low(TOK, D),
            low(2, TOK, D),
            low(2, D, FF),
            low(2, D, FF),
            dma((100,)),
            dma((76,)),
            dma((16,)),
            dma((16,)),
            dma((16,)),
            dma((16,)),
            dma((13,)),
        ],
        compiler_params=pltpu.CompilerParams(
            collective_id=1, has_side_effects=True, vmem_limit_bytes=VMEM_BYTES
        ),
        name="main",
    )(
        tokens, wq, wk, wv, wo, ga.reshape(1, D), gm.reshape(1, D), router, cotangent, routes,
        lengths, jnp.asarray(cosine), jnp.asarray(sine), wg, wu, wd,
    )


def accumulate(target, *terms):
    total = target[...].astype(F32)
    for term in terms:
        total += term[...].astype(F32)
    target[...] = total.astype(target.dtype)


class PlaneReduce:
    OFF = (0, -1, 1, 2)

    def __init__(self, net, spot, slabs, rb, rc, rd, re, base):
        self.net, self.spot, self.slabs, self.base = net, spot, slabs, base
        self.rb, self.rc, self.rd, self.re = rb, rc, rd, re
        p, q, y, core = spot
        self.right, self.left = device(p + 1, q, y, core), device(p - 1, q, y, core)
        self.up, self.down = device(p, q + 1, y, core), device(p, q - 1, y, core)

    def slab(self, a, b):
        return slab(self.slabs, self.spot[0] + a, self.spot[1] + b)

    def send(self, source, target, recv, to):
        self.net.start(source, target, self.base + recv, to)

    def arrived(self, ref, recv):
        self.net.arrived(ref, self.base + recv)

    def bounce(self):
        for j in range(4):
            to = self.up if j < 2 else self.down
            self.send(self.slab(self.OFF[j], 2), self.rb.at[j], j, to)

    def to_up(self, j):
        self.send(self.slab(self.OFF[j], 1), self.rc.at[j], 4 + j, self.up)

    def to_down(self, j):
        self.send(self.slab(self.OFF[j], -1), self.rc.at[4 + j], 8 + j, self.down)

    def begin(self):
        self.bounce()
        for j in (3, 2):
            self.to_up(j)
        for j in (0, 1):
            self.to_down(j)

    def middle(self):
        for j in (3, 1, 2, 0):
            self.arrived(self.rb.at[j], j)
            accumulate(self.slab(self.OFF[j], 1 if j < 2 else -1), self.rb.at[j])
            (self.to_up if j < 2 else self.to_down)(j)

    def column(self, j):
        self.arrived(self.rc.at[j], 4 + j)
        self.arrived(self.rc.at[4 + j], 8 + j)
        accumulate(self.slab(self.OFF[j], 0), self.rc.at[j], self.rc.at[4 + j])

    def third(self):
        lo, hi = pl.ds(0, 64), pl.ds(64, 64)
        rd, re = self.rd, self.re
        self.column(3)
        self.send(self.slab(2, 0).at[lo], rd.at[lo], 12, self.right)
        self.send(self.slab(2, 0).at[hi], rd.at[hi], 13, self.left)
        self.column(2)
        self.send(self.slab(1, 0).at[hi], re.at[0, hi], 14, self.right)
        self.column(1)
        self.send(self.slab(-1, 0).at[lo], re.at[1, lo], 15, self.left)

    def fourth(self):
        lo, hi = pl.ds(0, 64), pl.ds(64, 64)
        rd, re = self.rd, self.re
        self.arrived(rd.at[lo], 12)
        accumulate(self.slab(1, 0).at[lo], rd.at[lo])
        self.send(self.slab(1, 0).at[lo], re.at[0, lo], 16, self.right)
        self.arrived(rd.at[hi], 13)
        accumulate(self.slab(-1, 0).at[hi], rd.at[hi])
        self.send(self.slab(-1, 0).at[hi], re.at[1, hi], 17, self.left)
        self.column(0)

    def finish(self):
        lo, hi = pl.ds(0, 64), pl.ds(64, 64)
        re = self.re
        self.arrived(re.at[0, hi], 14)
        self.arrived(re.at[1, lo], 15)
        self.arrived(re.at[0, lo], 16)
        self.arrived(re.at[1, hi], 17)
        return self.slab(0, 0)[...].astype(F32) + re[0].astype(F32) + re[1].astype(F32)


class RingReduce:
    def __init__(self, net, base, ahead, behind, portion, hops, lows, highs):
        self.net, self.base, self.ahead, self.behind = net, base, ahead, behind
        self.portion, self.hops, self.lows, self.highs = portion, hops, lows, highs
        self.n = len(hops[0])

    def send(self, sources, targets, group, to):
        for i, (source, target) in enumerate(zip(sources, targets)):
            self.net.start(source, target, self.base + group * self.n + i, to)

    def arrived(self, refs, group):
        for i, ref in enumerate(refs):
            self.net.arrived(ref, self.base + group * self.n + i)

    def begin(self):
        self.send(self.portion(2, 0), self.hops[0], 0, self.ahead)
        self.send(self.portion(2, 1), self.hops[1], 1, self.behind)

    def direct(self):
        self.send(self.portion(1, 1), self.lows[1], 2, self.ahead)
        self.send(self.portion(-1, 0), self.highs[0], 3, self.behind)

    def middle(self):
        for which, step, targets, to in (
            (0, 1, self.lows[0], self.ahead),
            (1, -1, self.highs[1], self.behind),
        ):
            self.arrived(self.hops[which], which)
            refs = self.portion(step, which)
            for ref, hop in zip(refs, self.hops[which]):
                accumulate(ref, hop)
            self.send(refs, targets, 4 + which, to)

    def finish(self):
        self.arrived(self.lows[1], 2)
        self.arrived(self.highs[0], 3)
        self.arrived(self.lows[0], 4)
        self.arrived(self.highs[1], 5)


class Total:
    def __init__(self, net, axis, source, result, span, rows, first, piece, buffers, sems):
        self.net, self.axis, self.source, self.result = net, axis, source, result
        self.span, self.rows, self.first, self.piece_size = span, rows, first, piece
        self.theirs, self.low, self.high, self.hop, self.pieces, self.done = buffers
        self.recv, self.plane_send, self.plane_recv, self.back_send, self.back_recv = sems
        dp, y = lax.axis_index("dp"), lax.axis_index("hid")
        self.core = lax.rem(dp, 2)
        self.here = (lax.div(dp, 8), y, lax.rem(lax.div(dp, 2), 4))
        self.sibling = self.at(self.here, 1 - self.core)
        self.plus, self.minus = self.along(1), self.along(-1)
        self.plane = [i for i in range(3) if i != axis]
        self.slab_rows = rows // 4
        half = self.slab_rows // 2
        self.lo, self.hi = pl.ds(0, half), pl.ds(half, half)

    def at(self, spot, on=None):
        spot = [wrap(v) for v in spot]
        return (spot[0] * 8 + spot[2] * 2 + (self.core if on is None else on), spot[1])

    def along(self, step):
        return self.at([self.here[i] + (step if i == self.axis else 0) for i in range(3)])

    def arrived(self, ref, i):
        pltpu.make_async_copy(ref, ref, self.recv.at[i]).wait()

    def put(self, source, target, i, to):
        self.net.put(source, target, self.recv.at[i], to)

    def block(self, ref, step, part=None):
        size = self.slab_rows
        start = self.core * self.span + self.first + wrap(self.here[self.axis] + step) * size
        if part is not None:
            size = size // 2
            start += part * size
        return ref.at[pl.ds(pl.multiple_of(start, size), size)]

    def own(self, step):
        return self.block(self.source, step)

    def begin(self):
        start = (1 - self.core) * self.span + self.first
        theirs = self.source.at[pl.ds(pl.multiple_of(start, self.rows), self.rows)]
        self.put(theirs, self.theirs, 0, self.sibling)

    def merge(self, step):
        size = self.slab_rows
        start = wrap(self.here[self.axis] + step) * size
        accumulate(self.own(step), self.theirs.at[pl.ds(pl.multiple_of(start, size), size)])

    def second(self):
        lo, hi = self.lo, self.hi
        self.arrived(self.theirs, 0)
        self.merge(2)
        far = self.own(2)
        self.put(far.at[lo], self.hop.at[lo], 1, self.plus)
        self.put(far.at[hi], self.hop.at[hi], 2, self.minus)
        self.merge(1)
        self.put(self.own(1).at[hi], self.low.at[hi], 3, self.plus)
        self.merge(-1)
        self.put(self.own(-1).at[lo], self.high.at[lo], 4, self.minus)
        self.merge(0)

    def third(self):
        lo, hi = self.lo, self.hi
        self.arrived(self.hop.at[lo], 1)
        near = self.own(1).at[lo]
        accumulate(near, self.hop.at[lo])
        self.put(near, self.low.at[lo], 5, self.plus)
        self.arrived(self.hop.at[hi], 2)
        near = self.own(-1).at[hi]
        accumulate(near, self.hop.at[hi])
        self.put(near, self.high.at[hi], 6, self.minus)

    def piece(self, ref, u, v):
        rows, cols = self.piece_size
        if self.slab_rows == 4 * rows:
            row, col = u * rows, v * cols
        else:
            row, col = lax.div(u, 2) * rows, (lax.rem(u, 2) * 4 + v) * cols
        return ref.at[
            pl.ds(pl.multiple_of(row, rows), rows), pl.ds(pl.multiple_of(col, cols), cols)
        ]

    def member(self, i):
        u, v = self.plane
        spot = list(self.here)
        spot[u] = wrap(spot[u] + lax.div(i, 4))
        spot[v] = wrap(spot[v] + lax.rem(i, 4))
        return spot[u], spot[v], self.at(spot)

    def mirror(self, i):
        return wrap(-lax.div(i, 4)) * 4 + wrap(-lax.rem(i, 4))

    def mine(self):
        return self.here[self.plane[0]], self.here[self.plane[1]]

    def remote(self, source, target, send, recv, to):
        return pltpu.make_async_remote_copy(
            src_ref=source, dst_ref=target, send_sem=send, recv_sem=recv,
            device_id=to, device_id_type=MESH,
        )

    def piece_copy(self, i):
        u, v, to = self.member(i)
        there = self.mirror(i)
        return self.remote(
            self.piece(self.own(0), u, v),
            self.pieces.at[there],
            self.plane_send.at[i],
            self.plane_recv.at[there],
            to,
        )

    def back_copy(self, i):
        spot = self.piece(self.done, *self.mine())
        return self.remote(
            spot, spot, self.back_send.at[i], self.back_recv.at[self.mirror(i)], self.member(i)[2]
        )

    def each(self, act):
        lax.fori_loop(1, 16, lambda i, carry: (act(i), carry)[1], 0)

    def take(self, sems):
        spot = self.pieces
        self.each(lambda i: pltpu.make_async_copy(spot.at[0], spot.at[0], sems.at[i]).wait())

    def fourth(self):
        lo, hi = self.lo, self.hi
        self.arrived(self.low.at[hi], 3)
        self.arrived(self.high.at[lo], 4)
        self.arrived(self.low.at[lo], 5)
        self.arrived(self.high.at[hi], 6)
        accumulate(self.own(0), self.low, self.high)
        self.each(lambda i: self.piece_copy(i).start())
        self.pieces[0] = self.piece(self.own(0), *self.mine())[...]

    def fifth(self):
        self.take(self.plane_recv)
        total = jnp.sum(self.pieces[...].astype(F32), axis=0)
        self.piece(self.done, *self.mine())[...] = total.astype(self.done.dtype)
        self.each(lambda i: self.back_copy(i).start())

    def sixth(self, sem):
        self.take(self.back_recv)
        spot = self.block(self.result, 0)
        self.put(self.done, spot, 7, self.plus)
        self.put(self.done, spot, 8, self.minus)
        self.put(self.done, spot, 11, self.sibling)
        self.store = pltpu.make_async_copy(self.done, spot, sem)
        self.store.start()

    def seventh(self):
        whole, spot = self.block(self.result, -1), self.block(self.result, -1, 0)
        self.arrived(whole, 7)
        self.put(spot, spot, 9, self.plus)
        self.put(whole, whole, 12, self.sibling)
        whole, spot = self.block(self.result, 1), self.block(self.result, 1, 1)
        self.arrived(whole, 8)
        self.put(spot, spot, 10, self.minus)
        self.put(whole, whole, 13, self.sibling)

    def eighth(self):
        whole = self.block(self.result, 2)
        self.arrived(self.block(self.result, 2, 0), 9)
        self.arrived(self.block(self.result, 2, 1), 10)
        self.put(whole, whole, 14, self.sibling)

    def finish(self):
        for i in range(11, 15):
            self.arrived(self.block(self.result, 0), i)
        self.each(lambda i: self.piece_copy(i).wait_send())
        self.each(lambda i: self.back_copy(i).wait_send())
        self.store.wait()


def back_kernel(
    rows_ref, gg_ref, x_ref, gates_ref, hidden_ref, gm_ref, ga_ref, router_ref, cot_ref, tok_ref,
    mixed_ref, query_ref, kv_ref, cos_ref, sin_ref, routes_ref, len_ref,
    probs_hbm, wo_hbm, wq_hbm, wk_hbm, wv_hbm, o_hbm, pg_hbm, pu_hbm, pd_hbm,
    layer_ref, input_ref, gate_out, up_out, down_out, q_hbm, o_sum_hbm, kv_hbm, narrow_hbm,
    probs, wo, wq, wk, wv, o_buf, rb, rc, rd, re,
    pg, pu, pd, sg, su, sd, hop_g, hop_ua, hop_ub, hop_d, low_g, low_u, low_d, high_g, high_u, high_d,
    grad_mixed, grad_query, grad_kv, kv_hops, kv_low, kv_high,
    dq_out, do_out, dkv_out, narrow_ref,
    their_a, their_b, their_c, their_n, low_a, low_b, low_c, low_n, high_a, high_b, high_c, high_n,
    hop_a, hop_b, hop_c, hop_n, piece_a, piece_b, piece_c, piece_n, done_a, done_b, done_c, done_n,
    send_sem, recv_sem, local_sem, t_recv, plane_send, plane_recv, back_send, back_recv,
):
    p, q, y, core = place()
    spot = (p, q, y, core)
    sibling = (chip_of(p, q, core) * 2 + 1 - core, y)
    ahead, behind = device(p, q, y + 1, core), device(p, q, y - 1, core)
    net = Sends(send_sem, recv_sem)
    pairs = (
        (o_hbm, o_buf), (wo_hbm, wo), (probs_hbm, probs), (wq_hbm, wq), (wk_hbm, wk), (wv_hbm, wv),
        (pg_hbm.at[core], pg), (pu_hbm.at[core], pu), (pd_hbm.at[core], pd),
    )
    loads = [pltpu.make_async_copy(s, d, local_sem.at[i]) for i, (s, d) in enumerate(pairs)]
    for load in loads:
        load.start()
    plane = PlaneReduce(net, spot, o_buf, rb, rc, rd, re, 0)

    def unit(k, axis, source, result, span, rows, first, piece, *buffers):
        sems = [ref.at[k] for ref in (t_recv, plane_send, plane_recv, back_send, back_recv)]
        return Total(net, axis, source, result, span, rows, first, piece, buffers, sems)

    sum_o = unit(
        0, 2, do_out, o_sum_hbm, 512, 512, 0, (32, 256), their_a, low_a, high_a, hop_a, piece_a, done_a
    )
    sum_q = unit(
        1, 0, dq_out, q_hbm, 512, 512, 0, (32, 256), their_b, low_b, high_b, hop_b, piece_b, done_b
    )
    sum_kv = [
        unit(
            2 + h, 2 * h, dkv_out, kv_hbm, 512, 256, 256 * h, (16, 256),
            *[ref.at[h] for ref in (their_c, low_c, high_c, hop_c, piece_c, done_c)],
        )
        for h in range(2)
    ]
    sum_n = unit(
        4, 1, narrow_ref, narrow_hbm, 64, 64, 0, (8, 128),
        their_n, low_n, high_n, hop_n, piece_n, done_n,
    )
    late = [*sum_kv, sum_n]
    everyone = [sum_o, sum_q, *late]
    here = sum_o.here
    partners = [
        sum_o.at([here[0] + i, here[1] + j, here[2] + k])
        for i in range(4)
        for j in range(4)
        for k in range(4)
        if (i or j or k) and not (i and j and k)
    ]
    greet(partners + [sibling])
    loads[0].wait()
    plane.begin()
    for i, (source, target) in enumerate(((pg_hbm, sg), (pu_hbm, su), (pd_hbm, sd))):
        net.start(source.at[1 - core], target, 18 + i, sibling)

    first = pl.multiple_of(y * TOK, TOK)
    row = lax.broadcasted_iota(jnp.int32, (TOK, 1), 0) + y * TOK
    upstream = jnp.where(row < len_ref[0], cot_ref[...].astype(F32), 0.0)
    gates = gates_ref[...]
    grad_gates = gg_ref[...].reshape(TOK, TOK).T
    grad_logits = gates * (grad_gates - jnp.sum(gates * grad_gates, axis=1, keepdims=True))
    grad_logits = grad_logits.astype(BF)
    wide = lax.dot_general(
        widen(), router_ref[...], (((0,), (0,)), ((), ())), preferred_element_type=F32
    ).astype(BF)
    by_row = (((0,), (0,)), ((), ()))
    by_col = (((1,), (1,)), ((), ()))
    grad_normed = rows_ref[...] + jnp.dot(grad_logits, wide, preferred_element_type=F32)
    hidden = hidden_ref[...]
    scale = root(hidden)
    grad_gain_moe = jnp.sum(grad_normed * hidden * scale, axis=0, keepdims=True)
    scaled = grad_normed * gm_ref[...]
    pull = jnp.mean(scaled * hidden, axis=1, keepdims=True)
    grad_hidden = upstream + scale * scaled - hidden * (scale * scale * scale) * pull
    input_ref[...] = grad_hidden
    low = grad_hidden.astype(BF)
    loads[1].wait()
    grad_mixed[...] = lax.dot_general(low, wo[...], by_col, preferred_element_type=F32).astype(BF)
    narrow_ref[...] = lax.dot_general(grad_logits, x_ref[...], by_row, preferred_element_type=F32)
    named = routed_mask(routes_ref[...], lax.broadcasted_iota(jnp.int32, (TOK, 1), 0))
    counts = jnp.sum(named.T, axis=0, keepdims=True)
    narrow_ref[3:4, :] = grad_gain_moe
    narrow_ref[4:5, :] = jnp.zeros((1, D), F32)
    narrow_ref[4:5, 0:TOK] = counts
    do_out[...] = lax.dot_general(
        mixed_ref[...], low, by_row, preferred_element_type=F32
    ).astype(BF)
    sum_o.begin()
    plane.middle()

    def block(ref, step, rows=None):
        span = pl.ds(pl.multiple_of(wrap(y + step) * TOK, TOK), TOK)
        return ref.at[:, span] if rows is None else ref.at[rows, span]

    def down_block(ref, step):
        return ref.at[pl.ds(pl.multiple_of(wrap(y + step) * TOK, TOK), TOK)]

    top, bottom = pl.ds(0, 512), pl.ds(512, 512)

    def weight_portion(step, which):
        if which == 0:
            return [block(pg, step), block(pu, step, top)]
        return [block(pu, step, bottom), down_block(pd, step)]

    def weight_merge(step):
        accumulate(block(pg, step), block(sg, step))
        accumulate(block(pu, step), block(su, step))
        accumulate(down_block(pd, step), down_block(sd, step))

    weights = RingReduce(
        net, 24, ahead, behind, weight_portion,
        ([hop_g, hop_ua], [hop_ub, hop_d]),
        ([low_g, low_u.at[top]], [low_u.at[bottom], low_d]),
        ([high_g, high_u.at[top]], [high_u.at[bottom], high_d]),
    )
    for load in loads[6:]:
        load.wait()
    for i, ref in enumerate((sg, su, sd)):
        net.arrived(ref, 18 + i)
    weight_merge(2)
    weights.begin()
    sum_o.second()

    cosine, sine = cos_ref[pl.ds(first, TOK), :], sin_ref[pl.ds(first, TOK), :]
    loads[2].wait()

    def attend(c, carry):
        span = pl.ds(pl.multiple_of(c * 128, 128), 128)
        value_span = pl.ds(pl.multiple_of(512 + c * 128, 128), 128)
        keys = kv_ref[:, :, span].reshape(512, 128)
        values = kv_ref[:, :, value_span].reshape(512, 128)
        grad_keys = jnp.zeros((512, 128), F32)
        grad_values = jnp.zeros((512, 128), F32)
        for half in range(2):
            m = c * 2 + half
            mine = pl.ds(pl.multiple_of(m * 128, 128), 128)
            pair = stack_heads(query_ref[:, mine].astype(F32), half)
            grad_pair = stack_heads(grad_mixed[:, mine].astype(F32), half)
            grad_probs = lax.dot_general(grad_pair, values, by_col, preferred_element_type=F32)
            prob = probs[m]
            wide_prob = prob.astype(F32)
            middle = jnp.sum(wide_prob * grad_probs, axis=1, keepdims=True)
            grad_scores = (wide_prob * (grad_probs - middle)).astype(BF)
            back = jnp.dot(grad_scores, keys, preferred_element_type=F32) * SCALE
            grad_query[:, mine] = turn(unstack_heads(back, half), cosine, -sine).astype(BF)
            grad_keys += lax.dot_general(grad_scores, pair, by_row, preferred_element_type=F32)
            grad_values += lax.dot_general(prob, grad_pair, by_row, preferred_element_type=F32)
        grad_kv[:, :, span] = (grad_keys * SCALE).astype(BF).reshape(4, TOK, 128)
        grad_kv[:, :, value_span] = grad_values.astype(BF).reshape(4, TOK, 128)
        return carry

    lax.fori_loop(0, 4, attend, 0)
    lo, hi = pl.ds(0, 64), pl.ds(64, 64)
    sums = RingReduce(
        net, 36, ahead, behind,
        lambda step, which: [grad_kv.at[wrap(y + step), hi if which else lo]],
        ([kv_hops.at[0]], [kv_hops.at[1]]),
        ([kv_low.at[lo]], [kv_low.at[hi]]),
        ([kv_high.at[lo]], [kv_high.at[hi]]),
    )
    sums.begin()
    sums.direct()
    plane.third()
    sum_o.third()
    tokens = tok_ref[...].astype(F32)
    scale = root(tokens)
    normed = (tokens * scale * ga_ref[...]).astype(BF)
    dq_out[...] = lax.dot_general(
        normed, grad_query[...], by_row, preferred_element_type=F32
    ).astype(BF)
    sum_q.begin()
    sums.middle()
    plane.fourth()
    sum_q.second()
    for load in loads[3:6]:
        load.wait()
    grad_normed = lax.dot_general(grad_query[...], wq[...], by_col, preferred_element_type=F32)
    weight_merge(1)
    weight_merge(-1)
    weight_merge(0)
    sum_o.fourth()
    sums.finish()
    weights.direct()
    both = grad_kv[y].astype(F32) + kv_low[...].astype(F32) + kv_high[...].astype(F32)
    grad_key = jnp.concatenate(
        [turn(both[:, c * 128 : (c + 1) * 128], cosine, -sine) for c in range(4)], axis=1
    ).astype(BF)
    grad_value = both[:, 512:].astype(BF)
    dkv_out[:, 0:512] = lax.dot_general(
        normed, grad_key, by_row, preferred_element_type=F32
    ).astype(BF)
    dkv_out[:, 512:1024] = lax.dot_general(
        normed, grad_value, by_row, preferred_element_type=F32
    ).astype(BF)
    sum_kv[0].begin()
    sum_kv[1].begin()
    grad_normed += lax.dot_general(grad_key, wk[...], by_col, preferred_element_type=F32)
    grad_normed += lax.dot_general(grad_value, wv[...], by_col, preferred_element_type=F32)
    narrow_ref[2:3, :] = jnp.sum(grad_normed * tokens * scale, axis=0, keepdims=True)
    sum_n.begin()
    sum_q.third()
    for one in late:
        one.second()
    weights.middle()
    sum_o.fifth()
    scaled = grad_normed * ga_ref[...]
    pull = jnp.mean(scaled * tokens, axis=1, keepdims=True)
    input_ref[...] += scale * scaled - tokens * (scale * scale * scale) * pull
    for one in late:
        one.third()
    sum_q.fourth()
    sum_o.sixth(local_sem.at[0])
    layer_ref[...] = (hidden_ref[...] + plane.finish()).astype(BF)
    for one in late:
        one.fourth()
    sum_q.fifth()
    sum_o.seventh()
    for one in late:
        one.fifth()
    sum_q.sixth(local_sem.at[1])
    sum_o.eighth()
    for i, one in enumerate(late):
        one.sixth(local_sem.at[2 + i])
    sum_q.seventh()
    weights.finish()
    gate_out[...] = (
        block(pg, 0)[...].astype(F32) + low_g[...].astype(F32) + high_g[...].astype(F32)
    )
    up_out[...] = block(pu, 0)[...].astype(F32) + low_u[...].astype(F32) + high_u[...].astype(F32)
    down_out[...] = (
        down_block(pd, 0)[...].astype(F32) + low_d[...].astype(F32) + high_d[...].astype(F32)
    )
    for one in late:
        one.seventh()
    sum_q.eighth()
    for one in late:
        one.eighth()
    for one in everyone:
        one.finish()
    net.drain()


def back(operands, arrays):
    any_space = pl.BlockSpec(memory_space=pl.ANY)
    vmem = pl.BlockSpec(memory_space=pltpu.VMEM)
    smem = pl.BlockSpec(memory_space=pltpu.SMEM)
    shape = jax.ShapeDtypeStruct
    dma = pltpu.SemaphoreType.DMA
    low = lambda *size: pltpu.VMEM(size, BF)
    return pl.pallas_call(
        back_kernel,
        out_shape=(
            shape((TOK, D), BF),
            shape((TOK, D), F32),
            shape((D, TOK), F32),
            shape((D, TOK), F32),
            shape((TOK, D), F32),
            shape((D, D), BF),
            shape((D, D), BF),
            shape((D, D), BF),
            shape((TOK, D), F32),
        ),
        in_specs=[vmem] * 16 + [smem] + [any_space] * 9,
        out_specs=(vmem,) * 5 + (any_space,) * 4,
        scratch_shapes=[
            low(8, 2 * TOK, 512),
            low(D, D),
            low(D, D),
            low(D, 512),
            low(D, 512),
            low(16, TOK, D),
            low(4, TOK, D),
            low(8, TOK, D),
            low(TOK, D),
            low(2, TOK, D),
            low(D, FF),
            low(D, FF),
            low(FF, D),
            low(D, FF),
            low(D, FF),
            low(FF, D),
            low(D, TOK),
            low(512, TOK),
            low(512, TOK),
            low(TOK, D),
            low(D, TOK),
            low(D, TOK),
            low(TOK, D),
            low(D, TOK),
            low(D, TOK),
            low(TOK, D),
            low(TOK, D),
            low(TOK, D),
            low(4, TOK, D),
            low(2, 64, D),
            low(TOK, D),
            low(TOK, D),
            low(D, D),
            low(D, D),
            low(D, D),
            pltpu.VMEM((TOK, D), F32),
            low(512, D),
            low(512, D),
            low(2, 256, D),
            pltpu.VMEM((64, D), F32),
            low(128, D),
            low(128, D),
            low(2, 64, D),
            pltpu.VMEM((16, D), F32),
            low(128, D),
            low(128, D),
            low(2, 64, D),
            pltpu.VMEM((16, D), F32),
            low(128, D),
            low(128, D),
            low(2, 64, D),
            pltpu.VMEM((16, D), F32),
            low(16, 32, 256),
            low(16, 32, 256),
            low(2, 16, 16, 256),
            pltpu.VMEM((16, 8, 128), F32),
            low(128, D),
            low(128, D),
            low(2, 64, D),
            pltpu.VMEM((16, D), F32),
            dma((120,)),
            dma((42,)),
            dma((9,)),
            dma((5, 15)),
            dma((5, 16)),
            dma((5, 16)),
            dma((5, 16)),
            dma((5, 16)),
        ],
        compiler_params=pltpu.CompilerParams(
            collective_id=4, has_side_effects=True, vmem_limit_bytes=VMEM_BYTES
        ),
        name="back",
    )(*operands, *arrays)


def results_kernel(
    q_ref, o_ref, kv_ref, n_ref, layer_ref, input_ref, gate_ref, up_ref, down_ref,
    q_out, o_out, k_out, v_out, router_out, one_out, two_out, count_out,
    layer_out, input_out, gate_out, up_out, down_out,
):
    layer_out[...] = layer_ref[...]
    input_out[...] = input_ref[...]
    gate_out[0] = gate_ref[...]
    up_out[0] = up_ref[...]
    down_out[0] = down_ref[...]
    q_out[...] = q_ref[...].astype(F32)
    o_out[...] = o_ref[...].astype(F32)
    k_out[...] = kv_ref[:, 0:512].astype(F32)
    v_out[...] = kv_ref[:, 512:1024].astype(F32)

    @pl.when(pl.program_id(0) == 0)
    def _():
        for j in range(16):
            router_out[2 * j : 2 * j + 2, :] = n_ref[8 * j : 8 * j + 2, :]
        one_out[...] = n_ref[2:3, :]
        two_out[...] = n_ref[3:4, :]
        count_out[...] = n_ref[4:5, 0:EXPERTS].astype(jnp.int32)


def results(q, o, kv, narrow, *own):
    rows = 256
    some = rows * TOK // D
    first = lambda *size: pl.BlockSpec((1, *size), lambda i: (0, i, 0))
    block = lambda width: pl.BlockSpec((rows, width), lambda i: (i, 0))
    whole = lambda *size: pl.BlockSpec(size, lambda i: (0, 0))
    shape = jax.ShapeDtypeStruct
    return pl.pallas_call(
        results_kernel,
        grid=(D // rows,),
        out_shape=(
            shape((D, D), F32),
            shape((D, D), F32),
            shape((D, 512), F32),
            shape((D, 512), F32),
            shape((EXPERTS, D), F32),
            shape((1, D), F32),
            shape((1, D), F32),
            shape((1, EXPERTS), jnp.int32),
            shape((TOK, D), BF),
            shape((TOK, D), F32),
            shape((1, D, TOK), F32),
            shape((1, D, TOK), F32),
            shape((1, TOK, D), F32),
        ),
        in_specs=[
            block(D), block(D), block(D), whole(TOK, D),
            pl.BlockSpec((some, D), lambda i: (i, 0)),
            pl.BlockSpec((some, D), lambda i: (i, 0)),
            block(TOK), block(TOK),
            pl.BlockSpec((some, D), lambda i: (i, 0)),
        ],
        out_specs=(
            block(D), block(D), block(512), block(512),
            whole(EXPERTS, D), whole(1, D), whole(1, D), whole(1, EXPERTS),
            pl.BlockSpec((some, D), lambda i: (i, 0)),
            pl.BlockSpec((some, D), lambda i: (i, 0)),
            first(rows, TOK), first(rows, TOK), first(some, D),
        ),
        name="results",
    )(q, o, kv, narrow, *own)


def shards(
    tokens,
    w_query,
    w_key,
    w_value,
    w_output,
    gain_attn,
    gain_moe,
    router,
    w_gate,
    w_up,
    w_down,
    cotangent,
    routes,
    lengths,
):
    (
        hidden, x, gates, mixed, query, kv, grad_rows, grad_gates, probs, out_parts, part_gate,
        part_up, part_down,
    ) = main(
        tokens, w_query, w_key, w_value, w_output, gain_attn, gain_moe, router.T, cotangent,
        routes.T, lengths, w_gate, w_up, w_down,
    )
    cosine, sine = turn_tables()
    layer_out, grad_input, grad_gate, grad_up, grad_down, sum_q, sum_o, sum_kv, narrow = back(
        (
            grad_rows, grad_gates, x, gates, hidden, gain_moe.reshape(1, D),
            gain_attn.reshape(1, D), router.T, cotangent, tokens, mixed, query, kv,
            jnp.asarray(cosine), jnp.asarray(sine), routes.T, lengths,
        ),
        (
            probs, w_output, w_query, w_key, w_value, out_parts, part_gate, part_up,
            part_down.reshape(2, FF, D),
        ),
    )
    (
        grad_q, grad_o, grad_k, grad_v, grad_router, gain_one, gain_two, counts,
        layer_out, grad_input, grad_gate, grad_up, grad_down,
    ) = results(
        sum_q, sum_o, sum_kv, narrow, layer_out, grad_input, grad_gate, grad_up, grad_down
    )
    return (
        layer_out,
        grad_input,
        grad_q,
        grad_k,
        grad_v,
        grad_o,
        gain_one.reshape(D),
        gain_two.reshape(D),
        grad_router.T,
        grad_gate,
        grad_up,
        grad_down,
        counts.reshape(EXPERTS),
    )


def solution(mesh):
    in_specs = (
        P(("dp", "hid"), None),
        P(),
        P(),
        P(),
        P(),
        P(),
        P(),
        P(),
        P("dp", None, "hid"),
        P("dp", None, "hid"),
        P("dp", "hid", None),
        P(("dp", "hid"), None),
        P(("dp", "hid"), None),
        P("dp"),
    )
    out_specs = (
        P(("dp", "hid"), None),
        P(("dp", "hid"), None),
        P(),
        P(),
        P(),
        P(),
        P(),
        P(),
        P(),
        P("dp", None, "hid"),
        P("dp", None, "hid"),
        P("dp", "hid", None),
        P(),
    )
    return jax.shard_map(shards, mesh=mesh, in_specs=in_specs, out_specs=out_specs, check_vma=False)
```

```python
import jax
import jax.numpy as jnp
import numpy as np
from jax import lax
from jax.experimental import pallas as pl
from jax.experimental.pallas import tpu as pltpu
from jax.sharding import PartitionSpec as P

D = 1024
HEADS = 16
KV_HEADS = 8
HEAD_DIM = 64
EXPERTS = 32
TOP = 8
FF = 512
TOK = 128

MESH = pl.DeviceIdType.MESH
BF = jnp.bfloat16
F32 = jnp.float32
SLOTS = 48
VMEM_BYTES = 60 * 2**20


def wrap(value):
    return lax.rem(value + 4, 4)


def place():
    dp = lax.axis_index("dp")
    y = lax.axis_index("hid")
    core = lax.rem(dp, 2)
    x = lax.div(dp, 8)
    z = lax.rem(lax.div(dp, 2), 4)
    p = jnp.where(core == 0, x, z)
    q = jnp.where(core == 0, z, x)
    return p, q, y, core


def device(p, q, y, core):
    p, q = wrap(p), wrap(q)
    return (jnp.where(core == 0, p * 8 + q * 2, q * 8 + p * 2) + core, wrap(y))


def chip_of(p, q, core):
    p, q = wrap(p), wrap(q)
    return jnp.where(core == 0, p * 4 + q, q * 4 + p)


def greet(devices):
    barrier = pltpu.get_barrier_semaphore()
    for other in devices:
        pl.semaphore_signal(barrier, inc=1, device_id=other, device_id_type=MESH)
    pl.semaphore_wait(barrier, len(devices))


class Sends:
    def __init__(self, send_sem, recv_sem):
        self.send_sem, self.recv_sem, self.made = send_sem, recv_sem, []

    def start(self, source, target, recv, to):
        self.put(source, target, self.recv_sem.at[recv], to)

    def put(self, source, target, sem, to):
        copy = pltpu.make_async_remote_copy(
            src_ref=source,
            dst_ref=target,
            send_sem=self.send_sem.at[len(self.made)],
            recv_sem=sem,
            device_id=to,
            device_id_type=MESH,
        )
        copy.start()
        self.made.append(copy)

    def arrived(self, ref, recv):
        pltpu.make_async_copy(ref, ref, self.recv_sem.at[recv]).wait()

    def drain(self):
        for copy in self.made:
            copy.wait_send()
        self.made = []


def slab(buffer, p, q):
    return buffer.at[wrap(p) * 4 + wrap(q)]


HALF = HEAD_DIM // 2
SCALE = HEAD_DIM**-0.5


def turn_tables():
    inverse = 10000.0 ** (-np.arange(HALF, dtype=np.float32) / HALF)
    phases = np.arange(4 * TOK, dtype=np.float32)[:, None] * inverse[None, :]
    cosine = np.tile(np.cos(phases), (1, 4)).astype(np.float32)
    sine = np.sin(phases)
    sine = np.tile(np.concatenate([-sine, sine], axis=1), (1, 2)).astype(np.float32)
    return cosine, sine


def lanes(rows, width=128):
    return lax.broadcasted_iota(jnp.int32, (rows, width), 1)


def turn(chunk, cosine, sine):
    front = lax.rem(lanes(chunk.shape[0]), HEAD_DIM) < HALF
    swapped = jnp.where(front, pltpu.roll(chunk, 128 - HALF, 1), pltpu.roll(chunk, HALF, 1))
    return chunk * cosine + swapped * sine


def stack_heads(chunk, half):
    low = lanes(chunk.shape[0]) < HEAD_DIM
    rolled = pltpu.roll(chunk, HEAD_DIM, 1)
    if half == 0:
        pair = (jnp.where(low, chunk, 0.0), jnp.where(low, rolled, 0.0))
    else:
        pair = (jnp.where(low, 0.0, rolled), jnp.where(low, 0.0, chunk))
    return jnp.concatenate(pair, axis=0).astype(BF)


def unstack_heads(pair, half):
    first, second = pair[:TOK], pair[TOK:]
    low = lanes(TOK) < HEAD_DIM
    if half == 0:
        return jnp.where(low, first, pltpu.roll(second, HEAD_DIM, 1))
    return jnp.where(low, pltpu.roll(first, HEAD_DIM, 1), second)


def root(values):
    return lax.rsqrt(jnp.mean(values * values, axis=1, keepdims=True) + 1e-06)


def widen():
    row = lax.broadcasted_iota(jnp.int32, (EXPERTS, TOK), 0)
    lane = lax.broadcasted_iota(jnp.int32, (EXPERTS, TOK), 1)
    return jnp.where(lane == lax.div(row, 2) * 8 + lax.rem(row, 2), 1.0, 0.0).astype(BF)


def routed_mask(routes, expert):
    hit = jnp.zeros((TOK, TOK), F32)
    for k in range(TOP):
        hit = hit + jnp.where(routes[k : k + 1, :] == expert, 1.0, 0.0)
    return hit


def wide_experts():
    row = lax.broadcasted_iota(jnp.int32, (TOK, 1), 0)
    return jnp.where(lax.rem(row, 8) < 2, lax.div(row, 8) * 2 + lax.rem(row, 8), -1)


class PlaneGather:
    def __init__(self, net, spot, slabs, base):
        self.net, self.spot, self.slabs, self.base = net, spot, slabs, base
        p, q, y, core = spot
        self.right, self.left = device(p + 1, q, y, core), device(p - 1, q, y, core)
        self.up, self.down = device(p, q + 1, y, core), device(p, q - 1, y, core)

    def slab(self, a, b):
        return slab(self.slabs, self.spot[0] + a, self.spot[1] + b)

    def send(self, ref, recv, to):
        self.net.start(ref, ref, self.base + recv, to)

    def arrived(self, ref, recv):
        self.net.arrived(ref, self.base + recv)

    def begin(self, own):
        for recv, to in ((0, self.right), (1, self.left), (4, self.up), (8, self.down)):
            self.net.start(own, self.slab(0, 0), self.base + recv, to)

    def second(self):
        s = self.slab(-1, 0)
        self.arrived(s, 0)
        self.send(s.at[0:64], 2, self.right)
        self.send(s, 5, self.up)
        s = self.slab(1, 0)
        self.arrived(s, 1)
        self.send(s.at[64:128], 3, self.left)
        self.send(s, 10, self.down)

    def third(self):
        s = self.slab(0, -1)
        self.arrived(s, 4)
        self.send(s, 12, self.up)
        s = self.slab(2, 0)
        self.arrived(s.at[0:64], 2)
        self.arrived(s.at[64:128], 3)
        self.send(s, 11, self.down)
        s = self.slab(-1, -1)
        self.arrived(s, 5)
        self.send(s, 13, self.up)
        self.send(self.slab(1, 0), 6, self.up)
        self.send(self.slab(2, 0), 7, self.up)
        self.send(self.slab(-1, 0), 9, self.down)

    def fourth(self, which):
        a, recv, far = ((1, 10, 14), (2, 11, 15))[which]
        s = self.slab(a, 1)
        self.arrived(s, recv)
        self.send(s, far, self.down)

    def finish(self):
        for a, b, recv in (
            (1, -1, 6), (2, -1, 7), (0, 1, 8), (-1, 1, 9),
            (0, 2, 12), (-1, 2, 13), (1, 2, 14), (2, 2, 15),
        ):
            self.arrived(self.slab(a, b), recv)


def main_kernel(
    tok_ref, wq_hbm, wk_hbm, wv_hbm, wo_hbm, ga_ref, gm_ref, router_ref, cot_ref, routes_ref,
    len_ref, cos_hbm, sin_hbm, wgs_hbm, wus_hbm, wds_hbm,
    gates_ref, grad_out, gg_out, hidden_hbm, x_hbm, mixed_hbm, query_hbm, kv_hbm,
    probs_hbm, o_hbm, dwg_hbm, dwu_hbm, dwd_hbm, hop_g_hbm, hop_u_hbm, hop_d_hbm,
    hidden_ref, x_ref, mixed_ref, query_ref, turns,
    wqo, wk, wv, u_own, kv, probs, bias, gt,
    xs, us, wg, wu, wd, gin, rank, ggo, picks, rows, slot_grads, acts, gparts, uparts,
    outs, pairs, o_buf, p_buf, rb, rc, rd, re, dwg, dwu,
    send_sem, recv_sem, g_send, g_recv, gg_send, gg_recv, local_sem, free_sem,
):
    p, q, y, core = place()
    spot = (p, q, y, core)
    sibling = (chip_of(p, q, core) * 2 + 1 - core, y)
    ahead, behind = device(p, q, y + 1, core), device(p, q, y - 1, core)
    up, down = device(p, q + 1, y, core), device(p, q - 1, y, core)
    right, left = device(p + 1, q, y, core), device(p - 1, q, y, core)
    others = [device(p + a, q + b, y, core) for a in range(4) for b in range(4) if a or b]
    my_chip = chip_of(p, q, core)
    net = Sends(send_sem, recv_sem)
    wq, wo = wqo.at[0], wqo.at[1]
    loads = {
        name: pltpu.make_async_copy(src, dst, local_sem.at[i])
        for i, (name, src, dst) in enumerate(
            (("k", wk_hbm, wk), ("v", wv_hbm, wv), ("q", wq_hbm, wq), ("o", wo_hbm, wo))
        )
    }
    for load in loads.values():
        load.start()
    first = pl.multiple_of(y * TOK, TOK)
    tables = [
        pltpu.make_async_copy(src.at[pl.ds(first, TOK)], turns.at[i], local_sem.at[16 + i])
        for i, src in enumerate((cos_hbm, sin_hbm))
    ]
    for load in tables:
        load.start()
    gather = PlaneGather(net, spot, us, 0)
    tokens_in = PlaneGather(net, spot, xs, 42)
    row = lax.broadcasted_iota(jnp.int32, (TOK, 1), 0) + y * TOK
    length = len_ref[0]
    u_own[...] = jnp.where(row < length, cot_ref[...].astype(F32), 0.0).astype(BF)
    greet(others + [ahead, behind, sibling])
    gather.begin(u_own)
    keep_own = pltpu.make_async_copy(u_own, gather.slab(0, 0), local_sem.at[4])
    keep_own.start()

    def weight(a, e, yy, rows=None):
        block = pl.ds(pl.multiple_of(wrap(yy) * TOK, TOK), TOK)
        if a == 2:
            return wd.at[e, block, :]
        full = (wg, wu)[a]
        return full.at[e, :, block] if rows is None else full.at[e, rows, block]

    shards = (wgs_hbm.at[0], wus_hbm.at[0], wds_hbm.at[0])
    top, bottom = pl.ds(0, 512), pl.ds(512, 512)
    keep = []

    def send_weight(a):
        net.start(shards[a], weight(a, core, y), 20 + a, ahead)
        net.start(shards[a], weight(a, core, y), 23 + a, behind)
        net.start(shards[a], weight(a, core, y), 30 + a, sibling)
        keep.append(pltpu.make_async_copy(shards[a], weight(a, core, y), local_sem.at[5 + a]))
        keep[-1].start()

    def pass_weight(a):
        before, after = weight(a, core, y - 1), weight(a, core, y + 1)
        net.arrived(before, 20 + a)
        if a == 0:
            net.start(before, before, 26, ahead)
        if a == 1:
            spot = weight(1, core, y - 1, top)
            net.start(spot, spot, 27, ahead)
        net.start(before, before, 33 + a, sibling)
        net.arrived(after, 23 + a)
        if a == 1:
            spot = weight(1, core, y + 1, bottom)
            net.start(spot, spot, 28, behind)
        if a == 2:
            net.start(after, after, 29, behind)
        net.start(after, after, 36 + a, sibling)

    send_weight(0)
    tokens = tok_ref[...].astype(F32)
    normed = (tokens * root(tokens) * ga_ref[...]).astype(BF)
    for load in tables:
        load.wait()
    cosine, sine = turns[0], turns[1]
    loads["k"].wait()
    keys = jnp.dot(normed, wk[...], preferred_element_type=F32)
    for c in range(4):
        span = slice(c * 128, (c + 1) * 128)
        kv[y, :, span] = turn(keys[:, span], cosine, sine).astype(BF)
    loads["v"].wait()
    kv[y, :, 512:1024] = jnp.dot(normed, wv[...], preferred_element_type=F32).astype(BF)
    own = kv.at[y]
    net.start(own, own, 16, ahead)
    net.start(own, own, 17, behind)

    loads["q"].wait()
    queries = jnp.dot(normed, wq[...], preferred_element_type=F32)
    for c in range(8):
        span = slice(c * 128, (c + 1) * 128)
        query_ref[:, span] = turn(queries[:, span], cosine, sine).astype(BF)
    key_pos = lanes(TOK, 512)
    bias[...] = jnp.where((key_pos <= row) & (key_pos < length), 0.0, -1e30)
    gather.second()
    s = kv.at[wrap(y - 1)]
    net.arrived(s, 16)
    net.start(s.at[0:64], s.at[0:64], 18, ahead)
    s = kv.at[wrap(y + 1)]
    net.arrived(s, 17)
    net.start(s.at[64:128], s.at[64:128], 19, behind)
    gather.third()
    s = kv.at[wrap(y + 2)]
    net.arrived(s.at[0:64], 18)
    net.arrived(s.at[64:128], 19)
    send_weight(1)
    send_weight(2)
    pass_weight(0)
    gather.fourth(0)

    def attend(c, carry):
        span = pl.ds(pl.multiple_of(c * 128, 128), 128)
        keys = kv[:, :, span].reshape(512, 128)
        values = kv[:, :, pl.ds(pl.multiple_of(512 + c * 128, 128), 128)].reshape(512, 128)
        for half in range(2):
            m = c * 2 + half
            mine = pl.ds(pl.multiple_of(m * 128, 128), 128)
            pair = stack_heads(query_ref[:, mine].astype(F32), half)
            scores = lax.dot_general(
                pair, keys, (((1,), (1,)), ((), ())), preferred_element_type=F32
            )
            scores = scores * SCALE + jnp.concatenate([bias[...], bias[...]], axis=0)
            scores = jnp.exp(scores - jnp.max(scores, axis=1, keepdims=True))
            low = (scores * (1.0 / jnp.sum(scores, axis=1, keepdims=True))).astype(BF)
            probs[m] = low
            out = jnp.dot(low, values, preferred_element_type=F32)
            mixed_ref[:, mine] = unstack_heads(out, half).astype(BF)
        return carry

    lax.fori_loop(0, 4, attend, 0)
    gather.fourth(1)
    keep_probs = pltpu.make_async_copy(probs, probs_hbm, local_sem.at[8])
    keep_probs.start()
    loads["o"].wait()
    hidden = tokens + jnp.dot(mixed_ref[...], wo[...], preferred_element_type=F32)
    hidden_ref[...] = hidden
    x = (hidden * root(hidden) * gm_ref[...]).astype(BF)
    x_ref[...] = x
    tokens_in.begin(x_ref)
    tokens_in.slab(0, 0)[...] = x
    wide = lax.dot_general(
        widen(), router_ref[...], (((0,), (0,)), ((), ())), preferred_element_type=F32
    ).astype(BF)
    logits = lax.dot_general(x, wide, (((1,), (1,)), ((), ())), preferred_element_type=F32)
    routed = routed_mask(routes_ref[...], wide_experts()).T > 0
    logits = jnp.where(routed, logits, -1e30)
    weights = jnp.where(routed, jnp.exp(logits - jnp.max(logits, axis=1, keepdims=True)), 0.0)
    weights = weights * (1.0 / jnp.sum(weights, axis=1, keepdims=True))
    gates_ref[...] = weights
    gt[...] = weights.T.reshape(16, 8, TOK)

    def gate_copy(i):
        a, b = lax.div(i, 4), lax.rem(i, 4)
        return pltpu.make_async_remote_copy(
            src_ref=gt.at[chip_of(p + a, q + b, core)],
            dst_ref=gin.at[p * 4 + q],
            send_sem=g_send.at[i],
            recv_sem=g_recv.at[wrap(-a) * 4 + wrap(-b)],
            device_id=device(p + a, q + b, y, core),
            device_id_type=MESH,
        )

    def start_gate(i, _):
        gate_copy(i).start()
        return 0

    lax.fori_loop(1, 16, start_gate, 0)
    gin[p * 4 + q] = gt[my_chip]

    keeps = [
        pltpu.make_async_copy(src, dst, local_sem.at[18 + i])
        for i, (src, dst) in enumerate(
            (
                (hidden_ref, hidden_hbm),
                (x_ref, x_hbm),
                (mixed_ref, mixed_hbm),
                (query_ref, query_hbm),
                (kv, kv_hbm),
            )
        )
    ]
    for store in keeps:
        store.start()
    tokens_in.second()
    pass_weight(1)
    tokens_in.third()
    pass_weight(2)

    def take_gate(i, _):
        pltpu.make_async_copy(gin.at[0], gin.at[0], g_recv.at[i]).wait()
        return 0

    lax.fori_loop(1, 16, take_gate, 0)
    ids = lax.broadcasted_iota(jnp.int32, (TOK, TOK), 0)
    cols = lax.broadcasted_iota(jnp.int32, (TOK, TOK), 1)
    before = jnp.where(ids < cols, 1.0, 0.0).astype(BF)
    routed = jnp.where(gin[...].reshape(TOK, TOK) > 0, 1.0, 0.0).astype(BF)
    rank[...] = jnp.dot(routed, before, preferred_element_type=F32).reshape(16, 8, TOK)
    gather.finish()
    ggo[...] = jnp.zeros_like(ggo)
    slot_ids = lax.broadcasted_iota(jnp.int32, (SLOTS, TOK), 0).astype(F32)

    def source_of(g, j):
        side = jnp.where((j < 2) == (g == 1), 3, 1)
        b = jnp.where(g == 0, 0, jnp.where(g == 2, 2, side))
        a = jnp.where(j == 0, 0, jnp.where(j == 1, 3, jnp.where(j == 2, 1, 2)))
        return wrap(p + a) * 4 + wrap(q + b)

    def pick_source(g, j):
        src = source_of(g, j)
        token_rows, up_rows = xs[src], us[src]
        base = pl.multiple_of(g * 4 * SLOTS + j * SLOTS, 16)
        for e in range(2):
            gate_row = gin[src, e : e + 1, :]
            hit = (rank[src, e : e + 1, :] == slot_ids) & (gate_row > 0)
            pick = jnp.where(hit, 1.0, 0.0)
            pick_low = pick.astype(BF)
            picks[src, e * SLOTS : (e + 1) * SLOTS, :] = pick_low
            gate_col = jnp.sum(pick * gate_row, axis=1, keepdims=True)
            rows[e, pl.ds(base, SLOTS), :] = jnp.dot(
                pick_low, token_rows, preferred_element_type=F32
            ).astype(BF)
            picked = jnp.dot(pick_low, up_rows, preferred_element_type=F32)
            wqo[e, pl.ds(base, SLOTS), :] = picked.astype(BF)
            slot_grads[e, pl.ds(base, SLOTS), :] = (picked * gate_col).astype(BF)

    def run_expert(g, e):
        base = pl.multiple_of(g * 4 * SLOTS, 16)
        span = pl.ds(base, 4 * SLOTS)
        taken = rows[e, span, :]
        gate = jnp.dot(taken, wg[e], preferred_element_type=F32)
        upv = jnp.dot(taken, wu[e], preferred_element_type=F32)
        sig = 1.0 / (1.0 + jnp.exp(-gate))
        silu = gate * sig
        act = (silu * upv).astype(BF)
        acts[e, span, :] = act
        grad_act = lax.dot_general(
            slot_grads[e, span, :], wd[e], (((1,), (1,)), ((), ())), preferred_element_type=F32
        )
        ggp = (grad_act * upv * sig * (1.0 + gate * (1.0 - sig))).astype(BF)
        gup = (grad_act * silu).astype(BF)
        gparts[e, span, :] = ggp
        uparts[e, span, :] = gup
        pair = lax.dot_general(ggp, wg[e], (((1,), (1,)), ((), ())), preferred_element_type=F32)
        pair += lax.dot_general(gup, wu[e], (((1,), (1,)), ((), ())), preferred_element_type=F32)
        pairs[e] = pair.astype(BF)

    def spread(g, j):
        src = source_of(g, j)
        span = pl.ds(pl.multiple_of(j * SLOTS, 16), SLOTS)
        both = jnp.concatenate([pairs[0, span, :], pairs[1, span, :]], axis=0)
        p_buf[src] = lax.dot_general(
            picks[src], both, (((0,), (0,)), ((), ())), preferred_element_type=F32
        ).astype(BF)

    def run_output(g, e):
        span = pl.ds(pl.multiple_of(g * 4 * SLOTS, 16), 4 * SLOTS)
        out = jnp.dot(acts[e, span, :], wd[e], preferred_element_type=F32).astype(BF)
        outs[e] = out
        gg_col = jnp.sum(out.astype(F32) * wqo[e, span, :].astype(F32), axis=1, keepdims=True)
        for j in range(4):
            src = source_of(g, j)
            pick = picks[src, pl.ds(pl.multiple_of(e * SLOTS, 16), SLOTS), :].astype(F32)
            part = gg_col[j * SLOTS : (j + 1) * SLOTS]
            ggo[src, pl.ds(e, 1), :] = jnp.sum(pick * part, axis=0, keepdims=True)

    def spread_output(g, j):
        src = source_of(g, j)
        pick = picks[src]
        span = pl.ds(pl.multiple_of(j * SLOTS, 16), SLOTS)
        gates = jnp.concatenate(
            [
                pick[e * SLOTS : (e + 1) * SLOTS].astype(F32) * gin[src, e : e + 1, :]
                for e in range(2)
            ],
            axis=0,
        ).astype(BF)
        both = jnp.concatenate([outs[0, span, :], outs[1, span, :]], axis=0)
        o_buf[src] = lax.dot_general(
            gates, both, (((0,), (0,)), ((), ())), preferred_element_type=F32
        ).astype(BF)

    def output(g, carry):
        lax.fori_loop(0, 2, lambda e, c: (run_output(g, e), c)[1], 0)
        lax.fori_loop(0, 4, lambda j, c: (spread_output(g, j), c)[1], 0)
        return carry

    def pick(g):
        lax.fori_loop(0, 4, lambda j, c: (pick_source(g, j), c)[1], 0)

    OFF = (0, -1, 1, 2)
    R = 58

    def make(source, target, recv, to, index):
        return pltpu.make_async_remote_copy(
            src_ref=source,
            dst_ref=target,
            send_sem=send_sem.at[index],
            recv_sem=recv_sem.at[recv],
            device_id=to,
            device_id_type=MESH,
        )

    first = 80
    bounce = [
        (lambda j=j: make(slab(p_buf, p + OFF[j], q + 2), rb.at[j], R + j, up if j < 2 else down, first + j))
        for j in range(4)
    ]
    to_down = [
        (lambda j=j: make(slab(p_buf, p + OFF[j], q - 1), rc.at[4 + j], R + 8 + j, down, first + 4 + j))
        for j in range(4)
    ]
    to_up = [
        (lambda j=j: make(slab(p_buf, p + OFF[j], q + 1), rc.at[j], R + 4 + j, up, first + 8 + j))
        for j in range(4)
    ]

    def add_bounce(j):
        net.arrived(rb.at[j], R + j)
        target = slab(p_buf, p + OFF[j], q + 1 if j < 2 else q - 1)
        target[...] = (target[...].astype(F32) + rb[j].astype(F32)).astype(BF)

    def step(g, carry):
        @pl.when(g == 2)
        def _():
            for j in range(4):
                tokens_in.arrived(slab(xs, p + OFF[j], q + 2), 12 + j)

        @pl.when(g == 3)
        def _():
            tokens_in.arrived(slab(xs, p + 1, q - 1), 6)
            tokens_in.arrived(slab(xs, p + 2, q - 1), 7)
            tokens_in.arrived(slab(xs, p, q + 1), 8)
            tokens_in.arrived(slab(xs, p - 1, q + 1), 9)
            for j in range(2):
                to_down[j]().start()
                to_up[3 - j]().start()

        @pl.when(g >= 2)
        def _():
            pick(g)

        lax.fori_loop(0, 2, lambda e, c: (run_expert(g, e), c)[1], 0)
        lax.fori_loop(0, 4, lambda j, c: (spread(g, j), c)[1], 0)

        @pl.when(g == 2)
        def _():
            for j in range(4):
                bounce[j]().start()

        return carry

    keep_own.wait()
    pick(0)
    tokens_in.fourth(0)
    tokens_in.fourth(1)
    pick(1)
    net.arrived(weight(0, core, y + 2), 26)
    net.arrived(weight(1, core, y + 2, top), 27)
    net.arrived(weight(1, core, y + 2, bottom), 28)
    net.arrived(weight(2, core, y + 2), 29)
    for a in range(3):
        net.start(weight(a, core, y + 2), weight(a, core, y + 2), 39 + a, sibling)
    for i, ahead_by in enumerate((0, -1, 1, 2)):
        for a in range(3):
            net.arrived(weight(a, 1 - core, y + ahead_by), 30 + 3 * i + a)
    for copy in keep:
        copy.wait()
    lax.fori_loop(0, 4, step, 0)
    net.drain()
    pl.semaphore_signal(free_sem.at[0], inc=1, device_id=sibling, device_id_type=MESH)
    for other in (ahead, behind):
        pl.semaphore_signal(free_sem.at[1], inc=1, device_id=other, device_id_type=MESH)

    def weight_tile(e, t):
        cols = pl.ds(pl.multiple_of(t * 256, 256), 256)
        dims = (((0,), (0,)), ((), ()))
        lhs = rows[e, :, cols]
        dwg[e, cols, :] = lax.dot_general(lhs, gparts[e], dims, preferred_element_type=F32).astype(BF)
        dwu[e, cols, :] = lax.dot_general(lhs, uparts[e], dims, preferred_element_type=F32).astype(BF)
        us[pl.ds(4 * e, 4), :, cols] = (
            lax.dot_general(acts[e], slot_grads[e, :, cols], dims, preferred_element_type=F32)
            .astype(BF)
            .reshape(4, TOK, 256)
        )

    def weight_grads(e):
        lax.fori_loop(0, 4, lambda t, c: (weight_tile(e, t), c)[1], 0)

    weight_grads(1 - core)
    pl.semaphore_wait(free_sem.at[0], 1)
    theirs = us.at[pl.ds(4 * (1 - core), 4)]
    net.start(dwg.at[1 - core], wg.at[0], 76, sibling)
    net.start(dwu.at[1 - core], wu.at[0], 77, sibling)
    net.start(theirs, xs.at[pl.ds(8, 4)], 78, sibling)
    weight_grads(core)
    for j in (3, 1, 2, 0):
        add_bounce(j)
        (to_up if j < 2 else to_down)[j]().start()
    lax.fori_loop(0, 2, output, 0)

    def grad_block(ref, step, rows=None):
        span = pl.ds(pl.multiple_of(wrap(y + step) * TOK, TOK), TOK)
        return ref.at[:, span] if rows is None else ref.at[rows, span]

    def weight_portion(step, which):
        if which == 0:
            return [grad_block(dwg.at[core], step), grad_block(dwu.at[core], step, top)]
        return [grad_block(dwu.at[core], step, bottom), us.at[4 * core + wrap(y + step)]]

    def weight_merge(step):
        accumulate(grad_block(dwg.at[core], step), grad_block(wg.at[0], step))
        accumulate(grad_block(dwu.at[core], step), grad_block(wu.at[0], step))
        accumulate(us.at[4 * core + wrap(y + step)], xs.at[8 + wrap(y + step)])

    hops = (wu.at[1, :, 0:128], wu.at[1, :, 128:256], xs.at[12])
    ring = RingReduce(
        net, 79, ahead, behind, weight_portion,
        ([hops[0], wu.at[1, top, 128:256]], [wu.at[1, bottom, 128:256], hops[2]]), None, None,
    )
    for i, ref in enumerate((wg.at[0], wu.at[0], xs.at[pl.ds(8, 4)])):
        net.arrived(ref, 76 + i)
    weight_merge(2)
    pl.semaphore_wait(free_sem.at[1], 2)
    ring.begin()
    for around in (1, -1, 0):
        weight_merge(around)
    stores = [
        pltpu.make_async_copy(src, dst, local_sem.at[10 + i])
        for i, (src, dst) in enumerate(
            (
                (dwg.at[core], dwg_hbm),
                (dwu.at[core], dwu_hbm),
                (us.at[pl.ds(4 * core, 4)], dwd_hbm),
            )
        )
    ]
    for store in stores:
        store.start()
    lax.fori_loop(2, 4, output, 0)

    def gg_copy(i):
        a, b = lax.div(i, 4), lax.rem(i, 4)
        return pltpu.make_async_remote_copy(
            src_ref=ggo.at[wrap(p + a) * 4 + wrap(q + b)],
            dst_ref=gg_out.at[my_chip],
            send_sem=gg_send.at[i],
            recv_sem=gg_recv.at[wrap(-a) * 4 + wrap(-b)],
            device_id=device(p + a, q + b, y, core),
            device_id_type=MESH,
        )

    def start_gg(i, _):
        gg_copy(i).start()
        return 0

    lax.fori_loop(1, 16, start_gg, 0)
    gg_out[my_chip] = ggo[p * 4 + q]
    o_store = pltpu.make_async_copy(o_buf, o_hbm, local_sem.at[9])
    o_store.start()

    def gather_sum(j):
        net.arrived(rc.at[j], R + 4 + j)
        net.arrived(rc.at[4 + j], R + 8 + j)
        target = slab(p_buf, p + OFF[j], q)
        target[...] = (
            target[...].astype(F32) + rc[j].astype(F32) + rc[4 + j].astype(F32)
        ).astype(BF)

    last = first + 12
    lo, hi = pl.ds(0, 64), pl.ds(64, 64)
    far_slab, next_slab, prev_slab = slab(p_buf, p + 2, q), slab(p_buf, p + 1, q), slab(p_buf, p - 1, q)
    tail = [
        make(far_slab.at[lo], rd.at[lo], R + 12, right, last),
        make(far_slab.at[hi], rd.at[hi], R + 13, left, last + 1),
        make(next_slab.at[hi], re.at[0, hi], R + 14, right, last + 2),
        make(prev_slab.at[lo], re.at[1, lo], R + 15, left, last + 3),
        make(next_slab.at[lo], re.at[0, lo], R + 16, right, last + 4),
        make(prev_slab.at[hi], re.at[1, hi], R + 17, left, last + 5),
    ]
    gather_sum(3)
    tail[0].start()
    tail[1].start()
    gather_sum(2)
    tail[2].start()
    gather_sum(1)
    tail[3].start()
    gather_sum(0)
    net.arrived(rd.at[lo], R + 12)
    next_slab[lo] = (next_slab[lo].astype(F32) + rd[lo].astype(F32)).astype(BF)
    tail[4].start()
    net.arrived(rd.at[hi], R + 13)
    prev_slab[hi] = (prev_slab[hi].astype(F32) + rd[hi].astype(F32)).astype(BF)
    tail[5].start()
    ring.arrived(ring.hops[0], 0)
    ring.arrived(ring.hops[1], 1)
    for i, (src, dst) in enumerate(zip(hops, (hop_g_hbm, hop_u_hbm, hop_d_hbm))):
        stores.append(pltpu.make_async_copy(src, dst, local_sem.at[13 + i]))
        stores[-1].start()
    net.arrived(re.at[0, hi], R + 14)
    net.arrived(re.at[1, lo], R + 15)
    net.arrived(re.at[0, lo], R + 16)
    net.arrived(re.at[1, hi], R + 17)
    grad_out[...] = slab(p_buf, p, q)[...].astype(F32) + re[0].astype(F32) + re[1].astype(F32)

    def take_gg(i, _):
        pltpu.make_async_copy(ggo.at[0], ggo.at[0], gg_recv.at[i]).wait()
        return 0

    lax.fori_loop(1, 16, take_gg, 0)
    for copy in bounce + to_down + to_up:
        copy().wait_send()
    for copy in tail:
        copy.wait_send()

    def drain_small(i, _):
        gate_copy(i).wait_send()
        gg_copy(i).wait_send()
        return 0

    lax.fori_loop(1, 16, drain_small, 0)
    net.drain()
    o_store.wait()
    for store in stores:
        store.wait()
    keep_probs.wait()
    for store in keeps:
        store.wait()


def main(tokens, wq, wk, wv, wo, ga, gm, router, cotangent, routes, lengths, wg, wu, wd):
    cosine, sine = turn_tables()
    any_space = pl.BlockSpec(memory_space=pl.ANY)
    vmem = pl.BlockSpec(memory_space=pltpu.VMEM)
    smem = pl.BlockSpec(memory_space=pltpu.SMEM)
    shape = jax.ShapeDtypeStruct
    dma = pltpu.SemaphoreType.DMA
    slots = 16 * SLOTS
    low = lambda *size: pltpu.VMEM(size, BF)
    return pl.pallas_call(
        main_kernel,
        out_shape=(
            shape((TOK, TOK), F32),
            shape((TOK, D), F32),
            shape((16, 8, TOK), F32),
            shape((TOK, D), F32),
            shape((TOK, D), BF),
            shape((TOK, D), BF),
            shape((TOK, D), BF),
            shape((4, TOK, D), BF),
            shape((8, 2 * TOK, 512), BF),
            shape((16, TOK, D), BF),
            shape((D, FF), BF),
            shape((D, FF), BF),
            shape((4, TOK, D), BF),
            shape((D, TOK), BF),
            shape((D, TOK), BF),
            shape((TOK, D), BF),
        ),
        in_specs=[vmem] + [any_space] * 4 + [vmem] * 5 + [smem] + [any_space] * 5,
        out_specs=(vmem,) * 3 + (any_space,) * 13,
        scratch_shapes=[
            pltpu.VMEM((TOK, D), F32),
            low(TOK, D),
            low(TOK, D),
            low(TOK, D),
            pltpu.VMEM((2, TOK, TOK), F32),
            low(2, D, D),
            low(D, 512),
            low(D, 512),
            low(TOK, D),
            low(4, TOK, D),
            low(8, 2 * TOK, 512),
            pltpu.VMEM((TOK, 512), F32),
            pltpu.VMEM((16, 8, TOK), F32),
            low(16, TOK, D),
            low(16, TOK, D),
            low(2, D, FF),
            low(2, D, FF),
            low(2, FF, D),
            pltpu.VMEM((16, 8, TOK), F32),
            pltpu.VMEM((16, 8, TOK), F32),
            pltpu.VMEM((16, 8, TOK), F32),
            low(16, 2 * SLOTS, TOK),
            low(2, slots, D),
            low(2, slots, D),
            low(2, slots, FF),
            low(2, slots, FF),
            low(2, slots, FF),
            low(2, 4 * SLOTS, D),
            low(2, 4 * SLOTS, D),
            low(16, TOK, D),
            low(16, TOK, D),
            low(4, TOK, D),
            low(8, TOK, D),
            low(TOK, D),
            low(2, TOK, D),
            low(2, D, FF),
            low(2, D, FF),
            dma((100,)),
            dma((83,)),
            dma((16,)),
            dma((16,)),
            dma((16,)),
            dma((16,)),
            dma((23,)),
            pltpu.SemaphoreType.REGULAR((2,)),
        ],
        compiler_params=pltpu.CompilerParams(
            collective_id=1, has_side_effects=True, vmem_limit_bytes=VMEM_BYTES
        ),
        name="main",
    )(
        tokens, wq, wk, wv, wo, ga.reshape(1, D), gm.reshape(1, D), router, cotangent, routes,
        lengths, jnp.asarray(cosine), jnp.asarray(sine), wg, wu, wd,
    )


def accumulate(target, *terms):
    total = target[...].astype(F32)
    for term in terms:
        total += term[...].astype(F32)
    target[...] = total.astype(target.dtype)


class PlaneReduce:
    OFF = (0, -1, 1, 2)

    def __init__(self, net, spot, slabs, rb, rc, rd, re, base):
        self.net, self.spot, self.slabs, self.base = net, spot, slabs, base
        self.rb, self.rc, self.rd, self.re = rb, rc, rd, re
        p, q, y, core = spot
        self.right, self.left = device(p + 1, q, y, core), device(p - 1, q, y, core)
        self.up, self.down = device(p, q + 1, y, core), device(p, q - 1, y, core)

    def slab(self, a, b):
        return slab(self.slabs, self.spot[0] + a, self.spot[1] + b)

    def send(self, source, target, recv, to):
        self.net.start(source, target, self.base + recv, to)

    def arrived(self, ref, recv):
        self.net.arrived(ref, self.base + recv)

    def bounce(self):
        for j in range(4):
            to = self.up if j < 2 else self.down
            self.send(self.slab(self.OFF[j], 2), self.rb.at[j], j, to)

    def to_up(self, j):
        self.send(self.slab(self.OFF[j], 1), self.rc.at[j], 4 + j, self.up)

    def to_down(self, j):
        self.send(self.slab(self.OFF[j], -1), self.rc.at[4 + j], 8 + j, self.down)

    def begin(self):
        self.bounce()
        for j in (3, 2):
            self.to_up(j)
        for j in (0, 1):
            self.to_down(j)

    def middle(self):
        for j in (3, 1, 2, 0):
            self.arrived(self.rb.at[j], j)
            accumulate(self.slab(self.OFF[j], 1 if j < 2 else -1), self.rb.at[j])
            (self.to_up if j < 2 else self.to_down)(j)

    def column(self, j):
        self.arrived(self.rc.at[j], 4 + j)
        self.arrived(self.rc.at[4 + j], 8 + j)
        accumulate(self.slab(self.OFF[j], 0), self.rc.at[j], self.rc.at[4 + j])

    def third(self):
        lo, hi = pl.ds(0, 64), pl.ds(64, 64)
        rd, re = self.rd, self.re
        self.column(3)
        self.send(self.slab(2, 0).at[lo], rd.at[lo], 12, self.right)
        self.send(self.slab(2, 0).at[hi], rd.at[hi], 13, self.left)
        self.column(2)
        self.send(self.slab(1, 0).at[hi], re.at[0, hi], 14, self.right)
        self.column(1)
        self.send(self.slab(-1, 0).at[lo], re.at[1, lo], 15, self.left)

    def fourth(self):
        lo, hi = pl.ds(0, 64), pl.ds(64, 64)
        rd, re = self.rd, self.re
        self.arrived(rd.at[lo], 12)
        accumulate(self.slab(1, 0).at[lo], rd.at[lo])
        self.send(self.slab(1, 0).at[lo], re.at[0, lo], 16, self.right)
        self.arrived(rd.at[hi], 13)
        accumulate(self.slab(-1, 0).at[hi], rd.at[hi])
        self.send(self.slab(-1, 0).at[hi], re.at[1, hi], 17, self.left)
        self.column(0)

    def finish(self):
        lo, hi = pl.ds(0, 64), pl.ds(64, 64)
        re = self.re
        self.arrived(re.at[0, hi], 14)
        self.arrived(re.at[1, lo], 15)
        self.arrived(re.at[0, lo], 16)
        self.arrived(re.at[1, hi], 17)
        return self.slab(0, 0)[...].astype(F32) + re[0].astype(F32) + re[1].astype(F32)


class RingReduce:
    def __init__(self, net, base, ahead, behind, portion, hops, lows, highs):
        self.net, self.base, self.ahead, self.behind = net, base, ahead, behind
        self.portion, self.hops, self.lows, self.highs = portion, hops, lows, highs
        self.n = len(hops[0])

    def send(self, sources, targets, group, to):
        for i, (source, target) in enumerate(zip(sources, targets)):
            self.net.start(source, target, self.base + group * self.n + i, to)

    def arrived(self, refs, group):
        for i, ref in enumerate(refs):
            self.net.arrived(ref, self.base + group * self.n + i)

    def begin(self):
        self.send(self.portion(2, 0), self.hops[0], 0, self.ahead)
        self.send(self.portion(2, 1), self.hops[1], 1, self.behind)

    def direct(self):
        self.send(self.portion(1, 1), self.lows[1], 2, self.ahead)
        self.send(self.portion(-1, 0), self.highs[0], 3, self.behind)

    def middle(self, here=False):
        for which, step, targets, to in (
            (0, 1, self.lows[0], self.ahead),
            (1, -1, self.highs[1], self.behind),
        ):
            if not here:
                self.arrived(self.hops[which], which)
            refs = self.portion(step, which)
            for ref, hop in zip(refs, self.hops[which]):
                accumulate(ref, hop)
            self.send(refs, targets, 4 + which, to)

    def finish(self):
        self.arrived(self.lows[1], 2)
        self.arrived(self.highs[0], 3)
        self.arrived(self.lows[0], 4)
        self.arrived(self.highs[1], 5)


class Total:
    def __init__(self, net, axis, source, result, span, rows, first, piece, buffers, sems):
        self.net, self.axis, self.source, self.result = net, axis, source, result
        self.span, self.rows, self.first, self.piece_size = span, rows, first, piece
        self.theirs, self.low, self.high, self.hop, self.pieces, self.done = buffers
        self.recv, self.plane_send, self.plane_recv, self.back_send, self.back_recv = sems
        dp, y = lax.axis_index("dp"), lax.axis_index("hid")
        self.core = lax.rem(dp, 2)
        self.here = (lax.div(dp, 8), y, lax.rem(lax.div(dp, 2), 4))
        self.sibling = self.at(self.here, 1 - self.core)
        self.plus, self.minus = self.along(1), self.along(-1)
        self.plane = [i for i in range(3) if i != axis]
        self.slab_rows = rows // 4
        half = self.slab_rows // 2
        self.lo, self.hi = pl.ds(0, half), pl.ds(half, half)

    def at(self, spot, on=None):
        spot = [wrap(v) for v in spot]
        return (spot[0] * 8 + spot[2] * 2 + (self.core if on is None else on), spot[1])

    def along(self, step):
        return self.at([self.here[i] + (step if i == self.axis else 0) for i in range(3)])

    def arrived(self, ref, i):
        pltpu.make_async_copy(ref, ref, self.recv.at[i]).wait()

    def put(self, source, target, i, to):
        self.net.put(source, target, self.recv.at[i], to)

    def block(self, ref, step, part=None):
        size = self.slab_rows
        start = self.core * self.span + self.first + wrap(self.here[self.axis] + step) * size
        if part is not None:
            size = size // 2
            start += part * size
        return ref.at[pl.ds(pl.multiple_of(start, size), size)]

    def own(self, step):
        return self.block(self.source, step)

    def begin(self):
        start = (1 - self.core) * self.span + self.first
        theirs = self.source.at[pl.ds(pl.multiple_of(start, self.rows), self.rows)]
        self.put(theirs, self.theirs, 0, self.sibling)

    def merge(self, step):
        size = self.slab_rows
        start = wrap(self.here[self.axis] + step) * size
        accumulate(self.own(step), self.theirs.at[pl.ds(pl.multiple_of(start, size), size)])

    def second(self):
        lo, hi = self.lo, self.hi
        self.arrived(self.theirs, 0)
        self.merge(2)
        far = self.own(2)
        self.put(far.at[lo], self.hop.at[lo], 1, self.plus)
        self.put(far.at[hi], self.hop.at[hi], 2, self.minus)
        self.merge(1)
        self.put(self.own(1).at[hi], self.low.at[hi], 3, self.plus)
        self.merge(-1)
        self.put(self.own(-1).at[lo], self.high.at[lo], 4, self.minus)
        self.merge(0)

    def third(self):
        lo, hi = self.lo, self.hi
        self.arrived(self.hop.at[lo], 1)
        near = self.own(1).at[lo]
        accumulate(near, self.hop.at[lo])
        self.put(near, self.low.at[lo], 5, self.plus)
        self.arrived(self.hop.at[hi], 2)
        near = self.own(-1).at[hi]
        accumulate(near, self.hop.at[hi])
        self.put(near, self.high.at[hi], 6, self.minus)

    def piece(self, ref, u, v):
        rows, cols = self.piece_size
        if self.slab_rows == 4 * rows:
            row, col = u * rows, v * cols
        else:
            row, col = lax.div(u, 2) * rows, (lax.rem(u, 2) * 4 + v) * cols
        return ref.at[
            pl.ds(pl.multiple_of(row, rows), rows), pl.ds(pl.multiple_of(col, cols), cols)
        ]

    def member(self, i):
        u, v = self.plane
        spot = list(self.here)
        spot[u] = wrap(spot[u] + lax.div(i, 4))
        spot[v] = wrap(spot[v] + lax.rem(i, 4))
        return spot[u], spot[v], self.at(spot)

    def mirror(self, i):
        return wrap(-lax.div(i, 4)) * 4 + wrap(-lax.rem(i, 4))

    def mine(self):
        return self.here[self.plane[0]], self.here[self.plane[1]]

    def remote(self, source, target, send, recv, to):
        return pltpu.make_async_remote_copy(
            src_ref=source, dst_ref=target, send_sem=send, recv_sem=recv,
            device_id=to, device_id_type=MESH,
        )

    def piece_copy(self, i):
        u, v, to = self.member(i)
        there = self.mirror(i)
        return self.remote(
            self.piece(self.own(0), u, v),
            self.pieces.at[there],
            self.plane_send.at[i],
            self.plane_recv.at[there],
            to,
        )

    def back_copy(self, i):
        spot = self.piece(self.done, *self.mine())
        return self.remote(
            spot, spot, self.back_send.at[i], self.back_recv.at[self.mirror(i)], self.member(i)[2]
        )

    def each(self, act):
        lax.fori_loop(1, 16, lambda i, carry: (act(i), carry)[1], 0)

    def take(self, sems):
        spot = self.pieces
        self.each(lambda i: pltpu.make_async_copy(spot.at[0], spot.at[0], sems.at[i]).wait())

    def fourth(self):
        lo, hi = self.lo, self.hi
        self.arrived(self.low.at[hi], 3)
        self.arrived(self.high.at[lo], 4)
        self.arrived(self.low.at[lo], 5)
        self.arrived(self.high.at[hi], 6)
        accumulate(self.own(0), self.low, self.high)
        self.each(lambda i: self.piece_copy(i).start())
        self.pieces[0] = self.piece(self.own(0), *self.mine())[...]

    def fifth(self):
        self.take(self.plane_recv)
        total = jnp.sum(self.pieces[...].astype(F32), axis=0)
        self.piece(self.done, *self.mine())[...] = total.astype(self.done.dtype)
        self.each(lambda i: self.back_copy(i).start())

    def sixth(self, sem):
        self.take(self.back_recv)
        spot = self.block(self.result, 0)
        self.put(self.done, spot, 7, self.plus)
        self.put(self.done, spot, 8, self.minus)
        self.put(self.done, spot, 11, self.sibling)
        self.store = pltpu.make_async_copy(self.done, spot, sem)
        self.store.start()

    def seventh(self):
        whole, spot = self.block(self.result, -1), self.block(self.result, -1, 0)
        self.arrived(whole, 7)
        self.put(spot, spot, 9, self.plus)
        self.put(whole, whole, 12, self.sibling)
        whole, spot = self.block(self.result, 1), self.block(self.result, 1, 1)
        self.arrived(whole, 8)
        self.put(spot, spot, 10, self.minus)
        self.put(whole, whole, 13, self.sibling)

    def eighth(self):
        whole = self.block(self.result, 2)
        self.arrived(self.block(self.result, 2, 0), 9)
        self.arrived(self.block(self.result, 2, 1), 10)
        self.put(whole, whole, 14, self.sibling)

    def finish(self):
        for i in range(11, 15):
            self.arrived(self.block(self.result, 0), i)
        self.each(lambda i: self.piece_copy(i).wait_send())
        self.each(lambda i: self.back_copy(i).wait_send())
        self.store.wait()


def back_kernel(
    rows_hbm, gg_ref, x_hbm, gates_ref, hidden_hbm, gm_ref, ga_ref, router_ref, cot_hbm, tok_hbm,
    mixed_hbm, query_hbm, kv_hbm, cos_hbm, sin_hbm, routes_ref, len_ref,
    probs_hbm, wo_hbm, wq_hbm, wk_hbm, wv_hbm, o_hbm, pg_hbm, pu_hbm, pd_hbm,
    hop_g_hbm, hop_u_hbm, hop_d_hbm,
    layer_hbm, input_hbm, gate_hbm, up_hbm, down_hbm, q_hbm, o_sum_hbm, kv_sum_hbm, narrow_hbm,
    layer_ref, input_ref, gate_out, up_out, down_out,
    rows_ref, x_ref, hidden_ref, cot_ref, tok_ref, mixed_ref, query_ref, kv_ref, turns,
    probs, wo, wq, wk, wv, o_buf, rb, rc, rd, re,
    pg, pu, pd, hop_g, hop_u, hop_d, low_g, low_u, low_d, high_g, high_u, high_d,
    grad_mixed, grad_query, grad_kv, kv_hops, kv_low, kv_high,
    dq_out, do_out, dkv_out, narrow_ref,
    their_a, their_b, their_c, their_n, low_a, low_b, low_c, low_n, high_a, high_b, high_c, high_n,
    hop_a, hop_b, hop_c, hop_n, piece_a, piece_b, piece_c, piece_n, done_a, done_b, done_c, done_n,
    send_sem, recv_sem, local_sem, t_recv, plane_send, plane_recv, back_send, back_recv,
):
    p, q, y, core = place()
    spot = (p, q, y, core)
    sibling = (chip_of(p, q, core) * 2 + 1 - core, y)
    ahead, behind = device(p, q, y + 1, core), device(p, q, y - 1, core)
    net = Sends(send_sem, recv_sem)
    first = pl.multiple_of(y * TOK, TOK)
    pairs = (
        (o_hbm, o_buf), (wo_hbm, wo), (probs_hbm, probs), (wq_hbm, wq), (wk_hbm, wk), (wv_hbm, wv),
        (pg_hbm, pg), (pu_hbm, pu), (pd_hbm, pd),
        (hop_g_hbm, hop_g), (hop_u_hbm, hop_u), (hop_d_hbm, hop_d),
        (rows_hbm, rows_ref), (x_hbm, x_ref), (hidden_hbm, hidden_ref), (cot_hbm, cot_ref),
        (tok_hbm, tok_ref), (mixed_hbm, mixed_ref), (query_hbm, query_ref), (kv_hbm, kv_ref),
        (cos_hbm.at[pl.ds(first, TOK)], turns.at[0]), (sin_hbm.at[pl.ds(first, TOK)], turns.at[1]),
    )
    loads = [pltpu.make_async_copy(s, d, local_sem.at[i]) for i, (s, d) in enumerate(pairs)]
    for load in loads:
        load.start()
    plane = PlaneReduce(net, spot, o_buf, rb, rc, rd, re, 0)

    def unit(k, axis, source, result, span, rows, first, piece, *buffers):
        sems = [ref.at[k] for ref in (t_recv, plane_send, plane_recv, back_send, back_recv)]
        return Total(net, axis, source, result, span, rows, first, piece, buffers, sems)

    sum_o = [
        unit(
            h, 2 * h, do_out, o_sum_hbm, 512, 256, 256 * h, (16, 256),
            *[ref.at[h] for ref in (their_a, low_a, high_a, hop_a, piece_a, done_a)],
        )
        for h in range(2)
    ]
    sum_q = unit(
        2, 1, dq_out, q_hbm, 512, 512, 0, (32, 256), their_b, low_b, high_b, hop_b, piece_b, done_b
    )
    sum_kv = [
        unit(
            3 + h, 2 * h, dkv_out, kv_sum_hbm, 512, 256, 256 * h, (16, 256),
            *[ref.at[h] for ref in (their_c, low_c, high_c, hop_c, piece_c, done_c)],
        )
        for h in range(2)
    ]
    sum_n = unit(
        5, 0, narrow_ref, narrow_hbm, 64, 64, 0, (8, 128),
        their_n, low_n, high_n, hop_n, piece_n, done_n,
    )
    late = [*sum_kv, sum_n]
    everyone = [*sum_o, sum_q, *late]
    here = sum_q.here
    partners = [
        sum_q.at([here[0] + i, here[1] + j, here[2] + k])
        for i in range(4)
        for j in range(4)
        for k in range(4)
        if (i or j or k) and not (i and j and k)
    ]
    greet(partners + [sibling])
    loads[0].wait()
    plane.begin()
    for load in loads[6:16]:
        load.wait()

    def block(ref, step, rows=None):
        span = pl.ds(pl.multiple_of(wrap(y + step) * TOK, TOK), TOK)
        return ref.at[:, span] if rows is None else ref.at[rows, span]

    def down_block(ref, step):
        return ref.at[pl.ds(pl.multiple_of(wrap(y + step) * TOK, TOK), TOK)]

    top, bottom = pl.ds(0, 512), pl.ds(512, 512)

    def weight_portion(step, which):
        if which == 0:
            return [block(pg, step), block(pu, step, top)]
        return [block(pu, step, bottom), down_block(pd, step)]

    weights = RingReduce(
        net, 24, ahead, behind, weight_portion,
        ([hop_g, hop_u.at[top]], [hop_u.at[bottom], hop_d]),
        ([low_g, low_u.at[top]], [low_u.at[bottom], low_d]),
        ([high_g, high_u.at[top]], [high_u.at[bottom], high_d]),
    )
    weights.direct()

    row = lax.broadcasted_iota(jnp.int32, (TOK, 1), 0) + y * TOK
    upstream = jnp.where(row < len_ref[0], cot_ref[...].astype(F32), 0.0)
    gates = gates_ref[...]
    grad_gates = gg_ref[...].reshape(TOK, TOK).T
    grad_logits = gates * (grad_gates - jnp.sum(gates * grad_gates, axis=1, keepdims=True))
    grad_logits = grad_logits.astype(BF)
    wide = lax.dot_general(
        widen(), router_ref[...], (((0,), (0,)), ((), ())), preferred_element_type=F32
    ).astype(BF)
    by_row = (((0,), (0,)), ((), ()))
    by_col = (((1,), (1,)), ((), ()))
    grad_normed = rows_ref[...] + jnp.dot(grad_logits, wide, preferred_element_type=F32)
    hidden = hidden_ref[...]
    scale = root(hidden)
    grad_gain_moe = jnp.sum(grad_normed * hidden * scale, axis=0, keepdims=True)
    scaled = grad_normed * gm_ref[...]
    pull = jnp.mean(scaled * hidden, axis=1, keepdims=True)
    grad_hidden = upstream + scale * scaled - hidden * (scale * scale * scale) * pull
    input_ref[...] = grad_hidden
    low = grad_hidden.astype(BF)
    loads[1].wait()
    grad_mixed[...] = lax.dot_general(low, wo[...], by_col, preferred_element_type=F32).astype(BF)
    narrow_ref[...] = lax.dot_general(grad_logits, x_ref[...], by_row, preferred_element_type=F32)
    named = routed_mask(routes_ref[...], lax.broadcasted_iota(jnp.int32, (TOK, 1), 0))
    counts = jnp.sum(named.T, axis=0, keepdims=True)
    narrow_ref[3:4, :] = grad_gain_moe
    narrow_ref[4:5, :] = jnp.zeros((1, D), F32)
    narrow_ref[4:5, 0:TOK] = counts
    for load in loads[16:]:
        load.wait()
    do_out[...] = lax.dot_general(
        mixed_ref[...], low, by_row, preferred_element_type=F32
    ).astype(BF)
    for one in sum_o:
        one.begin()

    cosine, sine = turns[0], turns[1]
    loads[2].wait()

    def attend(c, carry):
        span = pl.ds(pl.multiple_of(c * 128, 128), 128)
        value_span = pl.ds(pl.multiple_of(512 + c * 128, 128), 128)
        keys = kv_ref[:, :, span].reshape(512, 128)
        values = kv_ref[:, :, value_span].reshape(512, 128)
        grad_keys = jnp.zeros((512, 128), F32)
        grad_values = jnp.zeros((512, 128), F32)
        for half in range(2):
            m = c * 2 + half
            mine = pl.ds(pl.multiple_of(m * 128, 128), 128)
            pair = stack_heads(query_ref[:, mine].astype(F32), half)
            grad_pair = stack_heads(grad_mixed[:, mine].astype(F32), half)
            grad_probs = lax.dot_general(grad_pair, values, by_col, preferred_element_type=F32)
            prob = probs[m]
            wide_prob = prob.astype(F32)
            middle = jnp.sum(wide_prob * grad_probs, axis=1, keepdims=True)
            grad_scores = (wide_prob * (grad_probs - middle)).astype(BF)
            back = jnp.dot(grad_scores, keys, preferred_element_type=F32) * SCALE
            grad_query[:, mine] = turn(unstack_heads(back, half), cosine, -sine).astype(BF)
            grad_keys += lax.dot_general(grad_scores, pair, by_row, preferred_element_type=F32)
            grad_values += lax.dot_general(prob, grad_pair, by_row, preferred_element_type=F32)
        grad_kv[:, :, span] = (grad_keys * SCALE).astype(BF).reshape(4, TOK, 128)
        grad_kv[:, :, value_span] = grad_values.astype(BF).reshape(4, TOK, 128)
        return carry

    lax.fori_loop(0, 4, attend, 0)
    lo, hi = pl.ds(0, 64), pl.ds(64, 64)
    sums = RingReduce(
        net, 36, ahead, behind,
        lambda step, which: [grad_kv.at[wrap(y + step), hi if which else lo]],
        ([kv_hops.at[0]], [kv_hops.at[1]]),
        ([kv_low.at[lo]], [kv_low.at[hi]]),
        ([kv_high.at[lo]], [kv_high.at[hi]]),
    )
    sums.begin()
    sums.direct()
    for one in sum_o:
        one.second()
    plane.middle()
    tokens = tok_ref[...].astype(F32)
    scale = root(tokens)
    normed = (tokens * scale * ga_ref[...]).astype(BF)
    dq_out[...] = lax.dot_general(
        normed, grad_query[...], by_row, preferred_element_type=F32
    ).astype(BF)
    sum_q.begin()
    sums.middle()
    for load in loads[3:6]:
        load.wait()
    grad_normed = lax.dot_general(grad_query[...], wq[...], by_col, preferred_element_type=F32)
    sums.finish()
    both = grad_kv[y].astype(F32) + kv_low[...].astype(F32) + kv_high[...].astype(F32)
    grad_key = jnp.concatenate(
        [turn(both[:, c * 128 : (c + 1) * 128], cosine, -sine) for c in range(4)], axis=1
    ).astype(BF)
    grad_value = both[:, 512:].astype(BF)
    dkv_out[:, 0:512] = lax.dot_general(
        normed, grad_key, by_row, preferred_element_type=F32
    ).astype(BF)
    dkv_out[:, 512:1024] = lax.dot_general(
        normed, grad_value, by_row, preferred_element_type=F32
    ).astype(BF)
    sum_kv[0].begin()
    sum_kv[1].begin()
    sum_q.second()
    weights.middle(here=True)
    grad_normed += lax.dot_general(grad_key, wk[...], by_col, preferred_element_type=F32)
    grad_normed += lax.dot_general(grad_value, wv[...], by_col, preferred_element_type=F32)
    narrow_ref[2:3, :] = jnp.sum(grad_normed * tokens * scale, axis=0, keepdims=True)
    sum_n.begin()
    for one in late:
        one.second()
    for one in sum_o:
        one.third()
    scaled = grad_normed * ga_ref[...]
    pull = jnp.mean(scaled * tokens, axis=1, keepdims=True)
    input_ref[...] += scale * scaled - tokens * (scale * scale * scale) * pull
    for one in late:
        one.third()
    for one in sum_o:
        one.fourth()
    sum_q.third()
    plane.third()
    for one in late:
        one.fourth()
    for one in sum_o:
        one.fifth()
    plane.fourth()
    sum_q.fourth()
    for one in late:
        one.fifth()
    for i, one in enumerate(sum_o):
        one.sixth(local_sem.at[i])
    layer_ref[...] = (hidden_ref[...] + plane.finish()).astype(BF)
    sum_q.fifth()
    for i, one in enumerate(late):
        one.sixth(local_sem.at[3 + i])
    for one in sum_o:
        one.seventh()
    sum_q.sixth(local_sem.at[2])
    weights.finish()
    gate_out[...] = (
        block(pg, 0)[...].astype(F32) + low_g[...].astype(F32) + high_g[...].astype(F32)
    )
    up_out[...] = block(pu, 0)[...].astype(F32) + low_u[...].astype(F32) + high_u[...].astype(F32)
    down_out[...] = (
        down_block(pd, 0)[...].astype(F32) + low_d[...].astype(F32) + high_d[...].astype(F32)
    )
    stores = [
        pltpu.make_async_copy(src, dst, local_sem.at[9 + i])
        for i, (src, dst) in enumerate(
            (
                (layer_ref, layer_hbm),
                (input_ref, input_hbm),
                (gate_out, gate_hbm),
                (up_out, up_hbm),
                (down_out, down_hbm),
            )
        )
    ]
    for store in stores:
        store.start()
    for one in late:
        one.seventh()
    for one in sum_o:
        one.eighth()
    sum_q.seventh()
    for one in late:
        one.eighth()
    sum_q.eighth()
    for one in everyone:
        one.finish()
    net.drain()
    for store in stores:
        store.wait()


def back(operands, arrays):
    any_space = pl.BlockSpec(memory_space=pl.ANY)
    vmem = pl.BlockSpec(memory_space=pltpu.VMEM)
    smem = pl.BlockSpec(memory_space=pltpu.SMEM)
    shape = jax.ShapeDtypeStruct
    dma = pltpu.SemaphoreType.DMA
    low = lambda *size: pltpu.VMEM(size, BF)
    return pl.pallas_call(
        back_kernel,
        out_shape=(
            shape((TOK, D), BF),
            shape((TOK, D), F32),
            shape((D, TOK), F32),
            shape((D, TOK), F32),
            shape((TOK, D), F32),
            shape((D, D), BF),
            shape((D, D), BF),
            shape((D, D), BF),
            shape((TOK, D), F32),
        ),
        in_specs=[
            any_space, vmem, any_space, vmem, any_space, *[vmem] * 3, *[any_space] * 7, vmem, smem,
            *[any_space] * 12,
        ],
        out_specs=(any_space,) * 9,
        scratch_shapes=[
            low(TOK, D),
            pltpu.VMEM((TOK, D), F32),
            pltpu.VMEM((D, TOK), F32),
            pltpu.VMEM((D, TOK), F32),
            pltpu.VMEM((TOK, D), F32),
            pltpu.VMEM((TOK, D), F32),
            low(TOK, D),
            pltpu.VMEM((TOK, D), F32),
            low(TOK, D),
            low(TOK, D),
            low(TOK, D),
            low(TOK, D),
            low(4, TOK, D),
            pltpu.VMEM((2, TOK, TOK), F32),
            low(8, 2 * TOK, 512),
            low(D, D),
            low(D, D),
            low(D, 512),
            low(D, 512),
            low(16, TOK, D),
            low(4, TOK, D),
            low(8, TOK, D),
            low(TOK, D),
            low(2, TOK, D),
            low(D, FF),
            low(D, FF),
            low(FF, D),
            low(D, TOK),
            low(D, TOK),
            low(TOK, D),
            low(D, TOK),
            low(D, TOK),
            low(TOK, D),
            low(D, TOK),
            low(D, TOK),
            low(TOK, D),
            low(TOK, D),
            low(TOK, D),
            low(4, TOK, D),
            low(2, 64, D),
            low(TOK, D),
            low(TOK, D),
            low(D, D),
            low(D, D),
            low(D, D),
            pltpu.VMEM((TOK, D), F32),
            low(2, 256, D),
            low(512, D),
            low(2, 256, D),
            pltpu.VMEM((64, D), F32),
            low(2, 64, D),
            low(128, D),
            low(2, 64, D),
            pltpu.VMEM((16, D), F32),
            low(2, 64, D),
            low(128, D),
            low(2, 64, D),
            pltpu.VMEM((16, D), F32),
            low(2, 64, D),
            low(128, D),
            low(2, 64, D),
            pltpu.VMEM((16, D), F32),
            low(2, 16, 16, 256),
            low(16, 32, 256),
            low(2, 16, 16, 256),
            pltpu.VMEM((16, 8, 128), F32),
            low(2, 64, D),
            low(128, D),
            low(2, 64, D),
            pltpu.VMEM((16, D), F32),
            dma((160,)),
            dma((42,)),
            dma((22,)),
            dma((6, 15)),
            dma((6, 16)),
            dma((6, 16)),
            dma((6, 16)),
            dma((6, 16)),
        ],
        compiler_params=pltpu.CompilerParams(
            collective_id=4, has_side_effects=True, vmem_limit_bytes=VMEM_BYTES
        ),
        name="back",
    )(*operands, *arrays)


def results_kernel(
    q_ref, o_ref, kv_ref, n_ref, layer_ref, input_ref, gate_ref, up_ref, down_ref,
    q_out, o_out, k_out, v_out, router_out, one_out, two_out, count_out,
    layer_out, input_out, gate_out, up_out, down_out,
):
    layer_out[...] = layer_ref[...]
    input_out[...] = input_ref[...]
    gate_out[0] = gate_ref[...]
    up_out[0] = up_ref[...]
    down_out[0] = down_ref[...]
    q_out[...] = q_ref[...].astype(F32)
    o_out[...] = o_ref[...].astype(F32)
    k_out[...] = kv_ref[:, 0:512].astype(F32)
    v_out[...] = kv_ref[:, 512:1024].astype(F32)

    @pl.when(pl.program_id(0) == 0)
    def _():
        for j in range(16):
            router_out[2 * j : 2 * j + 2, :] = n_ref[8 * j : 8 * j + 2, :]
        one_out[...] = n_ref[2:3, :]
        two_out[...] = n_ref[3:4, :]
        count_out[...] = n_ref[4:5, 0:EXPERTS].astype(jnp.int32)


def results(q, o, kv, narrow, *own):
    rows = 256
    some = rows * TOK // D
    first = lambda *size: pl.BlockSpec((1, *size), lambda i: (0, i, 0))
    block = lambda width: pl.BlockSpec((rows, width), lambda i: (i, 0))
    whole = lambda *size: pl.BlockSpec(size, lambda i: (0, 0))
    shape = jax.ShapeDtypeStruct
    return pl.pallas_call(
        results_kernel,
        grid=(D // rows,),
        out_shape=(
            shape((D, D), F32),
            shape((D, D), F32),
            shape((D, 512), F32),
            shape((D, 512), F32),
            shape((EXPERTS, D), F32),
            shape((1, D), F32),
            shape((1, D), F32),
            shape((1, EXPERTS), jnp.int32),
            shape((TOK, D), BF),
            shape((TOK, D), F32),
            shape((1, D, TOK), F32),
            shape((1, D, TOK), F32),
            shape((1, TOK, D), F32),
        ),
        in_specs=[
            block(D), block(D), block(D), whole(TOK, D),
            pl.BlockSpec((some, D), lambda i: (i, 0)),
            pl.BlockSpec((some, D), lambda i: (i, 0)),
            block(TOK), block(TOK),
            pl.BlockSpec((some, D), lambda i: (i, 0)),
        ],
        out_specs=(
            block(D), block(D), block(512), block(512),
            whole(EXPERTS, D), whole(1, D), whole(1, D), whole(1, EXPERTS),
            pl.BlockSpec((some, D), lambda i: (i, 0)),
            pl.BlockSpec((some, D), lambda i: (i, 0)),
            first(rows, TOK), first(rows, TOK), first(some, D),
        ),
        name="results",
    )(q, o, kv, narrow, *own)


def shards(
    tokens,
    w_query,
    w_key,
    w_value,
    w_output,
    gain_attn,
    gain_moe,
    router,
    w_gate,
    w_up,
    w_down,
    cotangent,
    routes,
    lengths,
):
    (
        gates, grad_rows, grad_gates, hidden, x, mixed, query, kv, probs, out_parts, part_gate,
        part_up, part_down, *far_parts,
    ) = main(
        tokens, w_query, w_key, w_value, w_output, gain_attn, gain_moe, router.T, cotangent,
        routes.T, lengths, w_gate, w_up, w_down,
    )
    cosine, sine = turn_tables()
    layer_out, grad_input, grad_gate, grad_up, grad_down, sum_q, sum_o, sum_kv, narrow = back(
        (
            grad_rows, grad_gates, x, gates, hidden, gain_moe.reshape(1, D),
            gain_attn.reshape(1, D), router.T, cotangent, tokens, mixed, query, kv,
            jnp.asarray(cosine), jnp.asarray(sine), routes.T, lengths,
        ),
        (
            probs, w_output, w_query, w_key, w_value, out_parts, part_gate, part_up,
            part_down.reshape(FF, D),
            *far_parts,
        ),
    )
    (
        grad_q, grad_o, grad_k, grad_v, grad_router, gain_one, gain_two, counts,
        layer_out, grad_input, grad_gate, grad_up, grad_down,
    ) = results(
        sum_q, sum_o, sum_kv, narrow, layer_out, grad_input, grad_gate, grad_up, grad_down
    )
    return (
        layer_out,
        grad_input,
        grad_q,
        grad_k,
        grad_v,
        grad_o,
        gain_one.reshape(D),
        gain_two.reshape(D),
        grad_router.T,
        grad_gate,
        grad_up,
        grad_down,
        counts.reshape(EXPERTS),
    )


def solution(mesh):
    in_specs = (
        P(("dp", "hid"), None),
        P(),
        P(),
        P(),
        P(),
        P(),
        P(),
        P(),
        P("dp", None, "hid"),
        P("dp", None, "hid"),
        P("dp", "hid", None),
        P(("dp", "hid"), None),
        P(("dp", "hid"), None),
        P("dp"),
    )
    out_specs = (
        P(("dp", "hid"), None),
        P(("dp", "hid"), None),
        P(),
        P(),
        P(),
        P(),
        P(),
        P(),
        P(),
        P("dp", None, "hid"),
        P("dp", None, "hid"),
        P("dp", "hid", None),
        P(),
    )
    return jax.shard_map(shards, mesh=mesh, in_specs=in_specs, out_specs=out_specs, check_vma=False)
```

```python
import jax
import jax.numpy as jnp
import numpy as np
from jax import lax
from jax.experimental import pallas as pl
from jax.experimental.pallas import tpu as pltpu
from jax.sharding import PartitionSpec as P

D = 1024
HEADS = 16
KV_HEADS = 8
HEAD_DIM = 64
EXPERTS = 32
TOP = 8
FF = 512
TOK = 128

MESH = pl.DeviceIdType.MESH
BF = jnp.bfloat16
F32 = jnp.float32
SLOTS = 48
VMEM_BYTES = 60 * 2**20


def wrap(value):
    return lax.rem(value + 4, 4)


def place():
    dp = lax.axis_index("dp")
    y = lax.axis_index("hid")
    core = lax.rem(dp, 2)
    x = lax.div(dp, 8)
    z = lax.rem(lax.div(dp, 2), 4)
    p = jnp.where(core == 0, x, z)
    q = jnp.where(core == 0, z, x)
    return p, q, y, core


def device(p, q, y, core):
    p, q = wrap(p), wrap(q)
    return (jnp.where(core == 0, p * 8 + q * 2, q * 8 + p * 2) + core, wrap(y))


def chip_of(p, q, core):
    p, q = wrap(p), wrap(q)
    return jnp.where(core == 0, p * 4 + q, q * 4 + p)


def greet(devices):
    barrier = pltpu.get_barrier_semaphore()
    for other in devices:
        pl.semaphore_signal(barrier, inc=1, device_id=other, device_id_type=MESH)
    pl.semaphore_wait(barrier, len(devices))


class Sends:
    def __init__(self, send_sem, recv_sem):
        self.send_sem, self.recv_sem, self.made = send_sem, recv_sem, []

    def start(self, source, target, recv, to):
        self.put(source, target, self.recv_sem.at[recv], to)

    def put(self, source, target, sem, to):
        copy = pltpu.make_async_remote_copy(
            src_ref=source,
            dst_ref=target,
            send_sem=self.send_sem.at[len(self.made)],
            recv_sem=sem,
            device_id=to,
            device_id_type=MESH,
        )
        copy.start()
        self.made.append(copy)

    def arrived(self, ref, recv):
        pltpu.make_async_copy(ref, ref, self.recv_sem.at[recv]).wait()

    def drain(self):
        for copy in self.made:
            copy.wait_send()
        self.made = []


def slab(buffer, p, q):
    return buffer.at[wrap(p) * 4 + wrap(q)]


HALF = HEAD_DIM // 2
SCALE = HEAD_DIM**-0.5


def turn_tables():
    inverse = 10000.0 ** (-np.arange(HALF, dtype=np.float32) / HALF)
    phases = np.arange(4 * TOK, dtype=np.float32)[:, None] * inverse[None, :]
    cosine = np.tile(np.cos(phases), (1, 4)).astype(np.float32)
    sine = np.sin(phases)
    sine = np.tile(np.concatenate([-sine, sine], axis=1), (1, 2)).astype(np.float32)
    return cosine, sine


def lanes(rows, width=128):
    return lax.broadcasted_iota(jnp.int32, (rows, width), 1)


def turn(chunk, cosine, sine):
    front = lax.rem(lanes(chunk.shape[0]), HEAD_DIM) < HALF
    swapped = jnp.where(front, pltpu.roll(chunk, 128 - HALF, 1), pltpu.roll(chunk, HALF, 1))
    return chunk * cosine + swapped * sine


def stack_heads(chunk, half):
    low = lanes(chunk.shape[0]) < HEAD_DIM
    rolled = pltpu.roll(chunk, HEAD_DIM, 1)
    if half == 0:
        pair = (jnp.where(low, chunk, 0.0), jnp.where(low, rolled, 0.0))
    else:
        pair = (jnp.where(low, 0.0, rolled), jnp.where(low, 0.0, chunk))
    return jnp.concatenate(pair, axis=0).astype(BF)


def unstack_heads(pair, half):
    first, second = pair[:TOK], pair[TOK:]
    low = lanes(TOK) < HEAD_DIM
    if half == 0:
        return jnp.where(low, first, pltpu.roll(second, HEAD_DIM, 1))
    return jnp.where(low, pltpu.roll(first, HEAD_DIM, 1), second)


def root(values):
    return lax.rsqrt(jnp.mean(values * values, axis=1, keepdims=True) + 1e-06)


def widen():
    row = lax.broadcasted_iota(jnp.int32, (EXPERTS, TOK), 0)
    lane = lax.broadcasted_iota(jnp.int32, (EXPERTS, TOK), 1)
    return jnp.where(lane == lax.div(row, 2) * 8 + lax.rem(row, 2), 1.0, 0.0).astype(BF)


def routed_mask(routes, expert):
    hit = jnp.zeros((TOK, TOK), F32)
    for k in range(TOP):
        hit = hit + jnp.where(routes[k : k + 1, :] == expert, 1.0, 0.0)
    return hit


def wide_experts():
    row = lax.broadcasted_iota(jnp.int32, (TOK, 1), 0)
    return jnp.where(lax.rem(row, 8) < 2, lax.div(row, 8) * 2 + lax.rem(row, 8), -1)


class PlaneGather:
    def __init__(self, net, spot, slabs, base):
        self.net, self.spot, self.slabs, self.base = net, spot, slabs, base
        p, q, y, core = spot
        self.right, self.left = device(p + 1, q, y, core), device(p - 1, q, y, core)
        self.up, self.down = device(p, q + 1, y, core), device(p, q - 1, y, core)

    def slab(self, a, b):
        return slab(self.slabs, self.spot[0] + a, self.spot[1] + b)

    def send(self, ref, recv, to):
        self.net.start(ref, ref, self.base + recv, to)

    def arrived(self, ref, recv):
        self.net.arrived(ref, self.base + recv)

    def begin(self, own):
        for recv, to in ((0, self.right), (1, self.left), (4, self.up), (8, self.down)):
            self.net.start(own, self.slab(0, 0), self.base + recv, to)

    def second(self):
        s = self.slab(-1, 0)
        self.arrived(s, 0)
        self.send(s.at[0:64], 2, self.right)
        self.send(s, 5, self.up)
        s = self.slab(1, 0)
        self.arrived(s, 1)
        self.send(s.at[64:128], 3, self.left)
        self.send(s, 10, self.down)

    def third(self):
        s = self.slab(0, -1)
        self.arrived(s, 4)
        self.send(s, 12, self.up)
        s = self.slab(2, 0)
        self.arrived(s.at[0:64], 2)
        self.arrived(s.at[64:128], 3)
        self.send(s, 11, self.down)
        s = self.slab(-1, -1)
        self.arrived(s, 5)
        self.send(s, 13, self.up)
        self.send(self.slab(1, 0), 6, self.up)
        self.send(self.slab(2, 0), 7, self.up)
        self.send(self.slab(-1, 0), 9, self.down)

    def fourth(self, which):
        a, recv, far = ((1, 10, 14), (2, 11, 15))[which]
        s = self.slab(a, 1)
        self.arrived(s, recv)
        self.send(s, far, self.down)

    def finish(self):
        for a, b, recv in (
            (1, -1, 6), (2, -1, 7), (0, 1, 8), (-1, 1, 9),
            (0, 2, 12), (-1, 2, 13), (1, 2, 14), (2, 2, 15),
        ):
            self.arrived(self.slab(a, b), recv)


def main_kernel(
    tok_ref, wq_hbm, wk_hbm, wv_hbm, wo_hbm, ga_ref, gm_ref, router_ref, cot_ref, routes_ref,
    len_ref, cos_hbm, sin_hbm, wgs_hbm, wus_hbm, wds_hbm,
    gates_ref, grad_out, gg_out, hidden_hbm, x_hbm, mixed_hbm, query_hbm, kv_hbm,
    probs_hbm, o_hbm, dwg_hbm, dwu_hbm, dwd_hbm, hop_g_hbm, hop_u_hbm, hop_d_hbm,
    hidden_ref, x_ref, mixed_ref, query_ref, turns,
    wqo, wk, wv, u_own, kv, probs, bias, gt,
    xs, us, wg, wu, wd, gin, rank, ggo, picks, rows, slot_grads, acts, gparts, uparts,
    outs, pairs, o_buf, p_buf, rb, rc, rd, re, dwg, dwu,
    send_sem, recv_sem, g_send, g_recv, gg_send, gg_recv, local_sem, free_sem,
):
    p, q, y, core = place()
    spot = (p, q, y, core)
    sibling = (chip_of(p, q, core) * 2 + 1 - core, y)
    ahead, behind = device(p, q, y + 1, core), device(p, q, y - 1, core)
    up, down = device(p, q + 1, y, core), device(p, q - 1, y, core)
    right, left = device(p + 1, q, y, core), device(p - 1, q, y, core)
    others = [device(p + a, q + b, y, core) for a in range(4) for b in range(4) if a or b]
    my_chip = chip_of(p, q, core)
    net = Sends(send_sem, recv_sem)
    wq, wo = wqo.at[0], wqo.at[1]
    loads = {
        name: pltpu.make_async_copy(src, dst, local_sem.at[i])
        for i, (name, src, dst) in enumerate(
            (("k", wk_hbm, wk), ("v", wv_hbm, wv), ("q", wq_hbm, wq), ("o", wo_hbm, wo))
        )
    }
    for load in loads.values():
        load.start()
    first = pl.multiple_of(y * TOK, TOK)
    tables = [
        pltpu.make_async_copy(src.at[pl.ds(first, TOK)], turns.at[i], local_sem.at[16 + i])
        for i, src in enumerate((cos_hbm, sin_hbm))
    ]
    for load in tables:
        load.start()
    gather = PlaneGather(net, spot, us, 0)
    tokens_in = PlaneGather(net, spot, xs, 42)
    row = lax.broadcasted_iota(jnp.int32, (TOK, 1), 0) + y * TOK
    length = len_ref[0]
    u_own[...] = jnp.where(row < length, cot_ref[...].astype(F32), 0.0).astype(BF)
    greet(others + [ahead, behind, sibling])
    gather.begin(u_own)
    keep_own = pltpu.make_async_copy(u_own, gather.slab(0, 0), local_sem.at[4])
    keep_own.start()

    def weight(a, e, yy, rows=None):
        block = pl.ds(pl.multiple_of(wrap(yy) * TOK, TOK), TOK)
        if a == 2:
            return wd.at[e, block, :]
        full = (wg, wu)[a]
        return full.at[e, :, block] if rows is None else full.at[e, rows, block]

    shards = (wgs_hbm.at[0], wus_hbm.at[0], wds_hbm.at[0])
    top, bottom = pl.ds(0, 512), pl.ds(512, 512)
    keep = []

    def send_weight(a):
        net.start(shards[a], weight(a, core, y), 20 + a, ahead)
        net.start(shards[a], weight(a, core, y), 23 + a, behind)
        net.start(shards[a], weight(a, core, y), 30 + a, sibling)
        keep.append(pltpu.make_async_copy(shards[a], weight(a, core, y), local_sem.at[5 + a]))
        keep[-1].start()

    def pass_weight(a):
        before, after = weight(a, core, y - 1), weight(a, core, y + 1)
        net.arrived(before, 20 + a)
        if a == 0:
            net.start(before, before, 26, ahead)
        if a == 1:
            spot = weight(1, core, y - 1, top)
            net.start(spot, spot, 27, ahead)
        net.start(before, before, 33 + a, sibling)
        net.arrived(after, 23 + a)
        if a == 1:
            spot = weight(1, core, y + 1, bottom)
            net.start(spot, spot, 28, behind)
        if a == 2:
            net.start(after, after, 29, behind)
        net.start(after, after, 36 + a, sibling)

    send_weight(0)
    tokens = tok_ref[...].astype(F32)
    normed = (tokens * root(tokens) * ga_ref[...]).astype(BF)
    for load in tables:
        load.wait()
    cosine, sine = turns[0], turns[1]
    loads["k"].wait()
    keys = jnp.dot(normed, wk[...], preferred_element_type=F32)
    for c in range(4):
        span = slice(c * 128, (c + 1) * 128)
        kv[y, :, span] = turn(keys[:, span], cosine, sine).astype(BF)
    loads["v"].wait()
    kv[y, :, 512:1024] = jnp.dot(normed, wv[...], preferred_element_type=F32).astype(BF)
    own = kv.at[y]
    net.start(own, own, 16, ahead)
    net.start(own, own, 17, behind)

    loads["q"].wait()
    queries = jnp.dot(normed, wq[...], preferred_element_type=F32)
    for c in range(8):
        span = slice(c * 128, (c + 1) * 128)
        query_ref[:, span] = turn(queries[:, span], cosine, sine).astype(BF)
    key_pos = lanes(TOK, 512)
    bias[...] = jnp.where((key_pos <= row) & (key_pos < length), 0.0, -1e30)
    gather.second()
    s = kv.at[wrap(y - 1)]
    net.arrived(s, 16)
    net.start(s.at[0:64], s.at[0:64], 18, ahead)
    s = kv.at[wrap(y + 1)]
    net.arrived(s, 17)
    net.start(s.at[64:128], s.at[64:128], 19, behind)
    gather.third()
    s = kv.at[wrap(y + 2)]
    net.arrived(s.at[0:64], 18)
    net.arrived(s.at[64:128], 19)
    send_weight(1)
    send_weight(2)
    pass_weight(0)
    gather.fourth(0)

    def attend(c, carry):
        span = pl.ds(pl.multiple_of(c * 128, 128), 128)
        keys = kv[:, :, span].reshape(512, 128)
        values = kv[:, :, pl.ds(pl.multiple_of(512 + c * 128, 128), 128)].reshape(512, 128)
        for half in range(2):
            m = c * 2 + half
            mine = pl.ds(pl.multiple_of(m * 128, 128), 128)
            pair = stack_heads(query_ref[:, mine].astype(F32), half)
            scores = lax.dot_general(
                pair, keys, (((1,), (1,)), ((), ())), preferred_element_type=F32
            )
            scores = scores * SCALE + jnp.concatenate([bias[...], bias[...]], axis=0)
            scores = jnp.exp(scores - jnp.max(scores, axis=1, keepdims=True))
            low = (scores * (1.0 / jnp.sum(scores, axis=1, keepdims=True))).astype(BF)
            probs[m] = low
            out = jnp.dot(low, values, preferred_element_type=F32)
            mixed_ref[:, mine] = unstack_heads(out, half).astype(BF)
        return carry

    lax.fori_loop(0, 4, attend, 0)
    gather.fourth(1)
    keep_probs = pltpu.make_async_copy(probs, probs_hbm, local_sem.at[8])
    keep_probs.start()
    loads["o"].wait()
    hidden = tokens + jnp.dot(mixed_ref[...], wo[...], preferred_element_type=F32)
    hidden_ref[...] = hidden
    x = (hidden * root(hidden) * gm_ref[...]).astype(BF)
    x_ref[...] = x
    tokens_in.begin(x_ref)
    tokens_in.slab(0, 0)[...] = x
    wide = lax.dot_general(
        widen(), router_ref[...], (((0,), (0,)), ((), ())), preferred_element_type=F32
    ).astype(BF)
    logits = lax.dot_general(x, wide, (((1,), (1,)), ((), ())), preferred_element_type=F32)
    routed = routed_mask(routes_ref[...], wide_experts()).T > 0
    logits = jnp.where(routed, logits, -1e30)
    weights = jnp.where(routed, jnp.exp(logits - jnp.max(logits, axis=1, keepdims=True)), 0.0)
    weights = weights * (1.0 / jnp.sum(weights, axis=1, keepdims=True))
    gates_ref[...] = weights
    gt[...] = weights.T.reshape(16, 8, TOK)

    def gate_copy(i):
        a, b = lax.div(i, 4), lax.rem(i, 4)
        return pltpu.make_async_remote_copy(
            src_ref=gt.at[chip_of(p + a, q + b, core)],
            dst_ref=gin.at[p * 4 + q],
            send_sem=g_send.at[i],
            recv_sem=g_recv.at[wrap(-a) * 4 + wrap(-b)],
            device_id=device(p + a, q + b, y, core),
            device_id_type=MESH,
        )

    def start_gate(i, _):
        gate_copy(i).start()
        return 0

    lax.fori_loop(1, 16, start_gate, 0)
    gin[p * 4 + q] = gt[my_chip]

    keeps = [
        pltpu.make_async_copy(src, dst, local_sem.at[18 + i])
        for i, (src, dst) in enumerate(
            (
                (hidden_ref, hidden_hbm),
                (x_ref, x_hbm),
                (mixed_ref, mixed_hbm),
                (query_ref, query_hbm),
                (kv, kv_hbm),
            )
        )
    ]
    for store in keeps:
        store.start()
    tokens_in.second()
    pass_weight(1)
    tokens_in.third()
    pass_weight(2)

    def take_gate(i, _):
        pltpu.make_async_copy(gin.at[0], gin.at[0], g_recv.at[i]).wait()
        return 0

    lax.fori_loop(1, 16, take_gate, 0)
    ids = lax.broadcasted_iota(jnp.int32, (TOK, TOK), 0)
    cols = lax.broadcasted_iota(jnp.int32, (TOK, TOK), 1)
    before = jnp.where(ids < cols, 1.0, 0.0).astype(BF)
    routed = jnp.where(gin[...].reshape(TOK, TOK) > 0, 1.0, 0.0).astype(BF)
    rank[...] = jnp.dot(routed, before, preferred_element_type=F32).reshape(16, 8, TOK)
    gather.finish()
    ggo[...] = jnp.zeros_like(ggo)
    slot_ids = lax.broadcasted_iota(jnp.int32, (SLOTS, TOK), 0).astype(F32)

    def source_of(g, j):
        side = jnp.where((j < 2) == (g == 1), 3, 1)
        b = jnp.where(g == 0, 0, jnp.where(g == 2, 2, side))
        a = jnp.where(j == 0, 0, jnp.where(j == 1, 3, jnp.where(j == 2, 1, 2)))
        return wrap(p + a) * 4 + wrap(q + b)

    def pick_source(g, j):
        src = source_of(g, j)
        token_rows, up_rows = xs[src], us[src]
        base = pl.multiple_of(g * 4 * SLOTS + j * SLOTS, 16)
        for e in range(2):
            gate_row = gin[src, e : e + 1, :]
            hit = (rank[src, e : e + 1, :] == slot_ids) & (gate_row > 0)
            pick = jnp.where(hit, 1.0, 0.0)
            pick_low = pick.astype(BF)
            picks[src, e * SLOTS : (e + 1) * SLOTS, :] = pick_low
            gate_col = jnp.sum(pick * gate_row, axis=1, keepdims=True)
            rows[e, pl.ds(base, SLOTS), :] = jnp.dot(
                pick_low, token_rows, preferred_element_type=F32
            ).astype(BF)
            picked = jnp.dot(pick_low, up_rows, preferred_element_type=F32)
            wqo[e, pl.ds(base, SLOTS), :] = picked.astype(BF)
            slot_grads[e, pl.ds(base, SLOTS), :] = (picked * gate_col).astype(BF)

    def run_expert(g, e):
        base = pl.multiple_of(g * 4 * SLOTS, 16)
        span = pl.ds(base, 4 * SLOTS)
        taken = rows[e, span, :]
        gate = jnp.dot(taken, wg[e], preferred_element_type=F32)
        upv = jnp.dot(taken, wu[e], preferred_element_type=F32)
        sig = 1.0 / (1.0 + jnp.exp(-gate))
        silu = gate * sig
        act = (silu * upv).astype(BF)
        acts[e, span, :] = act
        grad_act = lax.dot_general(
            slot_grads[e, span, :], wd[e], (((1,), (1,)), ((), ())), preferred_element_type=F32
        )
        ggp = (grad_act * upv * sig * (1.0 + gate * (1.0 - sig))).astype(BF)
        gup = (grad_act * silu).astype(BF)
        gparts[e, span, :] = ggp
        uparts[e, span, :] = gup
        pair = lax.dot_general(ggp, wg[e], (((1,), (1,)), ((), ())), preferred_element_type=F32)
        pair += lax.dot_general(gup, wu[e], (((1,), (1,)), ((), ())), preferred_element_type=F32)
        pairs[e] = pair.astype(BF)

    def spread(g, j):
        src = source_of(g, j)
        span = pl.ds(pl.multiple_of(j * SLOTS, 16), SLOTS)
        both = jnp.concatenate([pairs[0, span, :], pairs[1, span, :]], axis=0)
        p_buf[src] = lax.dot_general(
            picks[src], both, (((0,), (0,)), ((), ())), preferred_element_type=F32
        ).astype(BF)

    def run_output(g, e):
        span = pl.ds(pl.multiple_of(g * 4 * SLOTS, 16), 4 * SLOTS)
        out = jnp.dot(acts[e, span, :], wd[e], preferred_element_type=F32).astype(BF)
        outs[e] = out
        gg_col = jnp.sum(out.astype(F32) * wqo[e, span, :].astype(F32), axis=1, keepdims=True)
        for j in range(4):
            src = source_of(g, j)
            pick = picks[src, pl.ds(pl.multiple_of(e * SLOTS, 16), SLOTS), :].astype(F32)
            part = gg_col[j * SLOTS : (j + 1) * SLOTS]
            ggo[src, pl.ds(e, 1), :] = jnp.sum(pick * part, axis=0, keepdims=True)

    def spread_output(g, j):
        src = source_of(g, j)
        pick = picks[src]
        span = pl.ds(pl.multiple_of(j * SLOTS, 16), SLOTS)
        gates = jnp.concatenate(
            [
                pick[e * SLOTS : (e + 1) * SLOTS].astype(F32) * gin[src, e : e + 1, :]
                for e in range(2)
            ],
            axis=0,
        ).astype(BF)
        both = jnp.concatenate([outs[0, span, :], outs[1, span, :]], axis=0)
        o_buf[src] = lax.dot_general(
            gates, both, (((0,), (0,)), ((), ())), preferred_element_type=F32
        ).astype(BF)

    def output(g, carry):
        lax.fori_loop(0, 2, lambda e, c: (run_output(g, e), c)[1], 0)
        lax.fori_loop(0, 4, lambda j, c: (spread_output(g, j), c)[1], 0)
        return carry

    def pick(g):
        lax.fori_loop(0, 4, lambda j, c: (pick_source(g, j), c)[1], 0)

    OFF = (0, -1, 1, 2)
    R = 58

    def make(source, target, recv, to, index):
        return pltpu.make_async_remote_copy(
            src_ref=source,
            dst_ref=target,
            send_sem=send_sem.at[index],
            recv_sem=recv_sem.at[recv],
            device_id=to,
            device_id_type=MESH,
        )

    first = 80
    bounce = [
        (lambda j=j: make(slab(p_buf, p + OFF[j], q + 2), rb.at[j], R + j, up if j < 2 else down, first + j))
        for j in range(4)
    ]
    to_down = [
        (lambda j=j: make(slab(p_buf, p + OFF[j], q - 1), rc.at[4 + j], R + 8 + j, down, first + 4 + j))
        for j in range(4)
    ]
    to_up = [
        (lambda j=j: make(slab(p_buf, p + OFF[j], q + 1), rc.at[j], R + 4 + j, up, first + 8 + j))
        for j in range(4)
    ]

    def add_bounce(j):
        net.arrived(rb.at[j], R + j)
        target = slab(p_buf, p + OFF[j], q + 1 if j < 2 else q - 1)
        target[...] = (target[...].astype(F32) + rb[j].astype(F32)).astype(BF)

    def step(g, carry):
        @pl.when(g == 2)
        def _():
            for j in range(4):
                tokens_in.arrived(slab(xs, p + OFF[j], q + 2), 12 + j)

        @pl.when(g == 3)
        def _():
            tokens_in.arrived(slab(xs, p + 1, q - 1), 6)
            tokens_in.arrived(slab(xs, p + 2, q - 1), 7)
            tokens_in.arrived(slab(xs, p, q + 1), 8)
            tokens_in.arrived(slab(xs, p - 1, q + 1), 9)
            for j in range(2):
                to_down[j]().start()
                to_up[3 - j]().start()

        @pl.when(g >= 2)
        def _():
            pick(g)

        lax.fori_loop(0, 2, lambda e, c: (run_expert(g, e), c)[1], 0)
        lax.fori_loop(0, 4, lambda j, c: (spread(g, j), c)[1], 0)

        @pl.when(g == 2)
        def _():
            for j in range(4):
                bounce[j]().start()

        return carry

    keep_own.wait()
    pick(0)
    tokens_in.fourth(0)
    tokens_in.fourth(1)
    pick(1)
    net.arrived(weight(0, core, y + 2), 26)
    net.arrived(weight(1, core, y + 2, top), 27)
    net.arrived(weight(1, core, y + 2, bottom), 28)
    net.arrived(weight(2, core, y + 2), 29)
    for a in range(3):
        net.start(weight(a, core, y + 2), weight(a, core, y + 2), 39 + a, sibling)
    for i, ahead_by in enumerate((0, -1, 1, 2)):
        for a in range(3):
            net.arrived(weight(a, 1 - core, y + ahead_by), 30 + 3 * i + a)
    for copy in keep:
        copy.wait()
    lax.fori_loop(0, 4, step, 0)
    net.drain()
    pl.semaphore_signal(free_sem.at[0], inc=1, device_id=sibling, device_id_type=MESH)
    for other in (ahead, behind):
        pl.semaphore_signal(free_sem.at[1], inc=1, device_id=other, device_id_type=MESH)

    def weight_tile(e, t):
        cols = pl.ds(pl.multiple_of(t * 256, 256), 256)
        dims = (((0,), (0,)), ((), ()))
        lhs = rows[e, :, cols]
        dwg[e, cols, :] = lax.dot_general(lhs, gparts[e], dims, preferred_element_type=F32).astype(BF)
        dwu[e, cols, :] = lax.dot_general(lhs, uparts[e], dims, preferred_element_type=F32).astype(BF)
        us[pl.ds(4 * e, 4), :, cols] = (
            lax.dot_general(acts[e], slot_grads[e, :, cols], dims, preferred_element_type=F32)
            .astype(BF)
            .reshape(4, TOK, 256)
        )

    def weight_grads(e):
        lax.fori_loop(0, 4, lambda t, c: (weight_tile(e, t), c)[1], 0)

    weight_grads(1 - core)
    pl.semaphore_wait(free_sem.at[0], 1)
    theirs = us.at[pl.ds(4 * (1 - core), 4)]
    net.start(dwg.at[1 - core], wg.at[0], 76, sibling)
    net.start(dwu.at[1 - core], wu.at[0], 77, sibling)
    net.start(theirs, xs.at[pl.ds(8, 4)], 78, sibling)
    weight_grads(core)
    for j in (3, 1, 2, 0):
        add_bounce(j)
        (to_up if j < 2 else to_down)[j]().start()
    lax.fori_loop(0, 2, output, 0)

    def grad_block(ref, step, rows=None):
        span = pl.ds(pl.multiple_of(wrap(y + step) * TOK, TOK), TOK)
        return ref.at[:, span] if rows is None else ref.at[rows, span]

    def weight_portion(step, which):
        if which == 0:
            return [grad_block(dwg.at[core], step), grad_block(dwu.at[core], step, top)]
        return [grad_block(dwu.at[core], step, bottom), us.at[4 * core + wrap(y + step)]]

    def weight_merge(step):
        accumulate(grad_block(dwg.at[core], step), grad_block(wg.at[0], step))
        accumulate(grad_block(dwu.at[core], step), grad_block(wu.at[0], step))
        accumulate(us.at[4 * core + wrap(y + step)], xs.at[8 + wrap(y + step)])

    hops = (wu.at[1, :, 0:128], wu.at[1, :, 128:256], xs.at[12])
    ring = RingReduce(
        net, 79, ahead, behind, weight_portion,
        ([hops[0], wu.at[1, top, 128:256]], [wu.at[1, bottom, 128:256], hops[2]]), None, None,
    )
    for i, ref in enumerate((wg.at[0], wu.at[0], xs.at[pl.ds(8, 4)])):
        net.arrived(ref, 76 + i)
    weight_merge(2)
    pl.semaphore_wait(free_sem.at[1], 2)
    ring.begin()
    for around in (1, -1, 0):
        weight_merge(around)
    stores = [
        pltpu.make_async_copy(src, dst, local_sem.at[10 + i])
        for i, (src, dst) in enumerate(
            (
                (dwg.at[core], dwg_hbm),
                (dwu.at[core], dwu_hbm),
                (us.at[pl.ds(4 * core, 4)], dwd_hbm),
            )
        )
    ]
    for store in stores:
        store.start()
    lax.fori_loop(2, 4, output, 0)

    def gg_copy(i):
        a, b = lax.div(i, 4), lax.rem(i, 4)
        return pltpu.make_async_remote_copy(
            src_ref=ggo.at[wrap(p + a) * 4 + wrap(q + b)],
            dst_ref=gg_out.at[my_chip],
            send_sem=gg_send.at[i],
            recv_sem=gg_recv.at[wrap(-a) * 4 + wrap(-b)],
            device_id=device(p + a, q + b, y, core),
            device_id_type=MESH,
        )

    def start_gg(i, _):
        gg_copy(i).start()
        return 0

    lax.fori_loop(1, 16, start_gg, 0)
    gg_out[my_chip] = ggo[p * 4 + q]
    o_store = pltpu.make_async_copy(o_buf, o_hbm, local_sem.at[9])
    o_store.start()

    def gather_sum(j):
        net.arrived(rc.at[j], R + 4 + j)
        net.arrived(rc.at[4 + j], R + 8 + j)
        target = slab(p_buf, p + OFF[j], q)
        target[...] = (
            target[...].astype(F32) + rc[j].astype(F32) + rc[4 + j].astype(F32)
        ).astype(BF)

    last = first + 12
    lo, hi = pl.ds(0, 64), pl.ds(64, 64)
    far_slab, next_slab, prev_slab = slab(p_buf, p + 2, q), slab(p_buf, p + 1, q), slab(p_buf, p - 1, q)
    tail = [
        make(far_slab.at[lo], rd.at[lo], R + 12, right, last),
        make(far_slab.at[hi], rd.at[hi], R + 13, left, last + 1),
        make(next_slab.at[hi], re.at[0, hi], R + 14, right, last + 2),
        make(prev_slab.at[lo], re.at[1, lo], R + 15, left, last + 3),
        make(next_slab.at[lo], re.at[0, lo], R + 16, right, last + 4),
        make(prev_slab.at[hi], re.at[1, hi], R + 17, left, last + 5),
    ]
    gather_sum(3)
    tail[0].start()
    tail[1].start()
    gather_sum(2)
    tail[2].start()
    gather_sum(1)
    tail[3].start()
    gather_sum(0)
    net.arrived(rd.at[lo], R + 12)
    next_slab[lo] = (next_slab[lo].astype(F32) + rd[lo].astype(F32)).astype(BF)
    tail[4].start()
    net.arrived(rd.at[hi], R + 13)
    prev_slab[hi] = (prev_slab[hi].astype(F32) + rd[hi].astype(F32)).astype(BF)
    tail[5].start()
    ring.arrived(ring.hops[0], 0)
    ring.arrived(ring.hops[1], 1)
    for i, (src, dst) in enumerate(zip(hops, (hop_g_hbm, hop_u_hbm, hop_d_hbm))):
        stores.append(pltpu.make_async_copy(src, dst, local_sem.at[13 + i]))
        stores[-1].start()
    net.arrived(re.at[0, hi], R + 14)
    net.arrived(re.at[1, lo], R + 15)
    net.arrived(re.at[0, lo], R + 16)
    net.arrived(re.at[1, hi], R + 17)
    grad_out[...] = slab(p_buf, p, q)[...].astype(F32) + re[0].astype(F32) + re[1].astype(F32)

    def take_gg(i, _):
        pltpu.make_async_copy(ggo.at[0], ggo.at[0], gg_recv.at[i]).wait()
        return 0

    lax.fori_loop(1, 16, take_gg, 0)
    for copy in bounce + to_down + to_up:
        copy().wait_send()
    for copy in tail:
        copy.wait_send()

    def drain_small(i, _):
        gate_copy(i).wait_send()
        gg_copy(i).wait_send()
        return 0

    lax.fori_loop(1, 16, drain_small, 0)
    net.drain()
    o_store.wait()
    for store in stores:
        store.wait()
    keep_probs.wait()
    for store in keeps:
        store.wait()


def main(tokens, wq, wk, wv, wo, ga, gm, router, cotangent, routes, lengths, wg, wu, wd):
    cosine, sine = turn_tables()
    any_space = pl.BlockSpec(memory_space=pl.ANY)
    vmem = pl.BlockSpec(memory_space=pltpu.VMEM)
    smem = pl.BlockSpec(memory_space=pltpu.SMEM)
    shape = jax.ShapeDtypeStruct
    dma = pltpu.SemaphoreType.DMA
    slots = 16 * SLOTS
    low = lambda *size: pltpu.VMEM(size, BF)
    return pl.pallas_call(
        main_kernel,
        out_shape=(
            shape((TOK, TOK), F32),
            shape((TOK, D), F32),
            shape((16, 8, TOK), F32),
            shape((TOK, D), F32),
            shape((TOK, D), BF),
            shape((TOK, D), BF),
            shape((TOK, D), BF),
            shape((4, TOK, D), BF),
            shape((8, 2 * TOK, 512), BF),
            shape((16, TOK, D), BF),
            shape((D, FF), BF),
            shape((D, FF), BF),
            shape((4, TOK, D), BF),
            shape((D, TOK), BF),
            shape((D, TOK), BF),
            shape((TOK, D), BF),
        ),
        in_specs=[vmem] + [any_space] * 4 + [vmem] * 5 + [smem] + [any_space] * 5,
        out_specs=(vmem,) * 3 + (any_space,) * 13,
        scratch_shapes=[
            pltpu.VMEM((TOK, D), F32),
            low(TOK, D),
            low(TOK, D),
            low(TOK, D),
            pltpu.VMEM((2, TOK, TOK), F32),
            low(2, D, D),
            low(D, 512),
            low(D, 512),
            low(TOK, D),
            low(4, TOK, D),
            low(8, 2 * TOK, 512),
            pltpu.VMEM((TOK, 512), F32),
            pltpu.VMEM((16, 8, TOK), F32),
            low(16, TOK, D),
            low(16, TOK, D),
            low(2, D, FF),
            low(2, D, FF),
            low(2, FF, D),
            pltpu.VMEM((16, 8, TOK), F32),
            pltpu.VMEM((16, 8, TOK), F32),
            pltpu.VMEM((16, 8, TOK), F32),
            low(16, 2 * SLOTS, TOK),
            low(2, slots, D),
            low(2, slots, D),
            low(2, slots, FF),
            low(2, slots, FF),
            low(2, slots, FF),
            low(2, 4 * SLOTS, D),
            low(2, 4 * SLOTS, D),
            low(16, TOK, D),
            low(16, TOK, D),
            low(4, TOK, D),
            low(8, TOK, D),
            low(TOK, D),
            low(2, TOK, D),
            low(2, D, FF),
            low(2, D, FF),
            dma((100,)),
            dma((83,)),
            dma((16,)),
            dma((16,)),
            dma((16,)),
            dma((16,)),
            dma((23,)),
            pltpu.SemaphoreType.REGULAR((2,)),
        ],
        compiler_params=pltpu.CompilerParams(
            collective_id=1, has_side_effects=True, vmem_limit_bytes=VMEM_BYTES
        ),
        name="main",
    )(
        tokens, wq, wk, wv, wo, ga.reshape(1, D), gm.reshape(1, D), router, cotangent, routes,
        lengths, jnp.asarray(cosine), jnp.asarray(sine), wg, wu, wd,
    )


def accumulate(target, *terms):
    total = target[...].astype(F32)
    for term in terms:
        total += term[...].astype(F32)
    target[...] = total.astype(target.dtype)


class PlaneReduce:
    OFF = (0, -1, 1, 2)

    def __init__(self, net, spot, slabs, rb, rc, rd, re, base):
        self.net, self.spot, self.slabs, self.base = net, spot, slabs, base
        self.rb, self.rc, self.rd, self.re = rb, rc, rd, re
        p, q, y, core = spot
        self.right, self.left = device(p + 1, q, y, core), device(p - 1, q, y, core)
        self.up, self.down = device(p, q + 1, y, core), device(p, q - 1, y, core)

    def slab(self, a, b):
        return slab(self.slabs, self.spot[0] + a, self.spot[1] + b)

    def send(self, source, target, recv, to):
        self.net.start(source, target, self.base + recv, to)

    def arrived(self, ref, recv):
        self.net.arrived(ref, self.base + recv)

    def bounce(self):
        for j in range(4):
            to = self.up if j < 2 else self.down
            self.send(self.slab(self.OFF[j], 2), self.rb.at[j], j, to)

    def to_up(self, j):
        self.send(self.slab(self.OFF[j], 1), self.rc.at[j], 4 + j, self.up)

    def to_down(self, j):
        self.send(self.slab(self.OFF[j], -1), self.rc.at[4 + j], 8 + j, self.down)

    def begin(self):
        self.bounce()
        for j in (3, 2):
            self.to_up(j)
        for j in (0, 1):
            self.to_down(j)

    def middle(self):
        for j in (3, 1, 2, 0):
            self.arrived(self.rb.at[j], j)
            accumulate(self.slab(self.OFF[j], 1 if j < 2 else -1), self.rb.at[j])
            (self.to_up if j < 2 else self.to_down)(j)

    def column(self, j):
        self.arrived(self.rc.at[j], 4 + j)
        self.arrived(self.rc.at[4 + j], 8 + j)
        accumulate(self.slab(self.OFF[j], 0), self.rc.at[j], self.rc.at[4 + j])

    def third(self):
        lo, hi = pl.ds(0, 64), pl.ds(64, 64)
        rd, re = self.rd, self.re
        self.column(3)
        self.send(self.slab(2, 0).at[lo], rd.at[lo], 12, self.right)
        self.send(self.slab(2, 0).at[hi], rd.at[hi], 13, self.left)
        self.column(2)
        self.send(self.slab(1, 0).at[hi], re.at[0, hi], 14, self.right)
        self.column(1)
        self.send(self.slab(-1, 0).at[lo], re.at[1, lo], 15, self.left)

    def fourth(self):
        lo, hi = pl.ds(0, 64), pl.ds(64, 64)
        rd, re = self.rd, self.re
        self.arrived(rd.at[lo], 12)
        accumulate(self.slab(1, 0).at[lo], rd.at[lo])
        self.send(self.slab(1, 0).at[lo], re.at[0, lo], 16, self.right)
        self.arrived(rd.at[hi], 13)
        accumulate(self.slab(-1, 0).at[hi], rd.at[hi])
        self.send(self.slab(-1, 0).at[hi], re.at[1, hi], 17, self.left)
        self.column(0)

    def finish(self):
        lo, hi = pl.ds(0, 64), pl.ds(64, 64)
        re = self.re
        self.arrived(re.at[0, hi], 14)
        self.arrived(re.at[1, lo], 15)
        self.arrived(re.at[0, lo], 16)
        self.arrived(re.at[1, hi], 17)
        return self.slab(0, 0)[...].astype(F32) + re[0].astype(F32) + re[1].astype(F32)


class RingReduce:
    def __init__(self, net, base, ahead, behind, portion, hops, lows, highs):
        self.net, self.base, self.ahead, self.behind = net, base, ahead, behind
        self.portion, self.hops, self.lows, self.highs = portion, hops, lows, highs
        self.n = len(hops[0])

    def send(self, sources, targets, group, to):
        for i, (source, target) in enumerate(zip(sources, targets)):
            self.net.start(source, target, self.base + group * self.n + i, to)

    def arrived(self, refs, group):
        for i, ref in enumerate(refs):
            self.net.arrived(ref, self.base + group * self.n + i)

    def begin(self):
        self.send(self.portion(2, 0), self.hops[0], 0, self.ahead)
        self.send(self.portion(2, 1), self.hops[1], 1, self.behind)

    def direct(self):
        self.send(self.portion(1, 1), self.lows[1], 2, self.ahead)
        self.send(self.portion(-1, 0), self.highs[0], 3, self.behind)

    def middle(self, here=False):
        for which, step, targets, to in (
            (0, 1, self.lows[0], self.ahead),
            (1, -1, self.highs[1], self.behind),
        ):
            if not here:
                self.arrived(self.hops[which], which)
            refs = self.portion(step, which)
            for ref, hop in zip(refs, self.hops[which]):
                accumulate(ref, hop)
            self.send(refs, targets, 4 + which, to)

    def finish(self):
        self.arrived(self.lows[1], 2)
        self.arrived(self.highs[0], 3)
        self.arrived(self.lows[0], 4)
        self.arrived(self.highs[1], 5)


class Total:
    def __init__(self, net, axis, source, result, span, rows, first, piece, buffers, sems):
        self.net, self.axis, self.source, self.result = net, axis, source, result
        self.span, self.rows, self.first, self.piece_size = span, rows, first, piece
        self.theirs, self.low, self.high, self.hop, self.pieces, self.done = buffers
        self.recv, self.plane_send, self.plane_recv, self.back_send, self.back_recv = sems
        dp, y = lax.axis_index("dp"), lax.axis_index("hid")
        self.core = lax.rem(dp, 2)
        self.here = (lax.div(dp, 8), y, lax.rem(lax.div(dp, 2), 4))
        self.sibling = self.at(self.here, 1 - self.core)
        self.plus, self.minus = self.along(1), self.along(-1)
        self.plane = [i for i in range(3) if i != axis]
        self.slab_rows = rows // 4
        half = self.slab_rows // 2
        self.lo, self.hi = pl.ds(0, half), pl.ds(half, half)

    def at(self, spot, on=None):
        spot = [wrap(v) for v in spot]
        return (spot[0] * 8 + spot[2] * 2 + (self.core if on is None else on), spot[1])

    def along(self, step):
        return self.at([self.here[i] + (step if i == self.axis else 0) for i in range(3)])

    def arrived(self, ref, i):
        pltpu.make_async_copy(ref, ref, self.recv.at[i]).wait()

    def put(self, source, target, i, to):
        self.net.put(source, target, self.recv.at[i], to)

    def block(self, ref, step, part=None):
        size = self.slab_rows
        start = self.core * self.span + self.first + wrap(self.here[self.axis] + step) * size
        if part is not None:
            size = size // 2
            start += part * size
        return ref.at[pl.ds(pl.multiple_of(start, size), size)]

    def own(self, step):
        return self.block(self.source, step)

    def begin(self):
        start = (1 - self.core) * self.span + self.first
        theirs = self.source.at[pl.ds(pl.multiple_of(start, self.rows), self.rows)]
        self.put(theirs, self.theirs, 0, self.sibling)

    def merge(self, step):
        size = self.slab_rows
        start = wrap(self.here[self.axis] + step) * size
        accumulate(self.own(step), self.theirs.at[pl.ds(pl.multiple_of(start, size), size)])

    def second(self):
        lo, hi = self.lo, self.hi
        self.arrived(self.theirs, 0)
        self.merge(2)
        far = self.own(2)
        self.put(far.at[lo], self.hop.at[lo], 1, self.plus)
        self.put(far.at[hi], self.hop.at[hi], 2, self.minus)
        self.merge(1)
        self.put(self.own(1).at[hi], self.low.at[hi], 3, self.plus)
        self.merge(-1)
        self.put(self.own(-1).at[lo], self.high.at[lo], 4, self.minus)
        self.merge(0)

    def third(self):
        lo, hi = self.lo, self.hi
        self.arrived(self.hop.at[lo], 1)
        near = self.own(1).at[lo]
        accumulate(near, self.hop.at[lo])
        self.put(near, self.low.at[lo], 5, self.plus)
        self.arrived(self.hop.at[hi], 2)
        near = self.own(-1).at[hi]
        accumulate(near, self.hop.at[hi])
        self.put(near, self.high.at[hi], 6, self.minus)

    def piece(self, ref, u, v):
        rows, cols = self.piece_size
        if self.slab_rows == 4 * rows:
            row, col = u * rows, v * cols
        else:
            row, col = lax.div(u, 2) * rows, (lax.rem(u, 2) * 4 + v) * cols
        return ref.at[
            pl.ds(pl.multiple_of(row, rows), rows), pl.ds(pl.multiple_of(col, cols), cols)
        ]

    def member(self, i):
        u, v = self.plane
        spot = list(self.here)
        spot[u] = wrap(spot[u] + lax.div(i, 4))
        spot[v] = wrap(spot[v] + lax.rem(i, 4))
        return spot[u], spot[v], self.at(spot)

    def mirror(self, i):
        return wrap(-lax.div(i, 4)) * 4 + wrap(-lax.rem(i, 4))

    def mine(self):
        return self.here[self.plane[0]], self.here[self.plane[1]]

    def remote(self, source, target, send, recv, to):
        return pltpu.make_async_remote_copy(
            src_ref=source, dst_ref=target, send_sem=send, recv_sem=recv,
            device_id=to, device_id_type=MESH,
        )

    def piece_copy(self, i):
        u, v, to = self.member(i)
        there = self.mirror(i)
        return self.remote(
            self.piece(self.own(0), u, v),
            self.pieces.at[there],
            self.plane_send.at[i],
            self.plane_recv.at[there],
            to,
        )

    def back_copy(self, i):
        spot = self.piece(self.done, *self.mine())
        return self.remote(
            spot, spot, self.back_send.at[i], self.back_recv.at[self.mirror(i)], self.member(i)[2]
        )

    def each(self, act):
        lax.fori_loop(1, 16, lambda i, carry: (act(i), carry)[1], 0)

    def take(self, sems):
        spot = self.pieces
        self.each(lambda i: pltpu.make_async_copy(spot.at[0], spot.at[0], sems.at[i]).wait())

    def fourth(self):
        lo, hi = self.lo, self.hi
        self.arrived(self.low.at[hi], 3)
        self.arrived(self.high.at[lo], 4)
        self.arrived(self.low.at[lo], 5)
        self.arrived(self.high.at[hi], 6)
        accumulate(self.own(0), self.low, self.high)
        self.each(lambda i: self.piece_copy(i).start())
        self.pieces[0] = self.piece(self.own(0), *self.mine())[...]

    def fifth(self):
        self.take(self.plane_recv)
        total = jnp.sum(self.pieces[...].astype(F32), axis=0)
        self.piece(self.done, *self.mine())[...] = total.astype(self.done.dtype)
        self.each(lambda i: self.back_copy(i).start())

    def sixth(self, sem):
        self.take(self.back_recv)
        spot = self.block(self.result, 0)
        self.put(self.done, spot, 7, self.plus)
        self.put(self.done, spot, 8, self.minus)
        self.put(self.done, spot, 11, self.sibling)
        self.store = pltpu.make_async_copy(self.done, spot, sem)
        self.store.start()

    def seventh(self):
        whole, spot = self.block(self.result, -1), self.block(self.result, -1, 0)
        self.arrived(whole, 7)
        self.put(spot, spot, 9, self.plus)
        self.put(whole, whole, 12, self.sibling)
        whole, spot = self.block(self.result, 1), self.block(self.result, 1, 1)
        self.arrived(whole, 8)
        self.put(spot, spot, 10, self.minus)
        self.put(whole, whole, 13, self.sibling)

    def eighth(self):
        whole = self.block(self.result, 2)
        self.arrived(self.block(self.result, 2, 0), 9)
        self.arrived(self.block(self.result, 2, 1), 10)
        self.put(whole, whole, 14, self.sibling)

    def finish(self):
        for i in range(11, 15):
            self.arrived(self.block(self.result, 0), i)
        self.each(lambda i: self.piece_copy(i).wait_send())
        self.each(lambda i: self.back_copy(i).wait_send())
        self.store.wait()


def back_kernel(
    rows_hbm, gg_ref, x_hbm, gates_ref, hidden_hbm, gm_ref, ga_ref, router_ref, cot_hbm, tok_hbm,
    mixed_hbm, query_hbm, kv_hbm, cos_hbm, sin_hbm, routes_ref, len_ref,
    probs_hbm, wo_hbm, wq_hbm, wk_hbm, wv_hbm, o_hbm, pg_hbm, pu_hbm, pd_hbm,
    hop_g_hbm, hop_u_hbm, hop_d_hbm,
    layer_hbm, input_hbm, gate_hbm, up_hbm, down_hbm, q_hbm, o_sum_hbm, kv_sum_hbm, narrow_hbm,
    layer_ref, input_ref, gate_out, up_out, down_out,
    rows_ref, x_ref, hidden_ref, cot_ref, tok_ref, mixed_ref, query_ref, kv_ref, turns,
    probs, wo, wq, wk, wv, o_buf, rb, rc, rd, re,
    pg, pu, pd, hop_g, hop_u, hop_d, low_g, low_u, low_d, high_g, high_u, high_d,
    grad_mixed, grad_query, grad_kv, kv_hops, kv_low, kv_high,
    dq_out, do_out, dkv_out, narrow_ref,
    their_a, their_b, their_c, their_n, low_a, low_b, low_c, low_n, high_a, high_b, high_c, high_n,
    hop_a, hop_b, hop_c, hop_n, piece_a, piece_b, piece_c, piece_n, done_a, done_b, done_c, done_n,
    send_sem, recv_sem, local_sem, t_recv, plane_send, plane_recv, back_send, back_recv,
):
    p, q, y, core = place()
    spot = (p, q, y, core)
    sibling = (chip_of(p, q, core) * 2 + 1 - core, y)
    ahead, behind = device(p, q, y + 1, core), device(p, q, y - 1, core)
    net = Sends(send_sem, recv_sem)
    first = pl.multiple_of(y * TOK, TOK)
    pairs = (
        (o_hbm, o_buf), (wo_hbm, wo), (probs_hbm, probs), (wq_hbm, wq), (wk_hbm, wk), (wv_hbm, wv),
        (pg_hbm, pg), (pu_hbm, pu), (pd_hbm, pd),
        (hop_g_hbm, hop_g), (hop_u_hbm, hop_u), (hop_d_hbm, hop_d),
        (rows_hbm, rows_ref), (x_hbm, x_ref), (hidden_hbm, hidden_ref), (cot_hbm, cot_ref),
        (tok_hbm, tok_ref), (mixed_hbm, mixed_ref), (query_hbm, query_ref), (kv_hbm, kv_ref),
        (cos_hbm.at[pl.ds(first, TOK)], turns.at[0]), (sin_hbm.at[pl.ds(first, TOK)], turns.at[1]),
    )
    loads = [pltpu.make_async_copy(s, d, local_sem.at[i]) for i, (s, d) in enumerate(pairs)]
    for load in loads:
        load.start()
    plane = PlaneReduce(net, spot, o_buf, rb, rc, rd, re, 0)

    def unit(k, axis, source, result, span, rows, first, piece, *buffers):
        sems = [ref.at[k] for ref in (t_recv, plane_send, plane_recv, back_send, back_recv)]
        return Total(net, axis, source, result, span, rows, first, piece, buffers, sems)

    sum_o = unit(
        2, 1, do_out, o_sum_hbm, 512, 512, 0, (32, 256), their_b, low_b, high_b, hop_b, piece_b, done_b
    )
    sum_q = [
        unit(
            h, 2 * h, dq_out, q_hbm, 512, 256, 256 * h, (16, 256),
            *[ref.at[h] for ref in (their_a, low_a, high_a, hop_a, piece_a, done_a)],
        )
        for h in range(2)
    ]
    sum_kv = [
        unit(
            3 + h, 2 * h, dkv_out, kv_sum_hbm, 512, 256, 256 * h, (16, 256),
            *[ref.at[h] for ref in (their_c, low_c, high_c, hop_c, piece_c, done_c)],
        )
        for h in range(2)
    ]
    sum_n = unit(
        5, 0, narrow_ref, narrow_hbm, 64, 64, 0, (8, 128),
        their_n, low_n, high_n, hop_n, piece_n, done_n,
    )
    late = [*sum_kv, sum_n]
    everyone = [*sum_q, sum_o, *late]
    here = sum_o.here
    partners = [
        sum_o.at([here[0] + i, here[1] + j, here[2] + k])
        for i in range(4)
        for j in range(4)
        for k in range(4)
        if (i or j or k) and not (i and j and k)
    ]
    greet(partners + [sibling])
    loads[0].wait()
    plane.begin()
    for load in loads[6:16]:
        load.wait()

    def block(ref, step, rows=None):
        span = pl.ds(pl.multiple_of(wrap(y + step) * TOK, TOK), TOK)
        return ref.at[:, span] if rows is None else ref.at[rows, span]

    def down_block(ref, step):
        return ref.at[pl.ds(pl.multiple_of(wrap(y + step) * TOK, TOK), TOK)]

    top, bottom = pl.ds(0, 512), pl.ds(512, 512)

    def weight_portion(step, which):
        if which == 0:
            return [block(pg, step), block(pu, step, top)]
        return [block(pu, step, bottom), down_block(pd, step)]

    weights = RingReduce(
        net, 24, ahead, behind, weight_portion,
        ([hop_g, hop_u.at[top]], [hop_u.at[bottom], hop_d]),
        ([low_g, low_u.at[top]], [low_u.at[bottom], low_d]),
        ([high_g, high_u.at[top]], [high_u.at[bottom], high_d]),
    )
    weights.direct()

    row = lax.broadcasted_iota(jnp.int32, (TOK, 1), 0) + y * TOK
    upstream = jnp.where(row < len_ref[0], cot_ref[...].astype(F32), 0.0)
    gates = gates_ref[...]
    grad_gates = gg_ref[...].reshape(TOK, TOK).T
    grad_logits = gates * (grad_gates - jnp.sum(gates * grad_gates, axis=1, keepdims=True))
    grad_logits = grad_logits.astype(BF)
    wide = lax.dot_general(
        widen(), router_ref[...], (((0,), (0,)), ((), ())), preferred_element_type=F32
    ).astype(BF)
    by_row = (((0,), (0,)), ((), ()))
    by_col = (((1,), (1,)), ((), ()))
    grad_normed = rows_ref[...] + jnp.dot(grad_logits, wide, preferred_element_type=F32)
    hidden = hidden_ref[...]
    scale = root(hidden)
    grad_gain_moe = jnp.sum(grad_normed * hidden * scale, axis=0, keepdims=True)
    scaled = grad_normed * gm_ref[...]
    pull = jnp.mean(scaled * hidden, axis=1, keepdims=True)
    grad_hidden = upstream + scale * scaled - hidden * (scale * scale * scale) * pull
    input_ref[...] = grad_hidden
    low = grad_hidden.astype(BF)
    loads[1].wait()
    grad_mixed[...] = lax.dot_general(low, wo[...], by_col, preferred_element_type=F32).astype(BF)
    narrow_ref[...] = lax.dot_general(grad_logits, x_ref[...], by_row, preferred_element_type=F32)
    named = routed_mask(routes_ref[...], lax.broadcasted_iota(jnp.int32, (TOK, 1), 0))
    counts = jnp.sum(named.T, axis=0, keepdims=True)
    narrow_ref[3:4, :] = grad_gain_moe
    narrow_ref[4:5, :] = jnp.zeros((1, D), F32)
    narrow_ref[4:5, 0:TOK] = counts
    for load in loads[16:]:
        load.wait()
    do_out[...] = lax.dot_general(
        mixed_ref[...], low, by_row, preferred_element_type=F32
    ).astype(BF)
    sum_o.begin()

    cosine, sine = turns[0], turns[1]
    loads[2].wait()

    def attend(c, carry):
        span = pl.ds(pl.multiple_of(c * 128, 128), 128)
        value_span = pl.ds(pl.multiple_of(512 + c * 128, 128), 128)
        keys = kv_ref[:, :, span].reshape(512, 128)
        values = kv_ref[:, :, value_span].reshape(512, 128)
        grad_keys = jnp.zeros((512, 128), F32)
        grad_values = jnp.zeros((512, 128), F32)
        for half in range(2):
            m = c * 2 + half
            mine = pl.ds(pl.multiple_of(m * 128, 128), 128)
            pair = stack_heads(query_ref[:, mine].astype(F32), half)
            grad_pair = stack_heads(grad_mixed[:, mine].astype(F32), half)
            grad_probs = lax.dot_general(grad_pair, values, by_col, preferred_element_type=F32)
            prob = probs[m]
            wide_prob = prob.astype(F32)
            middle = jnp.sum(wide_prob * grad_probs, axis=1, keepdims=True)
            grad_scores = (wide_prob * (grad_probs - middle)).astype(BF)
            back = jnp.dot(grad_scores, keys, preferred_element_type=F32) * SCALE
            grad_query[:, mine] = turn(unstack_heads(back, half), cosine, -sine).astype(BF)
            grad_keys += lax.dot_general(grad_scores, pair, by_row, preferred_element_type=F32)
            grad_values += lax.dot_general(prob, grad_pair, by_row, preferred_element_type=F32)
        grad_kv[:, :, span] = (grad_keys * SCALE).astype(BF).reshape(4, TOK, 128)
        grad_kv[:, :, value_span] = grad_values.astype(BF).reshape(4, TOK, 128)
        return carry

    lax.fori_loop(0, 4, attend, 0)
    lo, hi = pl.ds(0, 64), pl.ds(64, 64)
    sums = RingReduce(
        net, 36, ahead, behind,
        lambda step, which: [grad_kv.at[wrap(y + step), hi if which else lo]],
        ([kv_hops.at[0]], [kv_hops.at[1]]),
        ([kv_low.at[lo]], [kv_low.at[hi]]),
        ([kv_high.at[lo]], [kv_high.at[hi]]),
    )
    sums.begin()
    sums.direct()
    plane.middle()
    tokens = tok_ref[...].astype(F32)
    scale = root(tokens)
    normed = (tokens * scale * ga_ref[...]).astype(BF)
    dq_out[...] = lax.dot_general(
        normed, grad_query[...], by_row, preferred_element_type=F32
    ).astype(BF)
    for one in sum_q:
        one.begin()
    sums.middle()
    for load in loads[3:6]:
        load.wait()
    grad_normed = lax.dot_general(grad_query[...], wq[...], by_col, preferred_element_type=F32)
    for one in sum_q:
        one.second()
    sums.finish()
    sum_o.second()
    both = grad_kv[y].astype(F32) + kv_low[...].astype(F32) + kv_high[...].astype(F32)
    grad_key = jnp.concatenate(
        [turn(both[:, c * 128 : (c + 1) * 128], cosine, -sine) for c in range(4)], axis=1
    ).astype(BF)
    grad_value = both[:, 512:].astype(BF)
    dkv_out[:, 0:512] = lax.dot_general(
        normed, grad_key, by_row, preferred_element_type=F32
    ).astype(BF)
    dkv_out[:, 512:1024] = lax.dot_general(
        normed, grad_value, by_row, preferred_element_type=F32
    ).astype(BF)
    sum_kv[0].begin()
    sum_kv[1].begin()
    grad_normed += lax.dot_general(grad_key, wk[...], by_col, preferred_element_type=F32)
    grad_normed += lax.dot_general(grad_value, wv[...], by_col, preferred_element_type=F32)
    narrow_ref[2:3, :] = jnp.sum(grad_normed * tokens * scale, axis=0, keepdims=True)
    sum_n.begin()
    for one in late:
        one.second()
    for one in sum_q:
        one.third()
    scaled = grad_normed * ga_ref[...]
    pull = jnp.mean(scaled * tokens, axis=1, keepdims=True)
    input_ref[...] += scale * scaled - tokens * (scale * scale * scale) * pull
    for one in late:
        one.third()
    sum_o.third()
    for one in sum_q:
        one.fourth()
    plane.third()
    for one in late:
        one.fourth()
    for one in sum_q:
        one.fifth()
    plane.fourth()
    sum_o.fourth()
    weights.middle(here=True)
    for one in late:
        one.fifth()
    for i, one in enumerate(sum_q):
        one.sixth(local_sem.at[i])
    layer_ref[...] = (hidden_ref[...] + plane.finish()).astype(BF)
    sum_o.fifth()
    for i, one in enumerate(late):
        one.sixth(local_sem.at[3 + i])
    for one in sum_q:
        one.seventh()
    sum_o.sixth(local_sem.at[2])
    weights.finish()
    gate_out[...] = (
        block(pg, 0)[...].astype(F32) + low_g[...].astype(F32) + high_g[...].astype(F32)
    )
    up_out[...] = block(pu, 0)[...].astype(F32) + low_u[...].astype(F32) + high_u[...].astype(F32)
    down_out[...] = (
        down_block(pd, 0)[...].astype(F32) + low_d[...].astype(F32) + high_d[...].astype(F32)
    )
    stores = [
        pltpu.make_async_copy(src, dst, local_sem.at[9 + i])
        for i, (src, dst) in enumerate(
            (
                (layer_ref, layer_hbm),
                (input_ref, input_hbm),
                (gate_out, gate_hbm),
                (up_out, up_hbm),
                (down_out, down_hbm),
            )
        )
    ]
    for store in stores:
        store.start()
    for one in late:
        one.seventh()
    for one in sum_q:
        one.eighth()
    sum_o.seventh()
    for one in late:
        one.eighth()
    sum_o.eighth()
    for one in everyone:
        one.finish()
    net.drain()
    for store in stores:
        store.wait()


def back(operands, arrays):
    any_space = pl.BlockSpec(memory_space=pl.ANY)
    vmem = pl.BlockSpec(memory_space=pltpu.VMEM)
    smem = pl.BlockSpec(memory_space=pltpu.SMEM)
    shape = jax.ShapeDtypeStruct
    dma = pltpu.SemaphoreType.DMA
    low = lambda *size: pltpu.VMEM(size, BF)
    return pl.pallas_call(
        back_kernel,
        out_shape=(
            shape((TOK, D), BF),
            shape((TOK, D), F32),
            shape((D, TOK), F32),
            shape((D, TOK), F32),
            shape((TOK, D), F32),
            shape((D, D), BF),
            shape((D, D), BF),
            shape((D, D), BF),
            shape((TOK, D), F32),
        ),
        in_specs=[
            any_space, vmem, any_space, vmem, any_space, *[vmem] * 3, *[any_space] * 7, vmem, smem,
            *[any_space] * 12,
        ],
        out_specs=(any_space,) * 9,
        scratch_shapes=[
            low(TOK, D),
            pltpu.VMEM((TOK, D), F32),
            pltpu.VMEM((D, TOK), F32),
            pltpu.VMEM((D, TOK), F32),
            pltpu.VMEM((TOK, D), F32),
            pltpu.VMEM((TOK, D), F32),
            low(TOK, D),
            pltpu.VMEM((TOK, D), F32),
            low(TOK, D),
            low(TOK, D),
            low(TOK, D),
            low(TOK, D),
            low(4, TOK, D),
            pltpu.VMEM((2, TOK, TOK), F32),
            low(8, 2 * TOK, 512),
            low(D, D),
            low(D, D),
            low(D, 512),
            low(D, 512),
            low(16, TOK, D),
            low(4, TOK, D),
            low(8, TOK, D),
            low(TOK, D),
            low(2, TOK, D),
            low(D, FF),
            low(D, FF),
            low(FF, D),
            low(D, TOK),
            low(D, TOK),
            low(TOK, D),
            low(D, TOK),
            low(D, TOK),
            low(TOK, D),
            low(D, TOK),
            low(D, TOK),
            low(TOK, D),
            low(TOK, D),
            low(TOK, D),
            low(4, TOK, D),
            low(2, 64, D),
            low(TOK, D),
            low(TOK, D),
            low(D, D),
            low(D, D),
            low(D, D),
            pltpu.VMEM((TOK, D), F32),
            low(2, 256, D),
            low(512, D),
            low(2, 256, D),
            pltpu.VMEM((64, D), F32),
            low(2, 64, D),
            low(128, D),
            low(2, 64, D),
            pltpu.VMEM((16, D), F32),
            low(2, 64, D),
            low(128, D),
            low(2, 64, D),
            pltpu.VMEM((16, D), F32),
            low(2, 64, D),
            low(128, D),
            low(2, 64, D),
            pltpu.VMEM((16, D), F32),
            low(2, 16, 16, 256),
            low(16, 32, 256),
            low(2, 16, 16, 256),
            pltpu.VMEM((16, 8, 128), F32),
            low(2, 64, D),
            low(128, D),
            low(2, 64, D),
            pltpu.VMEM((16, D), F32),
            dma((160,)),
            dma((42,)),
            dma((22,)),
            dma((6, 15)),
            dma((6, 16)),
            dma((6, 16)),
            dma((6, 16)),
            dma((6, 16)),
        ],
        compiler_params=pltpu.CompilerParams(
            collective_id=4, has_side_effects=True, vmem_limit_bytes=VMEM_BYTES
        ),
        name="back",
    )(*operands, *arrays)


def results_kernel(
    q_ref, o_ref, kv_ref, n_ref, layer_ref, input_ref, gate_ref, up_ref, down_ref,
    q_out, o_out, k_out, v_out, router_out, one_out, two_out, count_out,
    layer_out, input_out, gate_out, up_out, down_out,
):
    layer_out[...] = layer_ref[...]
    input_out[...] = input_ref[...]
    gate_out[0] = gate_ref[...]
    up_out[0] = up_ref[...]
    down_out[0] = down_ref[...]
    q_out[...] = q_ref[...].astype(F32)
    o_out[...] = o_ref[...].astype(F32)
    k_out[...] = kv_ref[:, 0:512].astype(F32)
    v_out[...] = kv_ref[:, 512:1024].astype(F32)

    @pl.when(pl.program_id(0) == 0)
    def _():
        for j in range(16):
            router_out[2 * j : 2 * j + 2, :] = n_ref[8 * j : 8 * j + 2, :]
        one_out[...] = n_ref[2:3, :]
        two_out[...] = n_ref[3:4, :]
        count_out[...] = n_ref[4:5, 0:EXPERTS].astype(jnp.int32)


def results(q, o, kv, narrow, *own):
    rows = 512
    some = rows * TOK // D
    first = lambda *size: pl.BlockSpec((1, *size), lambda i: (0, i, 0))
    block = lambda width: pl.BlockSpec((rows, width), lambda i: (i, 0))
    whole = lambda *size: pl.BlockSpec(size, lambda i: (0, 0))
    shape = jax.ShapeDtypeStruct
    return pl.pallas_call(
        results_kernel,
        grid=(D // rows,),
        out_shape=(
            shape((D, D), F32),
            shape((D, D), F32),
            shape((D, 512), F32),
            shape((D, 512), F32),
            shape((EXPERTS, D), F32),
            shape((1, D), F32),
            shape((1, D), F32),
            shape((1, EXPERTS), jnp.int32),
            shape((TOK, D), BF),
            shape((TOK, D), F32),
            shape((1, D, TOK), F32),
            shape((1, D, TOK), F32),
            shape((1, TOK, D), F32),
        ),
        in_specs=[
            block(D), block(D), block(D), whole(TOK, D),
            pl.BlockSpec((some, D), lambda i: (i, 0)),
            pl.BlockSpec((some, D), lambda i: (i, 0)),
            block(TOK), block(TOK),
            pl.BlockSpec((some, D), lambda i: (i, 0)),
        ],
        out_specs=(
            block(D), block(D), block(512), block(512),
            whole(EXPERTS, D), whole(1, D), whole(1, D), whole(1, EXPERTS),
            pl.BlockSpec((some, D), lambda i: (i, 0)),
            pl.BlockSpec((some, D), lambda i: (i, 0)),
            first(rows, TOK), first(rows, TOK), first(some, D),
        ),
        compiler_params=pltpu.CompilerParams(vmem_limit_bytes=VMEM_BYTES),
        name="results",
    )(q, o, kv, narrow, *own)


def shards(
    tokens,
    w_query,
    w_key,
    w_value,
    w_output,
    gain_attn,
    gain_moe,
    router,
    w_gate,
    w_up,
    w_down,
    cotangent,
    routes,
    lengths,
):
    (
        gates, grad_rows, grad_gates, hidden, x, mixed, query, kv, probs, out_parts, part_gate,
        part_up, part_down, *far_parts,
    ) = main(
        tokens, w_query, w_key, w_value, w_output, gain_attn, gain_moe, router.T, cotangent,
        routes.T, lengths, w_gate, w_up, w_down,
    )
    cosine, sine = turn_tables()
    layer_out, grad_input, grad_gate, grad_up, grad_down, sum_q, sum_o, sum_kv, narrow = back(
        (
            grad_rows, grad_gates, x, gates, hidden, gain_moe.reshape(1, D),
            gain_attn.reshape(1, D), router.T, cotangent, tokens, mixed, query, kv,
            jnp.asarray(cosine), jnp.asarray(sine), routes.T, lengths,
        ),
        (
            probs, w_output, w_query, w_key, w_value, out_parts, part_gate, part_up,
            part_down.reshape(FF, D),
            *far_parts,
        ),
    )
    (
        grad_q, grad_o, grad_k, grad_v, grad_router, gain_one, gain_two, counts,
        layer_out, grad_input, grad_gate, grad_up, grad_down,
    ) = results(
        sum_q, sum_o, sum_kv, narrow, layer_out, grad_input, grad_gate, grad_up, grad_down
    )
    return (
        layer_out,
        grad_input,
        grad_q,
        grad_k,
        grad_v,
        grad_o,
        gain_one.reshape(D),
        gain_two.reshape(D),
        grad_router.T,
        grad_gate,
        grad_up,
        grad_down,
        counts.reshape(EXPERTS),
    )


def solution(mesh):
    in_specs = (
        P(("dp", "hid"), None),
        P(),
        P(),
        P(),
        P(),
        P(),
        P(),
        P(),
        P("dp", None, "hid"),
        P("dp", None, "hid"),
        P("dp", "hid", None),
        P(("dp", "hid"), None),
        P(("dp", "hid"), None),
        P("dp"),
    )
    out_specs = (
        P(("dp", "hid"), None),
        P(("dp", "hid"), None),
        P(),
        P(),
        P(),
        P(),
        P(),
        P(),
        P(),
        P("dp", None, "hid"),
        P("dp", None, "hid"),
        P("dp", "hid", None),
        P(),
    )
    return jax.shard_map(shards, mesh=mesh, in_specs=in_specs, out_specs=out_specs, check_vma=False)
```

```python
import jax
import jax.numpy as jnp
import numpy as np
from jax import lax
from jax.experimental import pallas as pl
from jax.experimental.pallas import tpu as pltpu
from jax.sharding import PartitionSpec as P

D = 1024
HEADS = 16
KV_HEADS = 8
HEAD_DIM = 64
EXPERTS = 32
TOP = 8
FF = 512
TOK = 128

MESH = pl.DeviceIdType.MESH
BF = jnp.bfloat16
F32 = jnp.float32
SLOTS = 48
VMEM_BYTES = 60 * 2**20


def wrap(value):
    return lax.rem(value + 4, 4)


def place():
    dp = lax.axis_index("dp")
    y = lax.axis_index("hid")
    core = lax.rem(dp, 2)
    x = lax.div(dp, 8)
    z = lax.rem(lax.div(dp, 2), 4)
    p = jnp.where(core == 0, x, z)
    q = jnp.where(core == 0, z, x)
    return p, q, y, core


def device(p, q, y, core):
    p, q = wrap(p), wrap(q)
    return (jnp.where(core == 0, p * 8 + q * 2, q * 8 + p * 2) + core, wrap(y))


def chip_of(p, q, core):
    p, q = wrap(p), wrap(q)
    return jnp.where(core == 0, p * 4 + q, q * 4 + p)


def greet(devices):
    barrier = pltpu.get_barrier_semaphore()
    for other in devices:
        pl.semaphore_signal(barrier, inc=1, device_id=other, device_id_type=MESH)
    pl.semaphore_wait(barrier, len(devices))


class Sends:
    def __init__(self, send_sem, recv_sem):
        self.send_sem, self.recv_sem, self.made = send_sem, recv_sem, []

    def start(self, source, target, recv, to):
        self.put(source, target, self.recv_sem.at[recv], to)

    def put(self, source, target, sem, to):
        copy = pltpu.make_async_remote_copy(
            src_ref=source,
            dst_ref=target,
            send_sem=self.send_sem.at[len(self.made)],
            recv_sem=sem,
            device_id=to,
            device_id_type=MESH,
        )
        copy.start()
        self.made.append(copy)

    def arrived(self, ref, recv):
        pltpu.make_async_copy(ref, ref, self.recv_sem.at[recv]).wait()

    def drain(self):
        for copy in self.made:
            copy.wait_send()
        self.made = []


def slab(buffer, p, q):
    return buffer.at[wrap(p) * 4 + wrap(q)]


HALF = HEAD_DIM // 2
SCALE = HEAD_DIM**-0.5


def turn_tables():
    inverse = 10000.0 ** (-np.arange(HALF, dtype=np.float32) / HALF)
    phases = np.arange(4 * TOK, dtype=np.float32)[:, None] * inverse[None, :]
    cosine = np.tile(np.cos(phases), (1, 4)).astype(np.float32)
    sine = np.sin(phases)
    sine = np.tile(np.concatenate([-sine, sine], axis=1), (1, 2)).astype(np.float32)
    return cosine, sine


def lanes(rows, width=128):
    return lax.broadcasted_iota(jnp.int32, (rows, width), 1)


def turn(chunk, cosine, sine):
    front = lax.rem(lanes(chunk.shape[0]), HEAD_DIM) < HALF
    swapped = jnp.where(front, pltpu.roll(chunk, 128 - HALF, 1), pltpu.roll(chunk, HALF, 1))
    return chunk * cosine + swapped * sine


def stack_heads(chunk, half):
    low = lanes(chunk.shape[0]) < HEAD_DIM
    rolled = pltpu.roll(chunk, HEAD_DIM, 1)
    if half == 0:
        pair = (jnp.where(low, chunk, 0.0), jnp.where(low, rolled, 0.0))
    else:
        pair = (jnp.where(low, 0.0, rolled), jnp.where(low, 0.0, chunk))
    return jnp.concatenate(pair, axis=0).astype(BF)


def unstack_heads(pair, half):
    first, second = pair[:TOK], pair[TOK:]
    low = lanes(TOK) < HEAD_DIM
    if half == 0:
        return jnp.where(low, first, pltpu.roll(second, HEAD_DIM, 1))
    return jnp.where(low, pltpu.roll(first, HEAD_DIM, 1), second)


def root(values):
    return lax.rsqrt(jnp.mean(values * values, axis=1, keepdims=True) + 1e-06)


def widen():
    row = lax.broadcasted_iota(jnp.int32, (EXPERTS, TOK), 0)
    lane = lax.broadcasted_iota(jnp.int32, (EXPERTS, TOK), 1)
    return jnp.where(lane == lax.div(row, 2) * 8 + lax.rem(row, 2), 1.0, 0.0).astype(BF)


def routed_mask(routes, expert):
    hit = jnp.zeros((TOK, TOK), F32)
    for k in range(TOP):
        hit = hit + jnp.where(routes[k : k + 1, :] == expert, 1.0, 0.0)
    return hit


def wide_experts():
    row = lax.broadcasted_iota(jnp.int32, (TOK, 1), 0)
    return jnp.where(lax.rem(row, 8) < 2, lax.div(row, 8) * 2 + lax.rem(row, 8), -1)


class PlaneGather:
    def __init__(self, net, spot, slabs, base):
        self.net, self.spot, self.slabs, self.base = net, spot, slabs, base
        p, q, y, core = spot
        self.right, self.left = device(p + 1, q, y, core), device(p - 1, q, y, core)
        self.up, self.down = device(p, q + 1, y, core), device(p, q - 1, y, core)

    def slab(self, a, b):
        return slab(self.slabs, self.spot[0] + a, self.spot[1] + b)

    def send(self, ref, recv, to):
        self.net.start(ref, ref, self.base + recv, to)

    def arrived(self, ref, recv):
        self.net.arrived(ref, self.base + recv)

    def begin(self, own):
        for recv, to in ((0, self.right), (1, self.left), (4, self.up), (8, self.down)):
            self.net.start(own, self.slab(0, 0), self.base + recv, to)

    def second(self):
        s = self.slab(-1, 0)
        self.arrived(s, 0)
        self.send(s.at[0:64], 2, self.right)
        self.send(s, 5, self.up)
        s = self.slab(1, 0)
        self.arrived(s, 1)
        self.send(s.at[64:128], 3, self.left)
        self.send(s, 10, self.down)

    def third(self):
        s = self.slab(0, -1)
        self.arrived(s, 4)
        self.send(s, 12, self.up)
        s = self.slab(2, 0)
        self.arrived(s.at[0:64], 2)
        self.arrived(s.at[64:128], 3)
        self.send(s, 11, self.down)
        s = self.slab(-1, -1)
        self.arrived(s, 5)
        self.send(s, 13, self.up)
        self.send(self.slab(1, 0), 6, self.up)
        self.send(self.slab(2, 0), 7, self.up)
        self.send(self.slab(-1, 0), 9, self.down)

    def fourth(self, which):
        a, recv, far = ((1, 10, 14), (2, 11, 15))[which]
        s = self.slab(a, 1)
        self.arrived(s, recv)
        self.send(s, far, self.down)

    def finish(self):
        for a, b, recv in (
            (1, -1, 6), (2, -1, 7), (0, 1, 8), (-1, 1, 9),
            (0, 2, 12), (-1, 2, 13), (1, 2, 14), (2, 2, 15),
        ):
            self.arrived(self.slab(a, b), recv)


def main_kernel(
    tok_ref, wq_hbm, wk_hbm, wv_hbm, wo_hbm, ga_ref, gm_ref, router_ref, cot_ref, routes_ref,
    len_ref, cos_hbm, sin_hbm, wgs_hbm, wus_hbm, wds_hbm,
    gates_ref, grad_out, gg_out, hidden_hbm, x_hbm, mixed_hbm, query_hbm, kv_hbm,
    probs_hbm, o_hbm, dwg_hbm, dwu_hbm, dwd_hbm, hop_g_hbm, hop_u_hbm, hop_d_hbm,
    hidden_ref, x_ref, mixed_ref, query_ref, turns,
    wqo, wk, wv, u_own, kv, probs, bias, gt,
    xs, us, wg, wu, wd, gin, rank, ggo, picks, rows, slot_grads, acts, gparts, uparts,
    outs, pairs, o_buf, p_buf, rb, rc, rd, re, dwg, dwu,
    send_sem, recv_sem, g_send, g_recv, gg_send, gg_recv, local_sem, free_sem,
):
    p, q, y, core = place()
    spot = (p, q, y, core)
    sibling = (chip_of(p, q, core) * 2 + 1 - core, y)
    ahead, behind = device(p, q, y + 1, core), device(p, q, y - 1, core)
    up, down = device(p, q + 1, y, core), device(p, q - 1, y, core)
    right, left = device(p + 1, q, y, core), device(p - 1, q, y, core)
    others = [device(p + a, q + b, y, core) for a in range(4) for b in range(4) if a or b]
    my_chip = chip_of(p, q, core)
    net = Sends(send_sem, recv_sem)
    wq, wo = wqo.at[0], wqo.at[1]
    loads = {
        name: pltpu.make_async_copy(src, dst, local_sem.at[i])
        for i, (name, src, dst) in enumerate(
            (("k", wk_hbm, wk), ("v", wv_hbm, wv), ("q", wq_hbm, wq), ("o", wo_hbm, wo))
        )
    }
    for load in loads.values():
        load.start()
    first = pl.multiple_of(y * TOK, TOK)
    tables = [
        pltpu.make_async_copy(src.at[pl.ds(first, TOK)], turns.at[i], local_sem.at[16 + i])
        for i, src in enumerate((cos_hbm, sin_hbm))
    ]
    for load in tables:
        load.start()
    gather = PlaneGather(net, spot, us, 0)
    tokens_in = PlaneGather(net, spot, xs, 42)
    row = lax.broadcasted_iota(jnp.int32, (TOK, 1), 0) + y * TOK
    length = len_ref[0]
    u_own[...] = jnp.where(row < length, cot_ref[...].astype(F32), 0.0).astype(BF)
    greet(others + [ahead, behind, sibling])
    gather.begin(u_own)
    keep_own = pltpu.make_async_copy(u_own, gather.slab(0, 0), local_sem.at[4])
    keep_own.start()

    def weight(a, e, yy, rows=None):
        block = pl.ds(pl.multiple_of(wrap(yy) * TOK, TOK), TOK)
        if a == 2:
            return wd.at[e, block, :]
        full = (wg, wu)[a]
        return full.at[e, :, block] if rows is None else full.at[e, rows, block]

    shards = (wgs_hbm.at[0], wus_hbm.at[0], wds_hbm.at[0])
    top, bottom = pl.ds(0, 512), pl.ds(512, 512)
    keep = []

    def send_weight(a):
        net.start(shards[a], weight(a, core, y), 20 + a, ahead)
        net.start(shards[a], weight(a, core, y), 23 + a, behind)
        net.start(shards[a], weight(a, core, y), 30 + a, sibling)
        keep.append(pltpu.make_async_copy(shards[a], weight(a, core, y), local_sem.at[5 + a]))
        keep[-1].start()

    def pass_weight(a):
        before, after = weight(a, core, y - 1), weight(a, core, y + 1)
        net.arrived(before, 20 + a)
        if a == 0:
            net.start(before, before, 26, ahead)
        if a == 1:
            spot = weight(1, core, y - 1, top)
            net.start(spot, spot, 27, ahead)
        net.start(before, before, 33 + a, sibling)
        net.arrived(after, 23 + a)
        if a == 1:
            spot = weight(1, core, y + 1, bottom)
            net.start(spot, spot, 28, behind)
        if a == 2:
            net.start(after, after, 29, behind)
        net.start(after, after, 36 + a, sibling)

    send_weight(0)
    tokens = tok_ref[...].astype(F32)
    normed = (tokens * root(tokens) * ga_ref[...]).astype(BF)
    for load in tables:
        load.wait()
    cosine, sine = turns[0], turns[1]
    loads["k"].wait()
    keys = jnp.dot(normed, wk[...], preferred_element_type=F32)
    for c in range(4):
        span = slice(c * 128, (c + 1) * 128)
        kv[y, :, span] = turn(keys[:, span], cosine, sine).astype(BF)
    loads["v"].wait()
    kv[y, :, 512:1024] = jnp.dot(normed, wv[...], preferred_element_type=F32).astype(BF)
    own = kv.at[y]
    net.start(own, own, 16, ahead)
    net.start(own, own, 17, behind)

    loads["q"].wait()
    queries = jnp.dot(normed, wq[...], preferred_element_type=F32)
    for c in range(8):
        span = slice(c * 128, (c + 1) * 128)
        query_ref[:, span] = turn(queries[:, span], cosine, sine).astype(BF)
    key_pos = lanes(TOK, 512)
    bias[...] = jnp.where((key_pos <= row) & (key_pos < length), 0.0, -1e30)
    gather.second()
    s = kv.at[wrap(y - 1)]
    net.arrived(s, 16)
    net.start(s.at[0:64], s.at[0:64], 18, ahead)
    s = kv.at[wrap(y + 1)]
    net.arrived(s, 17)
    net.start(s.at[64:128], s.at[64:128], 19, behind)
    gather.third()
    s = kv.at[wrap(y + 2)]
    net.arrived(s.at[0:64], 18)
    net.arrived(s.at[64:128], 19)
    send_weight(1)
    send_weight(2)
    pass_weight(0)
    gather.fourth(0)

    def attend(c, carry):
        span = pl.ds(pl.multiple_of(c * 128, 128), 128)
        keys = kv[:, :, span].reshape(512, 128)
        values = kv[:, :, pl.ds(pl.multiple_of(512 + c * 128, 128), 128)].reshape(512, 128)
        for half in range(2):
            m = c * 2 + half
            mine = pl.ds(pl.multiple_of(m * 128, 128), 128)
            pair = stack_heads(query_ref[:, mine].astype(F32), half)
            scores = lax.dot_general(
                pair, keys, (((1,), (1,)), ((), ())), preferred_element_type=F32
            )
            scores = scores * SCALE + jnp.concatenate([bias[...], bias[...]], axis=0)
            scores = jnp.exp(scores - jnp.max(scores, axis=1, keepdims=True))
            low = (scores * (1.0 / jnp.sum(scores, axis=1, keepdims=True))).astype(BF)
            probs[m] = low
            out = jnp.dot(low, values, preferred_element_type=F32)
            mixed_ref[:, mine] = unstack_heads(out, half).astype(BF)
        return carry

    lax.fori_loop(0, 4, attend, 0)
    gather.fourth(1)
    keep_probs = pltpu.make_async_copy(probs, probs_hbm, local_sem.at[8])
    keep_probs.start()
    loads["o"].wait()
    hidden = tokens + jnp.dot(mixed_ref[...], wo[...], preferred_element_type=F32)
    hidden_ref[...] = hidden
    x = (hidden * root(hidden) * gm_ref[...]).astype(BF)
    x_ref[...] = x
    tokens_in.begin(x_ref)
    tokens_in.slab(0, 0)[...] = x
    wide = lax.dot_general(
        widen(), router_ref[...], (((0,), (0,)), ((), ())), preferred_element_type=F32
    ).astype(BF)
    logits = lax.dot_general(x, wide, (((1,), (1,)), ((), ())), preferred_element_type=F32)
    routed = routed_mask(routes_ref[...], wide_experts()).T > 0
    logits = jnp.where(routed, logits, -1e30)
    weights = jnp.where(routed, jnp.exp(logits - jnp.max(logits, axis=1, keepdims=True)), 0.0)
    weights = weights * (1.0 / jnp.sum(weights, axis=1, keepdims=True))
    gates_ref[...] = weights
    gt[...] = weights.T.reshape(16, 8, TOK)

    def gate_copy(i):
        a, b = lax.div(i, 4), lax.rem(i, 4)
        return pltpu.make_async_remote_copy(
            src_ref=gt.at[chip_of(p + a, q + b, core)],
            dst_ref=gin.at[p * 4 + q],
            send_sem=g_send.at[i],
            recv_sem=g_recv.at[wrap(-a) * 4 + wrap(-b)],
            device_id=device(p + a, q + b, y, core),
            device_id_type=MESH,
        )

    def start_gate(i, _):
        gate_copy(i).start()
        return 0

    lax.fori_loop(1, 16, start_gate, 0)
    gin[p * 4 + q] = gt[my_chip]

    keeps = [
        pltpu.make_async_copy(src, dst, local_sem.at[18 + i])
        for i, (src, dst) in enumerate(
            (
                (hidden_ref, hidden_hbm),
                (x_ref, x_hbm),
                (mixed_ref, mixed_hbm),
                (query_ref, query_hbm),
                (kv, kv_hbm),
            )
        )
    ]
    for store in keeps:
        store.start()
    tokens_in.second()
    pass_weight(1)
    tokens_in.third()
    pass_weight(2)

    def take_gate(i, _):
        pltpu.make_async_copy(gin.at[0], gin.at[0], g_recv.at[i]).wait()
        return 0

    lax.fori_loop(1, 16, take_gate, 0)
    ids = lax.broadcasted_iota(jnp.int32, (TOK, TOK), 0)
    cols = lax.broadcasted_iota(jnp.int32, (TOK, TOK), 1)
    before = jnp.where(ids < cols, 1.0, 0.0).astype(BF)
    routed = jnp.where(gin[...].reshape(TOK, TOK) > 0, 1.0, 0.0).astype(BF)
    rank[...] = jnp.dot(routed, before, preferred_element_type=F32).reshape(16, 8, TOK)
    gather.finish()
    ggo[...] = jnp.zeros_like(ggo)
    slot_ids = lax.broadcasted_iota(jnp.int32, (SLOTS, TOK), 0).astype(F32)

    def source_of(g, j):
        side = jnp.where((j < 2) == (g == 1), 3, 1)
        b = jnp.where(g == 0, 0, jnp.where(g == 2, 2, side))
        a = jnp.where(j == 0, 0, jnp.where(j == 1, 3, jnp.where(j == 2, 1, 2)))
        return wrap(p + a) * 4 + wrap(q + b)

    def pick_source(g, j):
        src = source_of(g, j)
        token_rows, up_rows = xs[src], us[src]
        base = pl.multiple_of(g * 4 * SLOTS + j * SLOTS, 16)
        for e in range(2):
            gate_row = gin[src, e : e + 1, :]
            hit = (rank[src, e : e + 1, :] == slot_ids) & (gate_row > 0)
            pick = jnp.where(hit, 1.0, 0.0)
            pick_low = pick.astype(BF)
            picks[src, e * SLOTS : (e + 1) * SLOTS, :] = pick_low
            gate_col = jnp.sum(pick * gate_row, axis=1, keepdims=True)
            rows[e, pl.ds(base, SLOTS), :] = jnp.dot(
                pick_low, token_rows, preferred_element_type=F32
            ).astype(BF)
            picked = jnp.dot(pick_low, up_rows, preferred_element_type=F32)
            wqo[e, pl.ds(base, SLOTS), :] = picked.astype(BF)
            slot_grads[e, pl.ds(base, SLOTS), :] = (picked * gate_col).astype(BF)

    def run_expert(g, e):
        base = pl.multiple_of(g * 4 * SLOTS, 16)
        span = pl.ds(base, 4 * SLOTS)
        taken = rows[e, span, :]
        gate = jnp.dot(taken, wg[e], preferred_element_type=F32)
        upv = jnp.dot(taken, wu[e], preferred_element_type=F32)
        sig = 1.0 / (1.0 + jnp.exp(-gate))
        silu = gate * sig
        act = (silu * upv).astype(BF)
        acts[e, span, :] = act
        grad_act = lax.dot_general(
            slot_grads[e, span, :], wd[e], (((1,), (1,)), ((), ())), preferred_element_type=F32
        )
        ggp = (grad_act * upv * sig * (1.0 + gate * (1.0 - sig))).astype(BF)
        gup = (grad_act * silu).astype(BF)
        gparts[e, span, :] = ggp
        uparts[e, span, :] = gup
        pair = lax.dot_general(ggp, wg[e], (((1,), (1,)), ((), ())), preferred_element_type=F32)
        pair += lax.dot_general(gup, wu[e], (((1,), (1,)), ((), ())), preferred_element_type=F32)
        pairs[e] = pair.astype(BF)

    def spread(g, j):
        src = source_of(g, j)
        span = pl.ds(pl.multiple_of(j * SLOTS, 16), SLOTS)
        both = jnp.concatenate([pairs[0, span, :], pairs[1, span, :]], axis=0)
        p_buf[src] = lax.dot_general(
            picks[src], both, (((0,), (0,)), ((), ())), preferred_element_type=F32
        ).astype(BF)

    def run_output(g, e):
        span = pl.ds(pl.multiple_of(g * 4 * SLOTS, 16), 4 * SLOTS)
        out = jnp.dot(acts[e, span, :], wd[e], preferred_element_type=F32).astype(BF)
        outs[e] = out
        gg_col = jnp.sum(out.astype(F32) * wqo[e, span, :].astype(F32), axis=1, keepdims=True)
        for j in range(4):
            src = source_of(g, j)
            pick = picks[src, pl.ds(pl.multiple_of(e * SLOTS, 16), SLOTS), :].astype(F32)
            part = gg_col[j * SLOTS : (j + 1) * SLOTS]
            ggo[src, pl.ds(e, 1), :] = jnp.sum(pick * part, axis=0, keepdims=True)

    def spread_output(g, j):
        src = source_of(g, j)
        pick = picks[src]
        span = pl.ds(pl.multiple_of(j * SLOTS, 16), SLOTS)
        gates = jnp.concatenate(
            [
                pick[e * SLOTS : (e + 1) * SLOTS].astype(F32) * gin[src, e : e + 1, :]
                for e in range(2)
            ],
            axis=0,
        ).astype(BF)
        both = jnp.concatenate([outs[0, span, :], outs[1, span, :]], axis=0)
        o_buf[src] = lax.dot_general(
            gates, both, (((0,), (0,)), ((), ())), preferred_element_type=F32
        ).astype(BF)

    def output(g, carry):
        lax.fori_loop(0, 2, lambda e, c: (run_output(g, e), c)[1], 0)
        lax.fori_loop(0, 4, lambda j, c: (spread_output(g, j), c)[1], 0)
        return carry

    def pick(g):
        lax.fori_loop(0, 4, lambda j, c: (pick_source(g, j), c)[1], 0)

    OFF = (0, -1, 1, 2)
    R = 58

    def make(source, target, recv, to, index):
        return pltpu.make_async_remote_copy(
            src_ref=source,
            dst_ref=target,
            send_sem=send_sem.at[index],
            recv_sem=recv_sem.at[recv],
            device_id=to,
            device_id_type=MESH,
        )

    first = 80
    bounce = [
        (lambda j=j: make(slab(p_buf, p + OFF[j], q + 2), rb.at[j], R + j, up if j < 2 else down, first + j))
        for j in range(4)
    ]
    to_down = [
        (lambda j=j: make(slab(p_buf, p + OFF[j], q - 1), rc.at[4 + j], R + 8 + j, down, first + 4 + j))
        for j in range(4)
    ]
    to_up = [
        (lambda j=j: make(slab(p_buf, p + OFF[j], q + 1), rc.at[j], R + 4 + j, up, first + 8 + j))
        for j in range(4)
    ]

    def add_bounce(j):
        net.arrived(rb.at[j], R + j)
        target = slab(p_buf, p + OFF[j], q + 1 if j < 2 else q - 1)
        target[...] = (target[...].astype(F32) + rb[j].astype(F32)).astype(BF)

    def step(g, carry):
        @pl.when(g == 2)
        def _():
            for j in range(4):
                tokens_in.arrived(slab(xs, p + OFF[j], q + 2), 12 + j)

        @pl.when(g == 3)
        def _():
            tokens_in.arrived(slab(xs, p + 1, q - 1), 6)
            tokens_in.arrived(slab(xs, p + 2, q - 1), 7)
            tokens_in.arrived(slab(xs, p, q + 1), 8)
            tokens_in.arrived(slab(xs, p - 1, q + 1), 9)
            for j in range(2):
                to_down[j]().start()
                to_up[3 - j]().start()

        @pl.when(g >= 2)
        def _():
            pick(g)

        lax.fori_loop(0, 2, lambda e, c: (run_expert(g, e), c)[1], 0)
        lax.fori_loop(0, 4, lambda j, c: (spread(g, j), c)[1], 0)

        @pl.when(g == 2)
        def _():
            for j in range(4):
                bounce[j]().start()

        return carry

    keep_own.wait()
    pick(0)
    tokens_in.fourth(0)
    tokens_in.fourth(1)
    pick(1)
    net.arrived(weight(0, core, y + 2), 26)
    net.arrived(weight(1, core, y + 2, top), 27)
    net.arrived(weight(1, core, y + 2, bottom), 28)
    net.arrived(weight(2, core, y + 2), 29)
    for a in range(3):
        net.start(weight(a, core, y + 2), weight(a, core, y + 2), 39 + a, sibling)
    for i, ahead_by in enumerate((0, -1, 1, 2)):
        for a in range(3):
            net.arrived(weight(a, 1 - core, y + ahead_by), 30 + 3 * i + a)
    for copy in keep:
        copy.wait()
    lax.fori_loop(0, 4, step, 0)
    net.drain()
    pl.semaphore_signal(free_sem.at[0], inc=1, device_id=sibling, device_id_type=MESH)
    for other in (ahead, behind):
        pl.semaphore_signal(free_sem.at[1], inc=1, device_id=other, device_id_type=MESH)

    def weight_tile(e, t):
        cols = pl.ds(pl.multiple_of(t * 256, 256), 256)
        dims = (((0,), (0,)), ((), ()))
        lhs = rows[e, :, cols]
        dwg[e, cols, :] = lax.dot_general(lhs, gparts[e], dims, preferred_element_type=F32).astype(BF)
        dwu[e, cols, :] = lax.dot_general(lhs, uparts[e], dims, preferred_element_type=F32).astype(BF)
        us[pl.ds(4 * e, 4), :, cols] = (
            lax.dot_general(acts[e], slot_grads[e, :, cols], dims, preferred_element_type=F32)
            .astype(BF)
            .reshape(4, TOK, 256)
        )

    def weight_grads(e):
        lax.fori_loop(0, 4, lambda t, c: (weight_tile(e, t), c)[1], 0)

    weight_grads(1 - core)
    pl.semaphore_wait(free_sem.at[0], 1)
    theirs = us.at[pl.ds(4 * (1 - core), 4)]
    net.start(dwg.at[1 - core], wg.at[0], 76, sibling)
    net.start(dwu.at[1 - core], wu.at[0], 77, sibling)
    net.start(theirs, xs.at[pl.ds(8, 4)], 78, sibling)
    weight_grads(core)
    for j in (3, 1, 2, 0):
        add_bounce(j)
        (to_up if j < 2 else to_down)[j]().start()
    lax.fori_loop(0, 2, output, 0)

    def grad_block(ref, step, rows=None):
        span = pl.ds(pl.multiple_of(wrap(y + step) * TOK, TOK), TOK)
        return ref.at[:, span] if rows is None else ref.at[rows, span]

    def weight_portion(step, which):
        if which == 0:
            return [grad_block(dwg.at[core], step), grad_block(dwu.at[core], step, top)]
        return [grad_block(dwu.at[core], step, bottom), us.at[4 * core + wrap(y + step)]]

    def weight_merge(step):
        accumulate(grad_block(dwg.at[core], step), grad_block(wg.at[0], step))
        accumulate(grad_block(dwu.at[core], step), grad_block(wu.at[0], step))
        accumulate(us.at[4 * core + wrap(y + step)], xs.at[8 + wrap(y + step)])

    hops = (wu.at[1, :, 0:128], wu.at[1, :, 128:256], xs.at[12])
    ring = RingReduce(
        net, 79, ahead, behind, weight_portion,
        ([hops[0], wu.at[1, top, 128:256]], [wu.at[1, bottom, 128:256], hops[2]]), None, None,
    )
    for i, ref in enumerate((wg.at[0], wu.at[0], xs.at[pl.ds(8, 4)])):
        net.arrived(ref, 76 + i)
    weight_merge(2)
    pl.semaphore_wait(free_sem.at[1], 2)
    ring.begin()
    for around in (1, -1, 0):
        weight_merge(around)
    stores = [
        pltpu.make_async_copy(src, dst, local_sem.at[10 + i])
        for i, (src, dst) in enumerate(
            (
                (dwg.at[core], dwg_hbm),
                (dwu.at[core], dwu_hbm),
                (us.at[pl.ds(4 * core, 4)], dwd_hbm),
            )
        )
    ]
    for store in stores:
        store.start()
    lax.fori_loop(2, 4, output, 0)

    def gg_copy(i):
        a, b = lax.div(i, 4), lax.rem(i, 4)
        return pltpu.make_async_remote_copy(
            src_ref=ggo.at[wrap(p + a) * 4 + wrap(q + b)],
            dst_ref=gg_out.at[my_chip],
            send_sem=gg_send.at[i],
            recv_sem=gg_recv.at[wrap(-a) * 4 + wrap(-b)],
            device_id=device(p + a, q + b, y, core),
            device_id_type=MESH,
        )

    def start_gg(i, _):
        gg_copy(i).start()
        return 0

    lax.fori_loop(1, 16, start_gg, 0)
    gg_out[my_chip] = ggo[p * 4 + q]
    o_store = pltpu.make_async_copy(o_buf, o_hbm, local_sem.at[9])
    o_store.start()

    def gather_sum(j):
        net.arrived(rc.at[j], R + 4 + j)
        net.arrived(rc.at[4 + j], R + 8 + j)
        target = slab(p_buf, p + OFF[j], q)
        target[...] = (
            target[...].astype(F32) + rc[j].astype(F32) + rc[4 + j].astype(F32)
        ).astype(BF)

    last = first + 12
    lo, hi = pl.ds(0, 64), pl.ds(64, 64)
    far_slab, next_slab, prev_slab = slab(p_buf, p + 2, q), slab(p_buf, p + 1, q), slab(p_buf, p - 1, q)
    tail = [
        make(far_slab.at[lo], rd.at[lo], R + 12, right, last),
        make(far_slab.at[hi], rd.at[hi], R + 13, left, last + 1),
        make(next_slab.at[hi], re.at[0, hi], R + 14, right, last + 2),
        make(prev_slab.at[lo], re.at[1, lo], R + 15, left, last + 3),
        make(next_slab.at[lo], re.at[0, lo], R + 16, right, last + 4),
        make(prev_slab.at[hi], re.at[1, hi], R + 17, left, last + 5),
    ]
    gather_sum(3)
    tail[0].start()
    tail[1].start()
    gather_sum(2)
    tail[2].start()
    gather_sum(1)
    tail[3].start()
    gather_sum(0)
    net.arrived(rd.at[lo], R + 12)
    next_slab[lo] = (next_slab[lo].astype(F32) + rd[lo].astype(F32)).astype(BF)
    tail[4].start()
    net.arrived(rd.at[hi], R + 13)
    prev_slab[hi] = (prev_slab[hi].astype(F32) + rd[hi].astype(F32)).astype(BF)
    tail[5].start()
    ring.arrived(ring.hops[0], 0)
    ring.arrived(ring.hops[1], 1)
    for i, (src, dst) in enumerate(zip(hops, (hop_g_hbm, hop_u_hbm, hop_d_hbm))):
        stores.append(pltpu.make_async_copy(src, dst, local_sem.at[13 + i]))
        stores[-1].start()
    net.arrived(re.at[0, hi], R + 14)
    net.arrived(re.at[1, lo], R + 15)
    net.arrived(re.at[0, lo], R + 16)
    net.arrived(re.at[1, hi], R + 17)
    grad_out[...] = slab(p_buf, p, q)[...].astype(F32) + re[0].astype(F32) + re[1].astype(F32)

    def take_gg(i, _):
        pltpu.make_async_copy(ggo.at[0], ggo.at[0], gg_recv.at[i]).wait()
        return 0

    lax.fori_loop(1, 16, take_gg, 0)
    for copy in bounce + to_down + to_up:
        copy().wait_send()
    for copy in tail:
        copy.wait_send()

    def drain_small(i, _):
        gate_copy(i).wait_send()
        gg_copy(i).wait_send()
        return 0

    lax.fori_loop(1, 16, drain_small, 0)
    net.drain()
    o_store.wait()
    for store in stores:
        store.wait()
    keep_probs.wait()
    for store in keeps:
        store.wait()


def main(tokens, wq, wk, wv, wo, ga, gm, router, cotangent, routes, lengths, wg, wu, wd):
    cosine, sine = turn_tables()
    any_space = pl.BlockSpec(memory_space=pl.ANY)
    vmem = pl.BlockSpec(memory_space=pltpu.VMEM)
    smem = pl.BlockSpec(memory_space=pltpu.SMEM)
    shape = jax.ShapeDtypeStruct
    dma = pltpu.SemaphoreType.DMA
    slots = 16 * SLOTS
    low = lambda *size: pltpu.VMEM(size, BF)
    return pl.pallas_call(
        main_kernel,
        out_shape=(
            shape((TOK, TOK), F32),
            shape((TOK, D), F32),
            shape((16, 8, TOK), F32),
            shape((TOK, D), F32),
            shape((TOK, D), BF),
            shape((TOK, D), BF),
            shape((TOK, D), BF),
            shape((4, TOK, D), BF),
            shape((8, 2 * TOK, 512), BF),
            shape((16, TOK, D), BF),
            shape((D, FF), BF),
            shape((D, FF), BF),
            shape((4, TOK, D), BF),
            shape((D, TOK), BF),
            shape((D, TOK), BF),
            shape((TOK, D), BF),
        ),
        in_specs=[vmem] + [any_space] * 4 + [vmem] * 5 + [smem] + [any_space] * 5,
        out_specs=(vmem,) * 3 + (any_space,) * 13,
        scratch_shapes=[
            pltpu.VMEM((TOK, D), F32),
            low(TOK, D),
            low(TOK, D),
            low(TOK, D),
            pltpu.VMEM((2, TOK, TOK), F32),
            low(2, D, D),
            low(D, 512),
            low(D, 512),
            low(TOK, D),
            low(4, TOK, D),
            low(8, 2 * TOK, 512),
            pltpu.VMEM((TOK, 512), F32),
            pltpu.VMEM((16, 8, TOK), F32),
            low(16, TOK, D),
            low(16, TOK, D),
            low(2, D, FF),
            low(2, D, FF),
            low(2, FF, D),
            pltpu.VMEM((16, 8, TOK), F32),
            pltpu.VMEM((16, 8, TOK), F32),
            pltpu.VMEM((16, 8, TOK), F32),
            low(16, 2 * SLOTS, TOK),
            low(2, slots, D),
            low(2, slots, D),
            low(2, slots, FF),
            low(2, slots, FF),
            low(2, slots, FF),
            low(2, 4 * SLOTS, D),
            low(2, 4 * SLOTS, D),
            low(16, TOK, D),
            low(16, TOK, D),
            low(4, TOK, D),
            low(8, TOK, D),
            low(TOK, D),
            low(2, TOK, D),
            low(2, D, FF),
            low(2, D, FF),
            dma((100,)),
            dma((83,)),
            dma((16,)),
            dma((16,)),
            dma((16,)),
            dma((16,)),
            dma((23,)),
            pltpu.SemaphoreType.REGULAR((2,)),
        ],
        compiler_params=pltpu.CompilerParams(
            collective_id=1, has_side_effects=True, vmem_limit_bytes=VMEM_BYTES
        ),
        name="main",
    )(
        tokens, wq, wk, wv, wo, ga.reshape(1, D), gm.reshape(1, D), router, cotangent, routes,
        lengths, jnp.asarray(cosine), jnp.asarray(sine), wg, wu, wd,
    )


def accumulate(target, *terms):
    total = target[...].astype(F32)
    for term in terms:
        total += term[...].astype(F32)
    target[...] = total.astype(target.dtype)


class PlaneReduce:
    OFF = (0, -1, 1, 2)

    def __init__(self, net, spot, slabs, rb, rc, rd, re, base):
        self.net, self.spot, self.slabs, self.base = net, spot, slabs, base
        self.rb, self.rc, self.rd, self.re = rb, rc, rd, re
        p, q, y, core = spot
        self.right, self.left = device(p + 1, q, y, core), device(p - 1, q, y, core)
        self.up, self.down = device(p, q + 1, y, core), device(p, q - 1, y, core)

    def slab(self, a, b):
        return slab(self.slabs, self.spot[0] + a, self.spot[1] + b)

    def send(self, source, target, recv, to):
        self.net.start(source, target, self.base + recv, to)

    def arrived(self, ref, recv):
        self.net.arrived(ref, self.base + recv)

    def bounce(self):
        for j in range(4):
            to = self.up if j < 2 else self.down
            self.send(self.slab(self.OFF[j], 2), self.rb.at[j], j, to)

    def to_up(self, j):
        self.send(self.slab(self.OFF[j], 1), self.rc.at[j], 4 + j, self.up)

    def to_down(self, j):
        self.send(self.slab(self.OFF[j], -1), self.rc.at[4 + j], 8 + j, self.down)

    def begin(self):
        self.bounce()
        for j in (3, 2):
            self.to_up(j)
        for j in (0, 1):
            self.to_down(j)

    def middle(self):
        for j in (3, 1, 2, 0):
            self.arrived(self.rb.at[j], j)
            accumulate(self.slab(self.OFF[j], 1 if j < 2 else -1), self.rb.at[j])
            (self.to_up if j < 2 else self.to_down)(j)

    def column(self, j):
        self.arrived(self.rc.at[j], 4 + j)
        self.arrived(self.rc.at[4 + j], 8 + j)
        accumulate(self.slab(self.OFF[j], 0), self.rc.at[j], self.rc.at[4 + j])

    def third(self):
        lo, hi = pl.ds(0, 64), pl.ds(64, 64)
        rd, re = self.rd, self.re
        self.column(3)
        self.send(self.slab(2, 0).at[lo], rd.at[lo], 12, self.right)
        self.send(self.slab(2, 0).at[hi], rd.at[hi], 13, self.left)
        self.column(2)
        self.send(self.slab(1, 0).at[hi], re.at[0, hi], 14, self.right)
        self.column(1)
        self.send(self.slab(-1, 0).at[lo], re.at[1, lo], 15, self.left)

    def fourth(self):
        lo, hi = pl.ds(0, 64), pl.ds(64, 64)
        rd, re = self.rd, self.re
        self.arrived(rd.at[lo], 12)
        accumulate(self.slab(1, 0).at[lo], rd.at[lo])
        self.send(self.slab(1, 0).at[lo], re.at[0, lo], 16, self.right)
        self.arrived(rd.at[hi], 13)
        accumulate(self.slab(-1, 0).at[hi], rd.at[hi])
        self.send(self.slab(-1, 0).at[hi], re.at[1, hi], 17, self.left)
        self.column(0)

    def finish(self):
        lo, hi = pl.ds(0, 64), pl.ds(64, 64)
        re = self.re
        self.arrived(re.at[0, hi], 14)
        self.arrived(re.at[1, lo], 15)
        self.arrived(re.at[0, lo], 16)
        self.arrived(re.at[1, hi], 17)
        return self.slab(0, 0)[...].astype(F32) + re[0].astype(F32) + re[1].astype(F32)


class RingReduce:
    def __init__(self, net, base, ahead, behind, portion, hops, lows, highs):
        self.net, self.base, self.ahead, self.behind = net, base, ahead, behind
        self.portion, self.hops, self.lows, self.highs = portion, hops, lows, highs
        self.n = len(hops[0])

    def send(self, sources, targets, group, to):
        for i, (source, target) in enumerate(zip(sources, targets)):
            self.net.start(source, target, self.base + group * self.n + i, to)

    def arrived(self, refs, group):
        for i, ref in enumerate(refs):
            self.net.arrived(ref, self.base + group * self.n + i)

    def begin(self):
        self.send(self.portion(2, 0), self.hops[0], 0, self.ahead)
        self.send(self.portion(2, 1), self.hops[1], 1, self.behind)

    def direct(self):
        self.send(self.portion(1, 1), self.lows[1], 2, self.ahead)
        self.send(self.portion(-1, 0), self.highs[0], 3, self.behind)

    def middle(self, here=False):
        for which, step, targets, to in (
            (0, 1, self.lows[0], self.ahead),
            (1, -1, self.highs[1], self.behind),
        ):
            if not here:
                self.arrived(self.hops[which], which)
            refs = self.portion(step, which)
            for ref, hop in zip(refs, self.hops[which]):
                accumulate(ref, hop)
            self.send(refs, targets, 4 + which, to)

    def finish(self):
        self.arrived(self.lows[1], 2)
        self.arrived(self.highs[0], 3)
        self.arrived(self.lows[0], 4)
        self.arrived(self.highs[1], 5)


class Total:
    def __init__(self, net, axis, source, result, span, rows, first, piece, buffers, sems):
        self.net, self.axis, self.source, self.result = net, axis, source, result
        self.span, self.rows, self.first, self.piece_size = span, rows, first, piece
        self.theirs, self.low, self.high, self.hop, self.pieces, self.done = buffers
        self.recv, self.plane_send, self.plane_recv, self.back_send, self.back_recv = sems
        dp, y = lax.axis_index("dp"), lax.axis_index("hid")
        self.core = lax.rem(dp, 2)
        self.here = (lax.div(dp, 8), y, lax.rem(lax.div(dp, 2), 4))
        self.sibling = self.at(self.here, 1 - self.core)
        self.plus, self.minus = self.along(1), self.along(-1)
        self.plane = [i for i in range(3) if i != axis]
        self.slab_rows = rows // 4
        half = self.slab_rows // 2
        self.lo, self.hi = pl.ds(0, half), pl.ds(half, half)

    def at(self, spot, on=None):
        spot = [wrap(v) for v in spot]
        return (spot[0] * 8 + spot[2] * 2 + (self.core if on is None else on), spot[1])

    def along(self, step):
        return self.at([self.here[i] + (step if i == self.axis else 0) for i in range(3)])

    def arrived(self, ref, i):
        pltpu.make_async_copy(ref, ref, self.recv.at[i]).wait()

    def put(self, source, target, i, to):
        self.net.put(source, target, self.recv.at[i], to)

    def block(self, ref, step, part=None):
        size = self.slab_rows
        start = self.core * self.span + self.first + wrap(self.here[self.axis] + step) * size
        if part is not None:
            size = size // 2
            start += part * size
        return ref.at[pl.ds(pl.multiple_of(start, size), size)]

    def own(self, step):
        return self.block(self.source, step)

    def begin(self):
        start = (1 - self.core) * self.span + self.first
        theirs = self.source.at[pl.ds(pl.multiple_of(start, self.rows), self.rows)]
        self.put(theirs, self.theirs, 0, self.sibling)

    def merge(self, step):
        size = self.slab_rows
        start = wrap(self.here[self.axis] + step) * size
        accumulate(self.own(step), self.theirs.at[pl.ds(pl.multiple_of(start, size), size)])

    def second(self):
        lo, hi = self.lo, self.hi
        self.arrived(self.theirs, 0)
        self.merge(2)
        far = self.own(2)
        self.put(far.at[lo], self.hop.at[lo], 1, self.plus)
        self.put(far.at[hi], self.hop.at[hi], 2, self.minus)
        self.merge(1)
        self.put(self.own(1).at[hi], self.low.at[hi], 3, self.plus)
        self.merge(-1)
        self.put(self.own(-1).at[lo], self.high.at[lo], 4, self.minus)
        self.merge(0)

    def third(self):
        lo, hi = self.lo, self.hi
        self.arrived(self.hop.at[lo], 1)
        near = self.own(1).at[lo]
        accumulate(near, self.hop.at[lo])
        self.put(near, self.low.at[lo], 5, self.plus)
        self.arrived(self.hop.at[hi], 2)
        near = self.own(-1).at[hi]
        accumulate(near, self.hop.at[hi])
        self.put(near, self.high.at[hi], 6, self.minus)

    def piece(self, ref, u, v):
        rows, cols = self.piece_size
        if self.slab_rows == 4 * rows:
            row, col = u * rows, v * cols
        else:
            row, col = lax.div(u, 2) * rows, (lax.rem(u, 2) * 4 + v) * cols
        return ref.at[
            pl.ds(pl.multiple_of(row, rows), rows), pl.ds(pl.multiple_of(col, cols), cols)
        ]

    def member(self, i):
        u, v = self.plane
        spot = list(self.here)
        spot[u] = wrap(spot[u] + lax.div(i, 4))
        spot[v] = wrap(spot[v] + lax.rem(i, 4))
        return spot[u], spot[v], self.at(spot)

    def mirror(self, i):
        return wrap(-lax.div(i, 4)) * 4 + wrap(-lax.rem(i, 4))

    def mine(self):
        return self.here[self.plane[0]], self.here[self.plane[1]]

    def remote(self, source, target, send, recv, to):
        return pltpu.make_async_remote_copy(
            src_ref=source, dst_ref=target, send_sem=send, recv_sem=recv,
            device_id=to, device_id_type=MESH,
        )

    def piece_copy(self, i):
        u, v, to = self.member(i)
        there = self.mirror(i)
        return self.remote(
            self.piece(self.own(0), u, v),
            self.pieces.at[there],
            self.plane_send.at[i],
            self.plane_recv.at[there],
            to,
        )

    def back_copy(self, i):
        spot = self.piece(self.done, *self.mine())
        return self.remote(
            spot, spot, self.back_send.at[i], self.back_recv.at[self.mirror(i)], self.member(i)[2]
        )

    def each(self, act):
        lax.fori_loop(1, 16, lambda i, carry: (act(i), carry)[1], 0)

    def take(self, sems):
        spot = self.pieces
        self.each(lambda i: pltpu.make_async_copy(spot.at[0], spot.at[0], sems.at[i]).wait())

    def fourth(self):
        lo, hi = self.lo, self.hi
        self.arrived(self.low.at[hi], 3)
        self.arrived(self.high.at[lo], 4)
        self.arrived(self.low.at[lo], 5)
        self.arrived(self.high.at[hi], 6)
        accumulate(self.own(0), self.low, self.high)
        self.each(lambda i: self.piece_copy(i).start())
        self.pieces[0] = self.piece(self.own(0), *self.mine())[...]

    def fifth(self):
        self.take(self.plane_recv)
        total = jnp.sum(self.pieces[...].astype(F32), axis=0)
        self.piece(self.done, *self.mine())[...] = total.astype(self.done.dtype)
        self.each(lambda i: self.back_copy(i).start())

    def sixth(self, sem):
        self.take(self.back_recv)
        spot = self.block(self.result, 0)
        self.put(self.done, spot, 7, self.plus)
        self.put(self.done, spot, 8, self.minus)
        self.put(self.done, spot, 11, self.sibling)
        self.store = pltpu.make_async_copy(self.done, spot, sem)
        self.store.start()

    def seventh(self):
        whole, spot = self.block(self.result, -1), self.block(self.result, -1, 0)
        self.arrived(whole, 7)
        self.put(spot, spot, 9, self.plus)
        self.put(whole, whole, 12, self.sibling)
        whole, spot = self.block(self.result, 1), self.block(self.result, 1, 1)
        self.arrived(whole, 8)
        self.put(spot, spot, 10, self.minus)
        self.put(whole, whole, 13, self.sibling)

    def eighth(self):
        whole = self.block(self.result, 2)
        self.arrived(self.block(self.result, 2, 0), 9)
        self.arrived(self.block(self.result, 2, 1), 10)
        self.put(whole, whole, 14, self.sibling)

    def finish(self):
        for i in range(11, 15):
            self.arrived(self.block(self.result, 0), i)
        self.each(lambda i: self.piece_copy(i).wait_send())
        self.each(lambda i: self.back_copy(i).wait_send())
        self.store.wait()


def back_kernel(
    rows_hbm, gg_ref, x_hbm, gates_ref, hidden_hbm, gm_ref, ga_ref, router_ref, cot_hbm, tok_hbm,
    mixed_hbm, query_hbm, kv_hbm, cos_hbm, sin_hbm, routes_ref, len_ref,
    probs_hbm, wo_hbm, wq_hbm, wk_hbm, wv_hbm, o_hbm, pg_hbm, pu_hbm, pd_hbm,
    hop_g_hbm, hop_u_hbm, hop_d_hbm,
    layer_hbm, input_hbm, gate_hbm, up_hbm, down_hbm, q_hbm, o_sum_hbm, kv_sum_hbm, narrow_hbm,
    layer_ref, input_ref, gate_out, up_out, down_out,
    rows_ref, x_ref, hidden_ref, cot_ref, tok_ref, mixed_ref, query_ref, kv_ref, turns,
    probs, wo, wq, wk, wv, o_buf, rb, rc, rd, re,
    pg, pu, pd, hop_g, hop_u, hop_d, low_g, low_u, low_d, high_g, high_u, high_d,
    grad_mixed, grad_query, grad_kv, kv_hops, kv_low, kv_high,
    dq_out, do_out, dkv_out, narrow_ref,
    their_a, their_b, their_c, their_n, low_a, low_b, low_c, low_n, high_a, high_b, high_c, high_n,
    hop_a, hop_b, hop_c, hop_n, piece_a, piece_b, piece_c, piece_n, done_a, done_b, done_c, done_n,
    send_sem, recv_sem, local_sem, t_recv, plane_send, plane_recv, back_send, back_recv,
):
    p, q, y, core = place()
    spot = (p, q, y, core)
    sibling = (chip_of(p, q, core) * 2 + 1 - core, y)
    ahead, behind = device(p, q, y + 1, core), device(p, q, y - 1, core)
    net = Sends(send_sem, recv_sem)
    first = pl.multiple_of(y * TOK, TOK)
    pairs = (
        (o_hbm, o_buf), (wo_hbm, wo), (probs_hbm, probs), (wq_hbm, wq), (wk_hbm, wk), (wv_hbm, wv),
        (pg_hbm, pg), (pu_hbm, pu), (pd_hbm, pd),
        (hop_g_hbm, hop_g), (hop_u_hbm, hop_u), (hop_d_hbm, hop_d),
        (rows_hbm, rows_ref), (x_hbm, x_ref), (hidden_hbm, hidden_ref), (cot_hbm, cot_ref),
        (tok_hbm, tok_ref), (mixed_hbm, mixed_ref), (query_hbm, query_ref), (kv_hbm, kv_ref),
        (cos_hbm.at[pl.ds(first, TOK)], turns.at[0]), (sin_hbm.at[pl.ds(first, TOK)], turns.at[1]),
    )
    loads = [pltpu.make_async_copy(s, d, local_sem.at[i]) for i, (s, d) in enumerate(pairs)]
    soon = (0, 12, 14, 15, 13, 1, 6, 7, 8, 9, 10, 11)
    for i in soon:
        loads[i].start()
    plane = PlaneReduce(net, spot, o_buf, rb, rc, rd, re, 0)

    def unit(k, axis, source, result, span, rows, first, piece, *buffers):
        sems = [ref.at[k] for ref in (t_recv, plane_send, plane_recv, back_send, back_recv)]
        return Total(net, axis, source, result, span, rows, first, piece, buffers, sems)

    sum_o = unit(
        2, 1, do_out, o_sum_hbm, 512, 512, 0, (32, 256), their_b, low_b, high_b, hop_b, piece_b, done_b
    )
    sum_q = [
        unit(
            h, 2 * h, dq_out, q_hbm, 512, 256, 256 * h, (16, 256),
            *[ref.at[h] for ref in (their_a, low_a, high_a, hop_a, piece_a, done_a)],
        )
        for h in range(2)
    ]
    sum_kv = [
        unit(
            3 + h, 2 * h, dkv_out, kv_sum_hbm, 512, 256, 256 * h, (16, 256),
            *[ref.at[h] for ref in (their_c, low_c, high_c, hop_c, piece_c, done_c)],
        )
        for h in range(2)
    ]
    sum_n = unit(
        5, 0, narrow_ref, narrow_hbm, 64, 64, 0, (8, 128),
        their_n, low_n, high_n, hop_n, piece_n, done_n,
    )
    late = [*sum_kv, sum_n]
    everyone = [*sum_q, sum_o, *late]
    here = sum_o.here
    partners = [
        sum_o.at([here[0] + i, here[1] + j, here[2] + k])
        for i in range(4)
        for j in range(4)
        for k in range(4)
        if (i or j or k) and not (i and j and k)
    ]
    greet(partners + [sibling])
    loads[0].wait()
    plane.begin()
    for load in loads[6:16]:
        load.wait()

    def block(ref, step, rows=None):
        span = pl.ds(pl.multiple_of(wrap(y + step) * TOK, TOK), TOK)
        return ref.at[:, span] if rows is None else ref.at[rows, span]

    def down_block(ref, step):
        return ref.at[pl.ds(pl.multiple_of(wrap(y + step) * TOK, TOK), TOK)]

    top, bottom = pl.ds(0, 512), pl.ds(512, 512)

    def weight_portion(step, which):
        if which == 0:
            return [block(pg, step), block(pu, step, top)]
        return [block(pu, step, bottom), down_block(pd, step)]

    weights = RingReduce(
        net, 24, ahead, behind, weight_portion,
        ([hop_g, hop_u.at[top]], [hop_u.at[bottom], hop_d]),
        ([low_g, low_u.at[top]], [low_u.at[bottom], low_d]),
        ([high_g, high_u.at[top]], [high_u.at[bottom], high_d]),
    )
    weights.direct()
    for i in (17, 18, 19, 20, 21, 16, 2, 3, 4, 5):
        loads[i].start()

    row = lax.broadcasted_iota(jnp.int32, (TOK, 1), 0) + y * TOK
    upstream = jnp.where(row < len_ref[0], cot_ref[...].astype(F32), 0.0)
    gates = gates_ref[...]
    grad_gates = gg_ref[...].reshape(TOK, TOK).T
    grad_logits = gates * (grad_gates - jnp.sum(gates * grad_gates, axis=1, keepdims=True))
    grad_logits = grad_logits.astype(BF)
    wide = lax.dot_general(
        widen(), router_ref[...], (((0,), (0,)), ((), ())), preferred_element_type=F32
    ).astype(BF)
    by_row = (((0,), (0,)), ((), ()))
    by_col = (((1,), (1,)), ((), ()))
    grad_normed = rows_ref[...] + jnp.dot(grad_logits, wide, preferred_element_type=F32)
    hidden = hidden_ref[...]
    scale = root(hidden)
    grad_gain_moe = jnp.sum(grad_normed * hidden * scale, axis=0, keepdims=True)
    scaled = grad_normed * gm_ref[...]
    pull = jnp.mean(scaled * hidden, axis=1, keepdims=True)
    grad_hidden = upstream + scale * scaled - hidden * (scale * scale * scale) * pull
    input_ref[...] = grad_hidden
    low = grad_hidden.astype(BF)
    loads[1].wait()
    grad_mixed[...] = lax.dot_general(low, wo[...], by_col, preferred_element_type=F32).astype(BF)
    narrow_ref[...] = lax.dot_general(grad_logits, x_ref[...], by_row, preferred_element_type=F32)
    named = routed_mask(routes_ref[...], lax.broadcasted_iota(jnp.int32, (TOK, 1), 0))
    counts = jnp.sum(named.T, axis=0, keepdims=True)
    narrow_ref[3:4, :] = grad_gain_moe
    narrow_ref[4:5, :] = jnp.zeros((1, D), F32)
    narrow_ref[4:5, 0:TOK] = counts
    for load in loads[16:]:
        load.wait()
    do_out[...] = lax.dot_general(
        mixed_ref[...], low, by_row, preferred_element_type=F32
    ).astype(BF)
    sum_o.begin()

    cosine, sine = turns[0], turns[1]
    loads[2].wait()

    def attend(c, carry):
        span = pl.ds(pl.multiple_of(c * 128, 128), 128)
        value_span = pl.ds(pl.multiple_of(512 + c * 128, 128), 128)
        keys = kv_ref[:, :, span].reshape(512, 128)
        values = kv_ref[:, :, value_span].reshape(512, 128)
        grad_keys = jnp.zeros((512, 128), F32)
        grad_values = jnp.zeros((512, 128), F32)
        for half in range(2):
            m = c * 2 + half
            mine = pl.ds(pl.multiple_of(m * 128, 128), 128)
            pair = stack_heads(query_ref[:, mine].astype(F32), half)
            grad_pair = stack_heads(grad_mixed[:, mine].astype(F32), half)
            grad_probs = lax.dot_general(grad_pair, values, by_col, preferred_element_type=F32)
            prob = probs[m]
            wide_prob = prob.astype(F32)
            middle = jnp.sum(wide_prob * grad_probs, axis=1, keepdims=True)
            grad_scores = (wide_prob * (grad_probs - middle)).astype(BF)
            back = jnp.dot(grad_scores, keys, preferred_element_type=F32) * SCALE
            grad_query[:, mine] = turn(unstack_heads(back, half), cosine, -sine).astype(BF)
            grad_keys += lax.dot_general(grad_scores, pair, by_row, preferred_element_type=F32)
            grad_values += lax.dot_general(prob, grad_pair, by_row, preferred_element_type=F32)
        grad_kv[:, :, span] = (grad_keys * SCALE).astype(BF).reshape(4, TOK, 128)
        grad_kv[:, :, value_span] = grad_values.astype(BF).reshape(4, TOK, 128)
        return carry

    lax.fori_loop(0, 4, attend, 0)
    lo, hi = pl.ds(0, 64), pl.ds(64, 64)
    sums = RingReduce(
        net, 36, ahead, behind,
        lambda step, which: [grad_kv.at[wrap(y + step), hi if which else lo]],
        ([kv_hops.at[0]], [kv_hops.at[1]]),
        ([kv_low.at[lo]], [kv_low.at[hi]]),
        ([kv_high.at[lo]], [kv_high.at[hi]]),
    )
    sums.begin()
    sums.direct()
    plane.middle()
    tokens = tok_ref[...].astype(F32)
    scale = root(tokens)
    normed = (tokens * scale * ga_ref[...]).astype(BF)
    dq_out[...] = lax.dot_general(
        normed, grad_query[...], by_row, preferred_element_type=F32
    ).astype(BF)
    for one in sum_q:
        one.begin()
    sums.middle()
    for load in loads[3:6]:
        load.wait()
    grad_normed = lax.dot_general(grad_query[...], wq[...], by_col, preferred_element_type=F32)
    for one in sum_q:
        one.second()
    sums.finish()
    both = grad_kv[y].astype(F32) + kv_low[...].astype(F32) + kv_high[...].astype(F32)
    grad_key = jnp.concatenate(
        [turn(both[:, c * 128 : (c + 1) * 128], cosine, -sine) for c in range(4)], axis=1
    ).astype(BF)
    grad_value = both[:, 512:].astype(BF)
    dkv_out[:, 0:512] = lax.dot_general(
        normed, grad_key, by_row, preferred_element_type=F32
    ).astype(BF)
    dkv_out[:, 512:1024] = lax.dot_general(
        normed, grad_value, by_row, preferred_element_type=F32
    ).astype(BF)
    sum_kv[0].begin()
    sum_kv[1].begin()
    sum_o.second()
    grad_normed += lax.dot_general(grad_key, wk[...], by_col, preferred_element_type=F32)
    grad_normed += lax.dot_general(grad_value, wv[...], by_col, preferred_element_type=F32)
    narrow_ref[2:3, :] = jnp.sum(grad_normed * tokens * scale, axis=0, keepdims=True)
    sum_n.begin()
    for one in late:
        one.second()
    scaled = grad_normed * ga_ref[...]
    pull = jnp.mean(scaled * tokens, axis=1, keepdims=True)
    input_ref[...] += scale * scaled - tokens * (scale * scale * scale) * pull
    for one in late:
        one.third()
    for one in sum_q:
        one.third()
    sum_o.third()
    for one in sum_q:
        one.fourth()
    plane.third()
    for one in late:
        one.fourth()
    for one in sum_q:
        one.fifth()
    plane.fourth()
    sum_o.fourth()
    weights.middle(here=True)
    for one in late:
        one.fifth()
    for i, one in enumerate(sum_q):
        one.sixth(local_sem.at[i])
    layer_ref[...] = (hidden_ref[...] + plane.finish()).astype(BF)
    sum_o.fifth()
    for i, one in enumerate(late):
        one.sixth(local_sem.at[3 + i])
    for one in sum_q:
        one.seventh()
    sum_o.sixth(local_sem.at[2])
    weights.finish()
    gate_out[...] = (
        block(pg, 0)[...].astype(F32) + low_g[...].astype(F32) + high_g[...].astype(F32)
    )
    up_out[...] = block(pu, 0)[...].astype(F32) + low_u[...].astype(F32) + high_u[...].astype(F32)
    down_out[...] = (
        down_block(pd, 0)[...].astype(F32) + low_d[...].astype(F32) + high_d[...].astype(F32)
    )
    stores = [
        pltpu.make_async_copy(src, dst, local_sem.at[9 + i])
        for i, (src, dst) in enumerate(
            (
                (layer_ref, layer_hbm),
                (input_ref, input_hbm),
                (gate_out, gate_hbm),
                (up_out, up_hbm),
                (down_out, down_hbm),
            )
        )
    ]
    for store in stores:
        store.start()
    for one in late:
        one.seventh()
    for one in sum_q:
        one.eighth()
    sum_o.seventh()
    for one in late:
        one.eighth()
    sum_o.eighth()
    for one in everyone:
        one.finish()
    net.drain()
    for store in stores:
        store.wait()


def back(operands, arrays):
    any_space = pl.BlockSpec(memory_space=pl.ANY)
    vmem = pl.BlockSpec(memory_space=pltpu.VMEM)
    smem = pl.BlockSpec(memory_space=pltpu.SMEM)
    shape = jax.ShapeDtypeStruct
    dma = pltpu.SemaphoreType.DMA
    low = lambda *size: pltpu.VMEM(size, BF)
    return pl.pallas_call(
        back_kernel,
        out_shape=(
            shape((TOK, D), BF),
            shape((TOK, D), F32),
            shape((D, TOK), F32),
            shape((D, TOK), F32),
            shape((TOK, D), F32),
            shape((D, D), BF),
            shape((D, D), BF),
            shape((D, D), BF),
            shape((TOK, D), F32),
        ),
        in_specs=[
            any_space, vmem, any_space, vmem, any_space, *[vmem] * 3, *[any_space] * 7, vmem, smem,
            *[any_space] * 12,
        ],
        out_specs=(any_space,) * 9,
        scratch_shapes=[
            low(TOK, D),
            pltpu.VMEM((TOK, D), F32),
            pltpu.VMEM((D, TOK), F32),
            pltpu.VMEM((D, TOK), F32),
            pltpu.VMEM((TOK, D), F32),
            pltpu.VMEM((TOK, D), F32),
            low(TOK, D),
            pltpu.VMEM((TOK, D), F32),
            low(TOK, D),
            low(TOK, D),
            low(TOK, D),
            low(TOK, D),
            low(4, TOK, D),
            pltpu.VMEM((2, TOK, TOK), F32),
            low(8, 2 * TOK, 512),
            low(D, D),
            low(D, D),
            low(D, 512),
            low(D, 512),
            low(16, TOK, D),
            low(4, TOK, D),
            low(8, TOK, D),
            low(TOK, D),
            low(2, TOK, D),
            low(D, FF),
            low(D, FF),
            low(FF, D),
            low(D, TOK),
            low(D, TOK),
            low(TOK, D),
            low(D, TOK),
            low(D, TOK),
            low(TOK, D),
            low(D, TOK),
            low(D, TOK),
            low(TOK, D),
            low(TOK, D),
            low(TOK, D),
            low(4, TOK, D),
            low(2, 64, D),
            low(TOK, D),
            low(TOK, D),
            low(D, D),
            low(D, D),
            low(D, D),
            pltpu.VMEM((TOK, D), F32),
            low(2, 256, D),
            low(512, D),
            low(2, 256, D),
            pltpu.VMEM((64, D), F32),
            low(2, 64, D),
            low(128, D),
            low(2, 64, D),
            pltpu.VMEM((16, D), F32),
            low(2, 64, D),
            low(128, D),
            low(2, 64, D),
            pltpu.VMEM((16, D), F32),
            low(2, 64, D),
            low(128, D),
            low(2, 64, D),
            pltpu.VMEM((16, D), F32),
            low(2, 16, 16, 256),
            low(16, 32, 256),
            low(2, 16, 16, 256),
            pltpu.VMEM((16, 8, 128), F32),
            low(2, 64, D),
            low(128, D),
            low(2, 64, D),
            pltpu.VMEM((16, D), F32),
            dma((160,)),
            dma((42,)),
            dma((22,)),
            dma((6, 15)),
            dma((6, 16)),
            dma((6, 16)),
            dma((6, 16)),
            dma((6, 16)),
        ],
        compiler_params=pltpu.CompilerParams(
            collective_id=4, has_side_effects=True, vmem_limit_bytes=VMEM_BYTES
        ),
        name="back",
    )(*operands, *arrays)


def results_kernel(
    q_ref, o_ref, kv_ref, n_ref, layer_ref, input_ref, gate_ref, up_ref, down_ref,
    q_out, o_out, k_out, v_out, router_out, one_out, two_out, count_out,
    layer_out, input_out, gate_out, up_out, down_out,
):
    layer_out[...] = layer_ref[...]
    input_out[...] = input_ref[...]
    gate_out[0] = gate_ref[...]
    up_out[0] = up_ref[...]
    down_out[0] = down_ref[...]
    q_out[...] = q_ref[...].astype(F32)
    o_out[...] = o_ref[...].astype(F32)
    k_out[...] = kv_ref[:, 0:512].astype(F32)
    v_out[...] = kv_ref[:, 512:1024].astype(F32)

    @pl.when(pl.program_id(0) == 0)
    def _():
        for j in range(16):
            router_out[2 * j : 2 * j + 2, :] = n_ref[8 * j : 8 * j + 2, :]
        one_out[...] = n_ref[2:3, :]
        two_out[...] = n_ref[3:4, :]
        count_out[...] = n_ref[4:5, 0:EXPERTS].astype(jnp.int32)


def results(q, o, kv, narrow, *own):
    rows = 512
    some = rows * TOK // D
    first = lambda *size: pl.BlockSpec((1, *size), lambda i: (0, i, 0))
    block = lambda width: pl.BlockSpec((rows, width), lambda i: (i, 0))
    whole = lambda *size: pl.BlockSpec(size, lambda i: (0, 0))
    shape = jax.ShapeDtypeStruct
    return pl.pallas_call(
        results_kernel,
        grid=(D // rows,),
        out_shape=(
            shape((D, D), F32),
            shape((D, D), F32),
            shape((D, 512), F32),
            shape((D, 512), F32),
            shape((EXPERTS, D), F32),
            shape((1, D), F32),
            shape((1, D), F32),
            shape((1, EXPERTS), jnp.int32),
            shape((TOK, D), BF),
            shape((TOK, D), F32),
            shape((1, D, TOK), F32),
            shape((1, D, TOK), F32),
            shape((1, TOK, D), F32),
        ),
        in_specs=[
            block(D), block(D), block(D), whole(TOK, D),
            pl.BlockSpec((some, D), lambda i: (i, 0)),
            pl.BlockSpec((some, D), lambda i: (i, 0)),
            block(TOK), block(TOK),
            pl.BlockSpec((some, D), lambda i: (i, 0)),
        ],
        out_specs=(
            block(D), block(D), block(512), block(512),
            whole(EXPERTS, D), whole(1, D), whole(1, D), whole(1, EXPERTS),
            pl.BlockSpec((some, D), lambda i: (i, 0)),
            pl.BlockSpec((some, D), lambda i: (i, 0)),
            first(rows, TOK), first(rows, TOK), first(some, D),
        ),
        compiler_params=pltpu.CompilerParams(vmem_limit_bytes=VMEM_BYTES),
        name="results",
    )(q, o, kv, narrow, *own)


def shards(
    tokens,
    w_query,
    w_key,
    w_value,
    w_output,
    gain_attn,
    gain_moe,
    router,
    w_gate,
    w_up,
    w_down,
    cotangent,
    routes,
    lengths,
):
    (
        gates, grad_rows, grad_gates, hidden, x, mixed, query, kv, probs, out_parts, part_gate,
        part_up, part_down, *far_parts,
    ) = main(
        tokens, w_query, w_key, w_value, w_output, gain_attn, gain_moe, router.T, cotangent,
        routes.T, lengths, w_gate, w_up, w_down,
    )
    cosine, sine = turn_tables()
    layer_out, grad_input, grad_gate, grad_up, grad_down, sum_q, sum_o, sum_kv, narrow = back(
        (
            grad_rows, grad_gates, x, gates, hidden, gain_moe.reshape(1, D),
            gain_attn.reshape(1, D), router.T, cotangent, tokens, mixed, query, kv,
            jnp.asarray(cosine), jnp.asarray(sine), routes.T, lengths,
        ),
        (
            probs, w_output, w_query, w_key, w_value, out_parts, part_gate, part_up,
            part_down.reshape(FF, D),
            *far_parts,
        ),
    )
    (
        grad_q, grad_o, grad_k, grad_v, grad_router, gain_one, gain_two, counts,
        layer_out, grad_input, grad_gate, grad_up, grad_down,
    ) = results(
        sum_q, sum_o, sum_kv, narrow, layer_out, grad_input, grad_gate, grad_up, grad_down
    )
    return (
        layer_out,
        grad_input,
        grad_q,
        grad_k,
        grad_v,
        grad_o,
        gain_one.reshape(D),
        gain_two.reshape(D),
        grad_router.T,
        grad_gate,
        grad_up,
        grad_down,
        counts.reshape(EXPERTS),
    )


def solution(mesh):
    in_specs = (
        P(("dp", "hid"), None),
        P(),
        P(),
        P(),
        P(),
        P(),
        P(),
        P(),
        P("dp", None, "hid"),
        P("dp", None, "hid"),
        P("dp", "hid", None),
        P(("dp", "hid"), None),
        P(("dp", "hid"), None),
        P("dp"),
    )
    out_specs = (
        P(("dp", "hid"), None),
        P(("dp", "hid"), None),
        P(),
        P(),
        P(),
        P(),
        P(),
        P(),
        P(),
        P("dp", None, "hid"),
        P("dp", None, "hid"),
        P("dp", "hid", None),
        P(),
    )
    return jax.shard_map(shards, mesh=mesh, in_specs=in_specs, out_specs=out_specs, check_vma=False)
```
